32 devices in a mesh: dp: 8 (over z, y), blk: 4 (over x, core).
Axes of the slice: x: 2, y: 2, z: 4, core: 2. Of those that a mesh axis runs over, the one named last changes fastest.
Arguments:
- long_input: bfloat16 [24, 512, 768], P('dp', 'blk'), may hold values from -6 to 6
- short_input: bfloat16 [8, 4, 8, 128, 768], P('dp', 'blk'), may hold values from -6 to 6
- long_cotan: bfloat16 [24, 512, 768], P('dp', 'blk'), may hold values from -6 to 6
- short_cotan: bfloat16 [8, 4, 8, 128, 768], P('dp', 'blk'), may hold values from -6 to 6
- live_slots: int32 [8, 4], P('dp', 'blk'), may hold values from 1 to 8, as said below
- w_project: bfloat16 [768, 1152], replicated, may hold values from -0.3125 to 0.3125
- bias_query: bfloat16 [384], replicated, may hold values from -3 to 3
- bias_value: bfloat16 [384], replicated, may hold values from -3 to 3
- depth_kernel: bfloat16 [9, 768], replicated, may hold values from -2 to 2
- w_point: bfloat16 [768, 384], replicated, may hold values from -0.21875 to 0.21875
- bias_point: bfloat16 [384], replicated, may hold values from -3 to 3
- w_span: bfloat16 [384, 54], replicated, may hold values from -0.3125 to 0.3125
- bias_span: bfloat16 [54], replicated, may hold values from -3 to 3
- w_unfold: bfloat16 [768, 384], replicated, may hold values from -0.21875 to 0.21875
- bias_unfold: bfloat16 [384], replicated, may hold values from -3 to 3
- w_output: bfloat16 [768, 768], replicated, may hold values from -0.875 to 0.875
- bias_output: bfloat16 [768], replicated, may hold values from -3 to 3
- gain_first: bfloat16 [768], replicated, may hold values from 0.25 to 1.75
- shift_first: bfloat16 [768], replicated, may hold values from -2 to 2
- w_inner: bfloat16 [2, 384, 1536], replicated, may hold values from -0.3125 to 0.3125
- bias_inner: bfloat16 [3072], replicated, may hold values from -3 to 3
- w_outer: bfloat16 [2, 1536, 384], replicated, may hold values from -0.15625 to 0.15625
- bias_outer: bfloat16 [768], replicated, may hold values from -3 to 3
- gain_second: bfloat16 [768], replicated, may hold values from 0.25 to 1.75
- shift_second: bfloat16 [768], replicated, may hold values from -2 to 2
Outputs:
- long_output: bfloat16 [24, 512, 768], P('dp', 'blk')
- short_output: bfloat16 [8, 4, 8, 128, 768], P('dp', 'blk')
- long_grad: float32 [24, 512, 768], P('dp', 'blk')
- short_grad: float32 [8, 4, 8, 128, 768], P('dp', 'blk')
- w_project_grad: float32 [768, 1152], replicated
- bias_query_grad: float32 [384], replicated
- bias_value_grad: float32 [384], replicated
- depth_kernel_grad: float32 [9, 768], replicated
- w_point_grad: float32 [768, 384], replicated
- bias_point_grad: float32 [384], replicated
- w_span_grad: float32 [384, 54], replicated
- bias_span_grad: float32 [54], replicated
- w_unfold_grad: float32 [768, 384], replicated
- bias_unfold_grad: float32 [384], replicated
- w_output_grad: float32 [768, 768], replicated
- bias_output_grad: float32 [768], replicated
- gain_first_grad: float32 [768], replicated
- shift_first_grad: float32 [768], replicated
- w_inner_grad: float32 [2, 384, 1536], replicated
- bias_inner_grad: float32 [3072], replicated
- w_outer_grad: float32 [2, 1536, 384], replicated
- bias_outer_grad: float32 [768], replicated
- gain_second_grad: float32 [768], replicated
- shift_second_grad: float32 [768], replicated
The draws below stay inside these ranges and needn't reach their ends.
Inputs may be any that keep to these rules, and one draw needn't show every extreme that they name: Device (i, j) uses its short row slots 0 to live_slots[i, j] - 1; in every draw some device uses all 8.
All inputs are finite; a program needn't handle non-finite values.
Results may differ from the reference program's by a relative error of at most 0.014.
The reference program's roundings to bfloat16 on the way count: a program that leaves them out, or rounds other values in their place, can miss the bound.
Values may be sent and summed in bfloat16 or wider, within the bound.
A program may use at most 192 MiB of HBM per device.

```python
import jax
import jax.numpy as jnp
from jax import lax

D = 768
FF = 3072
HEADS = 6
HEAD = 64
KERNEL = 9
GROUPS = 2
LONG_LEN = 512
SHORT_LEN = 128
LONG_DEV = 3
SLOTS = 8
ALL = 384
LONG_ROWS = 24
N_DP = 8
N_BLK = 4


def draw_live_slots(key, part):
    key = jax.random.fold_in(key, 11)
    count_key, pick_key = jax.random.split(key)
    row_counts = jax.random.randint(count_key, (N_DP * N_BLK,), 1, SLOTS + 1)
    full_device = jax.random.randint(pick_key, (), 0, N_DP * N_BLK)
    flattened = jnp.where(jnp.arange(N_DP * N_BLK) == full_device, SLOTS, row_counts)
    return flattened.reshape(N_DP, N_BLK).astype(jnp.int32)


def block_scale(key, dims, cuts, smallest, top_value):
    gain, own = 1.0, jax.random.fold_in(key, 6)
    for dim, shards_of in cuts:
        steps = jnp.exp(jax.random.uniform(jax.random.fold_in(own, dim), (shards_of,), jnp.float32, smallest / len(cuts), top_value / len(cuts)))
        gain = gain * jnp.repeat(steps, dims[dim] // shards_of).reshape([-1 if axis == dim else 1 for axis in range(len(dims))])
    return gain


def gaussian(stream_key, shape, scale, bound, cuts=(), held_as=jnp.bfloat16):
    loudness = block_scale(stream_key, shape, cuts, -0.22, 0.18) if cuts else 1.0
    result = jax.random.normal(stream_key, shape, jnp.float32) * scale * loudness
    return jnp.minimum(jnp.maximum(result, -bound), bound).astype(held_as)


def setup_inputs(seed: int = 0) -> dict:
    key_list = jax.random.split(jax.random.key(seed), 26)
    long_input = gaussian(key_list[0], (LONG_ROWS, LONG_LEN, D), 1.0, 6.0, ((0, 8), (1, 4)))
    short_input = gaussian(key_list[1], (N_DP, N_BLK, SLOTS, SHORT_LEN, D), 1.0, 6.0, ((0, 8), (1, 4)))
    long_cotan = gaussian(key_list[2], (LONG_ROWS, LONG_LEN, D), 1.0, 6.0, ((0, 8), (1, 4)))
    short_cotan = gaussian(key_list[3], (N_DP, N_BLK, SLOTS, SHORT_LEN, D), 1.0, 6.0, ((0, 8), (1, 4)))
    live_slots = draw_live_slots(jax.random.fold_in(key_list[25], 71), 0)
    w_project = gaussian(key_list[5], (D, 3 * ALL), (D // 2) ** -0.5, 0.3125)
    bias_query = gaussian(key_list[6], (ALL,), 0.5, 3.0)
    bias_value = gaussian(key_list[7], (ALL,), 0.5, 3.0)
    depth_kernel = gaussian(key_list[8], (KERNEL, D), KERNEL ** -0.5, 2.0)
    w_point = gaussian(key_list[9], (D, ALL), D ** -0.5, 0.21875)
    bias_point = gaussian(key_list[10], (ALL,), 0.5, 3.0)
    w_span = gaussian(key_list[11], (ALL, HEADS * KERNEL), ALL ** -0.5, 0.3125)
    bias_span = gaussian(key_list[12], (HEADS * KERNEL,), 0.5, 3.0)
    w_unfold = gaussian(key_list[13], (D, ALL), D ** -0.5, 0.21875)
    bias_unfold = gaussian(key_list[14], (ALL,), 0.5, 3.0)
    w_output = gaussian(key_list[15], (D, D), (D // 16) ** -0.5, 0.875)
    bias_output = gaussian(key_list[16], (D,), 0.5, 3.0)
    gain_first = jnp.clip(1.0 + 0.15 * jax.random.normal(key_list[17], (D,), jnp.float32), 0.25, 1.75).astype(jnp.bfloat16)
    shift_first = gaussian(key_list[18], (D,), 0.3, 2.0)
    w_inner = gaussian(key_list[19], (GROUPS, D // GROUPS, FF // GROUPS), (D // GROUPS) ** -0.5, 0.3125)
    bias_inner = gaussian(key_list[20], (FF,), 0.5, 3.0)
    w_outer = gaussian(key_list[21], (GROUPS, FF // GROUPS, D // GROUPS), (FF // GROUPS) ** -0.5, 0.15625)
    bias_outer = gaussian(key_list[22], (D,), 0.5, 3.0)
    gain_second = jnp.clip(1.0 + 0.15 * jax.random.normal(key_list[23], (D,), jnp.float32), 0.25, 1.75).astype(jnp.bfloat16)
    shift_second = gaussian(key_list[24], (D,), 0.3, 2.0)
    return {"long_input": long_input, "short_input": short_input, "long_cotan": long_cotan, "short_cotan": short_cotan, "live_slots": live_slots, "w_project": w_project, "bias_query": bias_query, "bias_value": bias_value, "depth_kernel": depth_kernel, "w_point": w_point, "bias_point": bias_point, "w_span": w_span, "bias_span": bias_span, "w_unfold": w_unfold, "bias_unfold": bias_unfold, "w_output": w_output, "bias_output": bias_output, "gain_first": gain_first, "shift_first": shift_first, "w_inner": w_inner, "bias_inner": bias_inner, "w_outer": w_outer, "bias_outer": bias_outer, "gain_second": gain_second, "shift_second": shift_second}


@jax.custom_vjp
def low(v):
    return lax.optimization_barrier(v.astype(jnp.bfloat16)).astype(jnp.float32)

@jax.custom_vjp
def low_back(v):
    return v

def low_keep(v):
    return (low(v), None)

def low_pass(kept, grad):
    return (grad,)

def back_keep(v):
    return (v, None)

def back_low(kept, grad):
    return (low(grad),)
low.defvjp(low_keep, low_pass)
low_back.defvjp(back_keep, back_low)
highest = lax.Precision.HIGHEST

def rounded(value_in):
    return low(low_back(value_in))

def matmul(left_side, right_side):
    return jnp.matmul(left_side, right_side, precision=highest)

def layer_norm(inputs, gain_vector, shift_vector):
    centre = inputs - lax.optimization_barrier(jnp.mean(inputs, axis=-1, keepdims=True))
    spread = lax.optimization_barrier(jnp.mean(centre * centre, axis=-1, keepdims=True))
    return centre * lax.rsqrt(spread + 1e-12) * gain_vector + shift_vector

def forward(params, tokens):
    w_project, bias_query, bias_value, depth_kernel, w_point, bias_point, w_span, bias_span, w_unfold, bias_unfold, w_output, bias_output, gain_first, shift_first, w_inner, bias_inner, w_outer, bias_outer, gain_second, shift_second = params
    count_rows, seq_length = (tokens.shape[0], tokens.shape[1])
    half_width = (KERNEL - 1) // 2
    score_scale = HEAD ** (-0.5)
    head_shape = (count_rows, seq_length, HEADS, HEAD)
    project = matmul(tokens, w_project)
    queries = rounded(project[..., :ALL] + bias_query)
    key_rows = rounded(project[..., ALL:2 * ALL])
    value_rows = rounded(project[..., 2 * ALL:] + bias_value)
    scores = low_back(jnp.einsum('rqhd,rkhd->rhqk', queries.reshape(head_shape), key_rows.reshape(head_shape), precision=highest) * score_scale)
    weights = low(jax.nn.softmax(scores, axis=-1))
    context = rounded(jnp.einsum('rhqk,rkhd->rqhd', weights, value_rows.reshape(head_shape), precision=highest).reshape(count_rows, seq_length, ALL))
    padded = jnp.pad(tokens, ((0, 0), (half_width, half_width), (0, 0)))
    depth_sum = low(sum((depth_kernel[offset] * padded[:, offset:offset + seq_length] for offset in range(KERNEL))))
    key_conv = low_back(matmul(depth_sum, w_point) + bias_point)
    span_rows = low(key_conv * queries)
    logits = low_back(matmul(span_rows, w_span) + bias_span).reshape(count_rows, seq_length, HEADS, KERNEL)
    kernel = jax.nn.softmax(logits, axis=-1)
    unfold_rows = low_back(matmul(tokens, w_unfold) + bias_unfold)
    unfold_pad = jnp.pad(unfold_rows, ((0, 0), (half_width, half_width), (0, 0))).reshape(count_rows, seq_length + 2 * half_width, HEADS, HEAD)
    conv_rows = sum((kernel[:, :, :, offset, None] * unfold_pad[:, offset:offset + seq_length] for offset in range(KERNEL)))
    conv_context = rounded(conv_rows.reshape(count_rows, seq_length, ALL))
    mixed_rows = jnp.concatenate([context, conv_context], axis=-1)
    attended = low_back(matmul(mixed_rows, w_output) + bias_output)
    first_norm = layer_norm(attended + tokens, gain_first, shift_first)
    grouped = low(first_norm).reshape(count_rows, seq_length, GROUPS, D // GROUPS)
    inner_sum = low_back(jnp.einsum('rlgi,gio->rlgo', grouped, w_inner, precision=highest).reshape(count_rows, seq_length, FF) + bias_inner)
    active = low(jax.nn.gelu(inner_sum, approximate=False)).reshape(count_rows, seq_length, GROUPS, FF // GROUPS)
    outer_sum = low_back(jnp.einsum('rlgi,gio->rlgo', active, w_outer, precision=highest).reshape(count_rows, seq_length, D) + bias_outer)
    return layer_norm(outer_sum + first_norm, gain_second, shift_second)

def reference(long_input, short_input, long_cotan, short_cotan, live_slots, w_project, bias_query, bias_value, depth_kernel, w_point, bias_point, w_span, bias_span, w_unfold, bias_unfold, w_output, bias_output, gain_first, shift_first, w_inner, bias_inner, w_outer, bias_outer, gain_second, shift_second):
    params = tuple((weight_in.astype(jnp.float32) for weight_in in (w_project, bias_query, bias_value, depth_kernel, w_point, bias_point, w_span, bias_span, w_unfold, bias_unfold, w_output, bias_output, gain_first, shift_first, w_inner, bias_inner, w_outer, bias_outer, gain_second, shift_second)))
    long_rows = long_input.astype(jnp.float32).reshape(N_DP, LONG_DEV, LONG_LEN, D)
    long_seed = long_cotan.astype(jnp.float32).reshape(N_DP, LONG_DEV, LONG_LEN, D)
    short_rows = short_input.astype(jnp.float32).reshape(N_DP, N_BLK * SLOTS, SHORT_LEN, D)
    live_mask = (jnp.arange(SLOTS, dtype=jnp.int32)[None, None, :] < live_slots[:, :, None]).astype(jnp.float32).reshape(N_DP, N_BLK * SLOTS)
    short_seed = short_cotan.astype(jnp.float32).reshape(N_DP, N_BLK * SLOTS, SHORT_LEN, D) * live_mask[:, :, None, None]

    def both_kinds(params_in, long_part, short_part):
        return (forward(params_in, long_part), forward(params_in, short_part))

    def scan_step(totals, items):
        long_part, long_cot, short_part, short_cot = items
        outputs, pull_back = jax.vjp(both_kinds, params, long_part, short_part)
        param_grads, long_part_grad, short_part_grad = pull_back((long_cot, short_cot))
        totals = jax.tree.map(jnp.add, totals, param_grads)
        return (totals, (outputs[0].astype(jnp.bfloat16), outputs[1].astype(jnp.bfloat16), long_part_grad, short_part_grad))
    zero_grads = jax.tree.map(jnp.zeros_like, params)
    totals, results = lax.scan(scan_step, zero_grads, (long_rows, long_seed, short_rows, short_seed))
    long_output = results[0].reshape(LONG_ROWS, LONG_LEN, D)
    short_output = results[1].reshape(N_DP, N_BLK, SLOTS, SHORT_LEN, D)
    long_grad = results[2].reshape(LONG_ROWS, LONG_LEN, D)
    short_grad = results[3].reshape(N_DP, N_BLK, SLOTS, SHORT_LEN, D)
    return (long_output, short_output, long_grad, short_grad, totals[0], totals[1], totals[2], totals[3], totals[4], totals[5], totals[6], totals[7], totals[8], totals[9], totals[10], totals[11], totals[12], totals[13], totals[14], totals[15], totals[16], totals[17], totals[18], totals[19])
```

```python
import functools

import jax
import jax.numpy as jnp
import numpy as np
from jax import lax
from jax.experimental import pallas as pl
from jax.experimental.pallas import tpu as pltpu
from jax.sharding import PartitionSpec as P

D = 768
FF = 3072
HEADS = 6
HEAD = 64
KERNEL = 9
GROUPS = 2
ALL = 384
PAIRS = 3
TAPS = HEADS * KERNEL
HALF = KERNEL // 2

F32 = jnp.float32
BF = jnp.bfloat16
ROOT_HALF = 0.7071067811865476
DENSITY = 0.3989422804014327
VMEM_BYTES = 58 * 1024 * 1024


def nn(a, b):
    return lax.dot_general(a, b, (((1,), (0,)), ((), ())), preferred_element_type=F32)


def nt(a, b):
    return lax.dot_general(a, b, (((1,), (1,)), ((), ())), preferred_element_type=F32)


def tn(a, b):
    return lax.dot_general(a, b, (((0,), (0,)), ((), ())), preferred_element_type=F32)


def tap_tables():
    perm = np.zeros((128, 128), np.float32)
    spread = np.zeros((256, PAIRS * KERNEL * 128), np.float32)
    for h in range(HEADS):
        for j in range(KERNEL):
            lane = j * HEADS + h
            perm[h * KERNEL + j, lane] = 1
            perm[h * KERNEL + j, TAPS + lane] = 1
            start = ((h // 2) * KERNEL + j) * 128 + (h % 2) * HEAD
            spread[lane, start : start + HEAD] = 1
            spread[128 + lane, start : start + HEAD] = 1
    return perm.astype(jnp.bfloat16), spread.astype(jnp.bfloat16)


def window(values, op):
    left = lambda v, n: pltpu.roll(v, 128 - n, 1)
    one = op(values, left(values, 6))
    two = op(one, left(one, 12))
    four = op(two, left(two, 24))
    return op(four, left(values, 48))


def window_sum(values):
    return window(values + pltpu.roll(values, TAPS, 1), jnp.add)


def head_stack(rows, low_half):
    zero = jnp.zeros_like(rows)
    return jnp.concatenate(
        [jnp.where(low_half, rows, zero), jnp.where(low_half, zero, rows)], axis=0
    )


def two_parts(values):
    high = values.astype(BF)
    rest = (values - high.astype(F32)).astype(BF)
    return jnp.concatenate([high, rest], axis=1)


def fill_ends(xp, x_refs, rows, sides):
    if sides is None:
        zero = jnp.zeros((8, D), F32)
        xp[0:8, :] = zero
        xp[8 + rows : 16 + rows, :] = zero
    else:
        lower, upper = sides
        xp[0:8, :] = x_refs[1][0, rows - 16 :, :].astype(F32)[8:] * lower
        xp[8 + rows : 16 + rows, :] = x_refs[-1][0, :16, :].astype(F32)[:8] * upper
    xp[8 : 8 + rows, :] = x_refs[0][0].astype(F32)


def row_sides():
    place = lax.axis_index("blk")
    count = lax.axis_size("blk")
    return (place > 0).astype(F32), (place < count - 1).astype(F32)


def pre_body(n_x, *refs):
    x_refs = refs[:n_x]
    vec, w_project, w_point, w_span, w_unfold, spread, perm = refs[n_x : n_x + 7]
    q_out, k_out, v_out, p_out, kc_out, ker_out, dl_out, up_out, mix_out = refs[n_x + 7 : n_x + 16]
    (xp,) = refs[n_x + 16 :]
    rows = x_refs[0].shape[1]
    is_long = n_x > 1
    sides = row_sides() if is_long else None
    x = x_refs[0][0]
    fill_ends(xp, x_refs, rows, sides)
    bias_query = vec[0:1, :ALL]
    bias_value = vec[0:1, ALL:]
    if is_long:
        q = (nn(x, w_project[:, :ALL]) + bias_query).astype(BF)
        for i in range(n_x):
            both = nn(x_refs[i][0], w_project[:, ALL:])
            k_out[0, i * rows : (i + 1) * rows, :] = both[:, :ALL].astype(BF)
            v_out[0, i * rows : (i + 1) * rows, :] = (both[:, ALL:] + bias_value).astype(BF)
    else:
        both = nn(x, w_project[...])
        q = (both[:, :ALL] + bias_query).astype(BF)
        k_out[0] = both[:, ALL : 2 * ALL].astype(BF)
        v_out[0] = (both[:, 2 * ALL :] + bias_value).astype(BF)
    q_out[0] = q

    for c in range(D // 128):
        cols = slice(c * 128, (c + 1) * 128)
        total = vec[12:13, cols] * xp[4 : 4 + rows, cols]
        for j in range(1, KERNEL):
            total += vec[12 + j : 13 + j, cols] * xp[4 + j : 4 + j + rows, cols]
        dl_out[0, :, cols] = total.astype(BF)
    key_conv = nn(dl_out[0], w_point[...]) + vec[1:2, :ALL]
    kc_out[0] = key_conv
    span = (key_conv * q.astype(F32)).astype(BF)
    span_weights = nn(w_span[...], perm[:TAPS, :]).astype(BF)
    span_bias = nn(vec[16:24, :128].astype(BF), perm[...])[5:6]
    logits = nn(span, span_weights) + span_bias
    lane = lax.broadcasted_iota(jnp.int32, (rows, 128), 1)
    raised = jnp.where(lane < TAPS, jnp.exp(logits - window(logits, jnp.maximum)), 0.0)
    kernel = jnp.where(lane < TAPS, raised / window_sum(raised), 0.0)
    ker_out[0] = kernel

    bias_unfold = vec[1:2, ALL:]
    up_out[0, 8 : 8 + rows, :] = nn(x, w_unfold[...]) + bias_unfold
    if is_long:
        lower, upper = sides
        ends = jnp.concatenate([x_refs[1][0, rows - 16 :, :], x_refs[-1][0, :16, :]], axis=0)
        unfold_ends = nn(ends, w_unfold[...]) + bias_unfold
        up_out[0, 0:8, :] = unfold_ends[8:16] * lower
        up_out[0, 8 + rows : 16 + rows, :] = unfold_ends[16:24] * upper
    else:
        zero = jnp.zeros((8, ALL), F32)
        up_out[0, 0:8, :] = zero
        up_out[0, 8 + rows : 16 + rows, :] = zero

    low_half = lax.broadcasted_iota(jnp.int32, (1, 128), 1) < HEAD
    parts = two_parts(kernel)
    scaled = q * jnp.asarray(HEAD ** (-0.5), BF)
    keys = k_out.shape[1]
    for p in range(PAIRS):
        cols = slice(p * 128, (p + 1) * 128)
        wide = nn(parts, spread[:, p * KERNEL * 128 : (p + 1) * KERNEL * 128])
        total = wide[:, :128] * up_out[0, 4 : 4 + rows, cols]
        for j in range(1, KERNEL):
            total += wide[:, j * 128 : (j + 1) * 128] * up_out[0, 4 + j : 4 + j + rows, cols]
        mix_out[0, :, ALL + p * 128 : ALL + (p + 1) * 128] = total.astype(BF)

        scores = nt(head_stack(k_out[0, :, cols], low_half), scaled[:, cols])
        for half in range(2):
            part = scores[half * keys : (half + 1) * keys]
            top = jnp.max(part, axis=0, keepdims=True)
            grown = jnp.exp(part - top)
            share = 1.0 / jnp.sum(grown, axis=0, keepdims=True)
            p_out[0, p, half * keys : (half + 1) * keys, :] = (grown * share).astype(BF)
        context = tn(head_stack(v_out[0, :, cols], low_half), p_out[0, p])
        mix_out[0, :, cols] = context.astype(BF).T


def block_spec(shape, index_map):
    return pl.BlockSpec(shape, index_map)


def fixed(array):
    zeros = (0,) * array.ndim
    return pl.BlockSpec(array.shape, lambda *_: zeros, pipeline_mode=pl.Buffered(1))


def per_row(*shape):
    zeros = (0,) * len(shape)
    return pl.BlockSpec((1, *shape), lambda i: (i, *zeros))


def params(**more):
    return pltpu.CompilerParams(vmem_limit_bytes=VMEM_BYTES, **more)


def pre_call(xs, consts):
    count, rows = xs[0].shape[0], xs[0].shape[1]
    keys = rows * len(xs)
    shapes = [
        ((rows, ALL), BF),
        ((keys, ALL), BF),
        ((keys, ALL), BF),
        ((PAIRS, 2 * keys, rows), BF),
        ((rows, ALL), F32),
        ((rows, 128), F32),
        ((rows, D), BF),
        ((rows + 16, ALL), F32),
        ((rows, D), BF),
    ]
    return pl.pallas_call(
        functools.partial(pre_body, len(xs)),
        grid=(count,),
        in_specs=[per_row(rows, D)] * len(xs) + [fixed(c) for c in consts],
        out_specs=[per_row(*s) for s, _ in shapes],
        out_shape=[jax.ShapeDtypeStruct((count, *s), t) for s, t in shapes],
        scratch_shapes=[pltpu.VMEM((rows + 16, D), F32)],
        compiler_params=params(),
        cost_estimate=pl.CostEstimate(
            flops=count * rows * 6_000_000, bytes_accessed=20_000_000, transcendentals=1_000_000
        ),
        name="pre_long" if len(xs) > 1 else "pre_short",
    )(*xs, *consts)


def norm_stats(z):
    centre = z - jnp.mean(z, axis=-1, keepdims=True)
    inverse = lax.rsqrt(jnp.mean(centre * centre, axis=-1, keepdims=True) + 1e-12)
    return centre * inverse, inverse


def norm_back(upstream, normed, inverse, gain):
    scaled = upstream * gain
    plain = jnp.mean(scaled, axis=-1, keepdims=True)
    cross = jnp.mean(scaled * normed, axis=-1, keepdims=True)
    return inverse * (scaled - plain - normed * cross)


def fold8(values):
    return jnp.sum(values.reshape(values.shape[0] // 8, 8, values.shape[1]), axis=0)


def gelu_pair(v):
    t = 1.0 / (1.0 + (0.3275911 * ROOT_HALF) * jnp.abs(v))
    bell = jnp.exp(-0.5 * (v * v))
    poly = 0.5 * 1.061405429
    for term in (-1.453152027, 1.421413741, -0.284496736, 0.254829592):
        poly = poly * t + 0.5 * term
    tail = poly * t * bell
    cdf = jnp.where(v >= 0, 1.0 - tail, tail)
    return v * cdf, cdf + v * bell * DENSITY


def ffn_body(masked, *refs):
    if masked:
        live_ref, *refs = refs
    (mix_ref, x_ref, cot_ref, vec, w_output, w_inner, w_outer) = refs[:7]
    (out_ref, fig_ref, mg_ref, act_ref, inl_ref, al_ref, flt_ref, olt_ref, mixt_ref, xt_ref, stat) = refs[7:18]
    (slope,) = refs[18:]
    step = pl.program_id(0)
    rows = x_ref.shape[1]

    @pl.when(step == 0)
    def _():
        stat[...] = jnp.zeros_like(stat)

    x = x_ref[0]
    mixed = mix_ref[0]
    mixt_ref[...] = mixed.T
    xt_ref[...] = x.T
    first_normed, first_inverse = norm_stats(nn(mixed, w_output[...]) + vec[2:3, :] + x.astype(F32))
    first_norm = first_normed * vec[3:4, :] + vec[4:5, :]
    first_low = first_norm.astype(BF)
    flt_ref[...] = first_low.T
    outer = []
    for g in range(GROUPS):
        for c in range(2):
            k = g * 2 + c
            inner = nn(first_low[:, g * ALL : (g + 1) * ALL], w_inner[g, :, c * D : (c + 1) * D])
            for r in range(0, rows, 16):
                act, slo = gelu_pair(inner[r : r + 16] + vec[8 + k : 9 + k, :])
                act_ref[r : r + 16, k * D : (k + 1) * D] = act.astype(BF)
                slope[r : r + 16, k * D : (k + 1) * D] = slo
        outer.append(nn(act_ref[:, g * 2 * D : (g + 1) * 2 * D], w_outer[g]))
    second_normed, second_inverse = norm_stats(
        jnp.concatenate(outer, axis=1) + vec[5:6, :] + first_norm
    )
    gain_second = vec[6:7, :]
    out_ref[0] = (second_normed * gain_second + vec[7:8, :]).astype(BF)
    seed = cot_ref[0].astype(F32)
    if masked:
        seed = jnp.where(step < live_ref[0, 0], seed, 0.0)
    stat[0:8, :] += fold8(seed * second_normed)
    stat[8:16, :] += fold8(seed)
    second_grad = norm_back(seed, second_normed, second_inverse, gain_second)
    outer_low = second_grad.astype(BF)
    olt_ref[...] = outer_low.T
    stat[32:40, :] += fold8(outer_low.astype(F32))
    first_grad = []
    for g in range(GROUPS):
        for c in range(2):
            k = g * 2 + c
            back = nt(outer_low[:, g * ALL : (g + 1) * ALL], w_outer[g, c * D : (c + 1) * D, :])
            inl_ref[:, k * D : (k + 1) * D] = (back * slope[:, k * D : (k + 1) * D]).astype(BF)
        first_grad.append(nt(inl_ref[:, g * 2 * D : (g + 1) * 2 * D], w_inner[g]))
    first_grad = second_grad + jnp.concatenate(first_grad, axis=1)
    stat[16:24, :] += fold8(first_grad * first_normed)
    stat[24:32, :] += fold8(first_grad)
    first_in_grad = norm_back(first_grad, first_normed, first_inverse, vec[3:4, :])
    fig_ref[0] = first_in_grad
    attended_low = first_in_grad.astype(BF)
    al_ref[...] = attended_low
    mg_ref[0] = nt(attended_low, w_output[...]).astype(BF)


def ffn_call(live, mixed, x, cotan, consts):
    count, rows = x.shape[0], x.shape[1]
    total = count * rows
    out_shapes = [
        ((count, rows, D), BF, per_row(rows, D)),
        ((count, rows, D), F32, per_row(rows, D)),
        ((count, rows, D), BF, per_row(rows, D)),
        ((total, FF), BF, pl.BlockSpec((rows, FF), lambda i: (i, 0))),
        ((total, FF), BF, pl.BlockSpec((rows, FF), lambda i: (i, 0))),
        ((total, D), BF, pl.BlockSpec((rows, D), lambda i: (i, 0))),
        ((D, total), BF, pl.BlockSpec((D, rows), lambda i: (0, i))),
        ((D, total), BF, pl.BlockSpec((D, rows), lambda i: (0, i))),
        ((D, total), BF, pl.BlockSpec((D, rows), lambda i: (0, i))),
        ((D, total), BF, pl.BlockSpec((D, rows), lambda i: (0, i))),
        ((40, D), F32, pl.BlockSpec((40, D), lambda i: (0, 0))),
    ]
    masked = live is not None
    head = [live] if masked else []
    head_specs = [pl.BlockSpec(memory_space=pltpu.SMEM)] if masked else []
    return pl.pallas_call(
        functools.partial(ffn_body, masked),
        grid=(count,),
        in_specs=head_specs + [per_row(rows, D)] * 3 + [fixed(c) for c in consts],
        out_specs=[s for _, _, s in out_shapes],
        out_shape=[jax.ShapeDtypeStruct(s, t) for s, t, _ in out_shapes],
        scratch_shapes=[pltpu.VMEM((rows, FF), F32)],
        compiler_params=params(),
        cost_estimate=pl.CostEstimate(
            flops=total * 12_000_000, bytes_accessed=30_000_000, transcendentals=total * FF
        ),
        name="ffn_short" if masked else "ffn_long",
    )(*head, mixed, x, cotan, *consts)


def post_body(n_x, *refs):
    is_long = n_x > 1
    x_refs = refs[:n_x]
    refs = refs[n_x:]
    (mg_ref, fig_ref, q_ref, k_ref, v_ref, p_ref, kc_ref, ker_ref, dl_ref, up_ref) = refs[:10]
    (vec, w_point, w_span, spread, perm) = refs[10:15]
    refs = refs[15:]
    if not is_long:
        (w_project, w_unfold), refs = refs[:2], refs[2:]
    (pl_out, ll_out, dlt_out, spt_out, dkg), refs = refs[:5], refs[5:]
    if is_long:
        own_out, *far_outs = refs[:n_x]
        qt_out, ug_out, tg_out = refs[n_x : n_x + 3]
        xp, dgp, prp, dq_scr = refs[n_x + 3 :]
    else:
        tg_out, ru_out, dgp, prp, dq_scr = refs
    step = pl.program_id(0)
    rows = x_refs[0].shape[1]
    keys = k_ref.shape[1]
    ext = 8 if is_long else 0

    @pl.when(step == 0)
    def _():
        dkg[...] = jnp.zeros_like(dkg)
        dgp[...] = jnp.zeros_like(dgp)
        prp[...] = jnp.zeros_like(prp)

    if is_long:
        lower, upper = row_sides()
        fill_ends(xp, x_refs, rows, (lower, upper))

    q = q_ref[0]
    qf = q.astype(F32)
    scaled = q * jnp.asarray(HEAD ** (-0.5), BF)
    low_half = lax.broadcasted_iota(jnp.int32, (1, 128), 1) < HEAD
    for p in range(PAIRS):
        cols = slice(p * 128, (p + 1) * 128)
        grad = mg_ref[0, :, cols]
        weight_grad = nt(head_stack(v_ref[0, :, cols], low_half), grad)
        low = []
        for half in range(2):
            part = slice(half * keys, (half + 1) * keys)
            probs = p_ref[0, p, part, :].astype(F32)
            inner = jnp.sum(probs * weight_grad[part], axis=0, keepdims=True)
            low.append((probs * (weight_grad[part] - inner)).astype(BF))
        score_low = jnp.concatenate(low, axis=0)
        value_grad = nn(p_ref[0, p], grad)
        value_grad = jnp.where(low_half, value_grad[:keys], value_grad[keys:])
        key_grad = nn(score_low, scaled[:, cols])
        key_grad = jnp.where(low_half, key_grad[:keys], key_grad[keys:])
        query_grad = tn(head_stack(k_ref[0, :, cols], low_half), score_low) * HEAD ** (-0.5)
        dq_scr[:, cols] = query_grad.T
        if is_long:
            own_out[0, :, cols] = key_grad[:rows]
            own_out[0, :, ALL + p * 128 : ALL + (p + 1) * 128] = value_grad[:rows]
            for i in range(1, n_x):
                block = slice(i * rows, (i + 1) * rows)
                far_outs[i - 1][0, :rows, cols] = key_grad[block].astype(BF)
                far_outs[i - 1][0, :rows, ALL + p * 128 : ALL + (p + 1) * 128] = value_grad[
                    block
                ].astype(BF)
        else:
            ru_out[:, 2 * ALL + p * 128 : 2 * ALL + (p + 1) * 128] = key_grad.astype(BF)
            ru_out[:, 3 * ALL + p * 128 : 3 * ALL + (p + 1) * 128] = value_grad.astype(BF)

    kernel = ker_ref[0]
    parts = two_parts(kernel)
    kernel_grad = jnp.zeros((rows, 128), F32)
    span_rows = rows + 2 * ext
    for p in range(PAIRS):
        cols = slice(p * 128, (p + 1) * 128)
        table = slice(p * KERNEL * 128, (p + 1) * KERNEL * 128)
        grad = mg_ref[0, :, ALL + p * 128 : ALL + (p + 1) * 128].astype(F32)
        wide = nn(parts, spread[:, table])
        products = []
        for j in range(KERNEL):
            products.append((grad * up_ref[0, 4 + j : 4 + j + rows, cols]).astype(BF))
            prp[j, 16 : 16 + rows, :] = wide[:, j * 128 : (j + 1) * 128] * grad
        kernel_grad += nt(jnp.concatenate(products, axis=1), spread[:128, table])
        first = 20 - ext
        total = prp[0, first : first + span_rows, :]
        for j in range(1, KERNEL):
            total += prp[j, first - j : first - j + span_rows, :]
        if is_long:
            ug_out[0, :, cols] = total[ext : ext + rows]
            far_outs[0][0, rows + 8 : rows + 16, cols] = (total[:ext] * lower).astype(BF)
            far_outs[-1][0, rows + 8 : rows + 16, cols] = (total[ext + rows :] * upper).astype(BF)
        else:
            ru_out[:, cols] = total.astype(BF)
    if is_long:
        zero = jnp.zeros((8, ALL), BF)
        far_outs[0][0, rows + 8 : rows + 16, ALL:] = zero
        far_outs[-1][0, rows + 8 : rows + 16, ALL:] = zero

    logit_low = (kernel * (kernel_grad - window_sum(kernel * kernel_grad))).astype(BF)
    ll_out[...] = nt(logit_low, perm[...]).astype(BF)
    span_weights = nn(w_span[...], perm[:TAPS, :]).astype(BF)
    span_grad = nt(logit_low, span_weights)
    key_conv = kc_ref[0]
    spt_out[...] = (key_conv * qf).astype(BF).T
    dlt_out[...] = dl_ref[0].T
    point_low = (span_grad * qf).astype(BF)
    pl_out[...] = point_low
    query_total = (dq_scr[...] + span_grad * key_conv).astype(BF)
    dgp[16 : 16 + rows, :] = nt(point_low, w_point[...])

    if not is_long:
        ru_out[:, ALL : 2 * ALL] = query_total
        base = nt(ru_out[:, :ALL], w_unfold[...]) + nt(ru_out[:, ALL:], w_project[...])
    else:
        qt_out[0] = query_total
    for c in range(D // 128):
        cols = slice(c * 128, (c + 1) * 128)
        x_part = xp[:, cols] if is_long else x_refs[0][0, :, cols].astype(F32)
        first = 20 - ext
        total = None
        for j in range(KERNEL):
            moved = dgp[first - j : first - j + span_rows, cols]
            term = vec[12 + j : 13 + j, cols] * moved
            total = term if total is None else total + term
            dkg[j * 8 : (j + 1) * 8, cols] += fold8(moved * x_part)
        if is_long:
            tg_out[0, :, cols] = total[ext : ext + rows] + fig_ref[0, :, cols]
            far_outs[0][0, rows : rows + 8, cols] = (total[:ext] * lower).astype(BF)
            far_outs[-1][0, rows : rows + 8, cols] = (total[ext + rows :] * upper).astype(BF)
        else:
            tg_out[0, :, cols] = total + fig_ref[0, :, cols] + base[:, cols]


def post_call(xs, mg, fig, kept, consts):
    count, rows = xs[0].shape[0], xs[0].shape[1]
    keys = rows * len(xs)
    total = count * rows
    is_long = len(xs) > 1
    q, k, v, probs, kc, ker, dl, up = kept
    row_args = [mg, fig, q, k, v, probs, kc, ker, dl, up]
    outs = [
        ((total, ALL), BF, pl.BlockSpec((rows, ALL), lambda i: (i, 0))),
        ((total, 128), BF, pl.BlockSpec((rows, 128), lambda i: (i, 0))),
        ((D, total), BF, pl.BlockSpec((D, rows), lambda i: (0, i))),
        ((ALL, total), BF, pl.BlockSpec((ALL, rows), lambda i: (0, i))),
        ((KERNEL * 8, D), F32, pl.BlockSpec((KERNEL * 8, D), lambda i: (0, 0))),
    ]
    row_out = lambda r, c, t: ((count, r, c), t, per_row(r, c))
    scratch = []
    if is_long:
        outs.append(row_out(rows, D, F32))
        for i in range(1, len(xs)):
            outs.append(row_out(rows + 16 if i in (1, len(xs) - 1) else rows, D, BF))
        outs += [row_out(rows, ALL, BF), row_out(rows, ALL, F32), row_out(rows, D, F32)]
        scratch.append(pltpu.VMEM((rows + 16, D), F32))
    else:
        outs += [
            row_out(rows, D, F32),
            ((total, 4 * ALL), BF, pl.BlockSpec((rows, 4 * ALL), lambda i: (i, 0))),
        ]
    scratch += [
        pltpu.VMEM((rows + 32, D), F32),
        pltpu.VMEM((KERNEL, rows + 32, 128), F32),
        pltpu.VMEM((rows, ALL), F32),
    ]
    return pl.pallas_call(
        functools.partial(post_body, len(xs)),
        grid=(count,),
        in_specs=[per_row(rows, D)] * len(xs)
        + [per_row(*a.shape[1:]) for a in row_args]
        + [fixed(c) for c in consts],
        out_specs=[s for _, _, s in outs],
        out_shape=[jax.ShapeDtypeStruct(s, t) for s, t, _ in outs],
        scratch_shapes=scratch,
        compiler_params=params(),
        cost_estimate=pl.CostEstimate(
            flops=total * 10_000_000, bytes_accessed=30_000_000, transcendentals=0
        ),
        name="post_long" if is_long else "post_short",
    )(*xs, *row_args, *consts)


def end_body(n_x, *refs):
    own, *rest = refs[:n_x]
    qt, ug, tg, w_project, w_unfold, out_ref, ru_out = refs[n_x:]
    rows = own.shape[1]
    both = own[0]
    for far in rest:
        both = both + far[0, :rows, :].astype(F32)
    from_next, from_prev = rest[0], rest[-1]
    unfold = ug[0]
    after = from_next[0, rows:, :].astype(F32)
    before = from_prev[0, rows:, :].astype(F32)
    middle = unfold[8 : rows - 8]
    ru_out[:, :ALL] = jnp.concatenate(
        [unfold[:8] + before[8:, :ALL], middle, unfold[rows - 8 :] + after[8:, :ALL]], axis=0
    ).astype(BF)
    ru_out[:, ALL : 2 * ALL] = qt[0]
    ru_out[:, 2 * ALL :] = both.astype(BF)
    total = nt(ru_out[:, :ALL], w_unfold[...]) + nt(ru_out[:, ALL:], w_project[...]) + tg[0]
    out_ref[0] = total
    out_ref[0, :8, :] = total[:8] + before[:8]
    out_ref[0, rows - 8 :, :] = total[rows - 8 :] + after[:8]


def end_call(own, far, qt, ug, tg, w_project, w_unfold):
    count, rows = own.shape[0], own.shape[1]
    row_args = [own, *far, qt, ug, tg]
    return pl.pallas_call(
        functools.partial(end_body, 1 + len(far)),
        grid=(count,),
        in_specs=[per_row(*a.shape[1:]) for a in row_args] + [fixed(w_project), fixed(w_unfold)],
        out_specs=[per_row(rows, D), pl.BlockSpec((rows, 4 * ALL), lambda i: (i, 0))],
        out_shape=[
            jax.ShapeDtypeStruct((count, rows, D), F32),
            jax.ShapeDtypeStruct((count * rows, 4 * ALL), BF),
        ],
        compiler_params=params(),
        cost_estimate=pl.CostEstimate(
            flops=count * rows * 2_400_000, bytes_accessed=10_000_000, transcendentals=0
        ),
        name="end_long",
    )(*row_args, w_project, w_unfold)


def grad_body(flip, sums, *refs):
    left_long, left_short, right_long, right_short, out = refs[:5]
    value = nn(left_long[...], right_long[...]) + nn(left_short[...], right_short[...])
    out[0] = value.astype(BF).T if flip else value.astype(BF)
    if sums:
        one = lambda r: jnp.ones((16, r.shape[0]), BF)
        refs[5][...] = nn(one(right_long), right_long[...]) + nn(one(right_short), right_short[...])


def grad_call(left, right, tile, groups, flip, sums, name):
    high = left[0].shape[0] // groups
    wide = right[0].shape[1] // groups
    tiles = wide // tile
    n_long, n_short = right[0].shape[0], right[1].shape[0]
    if flip:
        out_shape = [jax.ShapeDtypeStruct((groups, wide, high), BF)]
        out_specs = [pl.BlockSpec((1, tile, high), lambda g, t: (g, t, 0))]
    else:
        out_shape = [jax.ShapeDtypeStruct((groups, high, wide), BF)]
        out_specs = [pl.BlockSpec((1, high, tile), lambda g, t: (g, 0, t))]
    if sums:
        out_shape.append(jax.ShapeDtypeStruct((16, groups * wide), F32))
        out_specs.append(pl.BlockSpec((16, tile), lambda g, t: (0, g * tiles + t)))
    return pl.pallas_call(
        functools.partial(grad_body, flip, sums),
        grid=(groups, tiles),
        in_specs=[
            pl.BlockSpec((high, n_long), lambda g, t: (g, 0)),
            pl.BlockSpec((high, n_short), lambda g, t: (g, 0)),
            pl.BlockSpec((n_long, tile), lambda g, t: (0, g * tiles + t)),
            pl.BlockSpec((n_short, tile), lambda g, t: (0, g * tiles + t)),
        ],
        out_specs=out_specs,
        out_shape=out_shape,
        compiler_params=params(),
        cost_estimate=pl.CostEstimate(
            flops=2 * groups * high * wide * (n_long + n_short),
            bytes_accessed=4_000_000,
            transcendentals=0,
        ),
        name=name,
    )(*left, *right)


def shards(
    long_input,
    short_input,
    long_cotan,
    short_cotan,
    live_slots,
    w_project,
    bias_query,
    bias_value,
    depth_kernel,
    w_point,
    bias_point,
    w_span,
    bias_span,
    w_unfold,
    bias_unfold,
    w_output,
    bias_output,
    gain_first,
    shift_first,
    w_inner,
    bias_inner,
    w_outer,
    bias_outer,
    gain_second,
    shift_second,
):
    n_blk = lax.axis_size("blk")
    short_x = short_input.reshape(short_input.shape[2:])
    short_cot = short_cotan.reshape(short_cotan.shape[2:])
    vec = jnp.concatenate(
        [
            bias_query,
            bias_value,
            bias_point,
            bias_unfold,
            bias_output,
            gain_first,
            shift_first,
            bias_outer,
            gain_second,
            shift_second,
            bias_inner,
            depth_kernel.reshape(-1),
            bias_span,
            jnp.zeros((24 * D - 21 * D - TAPS,), BF),
        ]
    ).reshape(24, D).astype(F32)
    perm, spread = (jnp.asarray(t) for t in tap_tables())
    xs = [long_input] + [
        lax.ppermute(long_input, "blk", [(i, (i + k) % n_blk) for i in range(n_blk)])
        for k in range(1, n_blk)
    ]
    pre_consts = (vec, w_project, w_point, w_span, w_unfold, spread, perm)
    ffn_consts = (vec, w_output, w_inner, w_outer)
    *short_kept, short_mixed = pre_call([short_x], pre_consts)
    *long_kept, long_mixed = pre_call(xs, pre_consts)

    f_long = ffn_call(None, long_mixed, long_input, long_cotan, ffn_consts)
    f_short = ffn_call(live_slots, short_mixed, short_x, short_cot, ffn_consts)
    (l_out, l_fig, l_mg, l_act, l_inl, l_al, l_flt, l_olt, l_mixt, l_xt, l_stat) = f_long
    (s_out, s_fig, s_mg, s_act, s_inl, s_al, s_flt, s_olt, s_mixt, s_xt, s_stat) = f_short

    post_consts = (vec, w_point, w_span, spread, perm)
    l_post = post_call(xs, l_mg, l_fig, long_kept, post_consts)
    (l_pl, l_ll, l_dlt, l_spt, l_dkg), l_rest = l_post[:5], l_post[5:]
    own, far, (l_qt, l_ug, l_tg) = l_rest[0], l_rest[1:n_blk], l_rest[n_blk:]
    far = [
        lax.ppermute(a, "blk", [(i, (i - k) % n_blk) for i in range(n_blk)])
        for k, a in enumerate(far, 1)
    ]
    s_post = post_call([short_x], s_mg, s_fig, short_kept, post_consts + (w_project, w_unfold))
    s_pl, s_ll, s_dlt, s_spt, s_dkg, short_grad, s_ru = s_post
    w_inner_grad, inner_sums = grad_call((l_flt, s_flt), (l_inl, s_inl), 512, 2, False, True, "grad_inner")
    (w_outer_grad,) = grad_call((l_olt, s_olt), (l_act, s_act), 512, 2, True, False, "grad_outer")
    w_output_grad, output_sums = grad_call((l_mixt, s_mixt), (l_al, s_al), 256, 1, False, True, "grad_output")
    w_point_grad, point_sums = grad_call((l_dlt, s_dlt), (l_pl, s_pl), 128, 1, False, True, "grad_point")
    w_span_grad, span_sums = grad_call((l_spt, s_spt), (l_ll, s_ll), 128, 1, False, True, "grad_span")
    long_grad, l_ru = end_call(own, far, l_qt, l_ug, l_tg, w_project, w_unfold)
    ru_grad, ru_sums = grad_call((l_xt, s_xt), (l_ru, s_ru), 256, 1, False, True, "grad_rows")

    stat = (l_stat + s_stat).reshape(5, 8, D).sum(1)
    dkg = (l_dkg + s_dkg).reshape(KERNEL, 8, D).sum(1)
    small = jnp.concatenate(
        [
            stat.reshape(-1),
            dkg.reshape(-1),
            inner_sums[0],
            output_sums[0],
            point_sums[0],
            span_sums[0],
            ru_sums[0],
        ]
    )
    axes = ("dp", "blk")
    small = lax.psum(small, axes)
    big = lax.psum((w_inner_grad, w_outer_grad, w_output_grad, w_point_grad, w_span_grad, ru_grad), axes)
    w_inner_grad, w_outer_grad, w_output_grad, w_point_grad, w_span_grad, ru_grad = (
        b.astype(F32) for b in big
    )
    sizes = [D] * 5 + [KERNEL * D, FF, D, ALL, 128, ALL, ALL, ALL, ALL]
    places = np.cumsum([0] + sizes)
    (gs, ss, gf, sf, bo, dk, bi, bout, bp, bs, bu, bq, _, bv) = (
        small[a:b] for a, b in zip(places[:-1], places[1:])
    )
    return (
        l_out,
        s_out.reshape(short_input.shape),
        long_grad,
        short_grad.reshape(short_input.shape),
        ru_grad[0][:, ALL:],
        bq,
        bv,
        dk.reshape(KERNEL, D),
        w_point_grad[0],
        bp,
        w_span_grad[0][:, :TAPS],
        bs[:TAPS],
        ru_grad[0][:, :ALL],
        bu,
        w_output_grad[0],
        bout,
        gf,
        sf,
        w_inner_grad,
        bi,
        w_outer_grad,
        bo,
        gs,
        ss,
    )


def solution(mesh):
    rows = P("dp", "blk", None)
    slots = P("dp", "blk", None, None, None)
    in_specs = (rows, slots, rows, slots, P("dp", "blk")) + (P(),) * 20
    out_specs = (rows, slots, rows, slots) + (P(),) * 20
    return jax.shard_map(shards, mesh=mesh, in_specs=in_specs, out_specs=out_specs, check_vma=False)
```

```python
import functools

import jax
import jax.numpy as jnp
import numpy as np
from jax import lax
from jax.experimental import pallas as pl
from jax.experimental.pallas import tpu as pltpu
from jax.sharding import PartitionSpec as P

D = 768
FF = 3072
HEADS = 6
HEAD = 64
KERNEL = 9
GROUPS = 2
ALL = 384
PAIRS = 3
TAPS = HEADS * KERNEL
HALF = KERNEL // 2

F32 = jnp.float32
BF = jnp.bfloat16
ROOT_HALF = 0.7071067811865476
DENSITY = 0.3989422804014327
VMEM_BYTES = 58 * 1024 * 1024


def nn(a, b):
    return lax.dot_general(a, b, (((1,), (0,)), ((), ())), preferred_element_type=F32)


def nt(a, b):
    return lax.dot_general(a, b, (((1,), (1,)), ((), ())), preferred_element_type=F32)


def tn(a, b):
    return lax.dot_general(a, b, (((0,), (0,)), ((), ())), preferred_element_type=F32)


def tap_tables():
    perm = np.zeros((128, 128), np.float32)
    spread = np.zeros((256, PAIRS * KERNEL * 128), np.float32)
    for h in range(HEADS):
        for j in range(KERNEL):
            lane = j * HEADS + h
            perm[h * KERNEL + j, lane] = 1
            perm[h * KERNEL + j, TAPS + lane] = 1
            start = ((h // 2) * KERNEL + j) * 128 + (h % 2) * HEAD
            spread[lane, start : start + HEAD] = 1
            spread[128 + lane, start : start + HEAD] = 1
    return perm.astype(jnp.bfloat16), spread.astype(jnp.bfloat16)


def window(values, op):
    left = lambda v, n: pltpu.roll(v, 128 - n, 1)
    one = op(values, left(values, 6))
    two = op(one, left(one, 12))
    four = op(two, left(two, 24))
    return op(four, left(values, 48))


def window_sum(values):
    return window(values + pltpu.roll(values, TAPS, 1), jnp.add)


def head_stack(rows, low_half):
    zero = jnp.zeros_like(rows)
    return jnp.concatenate(
        [jnp.where(low_half, rows, zero), jnp.where(low_half, zero, rows)], axis=0
    )


def two_parts(values):
    high = values.astype(BF)
    rest = (values - high.astype(F32)).astype(BF)
    return jnp.concatenate([high, rest], axis=1)


def fill_ends(xp, x_refs, rows, sides):
    if sides is None:
        zero = jnp.zeros((8, D), F32)
        xp[0:8, :] = zero
        xp[8 + rows : 16 + rows, :] = zero
    else:
        lower, upper = sides
        xp[0:8, :] = x_refs[1][0, rows - 16 :, :].astype(F32)[8:] * lower
        xp[8 + rows : 16 + rows, :] = x_refs[-1][0, :16, :].astype(F32)[:8] * upper
    xp[8 : 8 + rows, :] = x_refs[0][0].astype(F32)


def row_sides():
    place = lax.axis_index("blk")
    count = lax.axis_size("blk")
    return (place > 0).astype(F32), (place < count - 1).astype(F32)


def pre_body(n_x, *refs):
    x_refs = refs[:n_x]
    vec, w_project, w_point, w_span, w_unfold, spread, perm = refs[n_x : n_x + 7]
    q_out, k_out, v_out, p_out, kc_out, ker_out, dl_out, up_out, mix_out = refs[n_x + 7 : n_x + 16]
    (xp,) = refs[n_x + 16 :]
    rows = x_refs[0].shape[1]
    is_long = n_x > 1
    sides = row_sides() if is_long else None
    x = x_refs[0][0]
    fill_ends(xp, x_refs, rows, sides)
    bias_query = vec[0:1, :ALL]
    bias_value = vec[0:1, ALL:]
    if is_long:
        q = (nn(x, w_project[:, :ALL]) + bias_query).astype(BF)
        for i in range(n_x):
            both = nn(x_refs[i][0], w_project[:, ALL:])
            k_out[0, i * rows : (i + 1) * rows, :] = both[:, :ALL].astype(BF)
            v_out[0, i * rows : (i + 1) * rows, :] = (both[:, ALL:] + bias_value).astype(BF)
    else:
        both = nn(x, w_project[...])
        q = (both[:, :ALL] + bias_query).astype(BF)
        k_out[0] = both[:, ALL : 2 * ALL].astype(BF)
        v_out[0] = (both[:, 2 * ALL :] + bias_value).astype(BF)
    q_out[0] = q

    for c in range(D // 128):
        cols = slice(c * 128, (c + 1) * 128)
        total = vec[12:13, cols] * xp[4 : 4 + rows, cols]
        for j in range(1, KERNEL):
            total += vec[12 + j : 13 + j, cols] * xp[4 + j : 4 + j + rows, cols]
        dl_out[0, :, cols] = total.astype(BF)
    key_conv = nn(dl_out[0], w_point[...]) + vec[1:2, :ALL]
    kc_out[0] = key_conv
    span = (key_conv * q.astype(F32)).astype(BF)
    span_weights = nn(w_span[...], perm[:TAPS, :]).astype(BF)
    span_bias = nn(vec[16:24, :128].astype(BF), perm[...])[5:6]
    logits = nn(span, span_weights) + span_bias
    lane = lax.broadcasted_iota(jnp.int32, (rows, 128), 1)
    raised = jnp.where(lane < TAPS, jnp.exp(logits - window(logits, jnp.maximum)), 0.0)
    kernel = jnp.where(lane < TAPS, raised / window_sum(raised), 0.0)
    ker_out[0] = kernel

    bias_unfold = vec[1:2, ALL:]
    up_out[0, 8 : 8 + rows, :] = nn(x, w_unfold[...]) + bias_unfold
    if is_long:
        lower, upper = sides
        ends = jnp.concatenate([x_refs[1][0, rows - 16 :, :], x_refs[-1][0, :16, :]], axis=0)
        unfold_ends = nn(ends, w_unfold[...]) + bias_unfold
        up_out[0, 0:8, :] = unfold_ends[8:16] * lower
        up_out[0, 8 + rows : 16 + rows, :] = unfold_ends[16:24] * upper
    else:
        zero = jnp.zeros((8, ALL), F32)
        up_out[0, 0:8, :] = zero
        up_out[0, 8 + rows : 16 + rows, :] = zero

    low_half = lax.broadcasted_iota(jnp.int32, (1, 128), 1) < HEAD
    parts = two_parts(kernel)
    scaled = q * jnp.asarray(HEAD ** (-0.5), BF)
    keys = k_out.shape[1]
    for p in range(PAIRS):
        cols = slice(p * 128, (p + 1) * 128)
        wide = nn(parts, spread[:, p * KERNEL * 128 : (p + 1) * KERNEL * 128])
        total = wide[:, :128] * up_out[0, 4 : 4 + rows, cols]
        for j in range(1, KERNEL):
            total += wide[:, j * 128 : (j + 1) * 128] * up_out[0, 4 + j : 4 + j + rows, cols]
        mix_out[0, :, ALL + p * 128 : ALL + (p + 1) * 128] = total.astype(BF)

        scores = nt(head_stack(k_out[0, :, cols], low_half), scaled[:, cols])
        for half in range(2):
            part = scores[half * keys : (half + 1) * keys]
            top = jnp.max(part, axis=0, keepdims=True)
            grown = jnp.exp(part - top)
            share = 1.0 / jnp.sum(grown, axis=0, keepdims=True)
            p_out[0, p, half * keys : (half + 1) * keys, :] = (grown * share).astype(BF)
        context = tn(head_stack(v_out[0, :, cols], low_half), p_out[0, p])
        mix_out[0, :, cols] = context.astype(BF).T


def block_spec(shape, index_map):
    return pl.BlockSpec(shape, index_map)


def fixed(array):
    zeros = (0,) * array.ndim
    return pl.BlockSpec(array.shape, lambda *_: zeros, pipeline_mode=pl.Buffered(1))


def per_row(*shape):
    zeros = (0,) * len(shape)
    return pl.BlockSpec((1, *shape), lambda i: (i, *zeros))


def params(**more):
    return pltpu.CompilerParams(vmem_limit_bytes=VMEM_BYTES, **more)


def pre_call(xs, consts):
    count, rows = xs[0].shape[0], xs[0].shape[1]
    keys = rows * len(xs)
    shapes = [
        ((rows, ALL), BF),
        ((keys, ALL), BF),
        ((keys, ALL), BF),
        ((PAIRS, 2 * keys, rows), BF),
        ((rows, ALL), F32),
        ((rows, 128), F32),
        ((rows, D), BF),
        ((rows + 16, ALL), F32),
        ((rows, D), BF),
    ]
    return pl.pallas_call(
        functools.partial(pre_body, len(xs)),
        grid=(count,),
        in_specs=[per_row(rows, D)] * len(xs) + [fixed(c) for c in consts],
        out_specs=[per_row(*s) for s, _ in shapes],
        out_shape=[jax.ShapeDtypeStruct((count, *s), t) for s, t in shapes],
        scratch_shapes=[pltpu.VMEM((rows + 16, D), F32)],
        compiler_params=params(),
        cost_estimate=pl.CostEstimate(
            flops=count * rows * 6_000_000, bytes_accessed=20_000_000, transcendentals=1_000_000
        ),
        name="pre_long" if len(xs) > 1 else "pre_short",
    )(*xs, *consts)


def norm_stats(z):
    centre = z - jnp.mean(z, axis=-1, keepdims=True)
    inverse = lax.rsqrt(jnp.mean(centre * centre, axis=-1, keepdims=True) + 1e-12)
    return centre * inverse, inverse


def norm_back(upstream, normed, inverse, gain):
    scaled = upstream * gain
    plain = jnp.mean(scaled, axis=-1, keepdims=True)
    cross = jnp.mean(scaled * normed, axis=-1, keepdims=True)
    return inverse * (scaled - plain - normed * cross)


def fold8(values):
    return jnp.sum(values.reshape(values.shape[0] // 8, 8, values.shape[1]), axis=0)


def gelu_pair(v):
    t = 1.0 / (1.0 + (0.3275911 * ROOT_HALF) * jnp.abs(v))
    bell = jnp.exp(-0.5 * (v * v))
    poly = 0.5 * 1.061405429
    for term in (-1.453152027, 1.421413741, -0.284496736, 0.254829592):
        poly = poly * t + 0.5 * term
    tail = poly * t * bell
    cdf = jnp.where(v >= 0, 1.0 - tail, tail)
    return v * cdf, cdf + v * bell * DENSITY


def ffn_body(masked, *refs):
    if masked:
        live_ref, *refs = refs
        refs = refs[:7] + refs[9:]
    (mix_ref, x_ref, cot_ref, vec, w_output, w_inner, w_outer) = refs[:7]
    (out_ref, fig_ref, mg_ref, left, right, stat) = refs[7:13]
    (slope,) = refs[13:]
    inl_ref, act_ref = right.at[:, :FF], right.at[:, FF : 2 * FF]
    step = pl.program_id(0)
    rows = x_ref.shape[1]

    @pl.when(step == 0)
    def _():
        stat[...] = jnp.zeros_like(stat)

    x = x_ref[0]
    mixed = mix_ref[0]
    left[2 * D : 3 * D, :] = mixed.T
    left[3 * D :, :] = x.T
    first_normed, first_inverse = norm_stats(nn(mixed, w_output[...]) + vec[2:3, :] + x.astype(F32))
    first_norm = first_normed * vec[3:4, :] + vec[4:5, :]
    first_low = first_norm.astype(BF)
    left[:D, :] = first_low.T
    outer = []
    for g in range(GROUPS):
        for c in range(2):
            k = g * 2 + c
            inner = nn(first_low[:, g * ALL : (g + 1) * ALL], w_inner[g, :, c * D : (c + 1) * D])
            for r in range(0, rows, 16):
                act, slo = gelu_pair(inner[r : r + 16] + vec[8 + k : 9 + k, :])
                act_ref[r : r + 16, k * D : (k + 1) * D] = act.astype(BF)
                slope[r : r + 16, k * D : (k + 1) * D] = slo
        outer.append(nn(act_ref[:, g * 2 * D : (g + 1) * 2 * D], w_outer[g]))
    second_normed, second_inverse = norm_stats(
        jnp.concatenate(outer, axis=1) + vec[5:6, :] + first_norm
    )
    gain_second = vec[6:7, :]
    out_ref[0] = (second_normed * gain_second + vec[7:8, :]).astype(BF)
    seed = cot_ref[0].astype(F32)
    if masked:
        seed = jnp.where(step < live_ref[0, 0], seed, 0.0)
    stat[0:8, :] += fold8(seed * second_normed)
    stat[8:16, :] += fold8(seed)
    second_grad = norm_back(seed, second_normed, second_inverse, gain_second)
    outer_low = second_grad.astype(BF)
    left[D : 2 * D, :] = outer_low.T
    stat[32:40, :] += fold8(outer_low.astype(F32))
    first_grad = []
    for g in range(GROUPS):
        for c in range(2):
            k = g * 2 + c
            back = nt(outer_low[:, g * ALL : (g + 1) * ALL], w_outer[g, c * D : (c + 1) * D, :])
            inl_ref[:, k * D : (k + 1) * D] = (back * slope[:, k * D : (k + 1) * D]).astype(BF)
        first_grad.append(nt(inl_ref[:, g * 2 * D : (g + 1) * 2 * D], w_inner[g]))
    first_grad = second_grad + jnp.concatenate(first_grad, axis=1)
    stat[16:24, :] += fold8(first_grad * first_normed)
    stat[24:32, :] += fold8(first_grad)
    first_in_grad = norm_back(first_grad, first_normed, first_inverse, vec[3:4, :])
    fig_ref[0] = first_in_grad
    attended_low = first_in_grad.astype(BF)
    right[:, 2 * FF :] = attended_low
    mg_ref[0] = nt(attended_low, w_output[...]).astype(BF)


def ffn_call(live, mixed, x, cotan, consts, joint, tokens):
    count, rows = x.shape[0], x.shape[1]
    total = count * rows
    masked = live is not None
    first = tokens // rows - count if masked else 0
    out_shapes = [
        ((count, rows, D), BF, per_row(rows, D)),
        ((count, rows, D), F32, per_row(rows, D)),
        ((count, rows, D), BF, per_row(rows, D)),
        ((4 * D, tokens), BF, pl.BlockSpec((4 * D, rows), lambda i: (0, first + i))),
        ((tokens, 2 * FF + D), BF, pl.BlockSpec((rows, 2 * FF + D), lambda i: (first + i, 0))),
        ((40, D), F32, pl.BlockSpec((40, D), lambda i: (0, 0))),
    ]
    head = [live] if masked else []
    head_specs = [pl.BlockSpec(memory_space=pltpu.SMEM)] if masked else []
    return pl.pallas_call(
        functools.partial(ffn_body, masked),
        grid=(count,),
        in_specs=head_specs
        + [per_row(rows, D)] * 3
        + [fixed(c) for c in consts]
        + [pl.BlockSpec(memory_space=pl.ANY)] * len(joint),
        out_specs=[s for _, _, s in out_shapes],
        out_shape=[jax.ShapeDtypeStruct(s, t) for s, t, _ in out_shapes],
        scratch_shapes=[pltpu.VMEM((rows, FF), F32)],
        input_output_aliases={8: 3, 9: 4} if masked else {},
        compiler_params=params(),
        cost_estimate=pl.CostEstimate(
            flops=total * 12_000_000, bytes_accessed=30_000_000, transcendentals=total * FF
        ),
        name="ffn_short" if masked else "ffn_long",
    )(*head, mixed, x, cotan, *consts, *joint)


def post_body(n_x, *refs):
    is_long = n_x > 1
    x_refs = refs[:n_x]
    refs = refs[n_x:]
    (mg_ref, fig_ref, q_ref, k_ref, v_ref, p_ref, kc_ref, ker_ref, dl_ref, up_ref) = refs[:10]
    (vec, w_point, w_span, spread, perm) = refs[10:15]
    refs = refs[15:]
    if not is_long:
        (w_project, w_unfold), refs = refs[:2], refs[4:]
    (left, right, dkg), refs = refs[:3], refs[3:]
    if is_long:
        own_out, *far_outs = refs[:n_x]
        qt_out, ug_out, tg_out = refs[n_x : n_x + 3]
        xp, dgp, prp, dq_scr = refs[n_x + 3 :]
    else:
        tg_out, ru_out, dgp, prp, dq_scr = refs
    step = pl.program_id(0)
    rows = x_refs[0].shape[1]
    keys = k_ref.shape[1]
    ext = 8 if is_long else 0

    @pl.when(step == 0)
    def _():
        dkg[...] = jnp.zeros_like(dkg)
        dgp[...] = jnp.zeros_like(dgp)
        prp[...] = jnp.zeros_like(prp)

    if is_long:
        lower, upper = row_sides()
        fill_ends(xp, x_refs, rows, (lower, upper))

    q = q_ref[0]
    qf = q.astype(F32)
    scaled = q * jnp.asarray(HEAD ** (-0.5), BF)
    low_half = lax.broadcasted_iota(jnp.int32, (1, 128), 1) < HEAD
    for p in range(PAIRS):
        cols = slice(p * 128, (p + 1) * 128)
        grad = mg_ref[0, :, cols]
        weight_grad = nt(head_stack(v_ref[0, :, cols], low_half), grad)
        low = []
        for half in range(2):
            part = slice(half * keys, (half + 1) * keys)
            probs = p_ref[0, p, part, :].astype(F32)
            inner = jnp.sum(probs * weight_grad[part], axis=0, keepdims=True)
            low.append((probs * (weight_grad[part] - inner)).astype(BF))
        score_low = jnp.concatenate(low, axis=0)
        value_grad = nn(p_ref[0, p], grad)
        value_grad = jnp.where(low_half, value_grad[:keys], value_grad[keys:])
        key_grad = nn(score_low, scaled[:, cols])
        key_grad = jnp.where(low_half, key_grad[:keys], key_grad[keys:])
        query_grad = tn(head_stack(k_ref[0, :, cols], low_half), score_low) * HEAD ** (-0.5)
        dq_scr[:, cols] = query_grad.T
        if is_long:
            own_out[0, :, cols] = key_grad[:rows]
            own_out[0, :, ALL + p * 128 : ALL + (p + 1) * 128] = value_grad[:rows]
            for i in range(1, n_x):
                block = slice(i * rows, (i + 1) * rows)
                far_outs[i - 1][0, :rows, cols] = key_grad[block].astype(BF)
                far_outs[i - 1][0, :rows, ALL + p * 128 : ALL + (p + 1) * 128] = value_grad[
                    block
                ].astype(BF)
        else:
            ru_out[:, 2 * ALL + p * 128 : 2 * ALL + (p + 1) * 128] = key_grad.astype(BF)
            ru_out[:, 3 * ALL + p * 128 : 3 * ALL + (p + 1) * 128] = value_grad.astype(BF)

    kernel = ker_ref[0]
    parts = two_parts(kernel)
    kernel_grad = jnp.zeros((rows, 128), F32)
    span_rows = rows + 2 * ext
    for p in range(PAIRS):
        cols = slice(p * 128, (p + 1) * 128)
        table = slice(p * KERNEL * 128, (p + 1) * KERNEL * 128)
        grad = mg_ref[0, :, ALL + p * 128 : ALL + (p + 1) * 128].astype(F32)
        wide = nn(parts, spread[:, table])
        products = []
        for j in range(KERNEL):
            products.append((grad * up_ref[0, 4 + j : 4 + j + rows, cols]).astype(BF))
            prp[j, 16 : 16 + rows, :] = wide[:, j * 128 : (j + 1) * 128] * grad
        kernel_grad += nt(jnp.concatenate(products, axis=1), spread[:128, table])
        first = 20 - ext
        total = prp[0, first : first + span_rows, :]
        for j in range(1, KERNEL):
            total += prp[j, first - j : first - j + span_rows, :]
        if is_long:
            ug_out[0, :, cols] = total[ext : ext + rows]
            far_outs[0][0, rows + 8 : rows + 16, cols] = (total[:ext] * lower).astype(BF)
            far_outs[-1][0, rows + 8 : rows + 16, cols] = (total[ext + rows :] * upper).astype(BF)
        else:
            ru_out[:, cols] = total.astype(BF)
    if is_long:
        zero = jnp.zeros((8, ALL), BF)
        far_outs[0][0, rows + 8 : rows + 16, ALL:] = zero
        far_outs[-1][0, rows + 8 : rows + 16, ALL:] = zero

    logit_low = (kernel * (kernel_grad - window_sum(kernel * kernel_grad))).astype(BF)
    left[D:, :] = nt(perm[...], logit_low).astype(BF)
    span_weights = nn(w_span[...], perm[:TAPS, :]).astype(BF)
    span_grad = nt(logit_low, span_weights)
    key_conv = kc_ref[0]
    right[:, ALL:] = (key_conv * qf).astype(BF)
    left[:D, :] = dl_ref[0].T
    point_low = (span_grad * qf).astype(BF)
    right[:, :ALL] = point_low
    query_total = (dq_scr[...] + span_grad * key_conv).astype(BF)
    dgp[16 : 16 + rows, :] = nt(point_low, w_point[...])

    if not is_long:
        ru_out[:, ALL : 2 * ALL] = query_total
        base = nt(ru_out[:, :ALL], w_unfold[...]) + nt(ru_out[:, ALL:], w_project[...])
    else:
        qt_out[0] = query_total
    for c in range(D // 128):
        cols = slice(c * 128, (c + 1) * 128)
        x_part = xp[:, cols] if is_long else x_refs[0][0, :, cols].astype(F32)
        first = 20 - ext
        total = None
        for j in range(KERNEL):
            moved = dgp[first - j : first - j + span_rows, cols]
            term = vec[12 + j : 13 + j, cols] * moved
            total = term if total is None else total + term
            dkg[j * 8 : (j + 1) * 8, cols] += fold8(moved * x_part)
        if is_long:
            tg_out[0, :, cols] = total[ext : ext + rows] + fig_ref[0, :, cols]
            far_outs[0][0, rows : rows + 8, cols] = (total[:ext] * lower).astype(BF)
            far_outs[-1][0, rows : rows + 8, cols] = (total[ext + rows :] * upper).astype(BF)
        else:
            tg_out[0, :, cols] = total + fig_ref[0, :, cols] + base[:, cols]


def post_call(xs, mg, fig, kept, consts, joint, tokens):
    count, rows = xs[0].shape[0], xs[0].shape[1]
    keys = rows * len(xs)
    total = count * rows
    is_long = len(xs) > 1
    first = 0 if is_long else tokens // rows - count
    row_args = [mg, fig, *kept]
    outs = [
        ((D + 128, tokens), BF, pl.BlockSpec((D + 128, rows), lambda i: (0, first + i))),
        ((tokens, 2 * ALL), BF, pl.BlockSpec((rows, 2 * ALL), lambda i: (first + i, 0))),
        ((KERNEL * 8, D), F32, pl.BlockSpec((KERNEL * 8, D), lambda i: (0, 0))),
    ]
    row_out = lambda r, c, t: ((count, r, c), t, per_row(r, c))
    scratch = []
    if is_long:
        outs.append(row_out(rows, D, F32))
        for i in range(1, len(xs)):
            outs.append(row_out(rows + 16 if i in (1, len(xs) - 1) else rows, D, BF))
        outs += [row_out(rows, ALL, BF), row_out(rows, ALL, F32), row_out(rows, D, F32)]
        scratch.append(pltpu.VMEM((rows + 16, D), F32))
    else:
        outs += [
            row_out(rows, D, F32),
            ((tokens, 4 * ALL), BF, pl.BlockSpec((rows, 4 * ALL), lambda i: (first + i, 0))),
        ]
    scratch += [
        pltpu.VMEM((rows + 32, D), F32),
        pltpu.VMEM((KERNEL, rows + 32, 128), F32),
        pltpu.VMEM((rows, ALL), F32),
    ]
    inputs = [*xs, *row_args, *consts]
    return pl.pallas_call(
        functools.partial(post_body, len(xs)),
        grid=(count,),
        in_specs=[per_row(rows, D)] * len(xs)
        + [per_row(*a.shape[1:]) for a in row_args]
        + [fixed(c) for c in consts]
        + [pl.BlockSpec(memory_space=pl.ANY)] * len(joint),
        out_specs=[s for _, _, s in outs],
        out_shape=[jax.ShapeDtypeStruct(s, t) for s, t, _ in outs],
        scratch_shapes=scratch,
        input_output_aliases={len(inputs) + i: i for i in range(len(joint))},
        compiler_params=params(),
        cost_estimate=pl.CostEstimate(
            flops=total * 10_000_000, bytes_accessed=30_000_000, transcendentals=0
        ),
        name="post_long" if is_long else "post_short",
    )(*inputs, *joint)


def end_body(n_x, *refs):
    own, *rest = refs[:n_x]
    qt, ug, tg, w_project, w_unfold, _, out_ref, ru_out = refs[n_x:]
    rows = own.shape[1]
    both = own[0]
    for far in rest:
        both = both + far[0, :rows, :].astype(F32)
    from_next, from_prev = rest[0], rest[-1]
    unfold = ug[0]
    after = from_next[0, rows:, :].astype(F32)
    before = from_prev[0, rows:, :].astype(F32)
    middle = unfold[8 : rows - 8]
    ru_out[:, :ALL] = jnp.concatenate(
        [unfold[:8] + before[8:, :ALL], middle, unfold[rows - 8 :] + after[8:, :ALL]], axis=0
    ).astype(BF)
    ru_out[:, ALL : 2 * ALL] = qt[0]
    ru_out[:, 2 * ALL :] = both.astype(BF)
    total = nt(ru_out[:, :ALL], w_unfold[...]) + nt(ru_out[:, ALL:], w_project[...]) + tg[0]
    out_ref[0] = total
    out_ref[0, :8, :] = total[:8] + before[:8]
    out_ref[0, rows - 8 :, :] = total[rows - 8 :] + after[:8]


def end_call(own, far, qt, ug, tg, w_project, w_unfold, joint):
    count, rows = own.shape[0], own.shape[1]
    row_args = [own, *far, qt, ug, tg]
    return pl.pallas_call(
        functools.partial(end_body, 1 + len(far)),
        grid=(count,),
        in_specs=[per_row(*a.shape[1:]) for a in row_args]
        + [fixed(w_project), fixed(w_unfold), pl.BlockSpec(memory_space=pl.ANY)],
        out_specs=[per_row(rows, D), pl.BlockSpec((rows, 4 * ALL), lambda i: (i, 0))],
        out_shape=[
            jax.ShapeDtypeStruct((count, rows, D), F32),
            jax.ShapeDtypeStruct(joint.shape, BF),
        ],
        input_output_aliases={len(row_args) + 2: 1},
        compiler_params=params(),
        cost_estimate=pl.CostEstimate(
            flops=count * rows * 2_400_000, bytes_accessed=10_000_000, transcendentals=0
        ),
        name="end_long",
    )(*row_args, w_project, w_unfold, joint)


UNIT = 3 * ALL
CHUNK = 4 * UNIT
CHUNKS = 8
LAST = 6 * 512
PACKED = (CHUNKS - 1) * CHUNK + LAST
SPAN_ROW = (CHUNKS - 1) * CHUNK + 2 * UNIT
SMALL_ROW = SPAN_ROW + ALL
SMALL = 48
MESH = pl.DeviceIdType.MESH


def chunk_parts(k):
    blocks = CHUNK // 512 if k < CHUNKS - 1 else LAST // 512
    first = (blocks + 1) // 2 if k % 2 == 0 else blocks // 2
    start = k * CHUNK
    middle = start + first * 512
    return [(start, first * 512, "cxy"), (middle, (blocks - first) * 512, "cyx")]


def rows_of(ref, start, count):
    return ref.at[pl.ds(pl.multiple_of(start, 16), count), :]


def add_rows(out, start, sources, count):
    step = next(s for s in (160, 128, 96, 80, 64, 48, 32, 16) if count % s == 0)

    def body(i, carry):
        total = None
        for ref, first in sources:
            value = rows_of(ref, first + i * step, step)[...].astype(F32)
            total = value if total is None else total + value
        rows_of(out, start + i * step, step)[...] = total.astype(BF)
        return carry

    lax.fori_loop(0, count // step, body, 0)


class Exchange:
    def __init__(self, part, res, out, scratch):
        self.part, self.res, self.out = part, res, out
        self.got = scratch[0:3]
        self.got_z = scratch[3]
        self.acc = scratch[4:7]
        self.send_sem, self.recv_sem, self.out_sem = scratch[7:10]
        dp, blk = lax.axis_index("dp"), lax.axis_index("blk")
        core, x, y, z = lax.rem(blk, 2), blk // 2, lax.rem(dp, 2), dp // 2
        self.z = z
        self.bit = {"c": core, "x": x, "y": y}
        self.peer = {
            "c": (dp, blk + 1 - 2 * core),
            "x": (dp, blk + 2 - 4 * x),
            "y": (dp + 1 - 2 * y, blk),
        }
        self.z_peer = [(lax.rem(z + i, 4) * 2 + y, blk) for i in (1, 2, 3)]
        self.open = {}
        self.sends = []
        self.place = {}

    def greet(self):
        barrier = pltpu.get_barrier_semaphore()
        for device in [*self.peer.values(), *self.z_peer]:
            pl.semaphore_signal(barrier, inc=1, device_id=device, device_id_type=MESH)

    def await_greetings(self):
        pl.semaphore_wait(pltpu.get_barrier_semaphore(), 6)

    def start(self, n, slot, source, target, device):
        copy = pltpu.make_async_remote_copy(
            src_ref=source,
            dst_ref=target,
            send_sem=self.send_sem.at[n, slot],
            recv_sem=self.recv_sem.at[n, slot],
            device_id=device,
            device_id_type=MESH,
        )
        copy.start()
        self.open[n, slot] = copy
        self.sends.append(copy)

    def stage(self, n, part, s):
        row, count, order = part
        bit, peer, acc, got, res = self.bit, self.peer, self.acc, self.got, self.res
        if 1 <= s <= 3:
            size = count >> s
            self.open[n, s - 1].wait_recv()
            before, first = (self.part, row) if s == 1 else (acc[s - 2], row >> (s - 1))
            mine = first + bit[order[s - 1]] * size
            add_rows(acc[s - 1], row >> s, [(before, mine), (got[s - 1], row >> s)], size)
        if s <= 2:
            size = count >> (s + 1)
            source, first = (self.part, row) if s == 0 else (acc[s - 1], row >> s)
            axis = order[s]
            other = first + (1 - bit[axis]) * size
            self.start(n, s, rows_of(source, other, size), rows_of(got[s], row >> (s + 1), size), peer[axis])
        elif s == 3:
            size = count >> 5
            for i in range(3):
                theirs = (row >> 3) + lax.rem(self.z + i + 1, 4) * size
                target = rows_of(self.got_z.at[i], row >> 5, size)
                self.start(n, 3 + i, rows_of(acc[2], theirs, size), target, self.z_peer[i])
        elif s == 4:
            size = count >> 5
            for i in range(3):
                self.open[n, 3 + i].wait_recv()
            place = row
            for level in range(3):
                place = place + bit[order[level]] * (count >> (level + 1))
            self.place[n] = place
            mine = place + self.z * size
            others = [(self.got_z.at[i], row >> 5) for i in range(3)]
            add_rows(res, mine, [(acc[2], (row >> 3) + self.z * size), *others], size)
            for i in range(3):
                block = rows_of(res, mine, size)
                self.start(n, 6 + i, block, block, self.z_peer[i])
        elif s <= 7:
            for slot in (6, 7, 8) if s == 5 else (s + 3,):
                self.open[n, slot].wait_recv()
            level = 7 - s
            size = count >> (level + 1)
            block = rows_of(res, self.place[n], size)
            self.start(n, s + 4, block, block, peer[order[level]])
            self.place[n] = self.place[n] - bit[order[level]] * size
        else:
            self.open[n, 11].wait_recv()
            pltpu.make_async_copy(
                rows_of(res, row, count), rows_of(self.out, row, count), self.out_sem.at[n]
            ).start()

    def finish(self, parts):
        for copy in self.sends:
            copy.wait_send()
        for n, (row, count, _) in enumerate(parts):
            pltpu.make_async_copy(
                rows_of(self.res, row, count), rows_of(self.out, row, count), self.out_sem.at[n]
            ).wait()


def weights_body(remote, *refs):
    left, right, left_post, right_post, rows_grad, stat_a, stat_b, depth_a, depth_b, out = refs[:10]
    held_left, held_right, sums, part, load_sem = refs[10:15]
    scratch = refs[15:]
    tokens = right.shape[0]

    def loads(k):
        slot = k % 2
        if k < 4:
            pairs = [
                (left.at[k * ALL : (k + 1) * ALL, :], held_left.at[slot, :ALL, :]),
                (right.at[:, k * 4 * ALL : (k + 1) * 4 * ALL], held_right.at[slot]),
            ]
        elif k == 4:
            pairs = [
                (left.at[2 * D : 3 * D, :], held_left.at[slot, :D, :]),
                (right.at[:, 2 * FF :], held_right.at[slot, :, :D]),
            ]
        elif k < 7:
            first = 3 * D + (k - 5) * ALL
            pairs = [
                (left.at[first : first + ALL, :], held_left.at[slot, :ALL, :]),
                (rows_grad, held_right.at[slot]),
            ]
        else:
            pairs = [
                (left_post, held_left.at[slot]),
                (right_post, held_right.at[slot, :, :D]),
            ]
        return [
            pltpu.make_async_copy(source, target, load_sem.at[slot, i])
            for i, (source, target) in enumerate(pairs)
        ]

    def compute(k):
        for copy in loads(k):
            copy.wait()
        if k + 1 < CHUNKS:
            for copy in loads(k + 1):
                copy.start()
        slot = k % 2
        by_left = {4: 2, 7: 1}.get(k, 4)

        def unit(j, carry):
            if by_left == 4:
                a, b = 0, j
            elif by_left == 2:
                a, b = j // 2, lax.rem(j, 2)
            else:
                a, b = j, 0
            lhs = held_left[slot, pl.ds(pl.multiple_of(a * ALL, ALL), ALL), :]
            rhs = held_right[slot, :, pl.ds(pl.multiple_of(b * ALL, ALL), ALL)]
            value = nn(lhs, rhs)
            for c in range(3):
                rows_of(part, k * CHUNK + j * UNIT + c * ALL, ALL)[...] = value[
                    :, c * 128 : (c + 1) * 128
                ].astype(BF)
            return carry

        lax.fori_loop(0, 2 if k == 7 else 4, unit, 0)
        ones = jnp.ones((16, tokens), BF)
        if k in (0, 1, 4, 5):
            wide = 2 if k == 4 else 4
            first = {0: 28, 1: 32, 4: 36, 5: 38}[k]
            total = nn(ones, held_right[slot, :, : wide * ALL])
            for j in range(wide):
                sums[first + j : first + j + 1, :] = total[0:1, j * ALL : (j + 1) * ALL]
        if k == 7:
            span = nn(held_left[slot, D:, :], held_right[slot, :, ALL:D])
            for c in range(3):
                part[SPAN_ROW + c * 128 : SPAN_ROW + (c + 1) * 128, :] = span[
                    :, c * 128 : (c + 1) * 128
                ].astype(BF)
            sums[42:43, :] = nn(ones, held_right[slot, :, :ALL])[0:1]
            sums[43:44, :128] = nt(ones, held_left[slot, D:, :])[0:1]
            for first, a, b in ((0, stat_a, stat_b), (10, depth_a, depth_b)):
                for i in range(a.shape[0] // 8):
                    both = jnp.sum(a[i * 8 : i * 8 + 8] + b[i * 8 : i * 8 + 8], axis=0, keepdims=True)
                    sums[first + 2 * i : first + 2 * i + 1, :] = both[:, :ALL]
                    sums[first + 2 * i + 1 : first + 2 * i + 2, :] = both[:, ALL:]
            small = sums[...].astype(BF)
            for c in range(3):
                part[SMALL_ROW + c * SMALL : SMALL_ROW + (c + 1) * SMALL, :] = small[
                    :, c * 128 : (c + 1) * 128
                ]
            part[SMALL_ROW + 3 * SMALL :, :] = jnp.zeros((PACKED - SMALL_ROW - 3 * SMALL, 128), BF)

    for copy in loads(0):
        copy.start()
    sums[...] = jnp.zeros_like(sums)
    if not remote:
        for k in range(CHUNKS):
            compute(k)
        pltpu.sync_copy(part, out)
        return
    res, *scratch = scratch
    exchange = Exchange(part, res, out, scratch)
    exchange.greet()
    parts = [p for k in range(CHUNKS) for p in chunk_parts(k)]
    for t in range(CHUNKS + 8):
        if t < CHUNKS:
            compute(t)
        if t == 0:
            exchange.await_greetings()
        for k in range(CHUNKS):
            if 0 <= t - k <= 8:
                for n in (2 * k, 2 * k + 1):
                    exchange.stage(n, parts[n], t - k)
    exchange.finish(parts)


def weights_call(remote, big, small):
    tokens = big[1].shape[0]
    n_parts = 2 * CHUNKS
    scratch = [
        pltpu.VMEM((2, D + 128, tokens), BF),
        pltpu.VMEM((2, tokens, 4 * ALL), BF),
        pltpu.VMEM((SMALL, ALL), F32),
        pltpu.VMEM((PACKED, 128), BF),
        pltpu.SemaphoreType.DMA((2, 2)),
    ]
    if remote:
        scratch += [
            pltpu.VMEM((PACKED, 128), BF),
            pltpu.VMEM((PACKED >> 1, 128), BF),
            pltpu.VMEM((PACKED >> 2, 128), BF),
            pltpu.VMEM((PACKED >> 3, 128), BF),
            pltpu.VMEM((3, PACKED >> 5, 128), BF),
            pltpu.VMEM((PACKED >> 1, 128), BF),
            pltpu.VMEM((PACKED >> 2, 128), BF),
            pltpu.VMEM((PACKED >> 3, 128), BF),
            pltpu.SemaphoreType.DMA((n_parts, 12)),
            pltpu.SemaphoreType.DMA((n_parts, 12)),
            pltpu.SemaphoreType.DMA((n_parts,)),
        ]
    more = dict(collective_id=0, has_side_effects=True) if remote else {}
    return pl.pallas_call(
        functools.partial(weights_body, remote),
        in_specs=[pl.BlockSpec(memory_space=pl.ANY)] * len(big)
        + [pl.BlockSpec(memory_space=pltpu.VMEM)] * len(small),
        out_specs=pl.BlockSpec(memory_space=pl.ANY),
        out_shape=jax.ShapeDtypeStruct((PACKED, 128), BF),
        scratch_shapes=scratch,
        compiler_params=params(**more),
        cost_estimate=pl.CostEstimate(
            flops=2 * 31 * ALL * ALL * tokens, bytes_accessed=50_000_000, transcendentals=0
        ),
        name="weights",
    )(*big, *small)


SMALL_OUTS = [
    ("gain_second", 0, D),
    ("shift_second", 2, D),
    ("gain_first", 4, D),
    ("shift_first", 6, D),
    ("bias_outer", 8, D),
    ("bias_inner", 28, FF),
    ("bias_output", 36, D),
    ("bias_unfold", 38, ALL),
    ("bias_query", 39, ALL),
    ("bias_value", 41, ALL),
    ("bias_point", 42, ALL),
    ("bias_span", 43, TAPS),
]


def unpack_body(unit, tail, inner, outer, output, unfold, project, point, span, depth, *small):
    step = pl.program_id(0)

    def tile():
        return jnp.concatenate([unit[c * ALL : (c + 1) * ALL, :] for c in range(3)], axis=1)

    @pl.when(step < 8)
    def _():
        inner[0] = tile().astype(F32)

    @pl.when((step >= 8) & (step < 16))
    def _():
        outer[0] = tile().T.astype(F32)

    @pl.when((step >= 16) & (step < 20))
    def _():
        output[...] = tile().astype(F32)

    @pl.when((step == 20) | (step == 24))
    def _():
        unfold[...] = tile().astype(F32)

    @pl.when((step > 20) & (step < 28) & (step != 24))
    def _():
        project[...] = tile().astype(F32)

    @pl.when(step >= 28)
    def _():
        point[...] = tile().astype(F32)

    @pl.when(step == 29)
    def _():
        wide = jnp.concatenate([tail[c * 128 : (c + 1) * 128, :] for c in range(3)], axis=1)
        span[...] = wide.astype(F32).T[:, :TAPS]
        rows = jnp.concatenate(
            [tail[ALL + c * SMALL : ALL + (c + 1) * SMALL, :] for c in range(3)], axis=1
        ).astype(F32)
        for j in range(KERNEL):
            for half in range(2):
                depth[j : j + 1, half * ALL : (half + 1) * ALL] = rows[10 + 2 * j + half :][:1]
        for ref, (_, first, size) in zip(small, SMALL_OUTS):
            for i in range(max(1, size // ALL)):
                wide = min(size, ALL)
                ref[i * ALL : i * ALL + wide] = rows[first + i, :wide]


def unpack_call(packed):
    def span_of(first, count):
        return lambda s: jnp.clip(s - first, 0, count - 1)

    inner_at, outer_at, output_at, rows_at, point_at = (
        span_of(*v) for v in ((0, 8), (8, 8), (16, 4), (20, 8), (28, 2))
    )
    square = (ALL, ALL)
    specs = [
        ((GROUPS, ALL, 4 * ALL), pl.BlockSpec((1, ALL, ALL), lambda s: (inner_at(s) // 4, 0, inner_at(s) % 4))),
        ((GROUPS, 4 * ALL, ALL), pl.BlockSpec((1, ALL, ALL), lambda s: (outer_at(s) // 4, outer_at(s) % 4, 0))),
        ((D, D), pl.BlockSpec(square, lambda s: (output_at(s) // 2, output_at(s) % 2))),
        ((D, ALL), pl.BlockSpec(square, lambda s: (rows_at(s) // 4, 0))),
        ((D, 3 * ALL), pl.BlockSpec(square, lambda s: (rows_at(s) // 4, jnp.maximum(rows_at(s) % 4 - 1, 0)))),
        ((D, ALL), pl.BlockSpec(square, lambda s: (point_at(s), 0))),
        ((ALL, TAPS), pl.BlockSpec((ALL, TAPS), lambda s: (0, 0))),
        ((KERNEL, D), pl.BlockSpec((KERNEL, D), lambda s: (0, 0))),
    ]
    specs += [((size,), pl.BlockSpec((size,), lambda s: (0,))) for _, _, size in SMALL_OUTS]
    tail = 768
    return pl.pallas_call(
        unpack_body,
        grid=(30,),
        in_specs=[
            pl.BlockSpec((UNIT, 128), lambda s: (s, 0)),
            pl.BlockSpec((tail, 128), lambda s: (SPAN_ROW // tail, 0)),
        ],
        out_specs=[b for _, b in specs],
        out_shape=[jax.ShapeDtypeStruct(s, F32) for s, _ in specs],
        compiler_params=params(),
        cost_estimate=pl.CostEstimate(flops=0, bytes_accessed=27_000_000, transcendentals=0),
        name="unpack",
    )(packed, packed)


def shards(
    long_input,
    short_input,
    long_cotan,
    short_cotan,
    live_slots,
    w_project,
    bias_query,
    bias_value,
    depth_kernel,
    w_point,
    bias_point,
    w_span,
    bias_span,
    w_unfold,
    bias_unfold,
    w_output,
    bias_output,
    gain_first,
    shift_first,
    w_inner,
    bias_inner,
    w_outer,
    bias_outer,
    gain_second,
    shift_second,
):
    n_blk = lax.axis_size("blk")
    short_x = short_input.reshape(short_input.shape[2:])
    short_cot = short_cotan.reshape(short_cotan.shape[2:])
    vec = jnp.concatenate(
        [
            bias_query,
            bias_value,
            bias_point,
            bias_unfold,
            bias_output,
            gain_first,
            shift_first,
            bias_outer,
            gain_second,
            shift_second,
            bias_inner,
            depth_kernel.reshape(-1),
            bias_span,
            jnp.zeros((24 * D - 21 * D - TAPS,), BF),
        ]
    ).reshape(24, D).astype(F32)
    perm, spread = (jnp.asarray(t) for t in tap_tables())
    xs = [long_input] + [
        lax.ppermute(long_input, "blk", [(i, (i + k) % n_blk) for i in range(n_blk)])
        for k in range(1, n_blk)
    ]
    pre_consts = (vec, w_project, w_point, w_span, w_unfold, spread, perm)
    ffn_consts = (vec, w_output, w_inner, w_outer)
    *short_kept, short_mixed = pre_call([short_x], pre_consts)
    *long_kept, long_mixed = pre_call(xs, pre_consts)

    tokens = (long_input.shape[0] + short_x.shape[0]) * short_x.shape[1]
    l_out, l_fig, l_mg, *joint, l_stat = ffn_call(
        None, long_mixed, long_input, long_cotan, ffn_consts, (), tokens
    )
    s_out, s_fig, s_mg, left, right, s_stat = ffn_call(
        live_slots, short_mixed, short_x, short_cot, ffn_consts, joint, tokens
    )
    post_consts = (vec, w_point, w_span, spread, perm)
    l_post = post_call(xs, l_mg, l_fig, long_kept, post_consts, (), tokens)
    (*joint, l_dkg, own), l_rest = l_post[:4], l_post[4:]
    far, (l_qt, l_ug, l_tg) = l_rest[: n_blk - 1], l_rest[n_blk - 1 :]
    far = [
        lax.ppermute(a, "blk", [(i, (i - k) % n_blk) for i in range(n_blk)])
        for k, a in enumerate(far, 1)
    ]
    left_post, right_post, s_dkg, short_grad, rows_grad = post_call(
        [short_x], s_mg, s_fig, short_kept, post_consts + (w_project, w_unfold), joint, tokens
    )
    long_grad, rows_grad = end_call(own, far, l_qt, l_ug, l_tg, w_project, w_unfold, rows_grad)

    remote = lax.axis_size("dp") == 8 and n_blk == 4
    packed = weights_call(
        remote, (left, right, left_post, right_post, rows_grad), (l_stat, s_stat, l_dkg, s_dkg)
    )
    if not remote:
        packed = lax.psum(packed, ("dp", "blk"))
    inner, outer, output, unfold, project, point, span, depth, *small = unpack_call(packed)
    named = {name: value for (name, _, _), value in zip(SMALL_OUTS, small)}
    return (
        l_out,
        s_out.reshape(short_input.shape),
        long_grad,
        short_grad.reshape(short_input.shape),
        project,
        named["bias_query"],
        named["bias_value"],
        depth,
        point,
        named["bias_point"],
        span,
        named["bias_span"],
        unfold,
        named["bias_unfold"],
        output,
        named["bias_output"],
        named["gain_first"],
        named["shift_first"],
        inner,
        named["bias_inner"],
        outer,
        named["bias_outer"],
        named["gain_second"],
        named["shift_second"],
    )


def solution(mesh):
    rows = P("dp", "blk", None)
    slots = P("dp", "blk", None, None, None)
    in_specs = (rows, slots, rows, slots, P("dp", "blk")) + (P(),) * 20
    out_specs = (rows, slots, rows, slots) + (P(),) * 20
    return jax.shard_map(shards, mesh=mesh, in_specs=in_specs, out_specs=out_specs, check_vma=False)
```

```python
import functools

import jax
import jax.numpy as jnp
import numpy as np
from jax import lax
from jax.experimental import pallas as pl
from jax.experimental.pallas import tpu as pltpu
from jax.sharding import PartitionSpec as P

D = 768
FF = 3072
HEADS = 6
HEAD = 64
KERNEL = 9
GROUPS = 2
ALL = 384
PAIRS = 3
TAPS = HEADS * KERNEL
HALF = KERNEL // 2

F32 = jnp.float32
BF = jnp.bfloat16
ROOT_HALF = 0.7071067811865476
DENSITY = 0.3989422804014327
FFN_ROWS = 256
VMEM_BYTES = 58 * 1024 * 1024


def nn(a, b):
    return lax.dot_general(a, b, (((1,), (0,)), ((), ())), preferred_element_type=F32)


def nt(a, b):
    return lax.dot_general(a, b, (((1,), (1,)), ((), ())), preferred_element_type=F32)


def tn(a, b):
    return lax.dot_general(a, b, (((0,), (0,)), ((), ())), preferred_element_type=F32)


def tap_tables():
    perm = np.zeros((128, 128), np.float32)
    spread = np.zeros((256, PAIRS * KERNEL * 128), np.float32)
    for h in range(HEADS):
        for j in range(KERNEL):
            lane = j * HEADS + h
            perm[h * KERNEL + j, lane] = 1
            perm[h * KERNEL + j, TAPS + lane] = 1
            start = ((h // 2) * KERNEL + j) * 128 + (h % 2) * HEAD
            spread[lane, start : start + HEAD] = 1
            spread[128 + lane, start : start + HEAD] = 1
    return perm.astype(jnp.bfloat16), spread.astype(jnp.bfloat16)


def window(values, op):
    left = lambda v, n: pltpu.roll(v, 128 - n, 1)
    one = op(values, left(values, 6))
    two = op(one, left(one, 12))
    four = op(two, left(two, 24))
    return op(four, left(values, 48))


def window_sum(values):
    return window(values + pltpu.roll(values, TAPS, 1), jnp.add)


def head_stack(rows, low_half):
    zero = jnp.zeros_like(rows)
    return jnp.concatenate(
        [jnp.where(low_half, rows, zero), jnp.where(low_half, zero, rows)], axis=0
    )


def two_parts(values):
    high = values.astype(BF)
    rest = (values - high.astype(F32)).astype(BF)
    return jnp.concatenate([high, rest], axis=1)


def fill_ends(xp, x_refs, rows, sides):
    for c in range(D // 128):
        cols = slice(c * 128, (c + 1) * 128)
        if sides is None:
            zero = jnp.zeros((8, 128), F32)
            xp[c, 0:8, :] = zero
            xp[c, 8 + rows : 16 + rows, :] = zero
        else:
            lower, upper = sides
            xp[c, 0:8, :] = x_refs[1][0, rows - 16 :, cols].astype(F32)[8:] * lower
            xp[c, 8 + rows : 16 + rows, :] = x_refs[-1][0, :16, cols].astype(F32)[:8] * upper
        xp[c, 8 : 8 + rows, :] = x_refs[0][0, :, cols].astype(F32)


def row_sides():
    place = lax.axis_index("blk")
    count = lax.axis_size("blk")
    return (place > 0).astype(F32), (place < count - 1).astype(F32)


def as_row(ref):
    return ref[...].astype(F32).reshape(1, ref.shape[0])


def pre_body(n_x, *refs):
    x_refs, refs = refs[:n_x], refs[n_x:]
    bias_query, bias_value, bias_point, bias_span, bias_unfold, depth_kernel = refs[:6]
    w_project, w_point, w_span, w_unfold, spread, perm = refs[6:12]
    q_out, k_out, v_out, p_out, kc_out, ker_out, dl_out, up_out, mix_out = refs[12:21]
    xp, vec = refs[21:]

    @pl.when(pl.program_id(0) == 0)
    def _():
        vec[16:24, :] = jnp.zeros((8, D), F32)
        vec[0:1, :ALL] = as_row(bias_query)
        vec[0:1, ALL:] = as_row(bias_value)
        vec[1:2, :ALL] = as_row(bias_point)
        vec[1:2, ALL:] = as_row(bias_unfold)
        vec[21:22, :TAPS] = as_row(bias_span)
        vec[8:17, :] = depth_kernel[...].astype(F32)

    rows = x_refs[0].shape[1]
    is_long = n_x > 1
    sides = row_sides() if is_long else None
    x = x_refs[0][0]
    fill_ends(xp, x_refs, rows, sides)
    bias_query = vec[0:1, :ALL]
    bias_value = vec[0:1, ALL:]
    if is_long:
        q = (nn(x, w_project[:, :ALL]) + bias_query).astype(BF)
        for i in range(n_x):
            both = nn(x_refs[i][0], w_project[:, ALL:])
            k_out[0, i * rows : (i + 1) * rows, :] = both[:, :ALL].astype(BF)
            v_out[0, i * rows : (i + 1) * rows, :] = (both[:, ALL:] + bias_value).astype(BF)
    else:
        both = nn(x, w_project[...])
        q = (both[:, :ALL] + bias_query).astype(BF)
        k_out[0] = both[:, ALL : 2 * ALL].astype(BF)
        v_out[0] = (both[:, 2 * ALL :] + bias_value).astype(BF)
    q_out[0] = q

    for c in range(D // 128):
        cols = slice(c * 128, (c + 1) * 128)
        total = vec[8:9, cols] * xp[c, 4 : 4 + rows, :]
        for j in range(1, KERNEL):
            total += vec[8 + j : 9 + j, cols] * xp[c, 4 + j : 4 + j + rows, :]
        dl_out[0, :, cols] = total.astype(BF)
    key_conv = nn(dl_out[0], w_point[...]) + vec[1:2, :ALL]
    kc_out[0] = key_conv
    span = (key_conv * q.astype(F32)).astype(BF)
    span_weights = tn(w_span[...], perm[:TAPS, :]).astype(BF)
    span_bias = nn(vec[16:24, :128].astype(BF), perm[...])[5:6]
    logits = nn(span, span_weights) + span_bias
    lane = lax.broadcasted_iota(jnp.int32, (rows, 128), 1)
    raised = jnp.where(lane < TAPS, jnp.exp(logits - window(logits, jnp.maximum)), 0.0)
    kernel = jnp.where(lane < TAPS, raised / window_sum(raised), 0.0)
    ker_out[0] = kernel

    bias_unfold = vec[1:2, ALL:]
    unfold_rows = nn(x, w_unfold[...]) + bias_unfold
    for c in range(PAIRS):
        up_out[0, c, 8 : 8 + rows, :] = unfold_rows[:, c * 128 : (c + 1) * 128]
    if is_long:
        lower, upper = sides
        ends = jnp.concatenate([x_refs[1][0, rows - 16 :, :], x_refs[-1][0, :16, :]], axis=0)
        unfold_ends = nn(ends, w_unfold[...]) + bias_unfold
        for c in range(PAIRS):
            cols = slice(c * 128, (c + 1) * 128)
            up_out[0, c, 0:8, :] = unfold_ends[8:16, cols] * lower
            up_out[0, c, 8 + rows : 16 + rows, :] = unfold_ends[16:24, cols] * upper
    else:
        zero = jnp.zeros((8, 128), F32)
        for c in range(PAIRS):
            up_out[0, c, 0:8, :] = zero
            up_out[0, c, 8 + rows : 16 + rows, :] = zero

    low_half = lax.broadcasted_iota(jnp.int32, (1, 128), 1) < HEAD
    parts = two_parts(kernel)
    scaled = q * jnp.asarray(HEAD ** (-0.5), BF)
    keys = k_out.shape[1]
    for p in range(PAIRS):
        cols = slice(p * 128, (p + 1) * 128)
        wide = nn(parts, spread[:, p * KERNEL * 128 : (p + 1) * KERNEL * 128])
        total = wide[:, :128] * up_out[0, p, 4 : 4 + rows, :]
        for j in range(1, KERNEL):
            total += wide[:, j * 128 : (j + 1) * 128] * up_out[0, p, 4 + j : 4 + j + rows, :]
        mix_out[0, :, ALL + p * 128 : ALL + (p + 1) * 128] = total.astype(BF)

        scores = nt(head_stack(k_out[0, :, cols], low_half), scaled[:, cols])
        for half in range(2):
            part = scores[half * keys : (half + 1) * keys]
            top = jnp.max(part, axis=0, keepdims=True)
            grown = jnp.exp(part - top)
            share = 1.0 / jnp.sum(grown, axis=0, keepdims=True)
            p_out[0, p, half * keys : (half + 1) * keys, :] = (grown * share).astype(BF)
        context = tn(head_stack(v_out[0, :, cols], low_half), p_out[0, p])
        mix_out[0, :, cols] = context.astype(BF).T


def block_spec(shape, index_map):
    return pl.BlockSpec(shape, index_map)


def fixed(array):
    zeros = (0,) * array.ndim
    return pl.BlockSpec(array.shape, lambda *_: zeros, pipeline_mode=pl.Buffered(1))


def per_row(*shape):
    zeros = (0,) * len(shape)
    return pl.BlockSpec((1, *shape), lambda i: (i, *zeros))


def params(**more):
    return pltpu.CompilerParams(vmem_limit_bytes=VMEM_BYTES, **more)


def pre_call(xs, consts):
    count, rows = xs[0].shape[0], xs[0].shape[1]
    keys = rows * len(xs)
    shapes = [
        ((rows, ALL), BF),
        ((keys, ALL), BF),
        ((keys, ALL), BF),
        ((PAIRS, 2 * keys, rows), BF),
        ((rows, ALL), F32),
        ((rows, 128), F32),
        ((rows, D), BF),
        ((PAIRS, rows + 16, 128), F32),
        ((rows, D), BF),
    ]
    return pl.pallas_call(
        functools.partial(pre_body, len(xs)),
        grid=(count,),
        in_specs=[per_row(rows, D)] * len(xs) + [fixed(c) for c in consts],
        out_specs=[per_row(*s) for s, _ in shapes],
        out_shape=[jax.ShapeDtypeStruct((count, *s), t) for s, t in shapes],
        scratch_shapes=[pltpu.VMEM((D // 128, rows + 16, 128), F32), pltpu.VMEM((24, D), F32)],
        compiler_params=params(),
        cost_estimate=pl.CostEstimate(
            flops=count * rows * 6_000_000, bytes_accessed=20_000_000, transcendentals=1_000_000
        ),
        name="pre_long" if len(xs) > 1 else "pre_short",
    )(*xs, *consts)


def norm_stats(z):
    centre = z - jnp.mean(z, axis=-1, keepdims=True)
    inverse = lax.rsqrt(jnp.mean(centre * centre, axis=-1, keepdims=True) + 1e-12)
    return centre * inverse, inverse


def norm_back(upstream, normed, inverse, gain):
    scaled = upstream * gain
    plain = jnp.mean(scaled, axis=-1, keepdims=True)
    cross = jnp.mean(scaled * normed, axis=-1, keepdims=True)
    return inverse * (scaled - plain - normed * cross)


def fold8(values):
    return jnp.sum(values.reshape(values.shape[0] // 8, 8, values.shape[1]), axis=0)


def gelu_pair(v):
    cdf = 0.5 * (1.0 + lax.erf(v * ROOT_HALF))
    return v * cdf, cdf + v * jnp.exp(-0.5 * (v * v)) * DENSITY


def ffn_body(slot_rows, *refs):
    masked = slot_rows > 0
    if masked:
        live_ref, *refs = refs
    mix_ref, x_ref, cot_ref = refs[:3]
    vectors, (w_output, w_inner, w_outer) = refs[3:10], refs[10:13]
    out_ref, fig_ref, mg_ref, left, right, stat, slope, vec = refs[-8:]
    inl_ref, act_ref = right.at[:, :FF], right.at[:, FF : 2 * FF]
    step = pl.program_id(0)
    rows = x_ref.shape[1]

    @pl.when(step == 0)
    def _():
        stat[...] = jnp.zeros_like(stat)
        for i, ref in enumerate(vectors[:-1]):
            vec[2 + i : 3 + i, :] = as_row(ref)
        inner_row = as_row(vectors[-1])
        for i in range(FF // D):
            vec[8 + i : 9 + i, :] = inner_row[:, i * D : (i + 1) * D]

    x = x_ref[0]
    mixed = mix_ref[0]
    left[2 * D : 3 * D, :] = mixed.T
    left[3 * D :, :] = x.T
    first_normed, first_inverse = norm_stats(nn(mixed, w_output[...]) + vec[2:3, :] + x.astype(F32))
    first_norm = first_normed * vec[3:4, :] + vec[4:5, :]
    first_low = first_norm.astype(BF)
    left[:D, :] = first_low.T
    outer = []
    for g in range(GROUPS):
        for c in range(2):
            k = g * 2 + c
            inner = nn(first_low[:, g * ALL : (g + 1) * ALL], w_inner[g, :, c * D : (c + 1) * D])
            for r in range(0, rows, 16):
                act, slo = gelu_pair(inner[r : r + 16] + vec[8 + k : 9 + k, :])
                act_ref[r : r + 16, k * D : (k + 1) * D] = act.astype(BF)
                slope[r : r + 16, k * D : (k + 1) * D] = slo
        outer.append(nn(act_ref[:, g * 2 * D : (g + 1) * 2 * D], w_outer[g]))
    second_normed, second_inverse = norm_stats(
        jnp.concatenate(outer, axis=1) + vec[5:6, :] + first_norm
    )
    gain_second = vec[6:7, :]
    out_ref[0] = (second_normed * gain_second + vec[7:8, :]).astype(BF)
    seed = cot_ref[0].astype(F32)
    if masked:
        token = step * rows + lax.broadcasted_iota(jnp.int32, (rows, 1), 0)
        seed = jnp.where(token < live_ref[0, 0] * slot_rows, seed, 0.0)
    stat[0:8, :] += fold8(seed * second_normed)
    stat[8:16, :] += fold8(seed)
    second_grad = norm_back(seed, second_normed, second_inverse, gain_second)
    outer_low = second_grad.astype(BF)
    left[D : 2 * D, :] = outer_low.T
    stat[32:40, :] += fold8(outer_low.astype(F32))
    first_grad = []
    for g in range(GROUPS):
        for c in range(2):
            k = g * 2 + c
            back = nt(outer_low[:, g * ALL : (g + 1) * ALL], w_outer[g, c * D : (c + 1) * D, :])
            inl_ref[:, k * D : (k + 1) * D] = (back * slope[:, k * D : (k + 1) * D]).astype(BF)
        first_grad.append(nt(inl_ref[:, g * 2 * D : (g + 1) * 2 * D], w_inner[g]))
    first_grad = second_grad + jnp.concatenate(first_grad, axis=1)
    stat[16:24, :] += fold8(first_grad * first_normed)
    stat[24:32, :] += fold8(first_grad)
    first_in_grad = norm_back(first_grad, first_normed, first_inverse, vec[3:4, :])
    fig_ref[0] = first_in_grad
    attended_low = first_in_grad.astype(BF)
    right[:, 2 * FF :] = attended_low
    mg_ref[0] = nt(attended_low, w_output[...]).astype(BF)


def ffn_call(live, slot_rows, mixed, x, cotan, consts, joint, tokens):
    count, rows = x.shape[0], x.shape[1]
    total = count * rows
    masked = live is not None
    first = 0 if masked else tokens // rows - count
    n_in = (4 if masked else 3) + len(consts)
    out_shapes = [
        ((count, rows, D), BF, per_row(rows, D)),
        ((count, rows, D), F32, per_row(rows, D)),
        ((count, rows, D), BF, per_row(rows, D)),
        ((4 * D, tokens), BF, pl.BlockSpec((4 * D, rows), lambda i: (0, first + i))),
        ((tokens, 2 * FF + D), BF, pl.BlockSpec((rows, 2 * FF + D), lambda i: (first + i, 0))),
        ((40, D), F32, pl.BlockSpec((40, D), lambda i: (0, 0))),
    ]
    head = [live] if masked else []
    head_specs = [pl.BlockSpec(memory_space=pltpu.SMEM)] if masked else []
    return pl.pallas_call(
        functools.partial(ffn_body, slot_rows if masked else 0),
        grid=(count,),
        in_specs=head_specs
        + [per_row(rows, D)] * 3
        + [fixed(c) for c in consts]
        + [pl.BlockSpec(memory_space=pl.ANY)] * len(joint),
        out_specs=[s for _, _, s in out_shapes],
        out_shape=[jax.ShapeDtypeStruct(s, t) for s, t, _ in out_shapes],
        scratch_shapes=[pltpu.VMEM((rows, FF), F32), pltpu.VMEM((16, D), F32)],
        input_output_aliases={n_in: 3, n_in + 1: 4} if masked else {},
        compiler_params=params(),
        cost_estimate=pl.CostEstimate(
            flops=total * 12_000_000, bytes_accessed=30_000_000, transcendentals=total * FF
        ),
        name="ffn_short" if masked else "ffn_long",
    )(*head, mixed, x, cotan, *consts, *joint)


def post_body(n_x, *refs):
    is_long = n_x > 1
    x_refs = refs[:n_x]
    refs = refs[n_x:]
    (mg_ref, fig_ref, q_ref, k_ref, v_ref, p_ref, kc_ref, ker_ref, dl_ref, up_ref) = refs[:10]
    (depth_kernel, w_point, w_span, spread, perm) = refs[10:15]
    refs = refs[15:]
    if not is_long:
        (w_project, w_unfold), refs = refs[:2], refs[4:]
    (left, right, dkg), refs = refs[:3], refs[3:]
    if is_long:
        own_out, *far_outs = refs[:n_x]
        qt_out, ug_out, tg_out = refs[n_x : n_x + 3]
        xp, dgp, prp, dq_scr = refs[n_x + 3 :]
    else:
        tg_out, ru_out, dgp, prp, dq_scr = refs
    step = pl.program_id(0)
    rows = x_refs[0].shape[1]
    keys = k_ref.shape[1]
    ext = 8 if is_long else 0

    @pl.when(step == 0)
    def _():
        dkg[...] = jnp.zeros_like(dkg)
        dgp[...] = jnp.zeros_like(dgp)
        prp[...] = jnp.zeros_like(prp)

    if is_long:
        lower, upper = row_sides()
        fill_ends(xp, x_refs, rows, (lower, upper))

    q = q_ref[0]
    qf = q.astype(F32)
    scaled = q * jnp.asarray(HEAD ** (-0.5), BF)
    low_half = lax.broadcasted_iota(jnp.int32, (1, 128), 1) < HEAD
    for p in range(PAIRS):
        cols = slice(p * 128, (p + 1) * 128)
        grad = mg_ref[0, :, cols]
        weight_grad = nt(head_stack(v_ref[0, :, cols], low_half), grad)
        low = []
        for half in range(2):
            part = slice(half * keys, (half + 1) * keys)
            probs = p_ref[0, p, part, :].astype(F32)
            inner = jnp.sum(probs * weight_grad[part], axis=0, keepdims=True)
            low.append((probs * (weight_grad[part] - inner)).astype(BF))
        score_low = jnp.concatenate(low, axis=0)
        value_grad = nn(p_ref[0, p], grad)
        value_grad = jnp.where(low_half, value_grad[:keys], value_grad[keys:])
        key_grad = nn(score_low, scaled[:, cols])
        key_grad = jnp.where(low_half, key_grad[:keys], key_grad[keys:])
        query_grad = tn(head_stack(k_ref[0, :, cols], low_half), score_low) * HEAD ** (-0.5)
        dq_scr[:, cols] = query_grad.T
        if is_long:
            own_out[0, :, cols] = key_grad[:rows]
            own_out[0, :, ALL + p * 128 : ALL + (p + 1) * 128] = value_grad[:rows]
            for i in range(1, n_x):
                block = slice(i * rows, (i + 1) * rows)
                far_outs[i - 1][0, :rows, cols] = key_grad[block].astype(BF)
                far_outs[i - 1][0, :rows, ALL + p * 128 : ALL + (p + 1) * 128] = value_grad[
                    block
                ].astype(BF)
        else:
            ru_out[:, 2 * ALL + p * 128 : 2 * ALL + (p + 1) * 128] = key_grad.astype(BF)
            ru_out[:, 3 * ALL + p * 128 : 3 * ALL + (p + 1) * 128] = value_grad.astype(BF)

    kernel = ker_ref[0]
    parts = two_parts(kernel)
    kernel_grad = jnp.zeros((rows, 128), F32)
    span_rows = rows + 2 * ext
    for p in range(PAIRS):
        cols = slice(p * 128, (p + 1) * 128)
        table = slice(p * KERNEL * 128, (p + 1) * KERNEL * 128)
        grad = mg_ref[0, :, ALL + p * 128 : ALL + (p + 1) * 128].astype(F32)
        wide = nn(parts, spread[:, table])
        products = []
        for j in range(KERNEL):
            products.append((grad * up_ref[0, p, 4 + j : 4 + j + rows, :]).astype(BF))
            prp[j, 16 : 16 + rows, :] = wide[:, j * 128 : (j + 1) * 128] * grad
        kernel_grad += nt(jnp.concatenate(products, axis=1), spread[:128, table])
        first = 20 - ext
        total = prp[0, first : first + span_rows, :]
        for j in range(1, KERNEL):
            total += prp[j, first - j : first - j + span_rows, :]
        if is_long:
            ug_out[0, :, cols] = total[ext : ext + rows]
            far_outs[0][0, rows + 8 : rows + 16, cols] = (total[:ext] * lower).astype(BF)
            far_outs[-1][0, rows + 8 : rows + 16, cols] = (total[ext + rows :] * upper).astype(BF)
        else:
            ru_out[:, cols] = total.astype(BF)
    if is_long:
        zero = jnp.zeros((8, ALL), BF)
        far_outs[0][0, rows + 8 : rows + 16, ALL:] = zero
        far_outs[-1][0, rows + 8 : rows + 16, ALL:] = zero

    logit_low = (kernel * (kernel_grad - window_sum(kernel * kernel_grad))).astype(BF)
    left[D:, :] = nt(perm[...], logit_low).astype(BF)
    span_grad = nn(logit_low, tn(perm[:TAPS, :], w_span[...]).astype(BF))
    key_conv = kc_ref[0]
    right[:, ALL:] = (key_conv * qf).astype(BF)
    left[:D, :] = dl_ref[0].T
    point_low = (span_grad * qf).astype(BF)
    right[:, :ALL] = point_low
    query_total = (dq_scr[...] + span_grad * key_conv).astype(BF)
    depth_grad = nt(point_low, w_point[...])
    for c in range(D // 128):
        dgp[c, 16 : 16 + rows, :] = depth_grad[:, c * 128 : (c + 1) * 128]

    if not is_long:
        ru_out[:, ALL : 2 * ALL] = query_total
        base = nt(ru_out[:, :ALL], w_unfold[...]) + nt(ru_out[:, ALL:], w_project[...])
    else:
        qt_out[0] = query_total
    for c in range(D // 128):
        cols = slice(c * 128, (c + 1) * 128)
        x_part = xp[c] if is_long else x_refs[0][0, :, cols].astype(F32)
        first = 20 - ext
        total = None
        for j in range(KERNEL):
            moved = dgp[c, first - j : first - j + span_rows, :]
            term = depth_kernel[j : j + 1, cols].astype(F32) * moved
            total = term if total is None else total + term
            dkg[j * 8 : (j + 1) * 8, cols] += fold8(moved * x_part)
        if is_long:
            tg_out[0, :, cols] = total[ext : ext + rows] + fig_ref[0, :, cols]
            far_outs[0][0, rows : rows + 8, cols] = (total[:ext] * lower).astype(BF)
            far_outs[-1][0, rows : rows + 8, cols] = (total[ext + rows :] * upper).astype(BF)
        else:
            tg_out[0, :, cols] = total + fig_ref[0, :, cols] + base[:, cols]


def post_call(xs, mg, fig, kept, consts, joint, tokens):
    count, rows = xs[0].shape[0], xs[0].shape[1]
    keys = rows * len(xs)
    total = count * rows
    is_long = len(xs) > 1
    first = tokens // rows - count if is_long else 0
    row_args = [mg, fig, *kept]
    outs = [
        ((D + 128, tokens), BF, pl.BlockSpec((D + 128, rows), lambda i: (0, first + i))),
        ((tokens, 2 * ALL), BF, pl.BlockSpec((rows, 2 * ALL), lambda i: (first + i, 0))),
        ((KERNEL * 8, D), F32, pl.BlockSpec((KERNEL * 8, D), lambda i: (0, 0))),
    ]
    row_out = lambda r, c, t: ((count, r, c), t, per_row(r, c))
    scratch = []
    if is_long:
        outs.append(row_out(rows, D, F32))
        for i in range(1, len(xs)):
            outs.append(row_out(rows + 16 if i in (1, len(xs) - 1) else rows, D, BF))
        outs += [row_out(rows, ALL, BF), row_out(rows, ALL, F32), row_out(rows, D, F32)]
        scratch.append(pltpu.VMEM((D // 128, rows + 16, 128), F32))
    else:
        outs += [
            row_out(rows, D, F32),
            ((tokens, 4 * ALL), BF, pl.BlockSpec((rows, 4 * ALL), lambda i: (first + i, 0))),
        ]
    scratch += [
        pltpu.VMEM((D // 128, rows + 32, 128), F32),
        pltpu.VMEM((KERNEL, rows + 32, 128), F32),
        pltpu.VMEM((rows, ALL), F32),
    ]
    inputs = [*xs, *row_args, *consts]
    return pl.pallas_call(
        functools.partial(post_body, len(xs)),
        grid=(count,),
        in_specs=[per_row(rows, D)] * len(xs)
        + [per_row(*a.shape[1:]) for a in row_args]
        + [fixed(c) for c in consts]
        + [pl.BlockSpec(memory_space=pl.ANY)] * len(joint),
        out_specs=[s for _, _, s in outs],
        out_shape=[jax.ShapeDtypeStruct(s, t) for s, t, _ in outs],
        scratch_shapes=scratch,
        input_output_aliases={len(inputs) + i: i for i in range(len(joint))},
        compiler_params=params(),
        cost_estimate=pl.CostEstimate(
            flops=total * 10_000_000, bytes_accessed=30_000_000, transcendentals=0
        ),
        name="post_long" if is_long else "post_short",
    )(*inputs, *joint)


def end_body(n_x, *refs):
    own, *rest = refs[:n_x]
    qt, ug, tg, w_project, w_unfold, _, out_ref, ru_out = refs[n_x:]
    rows = own.shape[1]
    both = own[0]
    for far in rest:
        both = both + far[0, :rows, :].astype(F32)
    from_next, from_prev = rest[0], rest[-1]
    unfold = ug[0]
    after = from_next[0, rows:, :].astype(F32)
    before = from_prev[0, rows:, :].astype(F32)
    middle = unfold[8 : rows - 8]
    ru_out[:, :ALL] = jnp.concatenate(
        [unfold[:8] + before[8:, :ALL], middle, unfold[rows - 8 :] + after[8:, :ALL]], axis=0
    ).astype(BF)
    ru_out[:, ALL : 2 * ALL] = qt[0]
    ru_out[:, 2 * ALL :] = both.astype(BF)
    total = nt(ru_out[:, :ALL], w_unfold[...]) + nt(ru_out[:, ALL:], w_project[...]) + tg[0]
    out_ref[0] = total
    out_ref[0, :8, :] = total[:8] + before[:8]
    out_ref[0, rows - 8 :, :] = total[rows - 8 :] + after[:8]


def end_call(own, far, qt, ug, tg, w_project, w_unfold, joint):
    count, rows = own.shape[0], own.shape[1]
    first = joint.shape[0] // rows - count
    row_args = [own, *far, qt, ug, tg]
    return pl.pallas_call(
        functools.partial(end_body, 1 + len(far)),
        grid=(count,),
        in_specs=[per_row(*a.shape[1:]) for a in row_args]
        + [fixed(w_project), fixed(w_unfold), pl.BlockSpec(memory_space=pl.ANY)],
        out_specs=[per_row(rows, D), pl.BlockSpec((rows, 4 * ALL), lambda i: (first + i, 0))],
        out_shape=[
            jax.ShapeDtypeStruct((count, rows, D), F32),
            jax.ShapeDtypeStruct(joint.shape, BF),
        ],
        input_output_aliases={len(row_args) + 2: 1},
        compiler_params=params(),
        cost_estimate=pl.CostEstimate(
            flops=count * rows * 2_400_000, bytes_accessed=10_000_000, transcendentals=0
        ),
        name="end_long",
    )(*row_args, w_project, w_unfold, joint)


UNIT = 3 * ALL
CHUNK = 4 * UNIT
CHUNKS = 8
LAST = 6 * 512
PACKED = (CHUNKS - 1) * CHUNK + LAST
SPAN_ROW = (CHUNKS - 1) * CHUNK + 2 * UNIT
SMALL_ROW = SPAN_ROW + ALL
SMALL = 48
MESH = pl.DeviceIdType.MESH


def chunk_parts(k):
    blocks = CHUNK // 512 if k < CHUNKS - 1 else LAST // 512
    first = (blocks + 1) // 2 if k % 2 == 0 else blocks // 2
    start = k * CHUNK
    middle = start + first * 512
    return [(start, first * 512, "cxy"), (middle, (blocks - first) * 512, "cyx")]


def rows_of(ref, start, count):
    return ref.at[pl.ds(pl.multiple_of(start, 16), count), :]


def add_rows(out, start, sources, count):
    step = next(s for s in (160, 128, 96, 80, 64, 48, 32, 16) if count % s == 0)

    def body(i, carry):
        total = None
        for ref, first in sources:
            value = rows_of(ref, first + i * step, step)[...].astype(F32)
            total = value if total is None else total + value
        rows_of(out, start + i * step, step)[...] = total.astype(BF)
        return carry

    lax.fori_loop(0, count // step, body, 0)


class Exchange:
    def __init__(self, part, res, out, scratch):
        self.part, self.res, self.out = part, res, out
        self.got = scratch[0:3]
        self.got_z = scratch[3]
        self.acc = scratch[4:7]
        self.send_sem, self.recv_sem, self.out_sem = scratch[7:10]
        dp, blk = lax.axis_index("dp"), lax.axis_index("blk")
        core, x, y, z = lax.rem(blk, 2), blk // 2, lax.rem(dp, 2), dp // 2
        self.z = z
        self.bit = {"c": core, "x": x, "y": y}
        self.peer = {
            "c": (dp, blk + 1 - 2 * core),
            "x": (dp, blk + 2 - 4 * x),
            "y": (dp + 1 - 2 * y, blk),
        }
        self.z_peer = [(lax.rem(z + i, 4) * 2 + y, blk) for i in (1, 2, 3)]
        self.open = {}
        self.sends = []
        self.place = {}

    def greet(self):
        barrier = pltpu.get_barrier_semaphore()
        for device in [*self.peer.values(), *self.z_peer]:
            pl.semaphore_signal(barrier, inc=1, device_id=device, device_id_type=MESH)

    def await_greetings(self):
        pl.semaphore_wait(pltpu.get_barrier_semaphore(), 6)

    def start(self, n, slot, source, target, device):
        copy = pltpu.make_async_remote_copy(
            src_ref=source,
            dst_ref=target,
            send_sem=self.send_sem.at[n, slot],
            recv_sem=self.recv_sem.at[n, slot],
            device_id=device,
            device_id_type=MESH,
        )
        copy.start()
        self.open[n, slot] = copy
        self.sends.append(copy)

    def stage(self, n, part, s):
        row, count, order = part
        bit, peer, acc, got, res = self.bit, self.peer, self.acc, self.got, self.res
        if 1 <= s <= 3:
            size = count >> s
            self.open[n, s - 1].wait_recv()
            before, first = (self.part, row) if s == 1 else (acc[s - 2], row >> (s - 1))
            mine = first + bit[order[s - 1]] * size
            add_rows(acc[s - 1], row >> s, [(before, mine), (got[s - 1], row >> s)], size)
        if s <= 2:
            size = count >> (s + 1)
            source, first = (self.part, row) if s == 0 else (acc[s - 1], row >> s)
            axis = order[s]
            other = first + (1 - bit[axis]) * size
            self.start(n, s, rows_of(source, other, size), rows_of(got[s], row >> (s + 1), size), peer[axis])
        elif s == 3:
            size = count >> 5
            for i in range(3):
                theirs = (row >> 3) + lax.rem(self.z + i + 1, 4) * size
                target = rows_of(self.got_z.at[i], row >> 5, size)
                self.start(n, 3 + i, rows_of(acc[2], theirs, size), target, self.z_peer[i])
        elif s == 4:
            size = count >> 5
            for i in range(3):
                self.open[n, 3 + i].wait_recv()
            place = row
            for level in range(3):
                place = place + bit[order[level]] * (count >> (level + 1))
            self.place[n] = place
            mine = place + self.z * size
            others = [(self.got_z.at[i], row >> 5) for i in range(3)]
            add_rows(res, mine, [(acc[2], (row >> 3) + self.z * size), *others], size)
            for i in range(3):
                block = rows_of(res, mine, size)
                self.start(n, 6 + i, block, block, self.z_peer[i])
        elif s <= 7:
            for slot in (6, 7, 8) if s == 5 else (s + 3,):
                self.open[n, slot].wait_recv()
            level = 7 - s
            size = count >> (level + 1)
            block = rows_of(res, self.place[n], size)
            self.start(n, s + 4, block, block, peer[order[level]])
            self.place[n] = self.place[n] - bit[order[level]] * size
        else:
            self.open[n, 11].wait_recv()
            pltpu.make_async_copy(
                rows_of(res, row, count), rows_of(self.out, row, count), self.out_sem.at[n]
            ).start()

    def finish(self, parts):
        for copy in self.sends:
            copy.wait_send()
        for n, (row, count, _) in enumerate(parts):
            pltpu.make_async_copy(
                rows_of(self.res, row, count), rows_of(self.out, row, count), self.out_sem.at[n]
            ).wait()


def weights_body(remote, *refs):
    left, right, left_post, right_post, rows_grad, stat_a, stat_b, depth_a, depth_b, out = refs[:10]
    held_left, held_right, sums, part, load_sem = refs[10:15]
    scratch = refs[15:]
    tokens = right.shape[0]

    def loads(k):
        slot = k % 2
        if k < 4:
            pairs = [
                (left.at[k * ALL : (k + 1) * ALL, :], held_left.at[slot, :ALL, :]),
                (right.at[:, k * 4 * ALL : (k + 1) * 4 * ALL], held_right.at[slot]),
            ]
        elif k == 4:
            pairs = [
                (left.at[2 * D : 3 * D, :], held_left.at[slot, :D, :]),
                (right.at[:, 2 * FF :], held_right.at[slot, :, :D]),
            ]
        elif k < 7:
            first = 3 * D + (k - 5) * ALL
            pairs = [
                (left.at[first : first + ALL, :], held_left.at[slot, :ALL, :]),
                (rows_grad, held_right.at[slot]),
            ]
        else:
            pairs = [
                (left_post, held_left.at[slot]),
                (right_post, held_right.at[slot, :, :D]),
            ]
        return [
            pltpu.make_async_copy(source, target, load_sem.at[slot, i])
            for i, (source, target) in enumerate(pairs)
        ]

    def compute(k):
        for copy in loads(k):
            copy.wait()
        if k + 1 < CHUNKS:
            for copy in loads(k + 1):
                copy.start()
        slot = k % 2
        by_left = {4: 2, 7: 1}.get(k, 4)

        def unit(j, carry):
            if by_left == 4:
                a, b = 0, j
            elif by_left == 2:
                a, b = j // 2, lax.rem(j, 2)
            else:
                a, b = j, 0
            lhs = held_left[slot, pl.ds(pl.multiple_of(a * ALL, ALL), ALL), :]
            rhs = held_right[slot, :, pl.ds(pl.multiple_of(b * ALL, ALL), ALL)]
            value = nn(lhs, rhs)
            for c in range(3):
                rows_of(part, k * CHUNK + j * UNIT + c * ALL, ALL)[...] = value[
                    :, c * 128 : (c + 1) * 128
                ].astype(BF)
            return carry

        lax.fori_loop(0, 2 if k == 7 else 4, unit, 0)
        ones = jnp.ones((16, tokens), BF)
        if k in (0, 1, 4, 5):
            wide = 2 if k == 4 else 4
            first = {0: 28, 1: 32, 4: 36, 5: 38}[k]
            total = nn(ones, held_right[slot, :, : wide * ALL])
            for j in range(wide):
                sums[first + j : first + j + 1, :] = total[0:1, j * ALL : (j + 1) * ALL]
        if k == 7:
            span = nn(held_left[slot, D:, :], held_right[slot, :, ALL:D])
            for c in range(3):
                part[SPAN_ROW + c * 128 : SPAN_ROW + (c + 1) * 128, :] = span[
                    :, c * 128 : (c + 1) * 128
                ].astype(BF)
            sums[42:43, :] = nn(ones, held_right[slot, :, :ALL])[0:1]
            sums[43:44, :128] = nt(ones, held_left[slot, D:, :])[0:1]
            for first, a, b in ((0, stat_a, stat_b), (10, depth_a, depth_b)):
                for i in range(a.shape[0] // 8):
                    both = jnp.sum(a[i * 8 : i * 8 + 8] + b[i * 8 : i * 8 + 8], axis=0, keepdims=True)
                    sums[first + 2 * i : first + 2 * i + 1, :] = both[:, :ALL]
                    sums[first + 2 * i + 1 : first + 2 * i + 2, :] = both[:, ALL:]
            small = sums[...].astype(BF)
            for c in range(3):
                part[SMALL_ROW + c * SMALL : SMALL_ROW + (c + 1) * SMALL, :] = small[
                    :, c * 128 : (c + 1) * 128
                ]
            part[SMALL_ROW + 3 * SMALL :, :] = jnp.zeros((PACKED - SMALL_ROW - 3 * SMALL, 128), BF)

    for copy in loads(0):
        copy.start()
    sums[...] = jnp.zeros_like(sums)
    if not remote:
        for k in range(CHUNKS):
            compute(k)
        pltpu.sync_copy(part, out)
        return
    res, *scratch = scratch
    exchange = Exchange(part, res, out, scratch)
    exchange.greet()
    parts = [p for k in range(CHUNKS) for p in chunk_parts(k)]
    for t in range(CHUNKS + 8):
        if t < CHUNKS:
            compute(t)
        if t == 0:
            exchange.await_greetings()
        for k in range(CHUNKS):
            if 0 <= t - k <= 8:
                for n in (2 * k, 2 * k + 1):
                    exchange.stage(n, parts[n], t - k)
    exchange.finish(parts)


def weights_call(remote, big, small):
    tokens = big[1].shape[0]
    n_parts = 2 * CHUNKS
    scratch = [
        pltpu.VMEM((2, D + 128, tokens), BF),
        pltpu.VMEM((2, tokens, 4 * ALL), BF),
        pltpu.VMEM((SMALL, ALL), F32),
        pltpu.VMEM((PACKED, 128), BF),
        pltpu.SemaphoreType.DMA((2, 2)),
    ]
    if remote:
        scratch += [
            pltpu.VMEM((PACKED, 128), BF),
            pltpu.VMEM((PACKED >> 1, 128), BF),
            pltpu.VMEM((PACKED >> 2, 128), BF),
            pltpu.VMEM((PACKED >> 3, 128), BF),
            pltpu.VMEM((3, PACKED >> 5, 128), BF),
            pltpu.VMEM((PACKED >> 1, 128), BF),
            pltpu.VMEM((PACKED >> 2, 128), BF),
            pltpu.VMEM((PACKED >> 3, 128), BF),
            pltpu.SemaphoreType.DMA((n_parts, 12)),
            pltpu.SemaphoreType.DMA((n_parts, 12)),
            pltpu.SemaphoreType.DMA((n_parts,)),
        ]
    more = dict(collective_id=0, has_side_effects=True) if remote else {}
    return pl.pallas_call(
        functools.partial(weights_body, remote),
        in_specs=[pl.BlockSpec(memory_space=pl.ANY)] * len(big)
        + [pl.BlockSpec(memory_space=pltpu.VMEM)] * len(small),
        out_specs=pl.BlockSpec(memory_space=pl.ANY),
        out_shape=jax.ShapeDtypeStruct((PACKED, 128), BF),
        scratch_shapes=scratch,
        compiler_params=params(**more),
        cost_estimate=pl.CostEstimate(
            flops=2 * 31 * ALL * ALL * tokens, bytes_accessed=50_000_000, transcendentals=0
        ),
        name="weights",
    )(*big, *small)


SMALL_OUTS = [
    ("gain_second", 0, D),
    ("shift_second", 2, D),
    ("gain_first", 4, D),
    ("shift_first", 6, D),
    ("bias_outer", 8, D),
    ("bias_inner", 28, FF),
    ("bias_output", 36, D),
    ("bias_unfold", 38, ALL),
    ("bias_query", 39, ALL),
    ("bias_value", 41, ALL),
    ("bias_point", 42, ALL),
    ("bias_span", 43, TAPS),
]


def unpack_body(block, inner, outer, output, unfold, project, point, span, depth, *small):
    step = pl.program_id(0)

    def tile(unit):
        start = unit * UNIT
        return jnp.concatenate(
            [block[start + c * ALL : start + (c + 1) * ALL, :] for c in range(3)], axis=1
        )

    @pl.when(step < 2)
    def _():
        for i in range(4):
            inner[0, :, i * ALL : (i + 1) * ALL] = tile(i).astype(F32)

    @pl.when((step >= 2) & (step < 4))
    def _():
        for i in range(4):
            outer[0, i * ALL : (i + 1) * ALL, :] = tile(i).T.astype(F32)

    @pl.when(step == 4)
    def _():
        for i in range(4):
            a, b = divmod(i, 2)
            output[a * ALL : (a + 1) * ALL, b * ALL : (b + 1) * ALL] = tile(i).astype(F32)

    @pl.when((step == 5) | (step == 6))
    def _():
        unfold[...] = tile(0).astype(F32)
        for i in range(3):
            project[:, i * ALL : (i + 1) * ALL] = tile(i + 1).astype(F32)

    @pl.when(step == 7)
    def _():
        for i in range(2):
            point[i * ALL : (i + 1) * ALL, :] = tile(i).astype(F32)
        tail = 2 * UNIT
        wide = jnp.concatenate(
            [block[tail + c * 128 : tail + (c + 1) * 128, :] for c in range(3)], axis=1
        )
        span[...] = wide[:TAPS].astype(F32)
        tail += ALL
        rows = jnp.concatenate(
            [block[tail + c * SMALL : tail + (c + 1) * SMALL, :] for c in range(3)], axis=1
        ).astype(F32)
        for j in range(KERNEL):
            for half in range(2):
                place = 10 + 2 * j + half
                depth[j : j + 1, half * ALL : (half + 1) * ALL] = rows[place : place + 1]
        for ref, (_, first, size) in zip(small, SMALL_OUTS):
            for i in range(max(1, size // ALL)):
                wide = min(size, ALL)
                ref[i * ALL : i * ALL + wide] = rows[first + i, :wide]


def unpack_call(packed):
    def at(first, count):
        return lambda s: jnp.clip(s - first, 0, count - 1)

    inner_at, outer_at, rows_at = at(0, 2), at(2, 2), at(5, 2)
    whole = lambda *shape: (shape, pl.BlockSpec(shape, lambda s: (0,) * len(shape)))
    specs = [
        ((GROUPS, ALL, 4 * ALL), pl.BlockSpec((1, ALL, 4 * ALL), lambda s: (inner_at(s), 0, 0))),
        ((GROUPS, 4 * ALL, ALL), pl.BlockSpec((1, 4 * ALL, ALL), lambda s: (outer_at(s), 0, 0))),
        whole(D, D),
        ((D, ALL), pl.BlockSpec((ALL, ALL), lambda s: (rows_at(s), 0))),
        ((D, 3 * ALL), pl.BlockSpec((ALL, 3 * ALL), lambda s: (rows_at(s), 0))),
        whole(D, ALL),
        whole(TAPS, ALL),
        whole(KERNEL, D),
    ]
    specs += [whole(size) for _, _, size in SMALL_OUTS]
    return pl.pallas_call(
        unpack_body,
        grid=(CHUNKS,),
        in_specs=[pl.BlockSpec((CHUNK, 128), lambda s: (s, 0))],
        out_specs=[b for _, b in specs],
        out_shape=[jax.ShapeDtypeStruct(s, F32) for s, _ in specs],
        compiler_params=params(),
        cost_estimate=pl.CostEstimate(flops=0, bytes_accessed=27_000_000, transcendentals=0),
        name="unpack",
    )(packed)


def shards(
    long_input,
    short_input,
    long_cotan,
    short_cotan,
    live_slots,
    w_project,
    bias_query,
    bias_value,
    depth_kernel,
    w_point,
    bias_point,
    w_span,
    bias_span,
    w_unfold,
    bias_unfold,
    w_output,
    bias_output,
    gain_first,
    shift_first,
    w_inner,
    bias_inner,
    w_outer,
    bias_outer,
    gain_second,
    shift_second,
):
    n_blk = lax.axis_size("blk")
    short_x = short_input.reshape(short_input.shape[2:])
    short_cot = short_cotan.reshape(short_cotan.shape[2:])
    perm, spread = (jnp.asarray(t) for t in tap_tables())
    xs = [long_input] + [
        lax.ppermute(long_input, "blk", [(i, (i + k) % n_blk) for i in range(n_blk)])
        for k in range(1, n_blk)
    ]
    span_t = w_span.T
    pre_consts = (
        bias_query, bias_value, bias_point, bias_span, bias_unfold, depth_kernel,
        w_project, w_point, span_t, w_unfold, spread, perm,
    )
    ffn_consts = (
        bias_output, gain_first, shift_first, bias_outer, gain_second, shift_second, bias_inner,
        w_output, w_inner, w_outer,
    )
    *short_kept, short_mixed = pre_call([short_x], pre_consts)
    *long_kept, long_mixed = pre_call(xs, pre_consts)

    tokens = (long_input.shape[0] + short_x.shape[0]) * short_x.shape[1]
    l_out, l_fig, l_mg, *joint, l_stat = ffn_call(
        None, 0, long_mixed, long_input, long_cotan, ffn_consts, (), tokens
    )
    s_out, s_fig, s_mg, left, right, s_stat = ffn_call(
        live_slots,
        short_x.shape[1],
        *(a.reshape(-1, FFN_ROWS, D) for a in (short_mixed, short_x, short_cot)),
        ffn_consts,
        joint,
        tokens,
    )
    s_fig, s_mg = s_fig.reshape(short_x.shape), s_mg.reshape(short_x.shape)
    post_consts = (depth_kernel, w_point, span_t, spread, perm)
    l_post = post_call(xs, l_mg, l_fig, long_kept, post_consts, (), tokens)
    (*joint, l_dkg, own), l_rest = l_post[:4], l_post[4:]
    far, (l_qt, l_ug, l_tg) = l_rest[: n_blk - 1], l_rest[n_blk - 1 :]
    far = [
        lax.ppermute(a, "blk", [(i, (i - k) % n_blk) for i in range(n_blk)])
        for k, a in enumerate(far, 1)
    ]
    left_post, right_post, s_dkg, short_grad, rows_grad = post_call(
        [short_x], s_mg, s_fig, short_kept, post_consts + (w_project, w_unfold), joint, tokens
    )
    long_grad, rows_grad = end_call(own, far, l_qt, l_ug, l_tg, w_project, w_unfold, rows_grad)

    remote = lax.axis_size("dp") == 8 and n_blk == 4
    packed = weights_call(
        remote, (left, right, left_post, right_post, rows_grad), (l_stat, s_stat, l_dkg, s_dkg)
    )
    if not remote:
        packed = lax.psum(packed, ("dp", "blk"))
    inner, outer, output, unfold, project, point, span, depth, *small = unpack_call(packed)
    named = {name: value for (name, _, _), value in zip(SMALL_OUTS, small)}
    return (
        l_out,
        s_out.reshape(short_input.shape),
        long_grad,
        short_grad.reshape(short_input.shape),
        project,
        named["bias_query"],
        named["bias_value"],
        depth,
        point,
        named["bias_point"],
        span.T,
        named["bias_span"],
        unfold,
        named["bias_unfold"],
        output,
        named["bias_output"],
        named["gain_first"],
        named["shift_first"],
        inner,
        named["bias_inner"],
        outer,
        named["bias_outer"],
        named["gain_second"],
        named["shift_second"],
    )


def solution(mesh):
    rows = P("dp", "blk", None)
    slots = P("dp", "blk", None, None, None)
    in_specs = (rows, slots, rows, slots, P("dp", "blk")) + (P(),) * 20
    out_specs = (rows, slots, rows, slots) + (P(),) * 20
    return jax.shard_map(shards, mesh=mesh, in_specs=in_specs, out_specs=out_specs, check_vma=False)
```

```python
import functools

import jax
import jax.numpy as jnp
import numpy as np
from jax import lax
from jax.experimental import pallas as pl
from jax.experimental.pallas import tpu as pltpu
from jax.sharding import PartitionSpec as P

D = 768
FF = 3072
HEADS = 6
HEAD = 64
KERNEL = 9
GROUPS = 2
ALL = 384
PAIRS = 3
TAPS = HEADS * KERNEL
HALF = KERNEL // 2

F32 = jnp.float32
BF = jnp.bfloat16
ROOT_HALF = 0.7071067811865476
DENSITY = 0.3989422804014327
FFN_ROWS = 256
FFN_LONG = 384
SHORT_BATCH = 2
LONG_BATCH = 1
VMEM_BYTES = 58 * 1024 * 1024


def nn(a, b):
    return lax.dot_general(a, b, (((1,), (0,)), ((), ())), preferred_element_type=F32)


def nt(a, b):
    return lax.dot_general(a, b, (((1,), (1,)), ((), ())), preferred_element_type=F32)


def tn(a, b):
    return lax.dot_general(a, b, (((0,), (0,)), ((), ())), preferred_element_type=F32)


def tap_tables():
    perm = np.zeros((128, 128), np.float32)
    spread = np.zeros((256, PAIRS * KERNEL * 128), np.float32)
    for h in range(HEADS):
        for j in range(KERNEL):
            lane = j * HEADS + h
            perm[h * KERNEL + j, lane] = 1
            perm[h * KERNEL + j, TAPS + lane] = 1
            start = ((h // 2) * KERNEL + j) * 128 + (h % 2) * HEAD
            spread[lane, start : start + HEAD] = 1
            spread[128 + lane, start : start + HEAD] = 1
    return perm.astype(jnp.bfloat16), spread.astype(jnp.bfloat16)


def window(values, op):
    left = lambda v, n: pltpu.roll(v, 128 - n, 1)
    one = op(values, left(values, 6))
    two = op(one, left(one, 12))
    four = op(two, left(two, 24))
    return op(four, left(values, 48))


def window_sum(values):
    return window(values + pltpu.roll(values, TAPS, 1), jnp.add)


def head_stack(rows, low_half):
    zero = jnp.zeros_like(rows)
    return jnp.concatenate(
        [jnp.where(low_half, rows, zero), jnp.where(low_half, zero, rows)], axis=0
    )


def two_parts(values):
    high = values.astype(BF)
    rest = (values - high.astype(F32)).astype(BF)
    return jnp.concatenate([high, rest], axis=1)


def fill_ends(xp, x_refs, sides):
    batch, rows = x_refs[0].shape[:2]
    for r in range(batch):
        for c in range(D // 128):
            cols = slice(c * 128, (c + 1) * 128)
            if sides is None:
                zero = jnp.zeros((8, 128), F32)
                xp[r, c, 0:8, :] = zero
                xp[r, c, 8 + rows : 16 + rows, :] = zero
            else:
                lower, upper = sides
                xp[r, c, 0:8, :] = x_refs[1][r, rows - 16 :, cols].astype(F32)[8:] * lower
                xp[r, c, 8 + rows : 16 + rows, :] = x_refs[-1][r, :16, cols].astype(F32)[:8] * upper
            xp[r, c, 8 : 8 + rows, :] = x_refs[0][r, :, cols].astype(F32)


def row_sides():
    place = lax.axis_index("blk")
    count = lax.axis_size("blk")
    return (place > 0).astype(F32), (place < count - 1).astype(F32)


def as_row(ref):
    return ref[...].astype(F32).reshape(1, ref.shape[0])


def pre_body(n_x, *refs):
    x_refs, refs = refs[:n_x], refs[n_x:]
    bias_query, bias_value, bias_point, bias_span, bias_unfold, depth_kernel = refs[:6]
    w_project, w_point, w_span, w_unfold, spread, perm = refs[6:12]
    q_out, k_out, v_out, p_out, kc_out, ker_out, dl_out, up_out, mix_out = refs[12:21]
    xp, vec = refs[21:]

    @pl.when(pl.program_id(0) == 0)
    def _():
        vec[16:24, :] = jnp.zeros((8, D), F32)
        vec[0:1, :ALL] = as_row(bias_query)
        vec[0:1, ALL:] = as_row(bias_value)
        vec[1:2, :ALL] = as_row(bias_point)
        vec[1:2, ALL:] = as_row(bias_unfold)
        vec[21:22, :TAPS] = as_row(bias_span)
        vec[8:17, :] = depth_kernel[...].astype(F32)

    batch, rows = x_refs[0].shape[:2]
    total_rows = batch * rows
    is_long = n_x > 1
    sides = row_sides() if is_long else None
    x = x_refs[0][...].reshape(total_rows, D)
    fill_ends(xp, x_refs, sides)
    bias_query = vec[0:1, :ALL]
    bias_value = vec[0:1, ALL:]
    by_row = lambda v: v.reshape(batch, rows, v.shape[-1])
    if is_long:
        q = (nn(x, w_project[:, :ALL]) + bias_query).astype(BF)
        for i in range(n_x):
            both = nn(x_refs[i][...].reshape(total_rows, D), w_project[:, ALL:])
            k_out[:, i * rows : (i + 1) * rows, :] = by_row(both[:, :ALL].astype(BF))
            v_out[:, i * rows : (i + 1) * rows, :] = by_row((both[:, ALL:] + bias_value).astype(BF))
    else:
        both = nn(x, w_project[...])
        q = (both[:, :ALL] + bias_query).astype(BF)
        k_out[...] = by_row(both[:, ALL : 2 * ALL].astype(BF))
        v_out[...] = by_row((both[:, 2 * ALL :] + bias_value).astype(BF))
    q_out[...] = by_row(q)

    for r in range(batch):
        for c in range(D // 128):
            cols = slice(c * 128, (c + 1) * 128)
            total = vec[8:9, cols] * xp[r, c, 4 : 4 + rows, :]
            for j in range(1, KERNEL):
                total += vec[8 + j : 9 + j, cols] * xp[r, c, 4 + j : 4 + j + rows, :]
            dl_out[r, :, cols] = total.astype(BF)
    key_conv = nn(dl_out[...].reshape(total_rows, D), w_point[...]) + vec[1:2, :ALL]
    kc_out[...] = by_row(key_conv)
    span = (key_conv * q.astype(F32)).astype(BF)
    span_weights = tn(w_span[...], perm[:TAPS, :]).astype(BF)
    span_bias = nn(vec[16:24, :128].astype(BF), perm[...])[5:6]
    logits = nn(span, span_weights) + span_bias
    lane = lax.broadcasted_iota(jnp.int32, (1, 128), 1)
    raised = jnp.where(lane < TAPS, jnp.exp(logits - window(logits, jnp.maximum)), 0.0)
    kernel = jnp.where(lane < TAPS, raised / window_sum(raised), 0.0)
    ker_out[...] = by_row(kernel)

    bias_unfold = vec[1:2, ALL:]
    unfold_rows = nn(x, w_unfold[...]) + bias_unfold
    for r in range(batch):
        if is_long:
            lower, upper = sides
            ends = jnp.concatenate([x_refs[1][r, rows - 16 :, :], x_refs[-1][r, :16, :]], axis=0)
            unfold_ends = nn(ends, w_unfold[...]) + bias_unfold
        for c in range(PAIRS):
            cols = slice(c * 128, (c + 1) * 128)
            up_out[r, c, 8 : 8 + rows, :] = unfold_rows[r * rows : (r + 1) * rows, cols]
            if is_long:
                up_out[r, c, 0:8, :] = unfold_ends[8:16, cols] * lower
                up_out[r, c, 8 + rows : 16 + rows, :] = unfold_ends[16:24, cols] * upper
            else:
                zero = jnp.zeros((8, 128), F32)
                up_out[r, c, 0:8, :] = zero
                up_out[r, c, 8 + rows : 16 + rows, :] = zero

    low_half = lane < HEAD
    parts = two_parts(kernel)
    scaled = q * jnp.asarray(HEAD ** (-0.5), BF)
    keys = k_out.shape[1]
    for p in range(PAIRS):
        cols = slice(p * 128, (p + 1) * 128)
        wide = nn(parts, spread[:, p * KERNEL * 128 : (p + 1) * KERNEL * 128])
        for r in range(batch):
            here = slice(r * rows, (r + 1) * rows)
            total = wide[here, :128] * up_out[r, p, 4 : 4 + rows, :]
            for j in range(1, KERNEL):
                total += wide[here, j * 128 : (j + 1) * 128] * up_out[r, p, 4 + j : 4 + j + rows, :]
            mix_out[r, :, ALL + p * 128 : ALL + (p + 1) * 128] = total.astype(BF)

            scores = nt(head_stack(k_out[r, :, cols], low_half), scaled[here, cols])
            for half in range(2):
                part = scores[half * keys : (half + 1) * keys]
                top = jnp.max(part, axis=0, keepdims=True)
                grown = jnp.exp(part - top)
                share = 1.0 / jnp.sum(grown, axis=0, keepdims=True)
                p_out[r, p, half * keys : (half + 1) * keys, :] = (grown * share).astype(BF)
            context = tn(head_stack(v_out[r, :, cols], low_half), p_out[r, p])
            mix_out[r, :, cols] = context.astype(BF).T


def fixed(array):
    zeros = (0,) * array.ndim
    return pl.BlockSpec(array.shape, lambda *_: zeros, pipeline_mode=pl.Buffered(1))


def per_row(*shape, batch=1):
    zeros = (0,) * len(shape)
    return pl.BlockSpec((batch, *shape), lambda i: (i, *zeros))


def params(**more):
    return pltpu.CompilerParams(vmem_limit_bytes=VMEM_BYTES, **more)


def pre_call(xs, consts, batch):
    count, rows = xs[0].shape[0], xs[0].shape[1]
    keys = rows * len(xs)
    shapes = [
        ((rows, ALL), BF),
        ((keys, ALL), BF),
        ((keys, ALL), BF),
        ((PAIRS, 2 * keys, rows), BF),
        ((rows, ALL), F32),
        ((rows, 128), F32),
        ((rows, D), BF),
        ((PAIRS, rows + 16, 128), F32),
        ((rows, D), BF),
    ]
    return pl.pallas_call(
        functools.partial(pre_body, len(xs)),
        grid=(count // batch,),
        in_specs=[per_row(rows, D, batch=batch)] * len(xs) + [fixed(c) for c in consts],
        out_specs=[per_row(*s, batch=batch) for s, _ in shapes],
        out_shape=[jax.ShapeDtypeStruct((count, *s), t) for s, t in shapes],
        scratch_shapes=[pltpu.VMEM((batch, D // 128, rows + 16, 128), F32), pltpu.VMEM((24, D), F32)],
        compiler_params=params(),
        cost_estimate=pl.CostEstimate(
            flops=count * rows * 6_000_000, bytes_accessed=20_000_000, transcendentals=1_000_000
        ),
        name="pre_long" if len(xs) > 1 else "pre_short",
    )(*xs, *consts)


def norm_stats(z):
    centre = z - jnp.mean(z, axis=-1, keepdims=True)
    inverse = lax.rsqrt(jnp.mean(centre * centre, axis=-1, keepdims=True) + 1e-12)
    return centre * inverse, inverse


def norm_back(upstream, normed, inverse, gain):
    scaled = upstream * gain
    plain = jnp.mean(scaled, axis=-1, keepdims=True)
    cross = jnp.mean(scaled * normed, axis=-1, keepdims=True)
    return inverse * (scaled - plain - normed * cross)


def fold8(values):
    return jnp.sum(values.reshape(values.shape[0] // 8, 8, values.shape[1]), axis=0)


def gelu_pair(v):
    cdf = 0.5 * (1.0 + lax.erf(v * ROOT_HALF))
    return v * cdf, cdf + v * jnp.exp(-0.5 * (v * v)) * DENSITY


def ffn_body(slot_rows, *refs):
    masked = slot_rows > 0
    if masked:
        live_ref, *refs = refs
    mix_ref, x_ref, cot_ref = refs[:3]
    vectors, (w_output, w_inner, w_outer) = refs[3:10], refs[10:13]
    out_ref, fig_ref, mg_ref, left, right, stat, slope, vec = refs[-8:]
    inl_ref, act_ref = right.at[:, :FF], right.at[:, FF : 2 * FF]
    step = pl.program_id(0)
    rows = x_ref.shape[1]

    @pl.when(step == 0)
    def _():
        stat[...] = jnp.zeros_like(stat)
        for i, ref in enumerate(vectors[:-1]):
            vec[2 + i : 3 + i, :] = as_row(ref)
        inner_row = as_row(vectors[-1])
        for i in range(FF // D):
            vec[8 + i : 9 + i, :] = inner_row[:, i * D : (i + 1) * D]

    x = x_ref[0]
    mixed = mix_ref[0]
    left[2 * D : 3 * D, :] = mixed.T
    left[3 * D :, :] = x.T
    first_normed, first_inverse = norm_stats(nn(mixed, w_output[...]) + vec[2:3, :] + x.astype(F32))
    first_norm = first_normed * vec[3:4, :] + vec[4:5, :]
    first_low = first_norm.astype(BF)
    left[:D, :] = first_low.T
    outer = []
    for g in range(GROUPS):
        for c in range(2):
            k = g * 2 + c
            inner = nn(first_low[:, g * ALL : (g + 1) * ALL], w_inner[g, :, c * D : (c + 1) * D])
            for r in range(0, rows, 16):
                act, slo = gelu_pair(inner[r : r + 16] + vec[8 + k : 9 + k, :])
                act_ref[r : r + 16, k * D : (k + 1) * D] = act.astype(BF)
                slope[r : r + 16, k * D : (k + 1) * D] = slo
        outer.append(nn(act_ref[:, g * 2 * D : (g + 1) * 2 * D], w_outer[g]))
    second_normed, second_inverse = norm_stats(
        jnp.concatenate(outer, axis=1) + vec[5:6, :] + first_norm
    )
    gain_second = vec[6:7, :]
    out_ref[0] = (second_normed * gain_second + vec[7:8, :]).astype(BF)
    seed = cot_ref[0].astype(F32)
    if masked:
        token = step * rows + lax.broadcasted_iota(jnp.int32, (rows, 1), 0)
        seed = jnp.where(token < live_ref[0, 0] * slot_rows, seed, 0.0)
    stat[0:8, :] += fold8(seed * second_normed)
    stat[8:16, :] += fold8(seed)
    second_grad = norm_back(seed, second_normed, second_inverse, gain_second)
    outer_low = second_grad.astype(BF)
    left[D : 2 * D, :] = outer_low.T
    stat[32:40, :] += fold8(outer_low.astype(F32))
    first_grad = []
    for g in range(GROUPS):
        for c in range(2):
            k = g * 2 + c
            back = nt(outer_low[:, g * ALL : (g + 1) * ALL], w_outer[g, c * D : (c + 1) * D, :])
            inl_ref[:, k * D : (k + 1) * D] = (back * slope[:, k * D : (k + 1) * D]).astype(BF)
        first_grad.append(nt(inl_ref[:, g * 2 * D : (g + 1) * 2 * D], w_inner[g]))
    first_grad = second_grad + jnp.concatenate(first_grad, axis=1)
    stat[16:24, :] += fold8(first_grad * first_normed)
    stat[24:32, :] += fold8(first_grad)
    first_in_grad = norm_back(first_grad, first_normed, first_inverse, vec[3:4, :])
    fig_ref[0] = first_in_grad
    attended_low = first_in_grad.astype(BF)
    right[:, 2 * FF :] = attended_low
    mg_ref[0] = nt(attended_low, w_output[...]).astype(BF)


def ffn_call(live, slot_rows, mixed, x, cotan, consts, joint, tokens):
    count, rows = x.shape[0], x.shape[1]
    total = count * rows
    masked = live is not None
    first = 0 if masked else (tokens - total) // rows
    n_in = (4 if masked else 3) + len(consts)
    out_shapes = [
        ((count, rows, D), BF, per_row(rows, D)),
        ((count, rows, D), F32, per_row(rows, D)),
        ((count, rows, D), BF, per_row(rows, D)),
        ((4 * D, tokens), BF, pl.BlockSpec((4 * D, rows), lambda i: (0, first + i))),
        ((tokens, 2 * FF + D), BF, pl.BlockSpec((rows, 2 * FF + D), lambda i: (first + i, 0))),
        ((40, D), F32, pl.BlockSpec((40, D), lambda i: (0, 0))),
    ]
    head = [live] if masked else []
    head_specs = [pl.BlockSpec(memory_space=pltpu.SMEM)] if masked else []
    return pl.pallas_call(
        functools.partial(ffn_body, slot_rows if masked else 0),
        grid=(count,),
        in_specs=head_specs
        + [per_row(rows, D)] * 3
        + [fixed(c) for c in consts]
        + [pl.BlockSpec(memory_space=pl.ANY)] * len(joint),
        out_specs=[s for _, _, s in out_shapes],
        out_shape=[jax.ShapeDtypeStruct(s, t) for s, t, _ in out_shapes],
        scratch_shapes=[pltpu.VMEM((rows, FF), F32), pltpu.VMEM((16, D), F32)],
        input_output_aliases={n_in: 3, n_in + 1: 4} if masked else {},
        compiler_params=params(),
        cost_estimate=pl.CostEstimate(
            flops=total * 12_000_000, bytes_accessed=30_000_000, transcendentals=total * FF
        ),
        name="ffn_short" if masked else "ffn_long",
    )(*head, mixed, x, cotan, *consts, *joint)


def post_body(n_x, *refs):
    is_long = n_x > 1
    x_refs = refs[:n_x]
    refs = refs[n_x:]
    (mg_ref, fig_ref, q_ref, k_ref, v_ref, p_ref, kc_ref, ker_ref, dl_ref, up_ref) = refs[:10]
    (depth_kernel, w_point, w_span, spread, perm) = refs[10:15]
    refs = refs[15:]
    if not is_long:
        (w_project, w_unfold), refs = refs[:2], refs[4:]
    (left, right, dkg), refs = refs[:3], refs[3:]
    if is_long:
        own_out, *far_outs = refs[:n_x]
        qt_out, ug_out, tg_out = refs[n_x : n_x + 3]
        xp, dgp, prp, dq_scr = refs[n_x + 3 :]
    else:
        tg_out, ru_out, dgp, prp, dq_scr = refs
    step = pl.program_id(0)
    batch, rows = x_refs[0].shape[:2]
    total_rows = batch * rows
    keys = k_ref.shape[1]
    ext = 8 if is_long else 0
    flat = lambda ref: ref[...].reshape(total_rows, ref.shape[-1])

    @pl.when(step == 0)
    def _():
        dkg[...] = jnp.zeros_like(dkg)
        dgp[...] = jnp.zeros_like(dgp)
        prp[...] = jnp.zeros_like(prp)

    if is_long:
        lower, upper = row_sides()
        fill_ends(xp, x_refs, (lower, upper))

    q = flat(q_ref)
    qf = q.astype(F32)
    scaled = q * jnp.asarray(HEAD ** (-0.5), BF)
    low_half = lax.broadcasted_iota(jnp.int32, (1, 128), 1) < HEAD
    for p in range(PAIRS):
        cols = slice(p * 128, (p + 1) * 128)
        for r in range(batch):
            here = slice(r * rows, (r + 1) * rows)
            grad = mg_ref[r, :, cols]
            weight_grad = nt(head_stack(v_ref[r, :, cols], low_half), grad)
            low = []
            for half in range(2):
                part = slice(half * keys, (half + 1) * keys)
                probs = p_ref[r, p, part, :].astype(F32)
                inner = jnp.sum(probs * weight_grad[part], axis=0, keepdims=True)
                low.append((probs * (weight_grad[part] - inner)).astype(BF))
            score_low = jnp.concatenate(low, axis=0)
            value_grad = nn(p_ref[r, p], grad)
            value_grad = jnp.where(low_half, value_grad[:keys], value_grad[keys:])
            key_grad = nn(score_low, scaled[here, cols])
            key_grad = jnp.where(low_half, key_grad[:keys], key_grad[keys:])
            query_grad = tn(head_stack(k_ref[r, :, cols], low_half), score_low) * HEAD ** (-0.5)
            dq_scr[here, cols] = query_grad.T
            v_cols = slice(ALL + p * 128, ALL + (p + 1) * 128)
            if is_long:
                own_out[r, :, cols] = key_grad[:rows]
                own_out[r, :, v_cols] = value_grad[:rows]
                for i in range(1, n_x):
                    block = slice(i * rows, (i + 1) * rows)
                    far_outs[i - 1][r, :rows, cols] = key_grad[block].astype(BF)
                    far_outs[i - 1][r, :rows, v_cols] = value_grad[block].astype(BF)
            else:
                ru_out[here, 2 * ALL + p * 128 : 2 * ALL + (p + 1) * 128] = key_grad.astype(BF)
                ru_out[here, 3 * ALL + p * 128 : 3 * ALL + (p + 1) * 128] = value_grad.astype(BF)

    kernel = flat(ker_ref)
    parts = two_parts(kernel)
    kernel_grad = jnp.zeros((total_rows, 128), F32)
    span_rows = rows + 2 * ext
    for p in range(PAIRS):
        cols = slice(p * 128, (p + 1) * 128)
        table = slice(p * KERNEL * 128, (p + 1) * KERNEL * 128)
        wide = nn(parts, spread[:, table])
        all_products = []
        for r in range(batch):
            here = slice(r * rows, (r + 1) * rows)
            grad = mg_ref[r, :, ALL + p * 128 : ALL + (p + 1) * 128].astype(F32)
            products = []
            for j in range(KERNEL):
                products.append((grad * up_ref[r, p, 4 + j : 4 + j + rows, :]).astype(BF))
                prp[r, j, 16 : 16 + rows, :] = wide[here, j * 128 : (j + 1) * 128] * grad
            all_products.append(jnp.concatenate(products, axis=1))
            first = 20 - ext
            total = prp[r, 0, first : first + span_rows, :]
            for j in range(1, KERNEL):
                total += prp[r, j, first - j : first - j + span_rows, :]
            if is_long:
                ug_out[r, :, cols] = total[ext : ext + rows]
                far_outs[0][r, rows + 8 : rows + 16, cols] = (total[:ext] * lower).astype(BF)
                far_outs[-1][r, rows + 8 : rows + 16, cols] = (total[ext + rows :] * upper).astype(BF)
            else:
                ru_out[here, cols] = total.astype(BF)
        kernel_grad += nt(jnp.concatenate(all_products, axis=0), spread[:128, table])
    if is_long:
        zero = jnp.zeros((batch, 8, ALL), BF)
        far_outs[0][:, rows + 8 : rows + 16, ALL:] = zero
        far_outs[-1][:, rows + 8 : rows + 16, ALL:] = zero

    logit_low = (kernel * (kernel_grad - window_sum(kernel * kernel_grad))).astype(BF)
    left[D:, :] = nt(perm[...], logit_low).astype(BF)
    span_grad = nn(logit_low, tn(perm[:TAPS, :], w_span[...]).astype(BF))
    key_conv = flat(kc_ref)
    right[:, ALL:] = (key_conv * qf).astype(BF)
    left[:D, :] = flat(dl_ref).T
    point_low = (span_grad * qf).astype(BF)
    right[:, :ALL] = point_low
    query_total = (dq_scr[...] + span_grad * key_conv).astype(BF)
    depth_grad = nt(point_low, w_point[...])
    for r in range(batch):
        for c in range(D // 128):
            dgp[r, c, 16 : 16 + rows, :] = depth_grad[
                r * rows : (r + 1) * rows, c * 128 : (c + 1) * 128
            ]

    if not is_long:
        ru_out[:, ALL : 2 * ALL] = query_total
        base = nt(ru_out[:, :ALL], w_unfold[...]) + nt(ru_out[:, ALL:], w_project[...])
    else:
        qt_out[...] = query_total.reshape(batch, rows, ALL)
    for c in range(D // 128):
        cols = slice(c * 128, (c + 1) * 128)
        for r in range(batch):
            x_part = xp[r, c] if is_long else x_refs[0][r, :, cols].astype(F32)
            first = 20 - ext
            total = None
            for j in range(KERNEL):
                moved = dgp[r, c, first - j : first - j + span_rows, :]
                term = depth_kernel[j : j + 1, cols].astype(F32) * moved
                total = term if total is None else total + term
                dkg[j * 8 : (j + 1) * 8, cols] += fold8(moved * x_part)
            if is_long:
                tg_out[r, :, cols] = total[ext : ext + rows] + fig_ref[r, :, cols]
                far_outs[0][r, rows : rows + 8, cols] = (total[:ext] * lower).astype(BF)
                far_outs[-1][r, rows : rows + 8, cols] = (total[ext + rows :] * upper).astype(BF)
            else:
                tg_out[r, :, cols] = total + fig_ref[r, :, cols] + base[r * rows : (r + 1) * rows, cols]


def post_call(xs, mg, fig, kept, consts, joint, tokens, batch):
    count, rows = xs[0].shape[0], xs[0].shape[1]
    keys = rows * len(xs)
    total = count * rows
    is_long = len(xs) > 1
    wide = batch * rows
    first = (tokens - total) // wide if is_long else 0
    row_args = [mg, fig, *kept]
    outs = [
        ((D + 128, tokens), BF, pl.BlockSpec((D + 128, wide), lambda i: (0, first + i))),
        ((tokens, 2 * ALL), BF, pl.BlockSpec((wide, 2 * ALL), lambda i: (first + i, 0))),
        ((KERNEL * 8, D), F32, pl.BlockSpec((KERNEL * 8, D), lambda i: (0, 0))),
    ]
    row_out = lambda r, c, t: ((count, r, c), t, per_row(r, c, batch=batch))
    scratch = []
    if is_long:
        outs.append(row_out(rows, D, F32))
        for i in range(1, len(xs)):
            outs.append(row_out(rows + 16 if i in (1, len(xs) - 1) else rows, D, BF))
        outs += [row_out(rows, ALL, BF), row_out(rows, ALL, F32), row_out(rows, D, F32)]
        scratch.append(pltpu.VMEM((batch, D // 128, rows + 16, 128), F32))
    else:
        outs += [
            row_out(rows, D, F32),
            ((tokens, 4 * ALL), BF, pl.BlockSpec((wide, 4 * ALL), lambda i: (first + i, 0))),
        ]
    scratch += [
        pltpu.VMEM((batch, D // 128, rows + 32, 128), F32),
        pltpu.VMEM((batch, KERNEL, rows + 32, 128), F32),
        pltpu.VMEM((wide, ALL), F32),
    ]
    inputs = [*xs, *row_args, *consts]
    return pl.pallas_call(
        functools.partial(post_body, len(xs)),
        grid=(count // batch,),
        in_specs=[per_row(rows, D, batch=batch)] * len(xs)
        + [per_row(*a.shape[1:], batch=batch) for a in row_args]
        + [fixed(c) for c in consts]
        + [pl.BlockSpec(memory_space=pl.ANY)] * len(joint),
        out_specs=[s for _, _, s in outs],
        out_shape=[jax.ShapeDtypeStruct(s, t) for s, t, _ in outs],
        scratch_shapes=scratch,
        input_output_aliases={len(inputs) + i: i for i in range(len(joint))},
        compiler_params=params(),
        cost_estimate=pl.CostEstimate(
            flops=total * 10_000_000, bytes_accessed=30_000_000, transcendentals=0
        ),
        name="post_long" if is_long else "post_short",
    )(*inputs, *joint)


def end_body(n_x, *refs):
    own, *rest = refs[:n_x]
    qt, ug, tg, w_project, w_unfold, _, out_ref, ru_out = refs[n_x:]
    rows = own.shape[1]
    both = own[0]
    for far in rest:
        both = both + far[0, :rows, :].astype(F32)
    from_next, from_prev = rest[0], rest[-1]
    unfold = ug[0]
    after = from_next[0, rows:, :].astype(F32)
    before = from_prev[0, rows:, :].astype(F32)
    middle = unfold[8 : rows - 8]
    ru_out[:, :ALL] = jnp.concatenate(
        [unfold[:8] + before[8:, :ALL], middle, unfold[rows - 8 :] + after[8:, :ALL]], axis=0
    ).astype(BF)
    ru_out[:, ALL : 2 * ALL] = qt[0]
    ru_out[:, 2 * ALL :] = both.astype(BF)
    total = nt(ru_out[:, :ALL], w_unfold[...]) + nt(ru_out[:, ALL:], w_project[...]) + tg[0]
    out_ref[0] = total
    out_ref[0, :8, :] = total[:8] + before[:8]
    out_ref[0, rows - 8 :, :] = total[rows - 8 :] + after[:8]


def end_call(own, far, qt, ug, tg, w_project, w_unfold, joint):
    count, rows = own.shape[0], own.shape[1]
    first = (joint.shape[0] - count * rows) // rows
    row_args = [own, *far, qt, ug, tg]
    return pl.pallas_call(
        functools.partial(end_body, 1 + len(far)),
        grid=(count,),
        in_specs=[per_row(*a.shape[1:]) for a in row_args]
        + [fixed(w_project), fixed(w_unfold), pl.BlockSpec(memory_space=pl.ANY)],
        out_specs=[per_row(rows, D), pl.BlockSpec((rows, 4 * ALL), lambda i: (first + i, 0))],
        out_shape=[
            jax.ShapeDtypeStruct((count, rows, D), F32),
            jax.ShapeDtypeStruct(joint.shape, BF),
        ],
        input_output_aliases={len(row_args) + 2: 1},
        compiler_params=params(),
        cost_estimate=pl.CostEstimate(
            flops=count * rows * 2_400_000, bytes_accessed=10_000_000, transcendentals=0
        ),
        name="end_long",
    )(*row_args, w_project, w_unfold, joint)


UNIT = 3 * ALL
CHUNK = 4 * UNIT
CHUNKS = 8
LAST = 6 * 512
PACKED = (CHUNKS - 1) * CHUNK + LAST
SPAN_ROW = (CHUNKS - 1) * CHUNK + 2 * UNIT
SMALL_ROW = SPAN_ROW + ALL
SMALL = 48
MESH = pl.DeviceIdType.MESH


def chunk_parts(k):
    blocks = CHUNK // 512 if k < CHUNKS - 1 else LAST // 512
    first = (blocks + 1) // 2 if k % 2 == 0 else blocks // 2
    start = k * CHUNK
    middle = start + first * 512
    return [(start, first * 512, "cxy"), (middle, (blocks - first) * 512, "cyx")]


def rows_of(ref, start, count):
    return ref.at[pl.ds(pl.multiple_of(start, 16), count), :]


def add_rows(out, start, sources, count):
    step = next(s for s in (160, 128, 96, 80, 64, 48, 32, 16) if count % s == 0)

    def body(i, carry):
        total = None
        for ref, first in sources:
            value = rows_of(ref, first + i * step, step)[...].astype(F32)
            total = value if total is None else total + value
        rows_of(out, start + i * step, step)[...] = total.astype(BF)
        return carry

    lax.fori_loop(0, count // step, body, 0)


class Exchange:
    def __init__(self, part, res, out, scratch):
        self.part, self.res, self.out = part, res, out
        self.got = scratch[0:3]
        self.got_z = scratch[3]
        self.acc = scratch[4:7]
        self.send_sem, self.recv_sem, self.out_sem = scratch[7:10]
        dp, blk = lax.axis_index("dp"), lax.axis_index("blk")
        core, x, y, z = lax.rem(blk, 2), blk // 2, lax.rem(dp, 2), dp // 2
        self.z = z
        self.bit = {"c": core, "x": x, "y": y}
        self.peer = {
            "c": (dp, blk + 1 - 2 * core),
            "x": (dp, blk + 2 - 4 * x),
            "y": (dp + 1 - 2 * y, blk),
        }
        self.z_peer = [(lax.rem(z + i, 4) * 2 + y, blk) for i in (1, 2, 3)]
        self.open = {}
        self.sends = []
        self.place = {}

    def greet(self):
        barrier = pltpu.get_barrier_semaphore()
        for device in [*self.peer.values(), *self.z_peer]:
            pl.semaphore_signal(barrier, inc=1, device_id=device, device_id_type=MESH)

    def await_greetings(self):
        pl.semaphore_wait(pltpu.get_barrier_semaphore(), 6)

    def start(self, n, slot, source, target, device):
        copy = pltpu.make_async_remote_copy(
            src_ref=source,
            dst_ref=target,
            send_sem=self.send_sem.at[n, slot],
            recv_sem=self.recv_sem.at[n, slot],
            device_id=device,
            device_id_type=MESH,
        )
        copy.start()
        self.open[n, slot] = copy
        self.sends.append(copy)

    def stage(self, n, part, s):
        row, count, order = part
        bit, peer, acc, got, res = self.bit, self.peer, self.acc, self.got, self.res
        if 1 <= s <= 3:
            size = count >> s
            self.open[n, s - 1].wait_recv()
            before, first = (self.part, row) if s == 1 else (acc[s - 2], row >> (s - 1))
            mine = first + bit[order[s - 1]] * size
            add_rows(acc[s - 1], row >> s, [(before, mine), (got[s - 1], row >> s)], size)
        if s <= 2:
            size = count >> (s + 1)
            source, first = (self.part, row) if s == 0 else (acc[s - 1], row >> s)
            axis = order[s]
            other = first + (1 - bit[axis]) * size
            self.start(n, s, rows_of(source, other, size), rows_of(got[s], row >> (s + 1), size), peer[axis])
        elif s == 3:
            size = count >> 5
            for i in range(3):
                theirs = (row >> 3) + lax.rem(self.z + i + 1, 4) * size
                target = rows_of(self.got_z.at[i], row >> 5, size)
                self.start(n, 3 + i, rows_of(acc[2], theirs, size), target, self.z_peer[i])
        elif s == 4:
            size = count >> 5
            for i in range(3):
                self.open[n, 3 + i].wait_recv()
            place = row
            for level in range(3):
                place = place + bit[order[level]] * (count >> (level + 1))
            self.place[n] = place
            mine = place + self.z * size
            others = [(self.got_z.at[i], row >> 5) for i in range(3)]
            add_rows(res, mine, [(acc[2], (row >> 3) + self.z * size), *others], size)
            for i in range(3):
                block = rows_of(res, mine, size)
                self.start(n, 6 + i, block, block, self.z_peer[i])
        elif s <= 7:
            for slot in (6, 7, 8) if s == 5 else (s + 3,):
                self.open[n, slot].wait_recv()
            level = 7 - s
            size = count >> (level + 1)
            block = rows_of(res, self.place[n], size)
            self.start(n, s + 4, block, block, peer[order[level]])
            self.place[n] = self.place[n] - bit[order[level]] * size
        else:
            self.open[n, 11].wait_recv()
            pltpu.make_async_copy(
                rows_of(res, row, count), rows_of(self.out, row, count), self.out_sem.at[n]
            ).start()

    def finish(self, parts):
        for copy in self.sends:
            copy.wait_send()
        for n, (row, count, _) in enumerate(parts):
            pltpu.make_async_copy(
                rows_of(self.res, row, count), rows_of(self.out, row, count), self.out_sem.at[n]
            ).wait()


def weights_body(remote, ranges, *refs):
    left, right, left_post, right_post, rows_grad, stat_a, stat_b, depth_a, depth_b, out = refs[:10]
    held_left, held_right, sums, part, load_sem = refs[10:15]
    scratch = refs[15:]
    tokens = held_left.shape[2]

    def loads(k):
        slot = k % 2
        if k < 4:
            a, a_rows, b, b_cols = left, (k * ALL, ALL), right, (k * 4 * ALL, 4 * ALL)
        elif k == 4:
            a, a_rows, b, b_cols = left, (2 * D, D), right, (2 * FF, D)
        elif k < 7:
            a, a_rows, b, b_cols = left, (3 * D + (k - 5) * ALL, ALL), rows_grad, (0, 4 * ALL)
        else:
            a, a_rows, b, b_cols = left_post, (0, D + 128), right_post, (0, D)
        copies = []
        for i, (to, start, size) in enumerate(ranges):
            here, there = pl.ds(to, size), pl.ds(start, size)
            copies.append(
                pltpu.make_async_copy(
                    a.at[pl.ds(*a_rows), there],
                    held_left.at[slot, : a_rows[1], here],
                    load_sem.at[slot, 2 * i],
                )
            )
            copies.append(
                pltpu.make_async_copy(
                    b.at[there, pl.ds(*b_cols)],
                    held_right.at[slot, here, : b_cols[1]],
                    load_sem.at[slot, 2 * i + 1],
                )
            )
        return copies

    def compute(k):
        for copy in loads(k):
            copy.wait()
        if k + 1 < CHUNKS:
            for copy in loads(k + 1):
                copy.start()
        slot = k % 2
        by_left = {4: 2, 7: 1}.get(k, 4)

        def unit(j, carry):
            if by_left == 4:
                a, b = 0, j
            elif by_left == 2:
                a, b = j // 2, lax.rem(j, 2)
            else:
                a, b = j, 0
            lhs = held_left[slot, pl.ds(pl.multiple_of(a * ALL, ALL), ALL), :]
            rhs = held_right[slot, :, pl.ds(pl.multiple_of(b * ALL, ALL), ALL)]
            value = nn(lhs, rhs)
            for c in range(3):
                rows_of(part, k * CHUNK + j * UNIT + c * ALL, ALL)[...] = value[
                    :, c * 128 : (c + 1) * 128
                ].astype(BF)
            return carry

        lax.fori_loop(0, 2 if k == 7 else 4, unit, 0)
        ones = jnp.ones((16, tokens), BF)
        if k in (0, 1, 4, 5):
            wide = 2 if k == 4 else 4
            first = {0: 28, 1: 32, 4: 36, 5: 38}[k]
            total = nn(ones, held_right[slot, :, : wide * ALL])
            for j in range(wide):
                sums[first + j : first + j + 1, :] = total[0:1, j * ALL : (j + 1) * ALL]
        if k == 7:
            span = nn(held_left[slot, D:, :], held_right[slot, :, ALL:D])
            for c in range(3):
                part[SPAN_ROW + c * 128 : SPAN_ROW + (c + 1) * 128, :] = span[
                    :, c * 128 : (c + 1) * 128
                ].astype(BF)
            sums[42:43, :] = nn(ones, held_right[slot, :, :ALL])[0:1]
            sums[43:44, :128] = nt(ones, held_left[slot, D:, :])[0:1]
            for first, a, b in ((0, stat_a, stat_b), (10, depth_a, depth_b)):
                for i in range(a.shape[0] // 8):
                    both = jnp.sum(a[i * 8 : i * 8 + 8] + b[i * 8 : i * 8 + 8], axis=0, keepdims=True)
                    sums[first + 2 * i : first + 2 * i + 1, :] = both[:, :ALL]
                    sums[first + 2 * i + 1 : first + 2 * i + 2, :] = both[:, ALL:]
            small = sums[...].astype(BF)
            for c in range(3):
                part[SMALL_ROW + c * SMALL : SMALL_ROW + (c + 1) * SMALL, :] = small[
                    :, c * 128 : (c + 1) * 128
                ]
            part[SMALL_ROW + 3 * SMALL :, :] = jnp.zeros((PACKED - SMALL_ROW - 3 * SMALL, 128), BF)

    for copy in loads(0):
        copy.start()
    sums[...] = jnp.zeros_like(sums)
    if not remote:
        for k in range(CHUNKS):
            compute(k)
        pltpu.sync_copy(part, out)
        return
    res, *scratch = scratch
    exchange = Exchange(part, res, out, scratch)
    exchange.greet()
    parts = [p for k in range(CHUNKS) for p in chunk_parts(k)]
    for t in range(CHUNKS + 8):
        if t < CHUNKS:
            compute(t)
        if t == 0:
            exchange.await_greetings()
        for k in reversed(range(CHUNKS)):
            if 0 <= t - k <= 8:
                for n in (2 * k, 2 * k + 1):
                    exchange.stage(n, parts[n], t - k)
    exchange.finish(parts)


def weights_call(remote, n_short, n_long, big, small):
    tokens = n_short + n_long
    padded = big[1].shape[0]
    n_parts = 2 * CHUNKS
    scratch = [
        pltpu.VMEM((2, D + 128, tokens), BF),
        pltpu.VMEM((2, tokens, 4 * ALL), BF),
        pltpu.VMEM((SMALL, ALL), F32),
        pltpu.VMEM((PACKED, 128), BF),
        pltpu.SemaphoreType.DMA((2, 4)),
    ]
    if remote:
        scratch += [
            pltpu.VMEM((PACKED, 128), BF),
            pltpu.VMEM((PACKED >> 1, 128), BF),
            pltpu.VMEM((PACKED >> 2, 128), BF),
            pltpu.VMEM((PACKED >> 3, 128), BF),
            pltpu.VMEM((3, PACKED >> 5, 128), BF),
            pltpu.VMEM((PACKED >> 1, 128), BF),
            pltpu.VMEM((PACKED >> 2, 128), BF),
            pltpu.VMEM((PACKED >> 3, 128), BF),
            pltpu.SemaphoreType.DMA((n_parts, 12)),
            pltpu.SemaphoreType.DMA((n_parts, 12)),
            pltpu.SemaphoreType.DMA((n_parts,)),
        ]
    more = dict(collective_id=0, has_side_effects=True) if remote else {}
    return pl.pallas_call(
        functools.partial(weights_body, remote, ((0, 0, n_short), (n_short, padded - n_long, n_long))),
        in_specs=[pl.BlockSpec(memory_space=pl.ANY)] * len(big)
        + [pl.BlockSpec(memory_space=pltpu.VMEM)] * len(small),
        out_specs=pl.BlockSpec(memory_space=pl.ANY),
        out_shape=jax.ShapeDtypeStruct((PACKED, 128), BF),
        scratch_shapes=scratch,
        compiler_params=params(**more),
        cost_estimate=pl.CostEstimate(
            flops=2 * 31 * ALL * ALL * tokens, bytes_accessed=50_000_000, transcendentals=0
        ),
        name="weights",
    )(*big, *small)


SMALL_OUTS = [
    ("gain_second", 0, D),
    ("shift_second", 2, D),
    ("gain_first", 4, D),
    ("shift_first", 6, D),
    ("bias_outer", 8, D),
    ("bias_inner", 28, FF),
    ("bias_output", 36, D),
    ("bias_unfold", 38, ALL),
    ("bias_query", 39, ALL),
    ("bias_value", 41, ALL),
    ("bias_point", 42, ALL),
    ("bias_span", 43, TAPS),
]


def unpack_body(block, inner, outer, output, unfold, project, point, span, depth, *small):
    step = pl.program_id(0)

    def tile(unit):
        start = unit * UNIT
        return jnp.concatenate(
            [block[start + c * ALL : start + (c + 1) * ALL, :] for c in range(3)], axis=1
        )

    @pl.when(step < 2)
    def _():
        for i in range(4):
            inner[0, :, i * ALL : (i + 1) * ALL] = tile(i).astype(F32)

    @pl.when((step >= 2) & (step < 4))
    def _():
        for i in range(4):
            outer[0, i * ALL : (i + 1) * ALL, :] = tile(i).T.astype(F32)

    @pl.when(step == 4)
    def _():
        for i in range(4):
            a, b = divmod(i, 2)
            output[a * ALL : (a + 1) * ALL, b * ALL : (b + 1) * ALL] = tile(i).astype(F32)

    @pl.when((step == 5) | (step == 6))
    def _():
        unfold[...] = tile(0).astype(F32)
        for i in range(3):
            project[:, i * ALL : (i + 1) * ALL] = tile(i + 1).astype(F32)

    @pl.when(step == 7)
    def _():
        for i in range(2):
            point[i * ALL : (i + 1) * ALL, :] = tile(i).astype(F32)
        tail = 2 * UNIT
        wide = jnp.concatenate(
            [block[tail + c * 128 : tail + (c + 1) * 128, :] for c in range(3)], axis=1
        )
        span[...] = wide[:TAPS].astype(F32)
        tail += ALL
        rows = jnp.concatenate(
            [block[tail + c * SMALL : tail + (c + 1) * SMALL, :] for c in range(3)], axis=1
        ).astype(F32)
        for j in range(KERNEL):
            for half in range(2):
                place = 10 + 2 * j + half
                depth[j : j + 1, half * ALL : (half + 1) * ALL] = rows[place : place + 1]
        for ref, (_, first, size) in zip(small, SMALL_OUTS):
            for i in range(max(1, size // ALL)):
                wide = min(size, ALL)
                ref[i * ALL : i * ALL + wide] = rows[first + i, :wide]


def unpack_call(packed):
    def at(first, count):
        return lambda s: jnp.clip(s - first, 0, count - 1)

    inner_at, outer_at, rows_at = at(0, 2), at(2, 2), at(5, 2)
    whole = lambda *shape: (shape, pl.BlockSpec(shape, lambda s: (0,) * len(shape)))
    specs = [
        ((GROUPS, ALL, 4 * ALL), pl.BlockSpec((1, ALL, 4 * ALL), lambda s: (inner_at(s), 0, 0))),
        ((GROUPS, 4 * ALL, ALL), pl.BlockSpec((1, 4 * ALL, ALL), lambda s: (outer_at(s), 0, 0))),
        whole(D, D),
        ((D, ALL), pl.BlockSpec((ALL, ALL), lambda s: (rows_at(s), 0))),
        ((D, 3 * ALL), pl.BlockSpec((ALL, 3 * ALL), lambda s: (rows_at(s), 0))),
        whole(D, ALL),
        whole(TAPS, ALL),
        whole(KERNEL, D),
    ]
    specs += [whole(size) for _, _, size in SMALL_OUTS]
    return pl.pallas_call(
        unpack_body,
        grid=(CHUNKS,),
        in_specs=[pl.BlockSpec((CHUNK, 128), lambda s: (s, 0))],
        out_specs=[b for _, b in specs],
        out_shape=[jax.ShapeDtypeStruct(s, F32) for s, _ in specs],
        compiler_params=params(),
        cost_estimate=pl.CostEstimate(flops=0, bytes_accessed=27_000_000, transcendentals=0),
        name="unpack",
    )(packed)


def shards(
    long_input,
    short_input,
    long_cotan,
    short_cotan,
    live_slots,
    w_project,
    bias_query,
    bias_value,
    depth_kernel,
    w_point,
    bias_point,
    w_span,
    bias_span,
    w_unfold,
    bias_unfold,
    w_output,
    bias_output,
    gain_first,
    shift_first,
    w_inner,
    bias_inner,
    w_outer,
    bias_outer,
    gain_second,
    shift_second,
):
    n_blk = lax.axis_size("blk")
    short_x = short_input.reshape(short_input.shape[2:])
    short_cot = short_cotan.reshape(short_cotan.shape[2:])
    perm, spread = (jnp.asarray(t) for t in tap_tables())
    xs = [long_input] + [
        lax.ppermute(long_input, "blk", [(i, (i + k) % n_blk) for i in range(n_blk)])
        for k in range(1, n_blk)
    ]
    span_t = w_span.T
    pre_consts = (
        bias_query, bias_value, bias_point, bias_span, bias_unfold, depth_kernel,
        w_project, w_point, span_t, w_unfold, spread, perm,
    )
    ffn_consts = (
        bias_output, gain_first, shift_first, bias_outer, gain_second, shift_second, bias_inner,
        w_output, w_inner, w_outer,
    )
    *short_kept, short_mixed = pre_call([short_x], pre_consts, SHORT_BATCH)
    *long_kept, long_mixed = pre_call(xs, pre_consts, LONG_BATCH)

    n_long, n_short = (a.shape[0] * a.shape[1] for a in (long_input, short_x))
    tokens = (pl.cdiv(n_short, n_long) + 1) * n_long
    as_long = lambda a: a.reshape(-1, FFN_LONG, D)
    l_out, l_fig, l_mg, *joint, l_stat = ffn_call(
        None, 0, *map(as_long, (long_mixed, long_input, long_cotan)), ffn_consts, (), tokens
    )
    l_out, l_fig, l_mg = (a.reshape(long_input.shape) for a in (l_out, l_fig, l_mg))
    s_out, s_fig, s_mg, left, right, s_stat = ffn_call(
        live_slots,
        short_x.shape[1],
        *(a.reshape(-1, FFN_ROWS, D) for a in (short_mixed, short_x, short_cot)),
        ffn_consts,
        joint,
        tokens,
    )
    s_fig, s_mg = s_fig.reshape(short_x.shape), s_mg.reshape(short_x.shape)
    post_consts = (depth_kernel, w_point, span_t, spread, perm)
    l_post = post_call(xs, l_mg, l_fig, long_kept, post_consts, (), tokens, LONG_BATCH)
    (*joint, l_dkg, own), l_rest = l_post[:4], l_post[4:]
    far, (l_qt, l_ug, l_tg) = l_rest[: n_blk - 1], l_rest[n_blk - 1 :]
    far = [
        lax.ppermute(a, "blk", [(i, (i - k) % n_blk) for i in range(n_blk)])
        for k, a in enumerate(far, 1)
    ]
    left_post, right_post, s_dkg, short_grad, rows_grad = post_call(
        [short_x], s_mg, s_fig, short_kept, post_consts + (w_project, w_unfold), joint, tokens, SHORT_BATCH
    )
    long_grad, rows_grad = end_call(own, far, l_qt, l_ug, l_tg, w_project, w_unfold, rows_grad)

    remote = lax.axis_size("dp") == 8 and n_blk == 4
    packed = weights_call(
        remote, n_short, n_long, (left, right, left_post, right_post, rows_grad), (l_stat, s_stat, l_dkg, s_dkg)
    )
    if not remote:
        packed = lax.psum(packed, ("dp", "blk"))
    inner, outer, output, unfold, project, point, span, depth, *small = unpack_call(packed)
    named = {name: value for (name, _, _), value in zip(SMALL_OUTS, small)}
    return (
        l_out,
        s_out.reshape(short_input.shape),
        long_grad,
        short_grad.reshape(short_input.shape),
        project,
        named["bias_query"],
        named["bias_value"],
        depth,
        point,
        named["bias_point"],
        span.T,
        named["bias_span"],
        unfold,
        named["bias_unfold"],
        output,
        named["bias_output"],
        named["gain_first"],
        named["shift_first"],
        inner,
        named["bias_inner"],
        outer,
        named["bias_outer"],
        named["gain_second"],
        named["shift_second"],
    )


def solution(mesh):
    rows = P("dp", "blk", None)
    slots = P("dp", "blk", None, None, None)
    in_specs = (rows, slots, rows, slots, P("dp", "blk")) + (P(),) * 20
    out_specs = (rows, slots, rows, slots) + (P(),) * 20
    return jax.shard_map(shards, mesh=mesh, in_specs=in_specs, out_specs=out_specs, check_vma=False)
```

```python
import functools

import jax
import jax.numpy as jnp
import numpy as np
from jax import lax
from jax.experimental import pallas as pl
from jax.experimental.pallas import tpu as pltpu
from jax.sharding import PartitionSpec as P

D = 768
FF = 3072
HEADS = 6
HEAD = 64
KERNEL = 9
GROUPS = 2
ALL = 384
PAIRS = 3
TAPS = HEADS * KERNEL
HALF = KERNEL // 2

F32 = jnp.float32
BF = jnp.bfloat16
ROOT_HALF = 0.7071067811865476
DENSITY = 0.3989422804014327
FFN_ROWS = 256
FFN_LONG = 384
SHORT_BATCH = 2
LONG_BATCH = 1
VMEM_BYTES = 58 * 1024 * 1024


def nn(a, b):
    return lax.dot_general(a, b, (((1,), (0,)), ((), ())), preferred_element_type=F32)


def nt(a, b):
    return lax.dot_general(a, b, (((1,), (1,)), ((), ())), preferred_element_type=F32)


def tn(a, b):
    return lax.dot_general(a, b, (((0,), (0,)), ((), ())), preferred_element_type=F32)


def tap_tables():
    perm = np.zeros((128, 128), np.float32)
    spread = np.zeros((256, PAIRS * KERNEL * 128), np.float32)
    for h in range(HEADS):
        for j in range(KERNEL):
            lane = j * HEADS + h
            perm[h * KERNEL + j, lane] = 1
            perm[h * KERNEL + j, TAPS + lane] = 1
            start = ((h // 2) * KERNEL + j) * 128 + (h % 2) * HEAD
            spread[lane, start : start + HEAD] = 1
            spread[128 + lane, start : start + HEAD] = 1
    return perm.astype(jnp.bfloat16), spread.astype(jnp.bfloat16)


def window(values, op):
    left = lambda v, n: pltpu.roll(v, 128 - n, 1)
    one = op(values, left(values, 6))
    two = op(one, left(one, 12))
    four = op(two, left(two, 24))
    return op(four, left(values, 48))


def window_sum(values):
    return window(values + pltpu.roll(values, TAPS, 1), jnp.add)


def head_stack(rows, low_half):
    zero = jnp.zeros_like(rows)
    return jnp.concatenate(
        [jnp.where(low_half, rows, zero), jnp.where(low_half, zero, rows)], axis=0
    )


def two_parts(values):
    high = values.astype(BF)
    rest = (values - high.astype(F32)).astype(BF)
    return jnp.concatenate([high, rest], axis=1)


def row_sides():
    place = lax.axis_index("blk")
    count = lax.axis_size("blk")
    return (place > 0).astype(F32), (place < count - 1).astype(F32), lax.rem(place, 2) == 1


def pick(odd, first, second):
    return jnp.where(odd, first.astype(F32), second.astype(F32))


def row_ends(x_refs, r, sides):
    lower, upper, odd = sides
    rows = x_refs[0].shape[1]
    before = pick(odd, x_refs[1][r, rows - 16 :, :], x_refs[3][r, rows - 16 :, :])
    after = pick(odd, x_refs[3][r, :16, :], x_refs[1][r, :16, :])
    return before * lower, after * upper


def fill_ends(xp, x_refs, sides):
    batch, rows = x_refs[0].shape[:2]
    for r in range(batch):
        if sides is not None:
            before, after = row_ends(x_refs, r, sides)
        for c in range(D // 128):
            cols = slice(c * 128, (c + 1) * 128)
            zero = jnp.zeros((8, 128), F32)
            xp[r, c, 0:8, :] = zero if sides is None else before[8:, cols]
            xp[r, c, 8 + rows : 16 + rows, :] = zero if sides is None else after[:8, cols]
            xp[r, c, 8 : 8 + rows, :] = x_refs[0][r, :, cols].astype(F32)


def as_row(ref):
    return ref[...].astype(F32).reshape(1, ref.shape[0])


class Gather:
    def __init__(self, own, outs, send_sem, recv_sem):
        self.own, self.outs, self.send_sem, self.recv_sem = own, outs, send_sem, recv_sem
        dp, blk = lax.axis_index("dp"), lax.axis_index("blk")
        core, x = lax.rem(blk, 2), blk // 2
        self.core_peer = (dp, blk + 1 - 2 * core)
        self.x_peer = (dp, blk + 2 - 4 * x)

    def copy(self, i):
        source = self.outs[1] if i == 2 else self.own
        return pltpu.make_async_remote_copy(
            src_ref=source,
            dst_ref=self.outs[i],
            send_sem=self.send_sem.at[i],
            recv_sem=self.recv_sem.at[i],
            device_id=self.x_peer if i == 1 else self.core_peer,
            device_id_type=pl.DeviceIdType.MESH,
        )

    def begin(self):
        barrier = pltpu.get_barrier_semaphore()
        for device in (self.core_peer, self.x_peer):
            pl.semaphore_signal(
                barrier, inc=1, device_id=device, device_id_type=pl.DeviceIdType.MESH
            )
        pl.semaphore_wait(barrier, 2)
        self.copy(1).start()
        self.copy(0).start()

    def forward(self):
        self.copy(1).wait_recv()
        self.copy(2).start()

    def end(self):
        for i in (0, 2):
            self.copy(i).wait_recv()
        for i in range(3):
            self.copy(i).wait_send()


def pre_body(n_x, *refs):
    gather = None
    if n_x == 1:
        own, *refs = refs
        gather = Gather(own, refs[22:25], *refs[-2:])
        refs = refs[:22] + refs[25:-2]
    x_refs, refs = refs[:n_x], refs[n_x:]
    bias_query, bias_value, bias_point, bias_span, bias_unfold, depth_kernel = refs[:6]
    w_project, w_point, w_span, w_unfold, spread, perm = refs[6:12]
    q_out, k_out, v_out, p_out, kc_out, ker_out, dl_out, up_out, mix_out = refs[12:21]
    xp, vec = refs[21:]

    @pl.when(pl.program_id(0) == 0)
    def _():
        vec[16:24, :] = jnp.zeros((8, D), F32)
        vec[0:1, :ALL] = as_row(bias_query)
        vec[0:1, ALL:] = as_row(bias_value)
        vec[1:2, :ALL] = as_row(bias_point)
        vec[1:2, ALL:] = as_row(bias_unfold)
        vec[21:22, :TAPS] = as_row(bias_span)
        vec[8:17, :] = depth_kernel[...].astype(F32)
        if gather:
            gather.begin()

    batch, rows = x_refs[0].shape[:2]
    total_rows = batch * rows
    is_long = n_x > 1
    sides = row_sides() if is_long else None
    x = x_refs[0][...].reshape(total_rows, D)
    fill_ends(xp, x_refs, sides)
    bias_query = vec[0:1, :ALL]
    bias_value = vec[0:1, ALL:]
    by_row = lambda v: v.reshape(batch, rows, v.shape[-1])
    if is_long:
        q = (nn(x, w_project[:, :ALL]) + bias_query).astype(BF)
        for i in range(n_x):
            both = nn(x_refs[i][...].reshape(total_rows, D), w_project[:, ALL:])
            k_out[:, i * rows : (i + 1) * rows, :] = by_row(both[:, :ALL].astype(BF))
            v_out[:, i * rows : (i + 1) * rows, :] = by_row((both[:, ALL:] + bias_value).astype(BF))
    else:
        both = nn(x, w_project[...])
        q = (both[:, :ALL] + bias_query).astype(BF)
        k_out[...] = by_row(both[:, ALL : 2 * ALL].astype(BF))
        v_out[...] = by_row((both[:, 2 * ALL :] + bias_value).astype(BF))
    q_out[...] = by_row(q)

    for r in range(batch):
        for c in range(D // 128):
            cols = slice(c * 128, (c + 1) * 128)
            total = vec[8:9, cols] * xp[r, c, 4 : 4 + rows, :]
            for j in range(1, KERNEL):
                total += vec[8 + j : 9 + j, cols] * xp[r, c, 4 + j : 4 + j + rows, :]
            dl_out[r, :, cols] = total.astype(BF)
    key_conv = nn(dl_out[...].reshape(total_rows, D), w_point[...]) + vec[1:2, :ALL]
    kc_out[...] = by_row(key_conv)
    span = (key_conv * q.astype(F32)).astype(BF)
    span_weights = tn(w_span[...], perm[:TAPS, :]).astype(BF)
    span_bias = nn(vec[16:24, :128].astype(BF), perm[...])[5:6]
    logits = nn(span, span_weights) + span_bias
    lane = lax.broadcasted_iota(jnp.int32, (1, 128), 1)
    raised = jnp.where(lane < TAPS, jnp.exp(logits - window(logits, jnp.maximum)), 0.0)
    kernel = jnp.where(lane < TAPS, raised / window_sum(raised), 0.0)
    ker_out[...] = by_row(kernel)

    bias_unfold = vec[1:2, ALL:]
    unfold_rows = nn(x, w_unfold[...]) + bias_unfold
    for r in range(batch):
        if is_long:
            lower, upper, _ = sides
            ends = jnp.concatenate(row_ends(x_refs, r, sides), axis=0).astype(BF)
            unfold_ends = nn(ends, w_unfold[...]) + bias_unfold
        for c in range(PAIRS):
            cols = slice(c * 128, (c + 1) * 128)
            up_out[r, c, 8 : 8 + rows, :] = unfold_rows[r * rows : (r + 1) * rows, cols]
            if is_long:
                up_out[r, c, 0:8, :] = unfold_ends[8:16, cols] * lower
                up_out[r, c, 8 + rows : 16 + rows, :] = unfold_ends[16:24, cols] * upper
            else:
                zero = jnp.zeros((8, 128), F32)
                up_out[r, c, 0:8, :] = zero
                up_out[r, c, 8 + rows : 16 + rows, :] = zero

    if gather:

        @pl.when(pl.program_id(0) == pl.num_programs(0) - 1)
        def _():
            gather.forward()

    low_half = lane < HEAD
    parts = two_parts(kernel)
    scaled = q * jnp.asarray(HEAD ** (-0.5), BF)
    keys = k_out.shape[1]
    for p in range(PAIRS):
        cols = slice(p * 128, (p + 1) * 128)
        wide = nn(parts, spread[:, p * KERNEL * 128 : (p + 1) * KERNEL * 128])
        for r in range(batch):
            here = slice(r * rows, (r + 1) * rows)
            total = wide[here, :128] * up_out[r, p, 4 : 4 + rows, :]
            for j in range(1, KERNEL):
                total += wide[here, j * 128 : (j + 1) * 128] * up_out[r, p, 4 + j : 4 + j + rows, :]
            mix_out[r, :, ALL + p * 128 : ALL + (p + 1) * 128] = total.astype(BF)

            scores = nt(head_stack(k_out[r, :, cols], low_half), scaled[here, cols])
            for half in range(2):
                part = scores[half * keys : (half + 1) * keys]
                top = jnp.max(part, axis=0, keepdims=True)
                grown = jnp.exp(part - top)
                share = 1.0 / jnp.sum(grown, axis=0, keepdims=True)
                p_out[r, p, half * keys : (half + 1) * keys, :] = (grown * share).astype(BF)
            context = tn(head_stack(v_out[r, :, cols], low_half), p_out[r, p])
            mix_out[r, :, cols] = context.astype(BF).T

    if gather:

        @pl.when(pl.program_id(0) == pl.num_programs(0) - 1)
        def _():
            gather.end()


def fixed(array):
    zeros = (0,) * array.ndim
    return pl.BlockSpec(array.shape, lambda *_: zeros, pipeline_mode=pl.Buffered(1))


def per_row(*shape, batch=1):
    zeros = (0,) * len(shape)
    return pl.BlockSpec((batch, *shape), lambda i: (i, *zeros))


def params(**more):
    return pltpu.CompilerParams(vmem_limit_bytes=VMEM_BYTES, **more)


def pre_call(xs, consts, batch, gathered=()):
    anywhere = pl.BlockSpec(memory_space=pl.ANY)
    count, rows = xs[0].shape[0], xs[0].shape[1]
    keys = rows * len(xs)
    shapes = [
        ((rows, ALL), BF),
        ((keys, ALL), BF),
        ((keys, ALL), BF),
        ((PAIRS, 2 * keys, rows), BF),
        ((rows, ALL), F32),
        ((rows, 128), F32),
        ((rows, D), BF),
        ((PAIRS, rows + 16, 128), F32),
        ((rows, D), BF),
    ]
    return pl.pallas_call(
        functools.partial(pre_body, len(xs)),
        grid=(count // batch,),
        in_specs=[anywhere] * len(gathered)
        + [per_row(rows, D, batch=batch)] * len(xs) + [fixed(c) for c in consts],
        out_specs=[per_row(*s, batch=batch) for s, _ in shapes] + [anywhere] * (3 * len(gathered)),
        out_shape=[jax.ShapeDtypeStruct((count, *s), t) for s, t in shapes]
        + [jax.ShapeDtypeStruct(g.shape, g.dtype) for g in gathered] * 3,
        scratch_shapes=[pltpu.VMEM((batch, D // 128, rows + 16, 128), F32), pltpu.VMEM((24, D), F32)]
        + [pltpu.SemaphoreType.DMA((3,))] * (2 * len(gathered)),
        compiler_params=params(collective_id=1, has_side_effects=True) if gathered else params(),
        cost_estimate=pl.CostEstimate(
            flops=count * rows * 6_000_000, bytes_accessed=20_000_000, transcendentals=1_000_000
        ),
        name="pre_long" if len(xs) > 1 else "pre_short",
    )(*gathered, *xs, *consts)


def norm_stats(z):
    centre = z - jnp.mean(z, axis=-1, keepdims=True)
    inverse = lax.rsqrt(jnp.mean(centre * centre, axis=-1, keepdims=True) + 1e-12)
    return centre * inverse, inverse


def norm_back(upstream, normed, inverse, gain):
    scaled = upstream * gain
    plain = jnp.mean(scaled, axis=-1, keepdims=True)
    cross = jnp.mean(scaled * normed, axis=-1, keepdims=True)
    return inverse * (scaled - plain - normed * cross)


def fold8(values):
    return jnp.sum(values.reshape(values.shape[0] // 8, 8, values.shape[1]), axis=0)


def gelu_pair(v):
    cdf = 0.5 * (1.0 + lax.erf(v * ROOT_HALF))
    return v * cdf, cdf + v * jnp.exp(-0.5 * (v * v)) * DENSITY


def ffn_body(slot_rows, *refs):
    masked = slot_rows > 0
    if masked:
        live_ref, *refs = refs
    mix_ref, x_ref, cot_ref = refs[:3]
    vectors, (w_output, w_inner, w_outer) = refs[3:10], refs[10:13]
    out_ref, fig_ref, mg_ref, left, right, stat, slope, vec = refs[-8:]
    inl_ref, act_ref = right.at[:, :FF], right.at[:, FF : 2 * FF]
    step = pl.program_id(0)
    rows = x_ref.shape[1]

    @pl.when(step == 0)
    def _():
        stat[...] = jnp.zeros_like(stat)
        for i, ref in enumerate(vectors[:-1]):
            vec[2 + i : 3 + i, :] = as_row(ref)
        inner_row = as_row(vectors[-1])
        for i in range(FF // D):
            vec[8 + i : 9 + i, :] = inner_row[:, i * D : (i + 1) * D]

    x = x_ref[0]
    mixed = mix_ref[0]
    left[2 * D : 3 * D, :] = mixed.T
    left[3 * D :, :] = x.T
    first_normed, first_inverse = norm_stats(nn(mixed, w_output[...]) + vec[2:3, :] + x.astype(F32))
    first_norm = first_normed * vec[3:4, :] + vec[4:5, :]
    first_low = first_norm.astype(BF)
    left[:D, :] = first_low.T
    outer = []
    for g in range(GROUPS):
        for c in range(2):
            k = g * 2 + c
            inner = nn(first_low[:, g * ALL : (g + 1) * ALL], w_inner[g, :, c * D : (c + 1) * D])
            for r in range(0, rows, 16):
                act, slo = gelu_pair(inner[r : r + 16] + vec[8 + k : 9 + k, :])
                act_ref[r : r + 16, k * D : (k + 1) * D] = act.astype(BF)
                slope[r : r + 16, k * D : (k + 1) * D] = slo
        outer.append(nn(act_ref[:, g * 2 * D : (g + 1) * 2 * D], w_outer[g]))
    second_normed, second_inverse = norm_stats(
        jnp.concatenate(outer, axis=1) + vec[5:6, :] + first_norm
    )
    gain_second = vec[6:7, :]
    out_ref[0] = (second_normed * gain_second + vec[7:8, :]).astype(BF)
    seed = cot_ref[0].astype(F32)
    if masked:
        token = step * rows + lax.broadcasted_iota(jnp.int32, (rows, 1), 0)
        seed = jnp.where(token < live_ref[0, 0] * slot_rows, seed, 0.0)
    stat[0:8, :] += fold8(seed * second_normed)
    stat[8:16, :] += fold8(seed)
    second_grad = norm_back(seed, second_normed, second_inverse, gain_second)
    outer_low = second_grad.astype(BF)
    left[D : 2 * D, :] = outer_low.T
    stat[32:40, :] += fold8(outer_low.astype(F32))
    first_grad = []
    for g in range(GROUPS):
        for c in range(2):
            k = g * 2 + c
            back = nt(outer_low[:, g * ALL : (g + 1) * ALL], w_outer[g, c * D : (c + 1) * D, :])
            inl_ref[:, k * D : (k + 1) * D] = (back * slope[:, k * D : (k + 1) * D]).astype(BF)
        first_grad.append(nt(inl_ref[:, g * 2 * D : (g + 1) * 2 * D], w_inner[g]))
    first_grad = second_grad + jnp.concatenate(first_grad, axis=1)
    stat[16:24, :] += fold8(first_grad * first_normed)
    stat[24:32, :] += fold8(first_grad)
    first_in_grad = norm_back(first_grad, first_normed, first_inverse, vec[3:4, :])
    fig_ref[0] = first_in_grad
    attended_low = first_in_grad.astype(BF)
    right[:, 2 * FF :] = attended_low
    mg_ref[0] = nt(attended_low, w_output[...]).astype(BF)


def ffn_call(live, slot_rows, mixed, x, cotan, consts, joint, tokens):
    count, rows = x.shape[0], x.shape[1]
    total = count * rows
    masked = live is not None
    first = 0 if masked else (tokens - total) // rows
    n_in = (4 if masked else 3) + len(consts)
    out_shapes = [
        ((count, rows, D), BF, per_row(rows, D)),
        ((count, rows, D), F32, per_row(rows, D)),
        ((count, rows, D), BF, per_row(rows, D)),
        ((4 * D, tokens), BF, pl.BlockSpec((4 * D, rows), lambda i: (0, first + i))),
        ((tokens, 2 * FF + D), BF, pl.BlockSpec((rows, 2 * FF + D), lambda i: (first + i, 0))),
        ((40, D), F32, pl.BlockSpec((40, D), lambda i: (0, 0))),
    ]
    head = [live] if masked else []
    head_specs = [pl.BlockSpec(memory_space=pltpu.SMEM)] if masked else []
    return pl.pallas_call(
        functools.partial(ffn_body, slot_rows if masked else 0),
        grid=(count,),
        in_specs=head_specs
        + [per_row(rows, D)] * 3
        + [fixed(c) for c in consts]
        + [pl.BlockSpec(memory_space=pl.ANY)] * len(joint),
        out_specs=[s for _, _, s in out_shapes],
        out_shape=[jax.ShapeDtypeStruct(s, t) for s, t, _ in out_shapes],
        scratch_shapes=[pltpu.VMEM((rows, FF), F32), pltpu.VMEM((16, D), F32)],
        input_output_aliases={n_in: 3, n_in + 1: 4} if masked else {},
        compiler_params=params(),
        cost_estimate=pl.CostEstimate(
            flops=total * 12_000_000, bytes_accessed=30_000_000, transcendentals=total * FF
        ),
        name="ffn_short" if masked else "ffn_long",
    )(*head, mixed, x, cotan, *consts, *joint)


def post_body(n_x, *refs):
    is_long = n_x > 1
    x_refs = refs[:n_x]
    refs = refs[n_x:]
    (mg_ref, fig_ref, q_ref, k_ref, v_ref, p_ref, kc_ref, ker_ref, dl_ref, up_ref) = refs[:10]
    (depth_kernel, w_point, w_span, spread, perm) = refs[10:15]
    refs = refs[15:]
    if not is_long:
        (w_project, w_unfold), refs = refs[:2], refs[4:]
    (left, right, dkg), refs = refs[:3], refs[3:]
    if is_long:
        own_out, *far_outs = refs[:n_x]
        qt_out, ug_out, tg_out = refs[n_x : n_x + 3]
        xp, dgp, prp, dq_scr = refs[n_x + 3 :]
    else:
        tg_out, ru_out, dgp, prp, dq_scr = refs
    step = pl.program_id(0)
    batch, rows = x_refs[0].shape[:2]
    total_rows = batch * rows
    keys = k_ref.shape[1]
    ext = 8 if is_long else 0
    flat = lambda ref: ref[...].reshape(total_rows, ref.shape[-1])

    @pl.when(step == 0)
    def _():
        dkg[...] = jnp.zeros_like(dkg)
        dgp[...] = jnp.zeros_like(dgp)
        prp[...] = jnp.zeros_like(prp)

    if is_long:
        sides = lower, upper, odd = row_sides()
        fill_ends(xp, x_refs, sides)

        def send_rims(r, place, cols, total):
            before, after = total[:ext] * lower, total[ext + rows :] * upper
            far_outs[0][r, place : place + 8, cols] = pick(odd, before, after).astype(BF)
            far_outs[2][r, place : place + 8, cols] = pick(odd, after, before).astype(BF)


    q = flat(q_ref)
    qf = q.astype(F32)
    scaled = q * jnp.asarray(HEAD ** (-0.5), BF)
    low_half = lax.broadcasted_iota(jnp.int32, (1, 128), 1) < HEAD
    for p in range(PAIRS):
        cols = slice(p * 128, (p + 1) * 128)
        for r in range(batch):
            here = slice(r * rows, (r + 1) * rows)
            grad = mg_ref[r, :, cols]
            weight_grad = nt(head_stack(v_ref[r, :, cols], low_half), grad)
            low = []
            for half in range(2):
                part = slice(half * keys, (half + 1) * keys)
                probs = p_ref[r, p, part, :].astype(F32)
                inner = jnp.sum(probs * weight_grad[part], axis=0, keepdims=True)
                low.append((probs * (weight_grad[part] - inner)).astype(BF))
            score_low = jnp.concatenate(low, axis=0)
            value_grad = nn(p_ref[r, p], grad)
            value_grad = jnp.where(low_half, value_grad[:keys], value_grad[keys:])
            key_grad = nn(score_low, scaled[here, cols])
            key_grad = jnp.where(low_half, key_grad[:keys], key_grad[keys:])
            query_grad = tn(head_stack(k_ref[r, :, cols], low_half), score_low) * HEAD ** (-0.5)
            dq_scr[here, cols] = query_grad.T
            v_cols = slice(ALL + p * 128, ALL + (p + 1) * 128)
            if is_long:
                own_out[r, :, cols] = key_grad[:rows]
                own_out[r, :, v_cols] = value_grad[:rows]
                for i in range(1, n_x):
                    block = slice(i * rows, (i + 1) * rows)
                    far_outs[i - 1][r, :rows, cols] = key_grad[block].astype(BF)
                    far_outs[i - 1][r, :rows, v_cols] = value_grad[block].astype(BF)
            else:
                ru_out[here, 2 * ALL + p * 128 : 2 * ALL + (p + 1) * 128] = key_grad.astype(BF)
                ru_out[here, 3 * ALL + p * 128 : 3 * ALL + (p + 1) * 128] = value_grad.astype(BF)

    kernel = flat(ker_ref)
    parts = two_parts(kernel)
    kernel_grad = jnp.zeros((total_rows, 128), F32)
    span_rows = rows + 2 * ext
    for p in range(PAIRS):
        cols = slice(p * 128, (p + 1) * 128)
        table = slice(p * KERNEL * 128, (p + 1) * KERNEL * 128)
        wide = nn(parts, spread[:, table])
        all_products = []
        for r in range(batch):
            here = slice(r * rows, (r + 1) * rows)
            grad = mg_ref[r, :, ALL + p * 128 : ALL + (p + 1) * 128].astype(F32)
            products = []
            for j in range(KERNEL):
                products.append((grad * up_ref[r, p, 4 + j : 4 + j + rows, :]).astype(BF))
                prp[r, j, 16 : 16 + rows, :] = wide[here, j * 128 : (j + 1) * 128] * grad
            all_products.append(jnp.concatenate(products, axis=1))
            first = 20 - ext
            total = prp[r, 0, first : first + span_rows, :]
            for j in range(1, KERNEL):
                total += prp[r, j, first - j : first - j + span_rows, :]
            if is_long:
                ug_out[r, :, cols] = total[ext : ext + rows]
                send_rims(r, rows + 8, cols, total)
            else:
                ru_out[here, cols] = total.astype(BF)
        kernel_grad += nt(jnp.concatenate(all_products, axis=0), spread[:128, table])
    if is_long:
        zero = jnp.zeros((batch, 8, ALL), BF)
        far_outs[0][:, rows + 8 : rows + 16, ALL:] = zero
        far_outs[-1][:, rows + 8 : rows + 16, ALL:] = zero

    logit_low = (kernel * (kernel_grad - window_sum(kernel * kernel_grad))).astype(BF)
    left[D:, :] = nt(perm[...], logit_low).astype(BF)
    span_grad = nn(logit_low, tn(perm[:TAPS, :], w_span[...]).astype(BF))
    key_conv = flat(kc_ref)
    right[:, ALL:] = (key_conv * qf).astype(BF)
    left[:D, :] = flat(dl_ref).T
    point_low = (span_grad * qf).astype(BF)
    right[:, :ALL] = point_low
    query_total = (dq_scr[...] + span_grad * key_conv).astype(BF)
    depth_grad = nt(point_low, w_point[...])
    for r in range(batch):
        for c in range(D // 128):
            dgp[r, c, 16 : 16 + rows, :] = depth_grad[
                r * rows : (r + 1) * rows, c * 128 : (c + 1) * 128
            ]

    if not is_long:
        ru_out[:, ALL : 2 * ALL] = query_total
        base = nt(ru_out[:, :ALL], w_unfold[...]) + nt(ru_out[:, ALL:], w_project[...])
    else:
        qt_out[...] = query_total.reshape(batch, rows, ALL)
    for c in range(D // 128):
        cols = slice(c * 128, (c + 1) * 128)
        for r in range(batch):
            x_part = xp[r, c] if is_long else x_refs[0][r, :, cols].astype(F32)
            first = 20 - ext
            total = None
            for j in range(KERNEL):
                moved = dgp[r, c, first - j : first - j + span_rows, :]
                term = depth_kernel[j : j + 1, cols].astype(F32) * moved
                total = term if total is None else total + term
                dkg[j * 8 : (j + 1) * 8, cols] += fold8(moved * x_part)
            if is_long:
                tg_out[r, :, cols] = total[ext : ext + rows] + fig_ref[r, :, cols]
                send_rims(r, rows, cols, total)
            else:
                tg_out[r, :, cols] = total + fig_ref[r, :, cols] + base[r * rows : (r + 1) * rows, cols]


def post_call(xs, mg, fig, kept, consts, joint, tokens, batch):
    count, rows = xs[0].shape[0], xs[0].shape[1]
    keys = rows * len(xs)
    total = count * rows
    is_long = len(xs) > 1
    wide = batch * rows
    first = (tokens - total) // wide if is_long else 0
    row_args = [mg, fig, *kept]
    outs = [
        ((D + 128, tokens), BF, pl.BlockSpec((D + 128, wide), lambda i: (0, first + i))),
        ((tokens, 2 * ALL), BF, pl.BlockSpec((wide, 2 * ALL), lambda i: (first + i, 0))),
        ((KERNEL * 8, D), F32, pl.BlockSpec((KERNEL * 8, D), lambda i: (0, 0))),
    ]
    row_out = lambda r, c, t: ((count, r, c), t, per_row(r, c, batch=batch))
    scratch = []
    if is_long:
        outs.append(row_out(rows, D, F32))
        for i in range(1, len(xs)):
            outs.append(row_out(rows + 16 if i in (1, len(xs) - 1) else rows, D, BF))
        outs += [row_out(rows, ALL, BF), row_out(rows, ALL, F32), row_out(rows, D, F32)]
        scratch.append(pltpu.VMEM((batch, D // 128, rows + 16, 128), F32))
    else:
        outs += [
            row_out(rows, D, F32),
            ((tokens, 4 * ALL), BF, pl.BlockSpec((wide, 4 * ALL), lambda i: (first + i, 0))),
        ]
    scratch += [
        pltpu.VMEM((batch, D // 128, rows + 32, 128), F32),
        pltpu.VMEM((batch, KERNEL, rows + 32, 128), F32),
        pltpu.VMEM((wide, ALL), F32),
    ]
    inputs = [*xs, *row_args, *consts]
    return pl.pallas_call(
        functools.partial(post_body, len(xs)),
        grid=(count // batch,),
        in_specs=[per_row(rows, D, batch=batch)] * len(xs)
        + [per_row(*a.shape[1:], batch=batch) for a in row_args]
        + [fixed(c) for c in consts]
        + [pl.BlockSpec(memory_space=pl.ANY)] * len(joint),
        out_specs=[s for _, _, s in outs],
        out_shape=[jax.ShapeDtypeStruct(s, t) for s, t, _ in outs],
        scratch_shapes=scratch,
        input_output_aliases={len(inputs) + i: i for i in range(len(joint))},
        compiler_params=params(),
        cost_estimate=pl.CostEstimate(
            flops=total * 10_000_000, bytes_accessed=30_000_000, transcendentals=0
        ),
        name="post_long" if is_long else "post_short",
    )(*inputs, *joint)


def end_body(n_x, *refs):
    own, *rest = refs[:n_x]
    qt, ug, tg, w_project, w_unfold, _, out_ref, ru_out = refs[n_x:]
    rows = own.shape[1]
    both = own[0]
    for far in rest:
        both = both + far[0, :rows, :].astype(F32)
    _, _, odd = row_sides()
    unfold = ug[0]
    after = pick(odd, rest[2][0, rows:, :], rest[0][0, rows:, :])
    before = pick(odd, rest[0][0, rows:, :], rest[2][0, rows:, :])
    middle = unfold[8 : rows - 8]
    ru_out[:, :ALL] = jnp.concatenate(
        [unfold[:8] + before[8:, :ALL], middle, unfold[rows - 8 :] + after[8:, :ALL]], axis=0
    ).astype(BF)
    ru_out[:, ALL : 2 * ALL] = qt[0]
    ru_out[:, 2 * ALL :] = both.astype(BF)
    total = nt(ru_out[:, :ALL], w_unfold[...]) + nt(ru_out[:, ALL:], w_project[...]) + tg[0]
    out_ref[0] = total
    out_ref[0, :8, :] = total[:8] + before[:8]
    out_ref[0, rows - 8 :, :] = total[rows - 8 :] + after[:8]


def end_call(own, far, qt, ug, tg, w_project, w_unfold, joint):
    count, rows = own.shape[0], own.shape[1]
    first = (joint.shape[0] - count * rows) // rows
    row_args = [own, *far, qt, ug, tg]
    return pl.pallas_call(
        functools.partial(end_body, 1 + len(far)),
        grid=(count,),
        in_specs=[per_row(*a.shape[1:]) for a in row_args]
        + [fixed(w_project), fixed(w_unfold), pl.BlockSpec(memory_space=pl.ANY)],
        out_specs=[per_row(rows, D), pl.BlockSpec((rows, 4 * ALL), lambda i: (first + i, 0))],
        out_shape=[
            jax.ShapeDtypeStruct((count, rows, D), F32),
            jax.ShapeDtypeStruct(joint.shape, BF),
        ],
        input_output_aliases={len(row_args) + 2: 1},
        compiler_params=params(),
        cost_estimate=pl.CostEstimate(
            flops=count * rows * 2_400_000, bytes_accessed=10_000_000, transcendentals=0
        ),
        name="end_long",
    )(*row_args, w_project, w_unfold, joint)


UNIT = 3 * ALL
CHUNK = 4 * UNIT
CHUNKS = 8
LAST = 6 * 512
PACKED = (CHUNKS - 1) * CHUNK + LAST
SPAN_ROW = (CHUNKS - 1) * CHUNK + 2 * UNIT
SMALL_ROW = SPAN_ROW + ALL
SMALL = 48
MESH = pl.DeviceIdType.MESH


CHUNK_PARTS = (
    ((0, 2560, "cxyz"), (2560, 2048, "cyxz")),
    ((4608, 2560, "cxyz"), (7168, 2048, "cyxz")),
    ((9216, 2560, "cxyz"), (11776, 2048, "cyxz")),
    ((13824, 1536, "cxyz"), (15360, 3072, "cyxz")),
    ((18432, 2048, "cyxz"), (20480, 2048, "cxyz"), (22528, 512, "czxy")),
    ((23040, 2048, "cxyz"), (25088, 1024, "czxy"), (26112, 1536, "cyxz")),
    ((27648, 1536, "cxyz"), (29184, 1024, "czyx"), (30208, 2048, "cyxz")),
    ((32256, 1024, "cyxz"), (33280, 1536, "cxyz"), (34816, 512, "cyzx")),
)
PARTS = sum(CHUNK_PARTS, ())


def rows_of(ref, start, count):
    return ref.at[pl.ds(pl.multiple_of(start, 16), count), :]


def add_rows(out, start, sources, count):
    step = next(s for s in (160, 128, 96, 80, 64, 48, 32, 16) if count % s == 0)

    def body(i, carry):
        total = None
        for ref, first in sources:
            value = rows_of(ref, first + i * step, step)[...].astype(F32)
            total = value if total is None else total + value
        rows_of(out, start + i * step, step)[...] = total.astype(BF)
        return carry

    lax.fori_loop(0, count // step, body, 0)


class Exchange:
    def __init__(self, source, res, out, got, sems):
        self.source, self.res, self.out, self.got = source, res, out, got
        self.send_sem, self.recv_sem, self.out_sem = sems
        dp, blk = lax.axis_index("dp"), lax.axis_index("blk")
        core, x, y, z = lax.rem(blk, 2), blk // 2, lax.rem(dp, 2), dp // 2
        self.index = {"c": core, "x": x, "y": y, "z": z}
        self.peers = {
            "c": [(dp, blk + 1 - 2 * core)],
            "x": [(dp, blk + 2 - 4 * x)],
            "y": [(dp + 1 - 2 * y, blk)],
            "z": [(lax.rem(z + i, 4) * 2 + y, blk) for i in (1, 2, 3)],
        }
        self.sizes, self.slots, self.places = [], [], []
        used = 0
        for _, count, order in PARTS:
            sizes, slots, places = [count], [0], []
            for axis in order:
                sizes.append(sizes[-1] // (len(self.peers[axis]) + 1))
                slots.append(slots[-1] + len(self.peers[axis]))
                places.append(used)
                used += sizes[-1] * len(self.peers[axis])
            self.sizes.append(sizes)
            self.slots.append(slots)
            self.places.append(places)

    def greet(self):
        barrier = pltpu.get_barrier_semaphore()
        for devices in self.peers.values():
            for device in devices:
                pl.semaphore_signal(barrier, inc=1, device_id=device, device_id_type=MESH)

    def await_greetings(self):
        pl.semaphore_wait(pltpu.get_barrier_semaphore(), 6)

    def sum_at(self, n, level):
        return (self.source, PARTS[n][0]) if level == 0 else (self.got, self.places[n][level - 1])

    def held(self, n, level):
        row, _, order = PARTS[n]
        for i in range(level):
            row = row + self.index[order[i]] * self.sizes[n][i + 1]
        return row

    def copies(self, n, level, back):
        axis = PARTS[n][2][level]
        size = self.sizes[n][level + 1]
        result = []
        for i, device in enumerate(self.peers[axis]):
            if back:
                source = target = rows_of(self.res, self.held(n, level + 1), size)
            else:
                ref, first = self.sum_at(n, level)
                theirs = lax.rem(self.index[axis] + i + 1, len(self.peers[axis]) + 1)
                source = rows_of(ref, first + theirs * size, size)
                target = rows_of(self.got, self.places[n][level] + i * size, size)
            slot = self.slots[n][level] + i + (6 if back else 0)
            result.append(
                pltpu.make_async_remote_copy(
                    src_ref=source,
                    dst_ref=target,
                    send_sem=self.send_sem.at[n, slot],
                    recv_sem=self.recv_sem.at[n, slot],
                    device_id=device,
                    device_id_type=MESH,
                )
            )
        return result

    def copy_out(self, n):
        row, count, _ = PARTS[n]
        return pltpu.make_async_copy(
            rows_of(self.res, row, count), rows_of(self.out, row, count), self.out_sem.at[n]
        )

    def stage(self, n, s):
        if s:
            for copy in self.copies(n, s - 1 if s <= 4 else 8 - s, s > 4):
                copy.wait_recv()
        if 1 <= s <= 4:
            level = s - 1
            axis = PARTS[n][2][level]
            size = self.sizes[n][s]
            ref, first = self.sum_at(n, level)
            terms = [(ref, first + self.index[axis] * size)]
            terms += [
                (self.got, self.places[n][level] + i * size) for i in range(len(self.peers[axis]))
            ]
            into, start = self.sum_at(n, s) if s < 4 else (self.res, self.held(n, 4))
            add_rows(into, start, terms, size)
        if s < 8:
            for copy in self.copies(n, s if s < 4 else 7 - s, s >= 4):
                copy.start()
        else:
            self.copy_out(n).start()

    def finish(self):
        for n in range(len(PARTS)):
            for level in range(4):
                for back in (False, True):
                    for copy in self.copies(n, level, back):
                        copy.wait_send()
            self.copy_out(n).wait()


def weights_body(remote, ranges, *refs):
    left, right, left_post, right_post, rows_grad, stat_a, stat_b, depth_a, depth_b, out = refs[:10]
    held_left, held_right, sums, part, load_sem = refs[10:15]
    scratch = refs[15:]
    tokens = held_left.shape[2]

    def loads(k):
        slot = k % 2
        if k < 4:
            a, a_rows, b, b_cols = left, (k * ALL, ALL), right, (k * 4 * ALL, 4 * ALL)
        elif k == 4:
            a, a_rows, b, b_cols = left, (2 * D, D), right, (2 * FF, D)
        elif k < 7:
            a, a_rows, b, b_cols = left, (3 * D + (k - 5) * ALL, ALL), rows_grad, (0, 4 * ALL)
        else:
            a, a_rows, b, b_cols = left_post, (0, D + 128), right_post, (0, D)
        copies = []
        for i, (to, start, size) in enumerate(ranges):
            here, there = pl.ds(to, size), pl.ds(start, size)
            copies.append(
                pltpu.make_async_copy(
                    a.at[pl.ds(*a_rows), there],
                    held_left.at[slot, : a_rows[1], here],
                    load_sem.at[slot, 2 * i],
                )
            )
            copies.append(
                pltpu.make_async_copy(
                    b.at[there, pl.ds(*b_cols)],
                    held_right.at[slot, here, : b_cols[1]],
                    load_sem.at[slot, 2 * i + 1],
                )
            )
        return copies

    def compute(k):
        for copy in loads(k):
            copy.wait()
        if k + 1 < CHUNKS:
            for copy in loads(k + 1):
                copy.start()
        slot = k % 2
        by_left = {4: 2, 7: 1}.get(k, 4)

        def unit(j, carry):
            if by_left == 4:
                a, b = 0, j
            elif by_left == 2:
                a, b = j // 2, lax.rem(j, 2)
            else:
                a, b = j, 0
            lhs = held_left[slot, pl.ds(pl.multiple_of(a * ALL, ALL), ALL), :]
            rhs = held_right[slot, :, pl.ds(pl.multiple_of(b * ALL, ALL), ALL)]
            value = nn(lhs, rhs)
            for c in range(3):
                rows_of(part, k * CHUNK + j * UNIT + c * ALL, ALL)[...] = value[
                    :, c * 128 : (c + 1) * 128
                ].astype(BF)
            return carry

        lax.fori_loop(0, 2 if k == 7 else 4, unit, 0)
        ones = jnp.ones((16, tokens), BF)
        if k in (0, 1, 4, 5):
            wide = 2 if k == 4 else 4
            first = {0: 28, 1: 32, 4: 36, 5: 38}[k]
            total = nn(ones, held_right[slot, :, : wide * ALL])
            for j in range(wide):
                sums[first + j : first + j + 1, :] = total[0:1, j * ALL : (j + 1) * ALL]
        if k == 7:
            span = nn(held_left[slot, D:, :], held_right[slot, :, ALL:D])
            for c in range(3):
                part[SPAN_ROW + c * 128 : SPAN_ROW + (c + 1) * 128, :] = span[
                    :, c * 128 : (c + 1) * 128
                ].astype(BF)
            sums[42:43, :] = nn(ones, held_right[slot, :, :ALL])[0:1]
            sums[43:44, :128] = nt(ones, held_left[slot, D:, :])[0:1]
            for first, a, b in ((0, stat_a, stat_b), (10, depth_a, depth_b)):
                for i in range(a.shape[0] // 8):
                    both = jnp.sum(a[i * 8 : i * 8 + 8] + b[i * 8 : i * 8 + 8], axis=0, keepdims=True)
                    sums[first + 2 * i : first + 2 * i + 1, :] = both[:, :ALL]
                    sums[first + 2 * i + 1 : first + 2 * i + 2, :] = both[:, ALL:]
            small = sums[...].astype(BF)
            for c in range(3):
                part[SMALL_ROW + c * SMALL : SMALL_ROW + (c + 1) * SMALL, :] = small[
                    :, c * 128 : (c + 1) * 128
                ]
            part[SMALL_ROW + 3 * SMALL :, :] = jnp.zeros((PACKED - SMALL_ROW - 3 * SMALL, 128), BF)

    for copy in loads(0):
        copy.start()
    sums[...] = jnp.zeros_like(sums)
    if not remote:
        for k in range(CHUNKS):
            compute(k)
        pltpu.sync_copy(part, out)
        return
    res, got, *sems = scratch
    exchange = Exchange(part, res, out, got, sems)
    exchange.greet()
    for t in range(CHUNKS + 8):
        if t < CHUNKS:
            compute(t)
        if t == 0:
            exchange.await_greetings()
        for k in reversed(range(CHUNKS)):
            if 0 <= t - k <= 8:
                first = sum(len(p) for p in CHUNK_PARTS[:k])
                for n in range(first, first + len(CHUNK_PARTS[k])):
                    exchange.stage(n, t - k)
    exchange.finish()


def weights_call(remote, n_short, n_long, big, small):
    tokens = n_short + n_long
    padded = big[1].shape[0]
    n_parts = len(PARTS)
    scratch = [
        pltpu.VMEM((2, D + 128, tokens), BF),
        pltpu.VMEM((2, tokens, 4 * ALL), BF),
        pltpu.VMEM((SMALL, ALL), F32),
        pltpu.VMEM((PACKED, 128), BF),
        pltpu.SemaphoreType.DMA((2, 4)),
    ]
    if remote:
        scratch += [
            pltpu.VMEM((PACKED, 128), BF),
            pltpu.VMEM((PACKED - PACKED // 32, 128), BF),
            pltpu.SemaphoreType.DMA((n_parts, 12)),
            pltpu.SemaphoreType.DMA((n_parts, 12)),
            pltpu.SemaphoreType.DMA((n_parts,)),
        ]
    more = dict(collective_id=0, has_side_effects=True) if remote else {}
    return pl.pallas_call(
        functools.partial(weights_body, remote, ((0, 0, n_short), (n_short, padded - n_long, n_long))),
        in_specs=[pl.BlockSpec(memory_space=pl.ANY)] * len(big)
        + [pl.BlockSpec(memory_space=pltpu.VMEM)] * len(small),
        out_specs=pl.BlockSpec(memory_space=pl.ANY),
        out_shape=jax.ShapeDtypeStruct((PACKED, 128), BF),
        scratch_shapes=scratch,
        compiler_params=params(**more),
        cost_estimate=pl.CostEstimate(
            flops=2 * 31 * ALL * ALL * tokens, bytes_accessed=50_000_000, transcendentals=0
        ),
        name="weights",
    )(*big, *small)


SMALL_OUTS = [
    ("gain_second", 0, D),
    ("shift_second", 2, D),
    ("gain_first", 4, D),
    ("shift_first", 6, D),
    ("bias_outer", 8, D),
    ("bias_inner", 28, FF),
    ("bias_output", 36, D),
    ("bias_unfold", 38, ALL),
    ("bias_query", 39, ALL),
    ("bias_value", 41, ALL),
    ("bias_point", 42, ALL),
    ("bias_span", 43, TAPS),
]


def unpack_body(block, inner, outer, output, unfold, project, point, span, depth, *small):
    step = pl.program_id(0)

    def tile(unit):
        start = unit * UNIT
        return jnp.concatenate(
            [block[start + c * ALL : start + (c + 1) * ALL, :] for c in range(3)], axis=1
        )

    @pl.when(step < 2)
    def _():
        for i in range(4):
            inner[0, :, i * ALL : (i + 1) * ALL] = tile(i).astype(F32)

    @pl.when((step >= 2) & (step < 4))
    def _():
        for i in range(4):
            outer[0, i * ALL : (i + 1) * ALL, :] = tile(i).T.astype(F32)

    @pl.when(step == 4)
    def _():
        for i in range(4):
            a, b = divmod(i, 2)
            output[a * ALL : (a + 1) * ALL, b * ALL : (b + 1) * ALL] = tile(i).astype(F32)

    @pl.when((step == 5) | (step == 6))
    def _():
        unfold[...] = tile(0).astype(F32)
        for i in range(3):
            project[:, i * ALL : (i + 1) * ALL] = tile(i + 1).astype(F32)

    @pl.when(step == 7)
    def _():
        for i in range(2):
            point[i * ALL : (i + 1) * ALL, :] = tile(i).astype(F32)
        tail = 2 * UNIT
        wide = jnp.concatenate(
            [block[tail + c * 128 : tail + (c + 1) * 128, :] for c in range(3)], axis=1
        )
        span[...] = wide[:TAPS].astype(F32)
        tail += ALL
        rows = jnp.concatenate(
            [block[tail + c * SMALL : tail + (c + 1) * SMALL, :] for c in range(3)], axis=1
        ).astype(F32)
        for j in range(KERNEL):
            for half in range(2):
                place = 10 + 2 * j + half
                depth[j : j + 1, half * ALL : (half + 1) * ALL] = rows[place : place + 1]
        for ref, (_, first, size) in zip(small, SMALL_OUTS):
            for i in range(max(1, size // ALL)):
                wide = min(size, ALL)
                ref[i * ALL : i * ALL + wide] = rows[first + i, :wide]


def unpack_call(packed):
    def at(first, count):
        return lambda s: jnp.clip(s - first, 0, count - 1)

    inner_at, outer_at, rows_at = at(0, 2), at(2, 2), at(5, 2)
    whole = lambda *shape: (shape, pl.BlockSpec(shape, lambda s: (0,) * len(shape)))
    specs = [
        ((GROUPS, ALL, 4 * ALL), pl.BlockSpec((1, ALL, 4 * ALL), lambda s: (inner_at(s), 0, 0))),
        ((GROUPS, 4 * ALL, ALL), pl.BlockSpec((1, 4 * ALL, ALL), lambda s: (outer_at(s), 0, 0))),
        whole(D, D),
        ((D, ALL), pl.BlockSpec((ALL, ALL), lambda s: (rows_at(s), 0))),
        ((D, 3 * ALL), pl.BlockSpec((ALL, 3 * ALL), lambda s: (rows_at(s), 0))),
        whole(D, ALL),
        whole(TAPS, ALL),
        whole(KERNEL, D),
    ]
    specs += [whole(size) for _, _, size in SMALL_OUTS]
    return pl.pallas_call(
        unpack_body,
        grid=(CHUNKS,),
        in_specs=[pl.BlockSpec((CHUNK, 128), lambda s: (s, 0))],
        out_specs=[b for _, b in specs],
        out_shape=[jax.ShapeDtypeStruct(s, F32) for s, _ in specs],
        compiler_params=params(),
        cost_estimate=pl.CostEstimate(flops=0, bytes_accessed=27_000_000, transcendentals=0),
        name="unpack",
    )(packed)


def shards(
    long_input,
    short_input,
    long_cotan,
    short_cotan,
    live_slots,
    w_project,
    bias_query,
    bias_value,
    depth_kernel,
    w_point,
    bias_point,
    w_span,
    bias_span,
    w_unfold,
    bias_unfold,
    w_output,
    bias_output,
    gain_first,
    shift_first,
    w_inner,
    bias_inner,
    w_outer,
    bias_outer,
    gain_second,
    shift_second,
):
    n_blk = lax.axis_size("blk")
    short_x = short_input.reshape(short_input.shape[2:])
    short_cot = short_cotan.reshape(short_cotan.shape[2:])
    perm, spread = (jnp.asarray(t) for t in tap_tables())
    span_t = w_span.T
    pre_consts = (
        bias_query, bias_value, bias_point, bias_span, bias_unfold, depth_kernel,
        w_project, w_point, span_t, w_unfold, spread, perm,
    )
    ffn_consts = (
        bias_output, gain_first, shift_first, bias_outer, gain_second, shift_second, bias_inner,
        w_output, w_inner, w_outer,
    )
    *short_kept, short_mixed, near, far, both = pre_call(
        [short_x], pre_consts, SHORT_BATCH, (long_input,)
    )
    xs = [long_input, near, far, both]
    *long_kept, long_mixed = pre_call(xs, pre_consts, LONG_BATCH)

    n_long, n_short = (a.shape[0] * a.shape[1] for a in (long_input, short_x))
    tokens = (pl.cdiv(n_short, n_long) + 1) * n_long
    as_long = lambda a: a.reshape(-1, FFN_LONG, D)
    l_out, l_fig, l_mg, *joint, l_stat = ffn_call(
        None, 0, *map(as_long, (long_mixed, long_input, long_cotan)), ffn_consts, (), tokens
    )
    l_out, l_fig, l_mg = (a.reshape(long_input.shape) for a in (l_out, l_fig, l_mg))
    s_out, s_fig, s_mg, left, right, s_stat = ffn_call(
        live_slots,
        short_x.shape[1],
        *(a.reshape(-1, FFN_ROWS, D) for a in (short_mixed, short_x, short_cot)),
        ffn_consts,
        joint,
        tokens,
    )
    s_fig, s_mg = s_fig.reshape(short_x.shape), s_mg.reshape(short_x.shape)
    post_consts = (depth_kernel, w_point, span_t, spread, perm)
    l_post = post_call(xs, l_mg, l_fig, long_kept, post_consts, (), tokens, LONG_BATCH)
    (*joint, l_dkg, own), l_rest = l_post[:4], l_post[4:]
    far, (l_qt, l_ug, l_tg) = l_rest[: n_blk - 1], l_rest[n_blk - 1 :]
    far = [
        lax.ppermute(a, "blk", [(i, i ^ k) for i in range(n_blk)])
        for k, a in enumerate(far, 1)
    ]
    left_post, right_post, s_dkg, short_grad, rows_grad = post_call(
        [short_x], s_mg, s_fig, short_kept, post_consts + (w_project, w_unfold), joint, tokens, SHORT_BATCH
    )
    long_grad, rows_grad = end_call(own, far, l_qt, l_ug, l_tg, w_project, w_unfold, rows_grad)

    remote = lax.axis_size("dp") == 8 and n_blk == 4
    packed = weights_call(
        remote, n_short, n_long, (left, right, left_post, right_post, rows_grad), (l_stat, s_stat, l_dkg, s_dkg)
    )
    if not remote:
        packed = lax.psum(packed, ("dp", "blk"))
    inner, outer, output, unfold, project, point, span, depth, *small = unpack_call(packed)
    named = {name: value for (name, _, _), value in zip(SMALL_OUTS, small)}
    return (
        l_out,
        s_out.reshape(short_input.shape),
        long_grad,
        short_grad.reshape(short_input.shape),
        project,
        named["bias_query"],
        named["bias_value"],
        depth,
        point,
        named["bias_point"],
        span.T,
        named["bias_span"],
        unfold,
        named["bias_unfold"],
        output,
        named["bias_output"],
        named["gain_first"],
        named["shift_first"],
        inner,
        named["bias_inner"],
        outer,
        named["bias_outer"],
        named["gain_second"],
        named["shift_second"],
    )


def solution(mesh):
    rows = P("dp", "blk", None)
    slots = P("dp", "blk", None, None, None)
    in_specs = (rows, slots, rows, slots, P("dp", "blk")) + (P(),) * 20
    out_specs = (rows, slots, rows, slots) + (P(),) * 20
    return jax.shard_map(shards, mesh=mesh, in_specs=in_specs, out_specs=out_specs, check_vma=False)
```

```python
import functools

import jax
import jax.numpy as jnp
import numpy as np
from jax import lax
from jax.experimental import pallas as pl
from jax.experimental.pallas import tpu as pltpu
from jax.sharding import PartitionSpec as P

D = 768
FF = 3072
HEADS = 6
HEAD = 64
KERNEL = 9
GROUPS = 2
ALL = 384
PAIRS = 3
TAPS = HEADS * KERNEL
HALF = KERNEL // 2

F32 = jnp.float32
BF = jnp.bfloat16
ROOT_HALF = 0.7071067811865476
DENSITY = 0.3989422804014327
FFN_ROWS = 256
FFN_LONG = 384
SHORT_BATCH = 2
LONG_BATCH = 1
VMEM = {
    "pre_short": 58,
    "pre_long": 36,
    "ffn_short": 42,
    "ffn_long": 46,
    "post_short": 46,
    "post_long": 34,
    "end": 34,
    "weights": 48,
    "unpack": 48,
}


def nn(a, b):
    return lax.dot_general(a, b, (((1,), (0,)), ((), ())), preferred_element_type=F32)


def nt(a, b):
    return lax.dot_general(a, b, (((1,), (1,)), ((), ())), preferred_element_type=F32)


def tn(a, b):
    return lax.dot_general(a, b, (((0,), (0,)), ((), ())), preferred_element_type=F32)


def tap_tables():
    perm = np.zeros((128, 128), np.float32)
    spread = np.zeros((256, PAIRS * KERNEL * 128), np.float32)
    for h in range(HEADS):
        for j in range(KERNEL):
            lane = j * HEADS + h
            perm[h * KERNEL + j, lane] = 1
            perm[h * KERNEL + j, TAPS + lane] = 1
            start = ((h // 2) * KERNEL + j) * 128 + (h % 2) * HEAD
            spread[lane, start : start + HEAD] = 1
            spread[128 + lane, start : start + HEAD] = 1
    return perm.astype(jnp.bfloat16), spread.astype(jnp.bfloat16)


def window(values, op):
    left = lambda v, n: pltpu.roll(v, 128 - n, 1)
    one = op(values, left(values, 6))
    two = op(one, left(one, 12))
    four = op(two, left(two, 24))
    return op(four, left(values, 48))


def window_sum(values):
    return window(values + pltpu.roll(values, TAPS, 1), jnp.add)


def head_stack(rows, low_half):
    zero = jnp.zeros_like(rows)
    return jnp.concatenate(
        [jnp.where(low_half, rows, zero), jnp.where(low_half, zero, rows)], axis=0
    )


def two_parts(values):
    high = values.astype(BF)
    rest = (values - high.astype(F32)).astype(BF)
    return jnp.concatenate([high, rest], axis=1)


def row_sides():
    place = lax.axis_index("blk")
    count = lax.axis_size("blk")
    return (place > 0).astype(F32), (place < count - 1).astype(F32), lax.rem(place, 2) == 1


def pick(odd, first, second):
    return jnp.where(odd, first.astype(F32), second.astype(F32))


def row_ends(x_refs, r, sides):
    lower, upper, odd = sides
    rows = x_refs[0].shape[1]
    before = pick(odd, x_refs[1][r, rows - 16 :, :], x_refs[3][r, rows - 16 :, :])
    after = pick(odd, x_refs[3][r, :16, :], x_refs[1][r, :16, :])
    return before * lower, after * upper


def fill_ends(xp, x_refs, sides):
    batch, rows = x_refs[0].shape[:2]
    for r in range(batch):
        if sides is not None:
            before, after = row_ends(x_refs, r, sides)
        for c in range(D // 128):
            cols = slice(c * 128, (c + 1) * 128)
            zero = jnp.zeros((8, 128), F32)
            xp[r, c, 0:8, :] = zero if sides is None else before[8:, cols]
            xp[r, c, 8 + rows : 16 + rows, :] = zero if sides is None else after[:8, cols]
            xp[r, c, 8 : 8 + rows, :] = x_refs[0][r, :, cols].astype(F32)


def as_row(ref):
    return ref[...].astype(F32).reshape(1, ref.shape[0])


class Gather:
    def __init__(self, own, outs, send_sem, recv_sem):
        self.own, self.outs, self.send_sem, self.recv_sem = own, outs, send_sem, recv_sem
        dp, blk = lax.axis_index("dp"), lax.axis_index("blk")
        core, x = lax.rem(blk, 2), blk // 2
        self.core_peer = (dp, blk + 1 - 2 * core)
        self.x_peer = (dp, blk + 2 - 4 * x)

    def copy(self, i):
        source = self.outs[1] if i == 2 else self.own
        return pltpu.make_async_remote_copy(
            src_ref=source,
            dst_ref=self.outs[i],
            send_sem=self.send_sem.at[i],
            recv_sem=self.recv_sem.at[i],
            device_id=self.x_peer if i == 1 else self.core_peer,
            device_id_type=pl.DeviceIdType.MESH,
        )

    def begin(self):
        barrier = pltpu.get_barrier_semaphore()
        for device in (self.core_peer, self.x_peer):
            pl.semaphore_signal(
                barrier, inc=1, device_id=device, device_id_type=pl.DeviceIdType.MESH
            )
        pl.semaphore_wait(barrier, 2)
        self.copy(1).start()
        self.copy(0).start()

    def forward(self):
        self.copy(1).wait_recv()
        self.copy(2).start()

    def end(self):
        for i in (0, 2):
            self.copy(i).wait_recv()
        for i in range(3):
            self.copy(i).wait_send()


def pre_body(n_x, *refs):
    gather = None
    if n_x == 1:
        own, *refs = refs
        gather = Gather(own, refs[22:25], *refs[-2:])
        refs = refs[:22] + refs[25:-2]
    x_refs, refs = refs[:n_x], refs[n_x:]
    bias_query, bias_value, bias_point, bias_span, bias_unfold, depth_kernel = refs[:6]
    w_project, w_point, w_span, w_unfold, spread, perm = refs[6:12]
    q_out, k_out, v_out, p_out, kc_out, ker_out, dl_out, up_out, mix_out = refs[12:21]
    xp, vec = refs[21:]

    @pl.when(pl.program_id(0) == 0)
    def _():
        vec[16:24, :] = jnp.zeros((8, D), F32)
        vec[0:1, :ALL] = as_row(bias_query)
        vec[0:1, ALL:] = as_row(bias_value)
        vec[1:2, :ALL] = as_row(bias_point)
        vec[1:2, ALL:] = as_row(bias_unfold)
        vec[21:22, :TAPS] = as_row(bias_span)
        vec[8:17, :] = depth_kernel[...].astype(F32)
        if gather:
            gather.begin()

    batch, rows = x_refs[0].shape[:2]
    total_rows = batch * rows
    is_long = n_x > 1
    sides = row_sides() if is_long else None
    x = x_refs[0][...].reshape(total_rows, D)
    fill_ends(xp, x_refs, sides)
    bias_query = vec[0:1, :ALL]
    bias_value = vec[0:1, ALL:]
    by_row = lambda v: v.reshape(batch, rows, v.shape[-1])
    if is_long:
        q = (nn(x, w_project[:, :ALL]) + bias_query).astype(BF)
        for i in range(n_x):
            both = nn(x_refs[i][...].reshape(total_rows, D), w_project[:, ALL:])
            k_out[:, i * rows : (i + 1) * rows, :] = by_row(both[:, :ALL].astype(BF))
            v_out[:, i * rows : (i + 1) * rows, :] = by_row((both[:, ALL:] + bias_value).astype(BF))
    else:
        both = nn(x, w_project[...])
        q = (both[:, :ALL] + bias_query).astype(BF)
        k_out[...] = by_row(both[:, ALL : 2 * ALL].astype(BF))
        v_out[...] = by_row((both[:, 2 * ALL :] + bias_value).astype(BF))
    q_out[...] = by_row(q)

    for r in range(batch):
        for c in range(D // 128):
            cols = slice(c * 128, (c + 1) * 128)
            total = vec[8:9, cols] * xp[r, c, 4 : 4 + rows, :]
            for j in range(1, KERNEL):
                total += vec[8 + j : 9 + j, cols] * xp[r, c, 4 + j : 4 + j + rows, :]
            dl_out[r, :, cols] = total.astype(BF)
    key_conv = nn(dl_out[...].reshape(total_rows, D), w_point[...]) + vec[1:2, :ALL]
    kc_out[...] = by_row(key_conv)
    span = (key_conv * q.astype(F32)).astype(BF)
    span_weights = tn(w_span[...], perm[:TAPS, :]).astype(BF)
    span_bias = nn(vec[16:24, :128].astype(BF), perm[...])[5:6]
    logits = nn(span, span_weights) + span_bias
    lane = lax.broadcasted_iota(jnp.int32, (1, 128), 1)
    raised = jnp.where(lane < TAPS, jnp.exp(logits - window(logits, jnp.maximum)), 0.0)
    kernel = jnp.where(lane < TAPS, raised / window_sum(raised), 0.0)
    ker_out[...] = by_row(kernel)

    bias_unfold = vec[1:2, ALL:]
    unfold_rows = nn(x, w_unfold[...]) + bias_unfold
    for r in range(batch):
        if is_long:
            lower, upper, _ = sides
            ends = jnp.concatenate(row_ends(x_refs, r, sides), axis=0).astype(BF)
            unfold_ends = nn(ends, w_unfold[...]) + bias_unfold
        for c in range(PAIRS):
            cols = slice(c * 128, (c + 1) * 128)
            up_out[r, c, 8 : 8 + rows, :] = unfold_rows[r * rows : (r + 1) * rows, cols]
            if is_long:
                up_out[r, c, 0:8, :] = unfold_ends[8:16, cols] * lower
                up_out[r, c, 8 + rows : 16 + rows, :] = unfold_ends[16:24, cols] * upper
            else:
                zero = jnp.zeros((8, 128), F32)
                up_out[r, c, 0:8, :] = zero
                up_out[r, c, 8 + rows : 16 + rows, :] = zero

    if gather:

        @pl.when(pl.program_id(0) == pl.num_programs(0) - 1)
        def _():
            gather.forward()

    low_half = lane < HEAD
    parts = two_parts(kernel)
    scaled = q * jnp.asarray(HEAD ** (-0.5), BF)
    keys = k_out.shape[1]
    for p in range(PAIRS):
        cols = slice(p * 128, (p + 1) * 128)
        wide = nn(parts, spread[:, p * KERNEL * 128 : (p + 1) * KERNEL * 128])
        for r in range(batch):
            here = slice(r * rows, (r + 1) * rows)
            total = wide[here, :128] * up_out[r, p, 4 : 4 + rows, :]
            for j in range(1, KERNEL):
                total += wide[here, j * 128 : (j + 1) * 128] * up_out[r, p, 4 + j : 4 + j + rows, :]
            mix_out[r, :, ALL + p * 128 : ALL + (p + 1) * 128] = total.astype(BF)

            scores = nt(head_stack(k_out[r, :, cols], low_half), scaled[here, cols])
            for half in range(2):
                part = scores[half * keys : (half + 1) * keys]
                top = jnp.max(part, axis=0, keepdims=True)
                grown = jnp.exp(part - top)
                share = 1.0 / jnp.sum(grown, axis=0, keepdims=True)
                p_out[r, p, half * keys : (half + 1) * keys, :] = (grown * share).astype(BF)
            context = tn(head_stack(v_out[r, :, cols], low_half), p_out[r, p])
            mix_out[r, :, cols] = context.astype(BF).T

    if gather:

        @pl.when(pl.program_id(0) == pl.num_programs(0) - 1)
        def _():
            gather.end()


def fixed(array):
    zeros = (0,) * array.ndim
    return pl.BlockSpec(array.shape, lambda *_: zeros, pipeline_mode=pl.Buffered(1))


def per_row(*shape, batch=1):
    zeros = (0,) * len(shape)
    return pl.BlockSpec((batch, *shape), lambda i: (i, *zeros))


def in_vmem(shape, dtype):
    return pltpu.VMEM(shape, dtype)


def held(*arrays):
    return [pltpu.with_memory_space_constraint(a, pltpu.VMEM) for a in arrays]


def fetched(*arrays):
    return [pltpu.with_memory_space_constraint(a, pltpu.HBM) for a in arrays]


def params(name, **more):
    return pltpu.CompilerParams(vmem_limit_bytes=VMEM[name] * 1024 * 1024, **more)


def pre_call(xs, consts, batch, gathered=()):
    anywhere = pl.BlockSpec(memory_space=pl.ANY)
    count, rows = xs[0].shape[0], xs[0].shape[1]
    keys = rows * len(xs)
    shapes = [
        ((rows, ALL), BF),
        ((keys, ALL), BF),
        ((keys, ALL), BF),
        ((PAIRS, 2 * keys, rows), BF),
        ((rows, ALL), F32),
        ((rows, 128), F32),
        ((rows, D), BF),
        ((PAIRS, rows + 16, 128), F32),
        ((rows, D), BF),
    ]
    return pl.pallas_call(
        functools.partial(pre_body, len(xs)),
        grid=(count // batch,),
        in_specs=[anywhere] * len(gathered)
        + [per_row(rows, D, batch=batch)] * len(xs) + [fixed(c) for c in consts],
        out_specs=[per_row(*s, batch=batch) for s, _ in shapes] + [anywhere] * (3 * len(gathered)),
        out_shape=[
            (in_vmem if not gathered or i == 8 else pltpu.HBM)((count, *s), t)
            for i, (s, t) in enumerate(shapes)
        ]
        + [pltpu.HBM(g.shape, g.dtype) for g in gathered] * 3,
        scratch_shapes=[pltpu.VMEM((batch, D // 128, rows + 16, 128), F32), pltpu.VMEM((24, D), F32)]
        + [pltpu.SemaphoreType.DMA((3,))] * (2 * len(gathered)),
        compiler_params=params("pre_short", collective_id=1, has_side_effects=True)
        if gathered
        else params("pre_long"),
        cost_estimate=pl.CostEstimate(
            flops=count * rows * 6_000_000, bytes_accessed=20_000_000, transcendentals=1_000_000
        ),
        name="pre_long" if len(xs) > 1 else "pre_short",
    )(*fetched(*gathered, *xs, *consts))


def norm_stats(z):
    centre = z - jnp.mean(z, axis=-1, keepdims=True)
    inverse = lax.rsqrt(jnp.mean(centre * centre, axis=-1, keepdims=True) + 1e-12)
    return centre * inverse, inverse


def norm_back(upstream, normed, inverse, gain):
    scaled = upstream * gain
    plain = jnp.mean(scaled, axis=-1, keepdims=True)
    cross = jnp.mean(scaled * normed, axis=-1, keepdims=True)
    return inverse * (scaled - plain - normed * cross)


def fold8(values):
    return jnp.sum(values.reshape(values.shape[0] // 8, 8, values.shape[1]), axis=0)


def gelu_pair(v):
    cdf = 0.5 * (1.0 + lax.erf(v * ROOT_HALF))
    return v * cdf, cdf + v * jnp.exp(-0.5 * (v * v)) * DENSITY


def ffn_body(slot_rows, *refs):
    masked = slot_rows > 0
    if masked:
        live_ref, *refs = refs
    mix_ref, x_ref, cot_ref = refs[:3]
    vectors, (w_output, w_inner, w_outer) = refs[3:10], refs[10:13]
    out_ref, fig_ref, mg_ref, left, right, stat, slope, vec = refs[-8:]
    inl_ref, act_ref = right.at[:, :FF], right.at[:, FF : 2 * FF]
    step = pl.program_id(0)
    rows = x_ref.shape[1]

    @pl.when(step == 0)
    def _():
        stat[...] = jnp.zeros_like(stat)
        for i, ref in enumerate(vectors[:-1]):
            vec[2 + i : 3 + i, :] = as_row(ref)
        inner_row = as_row(vectors[-1])
        for i in range(FF // D):
            vec[8 + i : 9 + i, :] = inner_row[:, i * D : (i + 1) * D]

    x = x_ref[0]
    mixed = mix_ref[0]
    left[2 * D : 3 * D, :] = mixed.T
    left[3 * D :, :] = x.T
    first_normed, first_inverse = norm_stats(nn(mixed, w_output[...]) + vec[2:3, :] + x.astype(F32))
    first_norm = first_normed * vec[3:4, :] + vec[4:5, :]
    first_low = first_norm.astype(BF)
    left[:D, :] = first_low.T
    outer = []
    for g in range(GROUPS):
        for c in range(2):
            k = g * 2 + c
            inner = nn(first_low[:, g * ALL : (g + 1) * ALL], w_inner[g, :, c * D : (c + 1) * D])
            for r in range(0, rows, 16):
                act, slo = gelu_pair(inner[r : r + 16] + vec[8 + k : 9 + k, :])
                act_ref[r : r + 16, k * D : (k + 1) * D] = act.astype(BF)
                slope[r : r + 16, k * D : (k + 1) * D] = slo
        outer.append(nn(act_ref[:, g * 2 * D : (g + 1) * 2 * D], w_outer[g]))
    second_normed, second_inverse = norm_stats(
        jnp.concatenate(outer, axis=1) + vec[5:6, :] + first_norm
    )
    gain_second = vec[6:7, :]
    out_ref[0] = (second_normed * gain_second + vec[7:8, :]).astype(BF)
    seed = cot_ref[0].astype(F32)
    if masked:
        token = step * rows + lax.broadcasted_iota(jnp.int32, (rows, 1), 0)
        seed = jnp.where(token < live_ref[0, 0] * slot_rows, seed, 0.0)
    stat[0:8, :] += fold8(seed * second_normed)
    stat[8:16, :] += fold8(seed)
    second_grad = norm_back(seed, second_normed, second_inverse, gain_second)
    outer_low = second_grad.astype(BF)
    left[D : 2 * D, :] = outer_low.T
    stat[32:40, :] += fold8(outer_low.astype(F32))
    first_grad = []
    for g in range(GROUPS):
        for c in range(2):
            k = g * 2 + c
            back = nt(outer_low[:, g * ALL : (g + 1) * ALL], w_outer[g, c * D : (c + 1) * D, :])
            inl_ref[:, k * D : (k + 1) * D] = (back * slope[:, k * D : (k + 1) * D]).astype(BF)
        first_grad.append(nt(inl_ref[:, g * 2 * D : (g + 1) * 2 * D], w_inner[g]))
    first_grad = second_grad + jnp.concatenate(first_grad, axis=1)
    stat[16:24, :] += fold8(first_grad * first_normed)
    stat[24:32, :] += fold8(first_grad)
    first_in_grad = norm_back(first_grad, first_normed, first_inverse, vec[3:4, :])
    fig_ref[0] = first_in_grad
    attended_low = first_in_grad.astype(BF)
    right[:, 2 * FF :] = attended_low
    mg_ref[0] = nt(attended_low, w_output[...]).astype(BF)


def ffn_call(live, slot_rows, mixed, x, cotan, consts, joint, tokens):
    count, rows = x.shape[0], x.shape[1]
    total = count * rows
    masked = live is not None
    first = 0 if masked else (tokens - total) // rows
    n_in = (4 if masked else 3) + len(consts)
    out_shapes = [
        ((count, rows, D), BF, per_row(rows, D)),
        ((count, rows, D), F32, per_row(rows, D)),
        ((count, rows, D), BF, per_row(rows, D)),
        ((4 * D, tokens), BF, pl.BlockSpec((4 * D, rows), lambda i: (0, first + i))),
        ((tokens, 2 * FF + D), BF, pl.BlockSpec((rows, 2 * FF + D), lambda i: (first + i, 0))),
        ((40, D), F32, pl.BlockSpec((40, D), lambda i: (0, 0))),
    ]
    head = [live] if masked else []
    head_specs = [pl.BlockSpec(memory_space=pltpu.SMEM)] if masked else []
    return pl.pallas_call(
        functools.partial(ffn_body, slot_rows if masked else 0),
        grid=(count,),
        in_specs=head_specs
        + [per_row(rows, D)] * 3
        + [fixed(c) for c in consts]
        + [pl.BlockSpec(memory_space=pl.ANY)] * len(joint),
        out_specs=[s for _, _, s in out_shapes],
        out_shape=[
            (in_vmem if i in (1, 2) else pltpu.HBM)(s, t)
            for i, (s, t, _) in enumerate(out_shapes)
        ],
        scratch_shapes=[pltpu.VMEM((rows, FF), F32), pltpu.VMEM((16, D), F32)],
        input_output_aliases={n_in: 3, n_in + 1: 4} if masked else {},
        compiler_params=params("ffn_short" if masked else "ffn_long"),
        cost_estimate=pl.CostEstimate(
            flops=total * 12_000_000, bytes_accessed=30_000_000, transcendentals=total * FF
        ),
        name="ffn_short" if masked else "ffn_long",
    )(*head, *held(mixed), *fetched(x, cotan, *consts, *joint))


def post_body(n_x, *refs):
    is_long = n_x > 1
    x_refs = refs[:n_x]
    refs = refs[n_x:]
    (mg_ref, fig_ref, q_ref, k_ref, v_ref, p_ref, kc_ref, ker_ref, dl_ref, up_ref) = refs[:10]
    (depth_kernel, w_point, w_span, spread, perm) = refs[10:15]
    refs = refs[15:]
    if not is_long:
        (w_project, w_unfold), refs = refs[:2], refs[4:]
    (left, right, dkg), refs = refs[:3], refs[3:]
    if is_long:
        own_out, *far_outs = refs[:n_x]
        qt_out, ug_out, tg_out = refs[n_x : n_x + 3]
        xp, dgp, prp, dq_scr = refs[n_x + 3 :]
    else:
        tg_out, ru_out, dgp, prp, dq_scr = refs
    step = pl.program_id(0)
    batch, rows = x_refs[0].shape[:2]
    total_rows = batch * rows
    keys = k_ref.shape[1]
    ext = 8 if is_long else 0
    flat = lambda ref: ref[...].reshape(total_rows, ref.shape[-1])

    @pl.when(step == 0)
    def _():
        dkg[...] = jnp.zeros_like(dkg)
        dgp[...] = jnp.zeros_like(dgp)
        prp[...] = jnp.zeros_like(prp)

    if is_long:
        sides = lower, upper, odd = row_sides()
        fill_ends(xp, x_refs, sides)

        def send_rims(r, place, cols, total):
            before, after = total[:ext] * lower, total[ext + rows :] * upper
            far_outs[0][r, place : place + 8, cols] = pick(odd, before, after).astype(BF)
            far_outs[2][r, place : place + 8, cols] = pick(odd, after, before).astype(BF)


    q = flat(q_ref)
    qf = q.astype(F32)
    scaled = q * jnp.asarray(HEAD ** (-0.5), BF)
    low_half = lax.broadcasted_iota(jnp.int32, (1, 128), 1) < HEAD
    for p in range(PAIRS):
        cols = slice(p * 128, (p + 1) * 128)
        for r in range(batch):
            here = slice(r * rows, (r + 1) * rows)
            grad = mg_ref[r, :, cols]
            weight_grad = nt(head_stack(v_ref[r, :, cols], low_half), grad)
            low = []
            for half in range(2):
                part = slice(half * keys, (half + 1) * keys)
                probs = p_ref[r, p, part, :].astype(F32)
                inner = jnp.sum(probs * weight_grad[part], axis=0, keepdims=True)
                low.append((probs * (weight_grad[part] - inner)).astype(BF))
            score_low = jnp.concatenate(low, axis=0)
            value_grad = nn(p_ref[r, p], grad)
            value_grad = jnp.where(low_half, value_grad[:keys], value_grad[keys:])
            key_grad = nn(score_low, scaled[here, cols])
            key_grad = jnp.where(low_half, key_grad[:keys], key_grad[keys:])
            query_grad = tn(head_stack(k_ref[r, :, cols], low_half), score_low) * HEAD ** (-0.5)
            dq_scr[here, cols] = query_grad.T
            v_cols = slice(ALL + p * 128, ALL + (p + 1) * 128)
            if is_long:
                own_out[r, :, cols] = key_grad[:rows]
                own_out[r, :, v_cols] = value_grad[:rows]
                for i in range(1, n_x):
                    block = slice(i * rows, (i + 1) * rows)
                    far_outs[i - 1][r, :rows, cols] = key_grad[block].astype(BF)
                    far_outs[i - 1][r, :rows, v_cols] = value_grad[block].astype(BF)
            else:
                ru_out[here, 2 * ALL + p * 128 : 2 * ALL + (p + 1) * 128] = key_grad.astype(BF)
                ru_out[here, 3 * ALL + p * 128 : 3 * ALL + (p + 1) * 128] = value_grad.astype(BF)

    kernel = flat(ker_ref)
    parts = two_parts(kernel)
    kernel_grad = jnp.zeros((total_rows, 128), F32)
    span_rows = rows + 2 * ext
    for p in range(PAIRS):
        cols = slice(p * 128, (p + 1) * 128)
        table = slice(p * KERNEL * 128, (p + 1) * KERNEL * 128)
        wide = nn(parts, spread[:, table])
        all_products = []
        for r in range(batch):
            here = slice(r * rows, (r + 1) * rows)
            grad = mg_ref[r, :, ALL + p * 128 : ALL + (p + 1) * 128].astype(F32)
            products = []
            for j in range(KERNEL):
                products.append((grad * up_ref[r, p, 4 + j : 4 + j + rows, :]).astype(BF))
                prp[r, j, 16 : 16 + rows, :] = wide[here, j * 128 : (j + 1) * 128] * grad
            all_products.append(jnp.concatenate(products, axis=1))
            first = 20 - ext
            total = prp[r, 0, first : first + span_rows, :]
            for j in range(1, KERNEL):
                total += prp[r, j, first - j : first - j + span_rows, :]
            if is_long:
                ug_out[r, :, cols] = total[ext : ext + rows]
                send_rims(r, rows + 8, cols, total)
            else:
                ru_out[here, cols] = total.astype(BF)
        kernel_grad += nt(jnp.concatenate(all_products, axis=0), spread[:128, table])
    if is_long:
        zero = jnp.zeros((batch, 8, ALL), BF)
        far_outs[0][:, rows + 8 : rows + 16, ALL:] = zero
        far_outs[-1][:, rows + 8 : rows + 16, ALL:] = zero

    logit_low = (kernel * (kernel_grad - window_sum(kernel * kernel_grad))).astype(BF)
    left[D:, :] = nt(perm[...], logit_low).astype(BF)
    span_grad = nn(logit_low, tn(perm[:TAPS, :], w_span[...]).astype(BF))
    key_conv = flat(kc_ref)
    right[:, ALL:] = (key_conv * qf).astype(BF)
    left[:D, :] = flat(dl_ref).T
    point_low = (span_grad * qf).astype(BF)
    right[:, :ALL] = point_low
    query_total = (dq_scr[...] + span_grad * key_conv).astype(BF)
    depth_grad = nt(point_low, w_point[...])
    for r in range(batch):
        for c in range(D // 128):
            dgp[r, c, 16 : 16 + rows, :] = depth_grad[
                r * rows : (r + 1) * rows, c * 128 : (c + 1) * 128
            ]

    if not is_long:
        ru_out[:, ALL : 2 * ALL] = query_total
        base = nt(ru_out[:, :ALL], w_unfold[...]) + nt(ru_out[:, ALL:], w_project[...])
    else:
        qt_out[...] = query_total.reshape(batch, rows, ALL)
    for c in range(D // 128):
        cols = slice(c * 128, (c + 1) * 128)
        for r in range(batch):
            x_part = xp[r, c] if is_long else x_refs[0][r, :, cols].astype(F32)
            first = 20 - ext
            total = None
            for j in range(KERNEL):
                moved = dgp[r, c, first - j : first - j + span_rows, :]
                term = depth_kernel[j : j + 1, cols].astype(F32) * moved
                total = term if total is None else total + term
                dkg[j * 8 : (j + 1) * 8, cols] += fold8(moved * x_part)
            if is_long:
                tg_out[r, :, cols] = total[ext : ext + rows] + fig_ref[r, :, cols]
                send_rims(r, rows, cols, total)
            else:
                tg_out[r, :, cols] = total + fig_ref[r, :, cols] + base[r * rows : (r + 1) * rows, cols]


def post_call(xs, mg, fig, kept, consts, joint, tokens, batch):
    count, rows = xs[0].shape[0], xs[0].shape[1]
    keys = rows * len(xs)
    total = count * rows
    is_long = len(xs) > 1
    wide = batch * rows
    first = (tokens - total) // wide if is_long else 0
    row_args = [mg, fig, *kept]
    outs = [
        ((D + 128, tokens), BF, pl.BlockSpec((D + 128, wide), lambda i: (0, first + i))),
        ((tokens, 2 * ALL), BF, pl.BlockSpec((wide, 2 * ALL), lambda i: (first + i, 0))),
        ((KERNEL * 8, D), F32, pl.BlockSpec((KERNEL * 8, D), lambda i: (0, 0))),
    ]
    row_out = lambda r, c, t: ((count, r, c), t, per_row(r, c, batch=batch))
    scratch = []
    if is_long:
        outs.append(row_out(rows, D, F32))
        for i in range(1, len(xs)):
            outs.append(row_out(rows + 16 if i in (1, len(xs) - 1) else rows, D, BF))
        outs += [row_out(rows, ALL, BF), row_out(rows, ALL, F32), row_out(rows, D, F32)]
        scratch.append(pltpu.VMEM((batch, D // 128, rows + 16, 128), F32))
    else:
        outs += [
            row_out(rows, D, F32),
            ((tokens, 4 * ALL), BF, pl.BlockSpec((wide, 4 * ALL), lambda i: (first + i, 0))),
        ]
    scratch += [
        pltpu.VMEM((batch, D // 128, rows + 32, 128), F32),
        pltpu.VMEM((batch, KERNEL, rows + 32, 128), F32),
        pltpu.VMEM((wide, ALL), F32),
    ]
    row_args = held(*row_args) if is_long else held(mg, fig) + fetched(*row_args[2:])
    inputs = [*fetched(*xs), *row_args, *fetched(*consts)]
    return pl.pallas_call(
        functools.partial(post_body, len(xs)),
        grid=(count // batch,),
        in_specs=[per_row(rows, D, batch=batch)] * len(xs)
        + [per_row(*a.shape[1:], batch=batch) for a in row_args]
        + [fixed(c) for c in consts]
        + [pl.BlockSpec(memory_space=pl.ANY)] * len(joint),
        out_specs=[s for _, _, s in outs],
        out_shape=[
            (in_vmem if is_long and i in (3, 7, 8, 9) else pltpu.HBM)(s, t)
            for i, (s, t, _) in enumerate(outs)
        ],
        scratch_shapes=scratch,
        input_output_aliases={len(inputs) + i: i for i in range(len(joint))},
        compiler_params=params("post_long" if is_long else "post_short"),
        cost_estimate=pl.CostEstimate(
            flops=total * 10_000_000, bytes_accessed=30_000_000, transcendentals=0
        ),
        name="post_long" if is_long else "post_short",
    )(*inputs, *fetched(*joint))


def end_body(n_x, *refs):
    own, *rest = refs[:n_x]
    qt, ug, tg, w_project, w_unfold, _, out_ref, ru_out = refs[n_x:]
    rows = own.shape[1]
    both = own[0]
    for far in rest:
        both = both + far[0, :rows, :].astype(F32)
    _, _, odd = row_sides()
    unfold = ug[0]
    after = pick(odd, rest[2][0, rows:, :], rest[0][0, rows:, :])
    before = pick(odd, rest[0][0, rows:, :], rest[2][0, rows:, :])
    middle = unfold[8 : rows - 8]
    ru_out[:, :ALL] = jnp.concatenate(
        [unfold[:8] + before[8:, :ALL], middle, unfold[rows - 8 :] + after[8:, :ALL]], axis=0
    ).astype(BF)
    ru_out[:, ALL : 2 * ALL] = qt[0]
    ru_out[:, 2 * ALL :] = both.astype(BF)
    total = nt(ru_out[:, :ALL], w_unfold[...]) + nt(ru_out[:, ALL:], w_project[...]) + tg[0]
    out_ref[0] = total
    out_ref[0, :8, :] = total[:8] + before[:8]
    out_ref[0, rows - 8 :, :] = total[rows - 8 :] + after[:8]


def end_call(own, far, qt, ug, tg, w_project, w_unfold, joint):
    count, rows = own.shape[0], own.shape[1]
    first = (joint.shape[0] - count * rows) // rows
    (own,), (qt, ug, tg) = held(own), held(qt, ug, tg)
    row_args = [own, *fetched(*far), qt, ug, tg]
    return pl.pallas_call(
        functools.partial(end_body, 1 + len(far)),
        grid=(count,),
        in_specs=[per_row(*a.shape[1:]) for a in row_args]
        + [fixed(w_project), fixed(w_unfold), pl.BlockSpec(memory_space=pl.ANY)],
        out_specs=[per_row(rows, D), pl.BlockSpec((rows, 4 * ALL), lambda i: (first + i, 0))],
        out_shape=[
            jax.ShapeDtypeStruct((count, rows, D), F32),
            jax.ShapeDtypeStruct(joint.shape, BF),
        ],
        input_output_aliases={len(row_args) + 2: 1},
        compiler_params=params("end"),
        cost_estimate=pl.CostEstimate(
            flops=count * rows * 2_400_000, bytes_accessed=10_000_000, transcendentals=0
        ),
        name="end_long",
    )(*row_args, *fetched(w_project, w_unfold, joint))


UNIT = 3 * ALL
CHUNK = 4 * UNIT
CHUNKS = 8
LAST = 6 * 512
PACKED = (CHUNKS - 1) * CHUNK + LAST
SPAN_ROW = (CHUNKS - 1) * CHUNK + 2 * UNIT
SMALL_ROW = SPAN_ROW + ALL
SMALL = 48
MESH = pl.DeviceIdType.MESH


CHUNK_PARTS = (
    ((0, 2560, "cxyz"), (2560, 2048, "cyxz")),
    ((4608, 2560, "cxyz"), (7168, 2048, "cyxz")),
    ((9216, 2560, "cxyz"), (11776, 2048, "cyxz")),
    ((13824, 1536, "cxyz"), (15360, 3072, "cyxz")),
    ((18432, 2048, "cyxz"), (20480, 2048, "cxyz"), (22528, 512, "czxy")),
    ((23040, 2048, "cxyz"), (25088, 1024, "czxy"), (26112, 1536, "cyxz")),
    ((27648, 1536, "cxyz"), (29184, 1024, "czyx"), (30208, 2048, "cyxz")),
    ((32256, 1024, "cyxz"), (33280, 1536, "cxyz"), (34816, 512, "cyzx")),
)
PARTS = sum(CHUNK_PARTS, ())


def rows_of(ref, start, count):
    return ref.at[pl.ds(pl.multiple_of(start, 16), count), :]


def add_rows(out, start, sources, count):
    step = next(s for s in (160, 128, 96, 80, 64, 48, 32, 16) if count % s == 0)

    def body(i, carry):
        total = None
        for ref, first in sources:
            value = rows_of(ref, first + i * step, step)[...].astype(F32)
            total = value if total is None else total + value
        rows_of(out, start + i * step, step)[...] = total.astype(BF)
        return carry

    lax.fori_loop(0, count // step, body, 0)


class Exchange:
    def __init__(self, source, res, out, got, sems):
        self.source, self.res, self.out, self.got = source, res, out, got
        self.send_sem, self.recv_sem, self.out_sem = sems
        dp, blk = lax.axis_index("dp"), lax.axis_index("blk")
        core, x, y, z = lax.rem(blk, 2), blk // 2, lax.rem(dp, 2), dp // 2
        self.index = {"c": core, "x": x, "y": y, "z": z}
        self.peers = {
            "c": [(dp, blk + 1 - 2 * core)],
            "x": [(dp, blk + 2 - 4 * x)],
            "y": [(dp + 1 - 2 * y, blk)],
            "z": [(lax.rem(z + i, 4) * 2 + y, blk) for i in (1, 2, 3)],
        }
        self.sizes, self.slots, self.places = [], [], []
        used = 0
        for _, count, order in PARTS:
            sizes, slots, places = [count], [0], []
            for axis in order:
                sizes.append(sizes[-1] // (len(self.peers[axis]) + 1))
                slots.append(slots[-1] + len(self.peers[axis]))
                places.append(used)
                used += sizes[-1] * len(self.peers[axis])
            self.sizes.append(sizes)
            self.slots.append(slots)
            self.places.append(places)

    def greet(self):
        barrier = pltpu.get_barrier_semaphore()
        for devices in self.peers.values():
            for device in devices:
                pl.semaphore_signal(barrier, inc=1, device_id=device, device_id_type=MESH)

    def await_greetings(self):
        pl.semaphore_wait(pltpu.get_barrier_semaphore(), 6)

    def sum_at(self, n, level):
        return (self.source, PARTS[n][0]) if level == 0 else (self.got, self.places[n][level - 1])

    def held(self, n, level):
        row, _, order = PARTS[n]
        for i in range(level):
            row = row + self.index[order[i]] * self.sizes[n][i + 1]
        return row

    def copies(self, n, level, back):
        axis = PARTS[n][2][level]
        size = self.sizes[n][level + 1]
        result = []
        for i, device in enumerate(self.peers[axis]):
            if back:
                source = target = rows_of(self.res, self.held(n, level + 1), size)
            else:
                ref, first = self.sum_at(n, level)
                theirs = lax.rem(self.index[axis] + i + 1, len(self.peers[axis]) + 1)
                source = rows_of(ref, first + theirs * size, size)
                target = rows_of(self.got, self.places[n][level] + i * size, size)
            slot = self.slots[n][level] + i + (6 if back else 0)
            result.append(
                pltpu.make_async_remote_copy(
                    src_ref=source,
                    dst_ref=target,
                    send_sem=self.send_sem.at[n, slot],
                    recv_sem=self.recv_sem.at[n, slot],
                    device_id=device,
                    device_id_type=MESH,
                )
            )
        return result

    def copy_out(self, n):
        row, count, _ = PARTS[n]
        return pltpu.make_async_copy(
            rows_of(self.res, row, count), rows_of(self.out, row, count), self.out_sem.at[n]
        )

    def stage(self, n, s):
        if s:
            for copy in self.copies(n, s - 1 if s <= 4 else 8 - s, s > 4):
                copy.wait_recv()
        if 1 <= s <= 4:
            level = s - 1
            axis = PARTS[n][2][level]
            size = self.sizes[n][s]
            ref, first = self.sum_at(n, level)
            terms = [(ref, first + self.index[axis] * size)]
            terms += [
                (self.got, self.places[n][level] + i * size) for i in range(len(self.peers[axis]))
            ]
            into, start = self.sum_at(n, s) if s < 4 else (self.res, self.held(n, 4))
            add_rows(into, start, terms, size)
        if s < 8:
            for copy in self.copies(n, s if s < 4 else 7 - s, s >= 4):
                copy.start()
        else:
            self.copy_out(n).start()

    def finish(self):
        for n in range(len(PARTS)):
            for level in range(4):
                for back in (False, True):
                    for copy in self.copies(n, level, back):
                        copy.wait_send()
            self.copy_out(n).wait()


def weights_body(remote, ranges, *refs):
    left, right, left_post, right_post, rows_grad, stat_a, stat_b, depth_a, depth_b, out = refs[:10]
    held_left, held_right, sums, part, load_sem = refs[10:15]
    scratch = refs[15:]
    tokens = held_left.shape[2]

    def loads(k):
        slot = k % 2
        if k < 4:
            a, a_rows, b, b_cols = left, (k * ALL, ALL), right, (k * 4 * ALL, 4 * ALL)
        elif k == 4:
            a, a_rows, b, b_cols = left, (2 * D, D), right, (2 * FF, D)
        elif k < 7:
            a, a_rows, b, b_cols = left, (3 * D + (k - 5) * ALL, ALL), rows_grad, (0, 4 * ALL)
        else:
            a, a_rows, b, b_cols = left_post, (0, D + 128), right_post, (0, D)
        copies = []
        for i, (to, start, size) in enumerate(ranges):
            here, there = pl.ds(to, size), pl.ds(start, size)
            copies.append(
                pltpu.make_async_copy(
                    a.at[pl.ds(*a_rows), there],
                    held_left.at[slot, : a_rows[1], here],
                    load_sem.at[slot, 2 * i],
                )
            )
            copies.append(
                pltpu.make_async_copy(
                    b.at[there, pl.ds(*b_cols)],
                    held_right.at[slot, here, : b_cols[1]],
                    load_sem.at[slot, 2 * i + 1],
                )
            )
        return copies

    def compute(k):
        for copy in loads(k):
            copy.wait()
        if k + 1 < CHUNKS:
            for copy in loads(k + 1):
                copy.start()
        slot = k % 2
        by_left = {4: 2, 7: 1}.get(k, 4)

        def unit(j, carry):
            if by_left == 4:
                a, b = 0, j
            elif by_left == 2:
                a, b = j // 2, lax.rem(j, 2)
            else:
                a, b = j, 0
            lhs = held_left[slot, pl.ds(pl.multiple_of(a * ALL, ALL), ALL), :]
            rhs = held_right[slot, :, pl.ds(pl.multiple_of(b * ALL, ALL), ALL)]
            value = nn(lhs, rhs)
            for c in range(3):
                rows_of(part, k * CHUNK + j * UNIT + c * ALL, ALL)[...] = value[
                    :, c * 128 : (c + 1) * 128
                ].astype(BF)
            return carry

        lax.fori_loop(0, 2 if k == 7 else 4, unit, 0)
        ones = jnp.ones((16, tokens), BF)
        if k in (0, 1, 4, 5):
            wide = 2 if k == 4 else 4
            first = {0: 28, 1: 32, 4: 36, 5: 38}[k]
            total = nn(ones, held_right[slot, :, : wide * ALL])
            for j in range(wide):
                sums[first + j : first + j + 1, :] = total[0:1, j * ALL : (j + 1) * ALL]
        if k == 7:
            span = nn(held_left[slot, D:, :], held_right[slot, :, ALL:D])
            for c in range(3):
                part[SPAN_ROW + c * 128 : SPAN_ROW + (c + 1) * 128, :] = span[
                    :, c * 128 : (c + 1) * 128
                ].astype(BF)
            sums[42:43, :] = nn(ones, held_right[slot, :, :ALL])[0:1]
            sums[43:44, :128] = nt(ones, held_left[slot, D:, :])[0:1]
            for first, a, b in ((0, stat_a, stat_b), (10, depth_a, depth_b)):
                for i in range(a.shape[0] // 8):
                    both = jnp.sum(a[i * 8 : i * 8 + 8] + b[i * 8 : i * 8 + 8], axis=0, keepdims=True)
                    sums[first + 2 * i : first + 2 * i + 1, :] = both[:, :ALL]
                    sums[first + 2 * i + 1 : first + 2 * i + 2, :] = both[:, ALL:]
            small = sums[...].astype(BF)
            for c in range(3):
                part[SMALL_ROW + c * SMALL : SMALL_ROW + (c + 1) * SMALL, :] = small[
                    :, c * 128 : (c + 1) * 128
                ]
            part[SMALL_ROW + 3 * SMALL :, :] = jnp.zeros((PACKED - SMALL_ROW - 3 * SMALL, 128), BF)

    for copy in loads(0):
        copy.start()
    sums[...] = jnp.zeros_like(sums)
    if not remote:
        for k in range(CHUNKS):
            compute(k)
        pltpu.sync_copy(part, out)
        return
    res, got, *sems = scratch
    exchange = Exchange(part, res, out, got, sems)
    exchange.greet()
    for t in range(CHUNKS + 8):
        if t < CHUNKS:
            compute(t)
        if t == 0:
            exchange.await_greetings()
        for k in reversed(range(CHUNKS)):
            if 0 <= t - k <= 8:
                first = sum(len(p) for p in CHUNK_PARTS[:k])
                for n in range(first, first + len(CHUNK_PARTS[k])):
                    exchange.stage(n, t - k)
    exchange.finish()


def weights_call(remote, n_short, n_long, big, small):
    tokens = n_short + n_long
    padded = big[1].shape[0]
    n_parts = len(PARTS)
    scratch = [
        pltpu.VMEM((2, D + 128, tokens), BF),
        pltpu.VMEM((2, tokens, 4 * ALL), BF),
        pltpu.VMEM((SMALL, ALL), F32),
        pltpu.VMEM((PACKED, 128), BF),
        pltpu.SemaphoreType.DMA((2, 4)),
    ]
    if remote:
        scratch += [
            pltpu.VMEM((PACKED, 128), BF),
            pltpu.VMEM((PACKED - PACKED // 32, 128), BF),
            pltpu.SemaphoreType.DMA((n_parts, 12)),
            pltpu.SemaphoreType.DMA((n_parts, 12)),
            pltpu.SemaphoreType.DMA((n_parts,)),
        ]
    more = dict(collective_id=0, has_side_effects=True) if remote else {}
    return pl.pallas_call(
        functools.partial(weights_body, remote, ((0, 0, n_short), (n_short, padded - n_long, n_long))),
        in_specs=[pl.BlockSpec(memory_space=pl.ANY)] * len(big)
        + [pl.BlockSpec(memory_space=pltpu.VMEM)] * len(small),
        out_specs=pl.BlockSpec(memory_space=pl.ANY),
        out_shape=pltpu.VMEM((PACKED, 128), BF) if remote else jax.ShapeDtypeStruct((PACKED, 128), BF),
        scratch_shapes=scratch,
        compiler_params=params("weights", **more),
        cost_estimate=pl.CostEstimate(
            flops=2 * 31 * ALL * ALL * tokens, bytes_accessed=50_000_000, transcendentals=0
        ),
        name="weights",
    )(*fetched(*big, *small))


SMALL_OUTS = [
    ("gain_second", 0, D),
    ("shift_second", 2, D),
    ("gain_first", 4, D),
    ("shift_first", 6, D),
    ("bias_outer", 8, D),
    ("bias_inner", 28, FF),
    ("bias_output", 36, D),
    ("bias_unfold", 38, ALL),
    ("bias_query", 39, ALL),
    ("bias_value", 41, ALL),
    ("bias_point", 42, ALL),
    ("bias_span", 43, TAPS),
]


def unpack_body(block, inner, outer, output, unfold, project, point, span, depth, *small):
    step = pl.program_id(0)

    def tile(unit):
        start = unit * UNIT
        return jnp.concatenate(
            [block[start + c * ALL : start + (c + 1) * ALL, :] for c in range(3)], axis=1
        )

    @pl.when(step < 2)
    def _():
        for i in range(4):
            inner[0, :, i * ALL : (i + 1) * ALL] = tile(i).astype(F32)

    @pl.when((step >= 2) & (step < 4))
    def _():
        for i in range(4):
            outer[0, i * ALL : (i + 1) * ALL, :] = tile(i).T.astype(F32)

    @pl.when(step == 4)
    def _():
        for i in range(4):
            a, b = divmod(i, 2)
            output[a * ALL : (a + 1) * ALL, b * ALL : (b + 1) * ALL] = tile(i).astype(F32)

    @pl.when((step == 5) | (step == 6))
    def _():
        unfold[...] = tile(0).astype(F32)
        for i in range(3):
            project[:, i * ALL : (i + 1) * ALL] = tile(i + 1).astype(F32)

    @pl.when(step == 7)
    def _():
        for i in range(2):
            point[i * ALL : (i + 1) * ALL, :] = tile(i).astype(F32)
        tail = 2 * UNIT
        wide = jnp.concatenate(
            [block[tail + c * 128 : tail + (c + 1) * 128, :] for c in range(3)], axis=1
        )
        span[...] = wide[:TAPS].astype(F32)
        tail += ALL
        rows = jnp.concatenate(
            [block[tail + c * SMALL : tail + (c + 1) * SMALL, :] for c in range(3)], axis=1
        ).astype(F32)
        for j in range(KERNEL):
            for half in range(2):
                place = 10 + 2 * j + half
                depth[j : j + 1, half * ALL : (half + 1) * ALL] = rows[place : place + 1]
        for ref, (_, first, size) in zip(small, SMALL_OUTS):
            for i in range(max(1, size // ALL)):
                wide = min(size, ALL)
                ref[i * ALL : i * ALL + wide] = rows[first + i, :wide]


def unpack_call(packed):
    def at(first, count):
        return lambda s: jnp.clip(s - first, 0, count - 1)

    inner_at, outer_at, rows_at = at(0, 2), at(2, 2), at(5, 2)
    whole = lambda *shape: (shape, pl.BlockSpec(shape, lambda s: (0,) * len(shape)))
    specs = [
        ((GROUPS, ALL, 4 * ALL), pl.BlockSpec((1, ALL, 4 * ALL), lambda s: (inner_at(s), 0, 0))),
        ((GROUPS, 4 * ALL, ALL), pl.BlockSpec((1, 4 * ALL, ALL), lambda s: (outer_at(s), 0, 0))),
        whole(D, D),
        ((D, ALL), pl.BlockSpec((ALL, ALL), lambda s: (rows_at(s), 0))),
        ((D, 3 * ALL), pl.BlockSpec((ALL, 3 * ALL), lambda s: (rows_at(s), 0))),
        whole(D, ALL),
        whole(TAPS, ALL),
        whole(KERNEL, D),
    ]
    specs += [whole(size) for _, _, size in SMALL_OUTS]
    return pl.pallas_call(
        unpack_body,
        grid=(CHUNKS,),
        in_specs=[pl.BlockSpec((CHUNK, 128), lambda s: (s, 0))],
        out_specs=[b for _, b in specs],
        out_shape=[jax.ShapeDtypeStruct(s, F32) for s, _ in specs],
        compiler_params=params("unpack"),
        cost_estimate=pl.CostEstimate(flops=0, bytes_accessed=27_000_000, transcendentals=0),
        name="unpack",
    )(packed)


def shards(
    long_input,
    short_input,
    long_cotan,
    short_cotan,
    live_slots,
    w_project,
    bias_query,
    bias_value,
    depth_kernel,
    w_point,
    bias_point,
    w_span,
    bias_span,
    w_unfold,
    bias_unfold,
    w_output,
    bias_output,
    gain_first,
    shift_first,
    w_inner,
    bias_inner,
    w_outer,
    bias_outer,
    gain_second,
    shift_second,
):
    n_blk = lax.axis_size("blk")
    short_x = short_input.reshape(short_input.shape[2:])
    short_cot = short_cotan.reshape(short_cotan.shape[2:])
    perm, spread = (jnp.asarray(t) for t in tap_tables())
    span_t = w_span.T
    pre_consts = (
        bias_query, bias_value, bias_point, bias_span, bias_unfold, depth_kernel,
        w_project, w_point, span_t, w_unfold, spread, perm,
    )
    ffn_consts = (
        bias_output, gain_first, shift_first, bias_outer, gain_second, shift_second, bias_inner,
        w_output, w_inner, w_outer,
    )
    *short_kept, short_mixed, near, far, both = pre_call(
        [short_x], pre_consts, SHORT_BATCH, (long_input,)
    )
    xs = [long_input, near, far, both]
    *long_kept, long_mixed = pre_call(xs, pre_consts, long_input.shape[0])

    n_long, n_short = (a.shape[0] * a.shape[1] for a in (long_input, short_x))
    tokens = (pl.cdiv(n_short, n_long) + 1) * n_long
    as_long = lambda a: a.reshape(-1, FFN_LONG, D)
    l_out, l_fig, l_mg, *joint, l_stat = ffn_call(
        None, 0, *map(as_long, (long_mixed, long_input, long_cotan)), ffn_consts, (), tokens
    )
    l_out, l_fig, l_mg = (a.reshape(long_input.shape) for a in (l_out, l_fig, l_mg))
    s_out, s_fig, s_mg, left, right, s_stat = ffn_call(
        live_slots,
        short_x.shape[1],
        *(a.reshape(-1, FFN_ROWS, D) for a in (short_mixed, short_x, short_cot)),
        ffn_consts,
        joint,
        tokens,
    )
    s_fig, s_mg = s_fig.reshape(short_x.shape), s_mg.reshape(short_x.shape)
    post_consts = (depth_kernel, w_point, span_t, spread, perm)
    l_post = post_call(xs, l_mg, l_fig, long_kept, post_consts, (), tokens, LONG_BATCH)
    (*joint, l_dkg, own), l_rest = l_post[:4], l_post[4:]
    far, (l_qt, l_ug, l_tg) = l_rest[: n_blk - 1], l_rest[n_blk - 1 :]
    far = [
        lax.ppermute(a, "blk", [(i, i ^ k) for i in range(n_blk)])
        for k, a in enumerate(far, 1)
    ]
    left_post, right_post, s_dkg, short_grad, rows_grad = post_call(
        [short_x], s_mg, s_fig, short_kept, post_consts + (w_project, w_unfold), joint, tokens, SHORT_BATCH
    )
    long_grad, rows_grad = end_call(own, far, l_qt, l_ug, l_tg, w_project, w_unfold, rows_grad)

    remote = lax.axis_size("dp") == 8 and n_blk == 4
    packed = weights_call(
        remote, n_short, n_long, (left, right, left_post, right_post, rows_grad), (l_stat, s_stat, l_dkg, s_dkg)
    )
    if not remote:
        packed = lax.psum(packed, ("dp", "blk"))
    if remote:
        packed = pltpu.with_memory_space_constraint(packed, pltpu.VMEM)
    inner, outer, output, unfold, project, point, span, depth, *small = unpack_call(packed)
    named = {name: value for (name, _, _), value in zip(SMALL_OUTS, small)}
    return (
        l_out,
        s_out.reshape(short_input.shape),
        long_grad,
        short_grad.reshape(short_input.shape),
        project,
        named["bias_query"],
        named["bias_value"],
        depth,
        point,
        named["bias_point"],
        span.T,
        named["bias_span"],
        unfold,
        named["bias_unfold"],
        output,
        named["bias_output"],
        named["gain_first"],
        named["shift_first"],
        inner,
        named["bias_inner"],
        outer,
        named["bias_outer"],
        named["gain_second"],
        named["shift_second"],
    )


def solution(mesh):
    rows = P("dp", "blk", None)
    slots = P("dp", "blk", None, None, None)
    in_specs = (rows, slots, rows, slots, P("dp", "blk")) + (P(),) * 20
    out_specs = (rows, slots, rows, slots) + (P(),) * 20
    return jax.shard_map(shards, mesh=mesh, in_specs=in_specs, out_specs=out_specs, check_vma=False)
```

```python
import functools

import jax
import jax.numpy as jnp
import numpy as np
from jax import lax
from jax.experimental import pallas as pl
from jax.experimental.pallas import tpu as pltpu
from jax.sharding import PartitionSpec as P

D = 768
FF = 3072
HEADS = 6
HEAD = 64
KERNEL = 9
GROUPS = 2
ALL = 384
PAIRS = 3
TAPS = HEADS * KERNEL
HALF = KERNEL // 2

F32 = jnp.float32
BF = jnp.bfloat16
ROOT_HALF = 0.7071067811865476
DENSITY = 0.3989422804014327
FFN_ROWS = 256
FFN_LONG = 384
SHORT_BATCH = 2
LONG_BATCH = 1
VMEM = {
    "pre_short": 58,
    "pre_long": 36,
    "ffn_short": 42,
    "ffn_long": 46,
    "post_short": 46,
    "post_long": 34,
    "end": 34,
    "weights": 48,
    "unpack": 48,
}


def nn(a, b):
    return lax.dot_general(a, b, (((1,), (0,)), ((), ())), preferred_element_type=F32)


def nt(a, b):
    return lax.dot_general(a, b, (((1,), (1,)), ((), ())), preferred_element_type=F32)


def tn(a, b):
    return lax.dot_general(a, b, (((0,), (0,)), ((), ())), preferred_element_type=F32)


def tap_tables():
    perm = np.zeros((128, 128), np.float32)
    spread = np.zeros((256, PAIRS * KERNEL * 128), np.float32)
    for h in range(HEADS):
        for j in range(KERNEL):
            lane = j * HEADS + h
            perm[h * KERNEL + j, lane] = 1
            perm[h * KERNEL + j, TAPS + lane] = 1
            start = ((h // 2) * KERNEL + j) * 128 + (h % 2) * HEAD
            spread[lane, start : start + HEAD] = 1
            spread[128 + lane, start : start + HEAD] = 1
    return perm.astype(jnp.bfloat16), spread.astype(jnp.bfloat16)


def window(values, op):
    left = lambda v, n: pltpu.roll(v, 128 - n, 1)
    one = op(values, left(values, 6))
    two = op(one, left(one, 12))
    four = op(two, left(two, 24))
    return op(four, left(values, 48))


def window_sum(values):
    return window(values + pltpu.roll(values, TAPS, 1), jnp.add)


def head_stack(rows, low_half):
    zero = jnp.zeros_like(rows)
    return jnp.concatenate(
        [jnp.where(low_half, rows, zero), jnp.where(low_half, zero, rows)], axis=0
    )


def two_parts(values):
    high = values.astype(BF)
    rest = (values - high.astype(F32)).astype(BF)
    return jnp.concatenate([high, rest], axis=1)


def row_sides():
    place = lax.axis_index("blk")
    count = lax.axis_size("blk")
    return (place > 0).astype(F32), (place < count - 1).astype(F32), lax.rem(place, 2) == 1


def pick(odd, first, second):
    return jnp.where(odd, first.astype(F32), second.astype(F32))


def row_ends(x_refs, r, sides):
    lower, upper, odd = sides
    rows = x_refs[0].shape[1]
    before = pick(odd, x_refs[1][r, rows - 16 :, :], x_refs[3][r, rows - 16 :, :])
    after = pick(odd, x_refs[3][r, :16, :], x_refs[1][r, :16, :])
    return before * lower, after * upper


def fill_ends(xp, x_refs, sides):
    batch, rows = x_refs[0].shape[:2]
    for r in range(batch):
        if sides is not None:
            before, after = row_ends(x_refs, r, sides)
        for c in range(D // 128):
            cols = slice(c * 128, (c + 1) * 128)
            zero = jnp.zeros((8, 128), F32)
            xp[r, c, 0:8, :] = zero if sides is None else before[8:, cols]
            xp[r, c, 8 + rows : 16 + rows, :] = zero if sides is None else after[:8, cols]
            xp[r, c, 8 : 8 + rows, :] = x_refs[0][r, :, cols].astype(F32)


def as_row(ref):
    return ref[...].astype(F32).reshape(1, ref.shape[0])


class Gather:
    def __init__(self, own, outs, send_sem, recv_sem):
        self.own, self.outs, self.send_sem, self.recv_sem = own, outs, send_sem, recv_sem
        self.rows = own.shape[0]
        dp, blk = lax.axis_index("dp"), lax.axis_index("blk")
        core, x = lax.rem(blk, 2), blk // 2
        self.core_peer = (dp, blk + 1 - 2 * core)
        self.x_peer = (dp, blk + 2 - 4 * x)

    def copy(self, i, r):
        source = self.outs[1] if i == 2 else self.own
        return pltpu.make_async_remote_copy(
            src_ref=source.at[r],
            dst_ref=self.outs[i].at[r],
            send_sem=self.send_sem.at[i, r],
            recv_sem=self.recv_sem.at[i, r],
            device_id=self.x_peer if i == 1 else self.core_peer,
            device_id_type=pl.DeviceIdType.MESH,
        )

    def begin(self):
        barrier = pltpu.get_barrier_semaphore()
        for device in (self.core_peer, self.x_peer):
            pl.semaphore_signal(
                barrier, inc=1, device_id=device, device_id_type=pl.DeviceIdType.MESH
            )
        pl.semaphore_wait(barrier, 2)
        for i in (1, 0):
            for r in range(self.rows):
                self.copy(i, r).start()

    def forward(self, r):
        self.copy(1, r).wait_recv()
        self.copy(2, r).start()

    def end(self):
        for r in range(self.rows):
            for i in (0, 2):
                self.copy(i, r).wait_recv()
            for i in range(3):
                self.copy(i, r).wait_send()


def pre_body(n_x, *refs):
    gather = None
    if n_x == 1:
        own, *refs = refs
        gather = Gather(own, refs[22:25], *refs[-2:])
        refs = refs[:22] + refs[25:-2]
    x_refs, refs = refs[:n_x], refs[n_x:]
    bias_query, bias_value, bias_point, bias_span, bias_unfold, depth_kernel = refs[:6]
    w_project, w_point, w_span, w_unfold, spread, perm = refs[6:12]
    q_out, k_out, v_out, p_out, kc_out, ker_out, dl_out, up_out, mix_out = refs[12:21]
    xp, vec = refs[21:]

    @pl.when(pl.program_id(0) == 0)
    def _():
        vec[16:24, :] = jnp.zeros((8, D), F32)
        vec[0:1, :ALL] = as_row(bias_query)
        vec[0:1, ALL:] = as_row(bias_value)
        vec[1:2, :ALL] = as_row(bias_point)
        vec[1:2, ALL:] = as_row(bias_unfold)
        vec[21:22, :TAPS] = as_row(bias_span)
        vec[8:17, :] = depth_kernel[...].astype(F32)
        if gather:
            gather.begin()

    if gather:

        @pl.when(pl.program_id(0) == pl.num_programs(0) - 1)
        def _():
            for r in range(gather.rows - 1):
                gather.forward(r)

    batch, rows = x_refs[0].shape[:2]
    total_rows = batch * rows
    is_long = n_x > 1
    sides = row_sides() if is_long else None
    x = x_refs[0][...].reshape(total_rows, D)
    fill_ends(xp, x_refs, sides)
    bias_query = vec[0:1, :ALL]
    bias_value = vec[0:1, ALL:]
    by_row = lambda v: v.reshape(batch, rows, v.shape[-1])
    if is_long:
        q = (nn(x, w_project[:, :ALL]) + bias_query).astype(BF)
        for i in range(n_x):
            both = nn(x_refs[i][...].reshape(total_rows, D), w_project[:, ALL:])
            k_out[:, i * rows : (i + 1) * rows, :] = by_row(both[:, :ALL].astype(BF))
            v_out[:, i * rows : (i + 1) * rows, :] = by_row((both[:, ALL:] + bias_value).astype(BF))
    else:
        both = nn(x, w_project[...])
        q = (both[:, :ALL] + bias_query).astype(BF)
        k_out[...] = by_row(both[:, ALL : 2 * ALL].astype(BF))
        v_out[...] = by_row((both[:, 2 * ALL :] + bias_value).astype(BF))
    q_out[...] = by_row(q)

    for r in range(batch):
        for c in range(D // 128):
            cols = slice(c * 128, (c + 1) * 128)
            total = vec[8:9, cols] * xp[r, c, 4 : 4 + rows, :]
            for j in range(1, KERNEL):
                total += vec[8 + j : 9 + j, cols] * xp[r, c, 4 + j : 4 + j + rows, :]
            dl_out[r, :, cols] = total.astype(BF)
    key_conv = nn(dl_out[...].reshape(total_rows, D), w_point[...]) + vec[1:2, :ALL]
    kc_out[...] = by_row(key_conv)
    span = (key_conv * q.astype(F32)).astype(BF)
    span_weights = tn(w_span[...], perm[:TAPS, :]).astype(BF)
    span_bias = nn(vec[16:24, :128].astype(BF), perm[...])[5:6]
    logits = nn(span, span_weights) + span_bias
    lane = lax.broadcasted_iota(jnp.int32, (1, 128), 1)
    raised = jnp.where(lane < TAPS, jnp.exp(logits - window(logits, jnp.maximum)), 0.0)
    kernel = jnp.where(lane < TAPS, raised / window_sum(raised), 0.0)
    ker_out[...] = by_row(kernel)

    bias_unfold = vec[1:2, ALL:]
    unfold_rows = nn(x, w_unfold[...]) + bias_unfold
    for r in range(batch):
        if is_long:
            lower, upper, _ = sides
            ends = jnp.concatenate(row_ends(x_refs, r, sides), axis=0).astype(BF)
            unfold_ends = nn(ends, w_unfold[...]) + bias_unfold
        for c in range(PAIRS):
            cols = slice(c * 128, (c + 1) * 128)
            up_out[r, c, 8 : 8 + rows, :] = unfold_rows[r * rows : (r + 1) * rows, cols]
            if is_long:
                up_out[r, c, 0:8, :] = unfold_ends[8:16, cols] * lower
                up_out[r, c, 8 + rows : 16 + rows, :] = unfold_ends[16:24, cols] * upper
            else:
                zero = jnp.zeros((8, 128), F32)
                up_out[r, c, 0:8, :] = zero
                up_out[r, c, 8 + rows : 16 + rows, :] = zero

    if gather:

        @pl.when(pl.program_id(0) == pl.num_programs(0) - 1)
        def _():
            gather.forward(gather.rows - 1)

    low_half = lane < HEAD
    parts = two_parts(kernel)
    scaled = q * jnp.asarray(HEAD ** (-0.5), BF)
    keys = k_out.shape[1]
    for p in range(PAIRS):
        cols = slice(p * 128, (p + 1) * 128)
        wide = nn(parts, spread[:, p * KERNEL * 128 : (p + 1) * KERNEL * 128])
        for r in range(batch):
            here = slice(r * rows, (r + 1) * rows)
            total = wide[here, :128] * up_out[r, p, 4 : 4 + rows, :]
            for j in range(1, KERNEL):
                total += wide[here, j * 128 : (j + 1) * 128] * up_out[r, p, 4 + j : 4 + j + rows, :]
            mix_out[r, :, ALL + p * 128 : ALL + (p + 1) * 128] = total.astype(BF)

            scores = nt(head_stack(k_out[r, :, cols], low_half), scaled[here, cols])
            for half in range(2):
                part = scores[half * keys : (half + 1) * keys]
                top = jnp.max(part, axis=0, keepdims=True)
                grown = jnp.exp(part - top)
                share = 1.0 / jnp.sum(grown, axis=0, keepdims=True)
                p_out[r, p, half * keys : (half + 1) * keys, :] = (grown * share).astype(BF)
            context = tn(head_stack(v_out[r, :, cols], low_half), p_out[r, p])
            mix_out[r, :, cols] = context.astype(BF).T

    if gather:

        @pl.when(pl.program_id(0) == pl.num_programs(0) - 1)
        def _():
            gather.end()


def fixed(array):
    zeros = (0,) * array.ndim
    return pl.BlockSpec(array.shape, lambda *_: zeros, pipeline_mode=pl.Buffered(1))


def per_row(*shape, batch=1):
    zeros = (0,) * len(shape)
    return pl.BlockSpec((batch, *shape), lambda i: (i, *zeros))


def in_vmem(shape, dtype):
    return pltpu.VMEM(shape, dtype)


def held(*arrays):
    return [pltpu.with_memory_space_constraint(a, pltpu.VMEM) for a in arrays]


def fetched(*arrays):
    return [pltpu.with_memory_space_constraint(a, pltpu.HBM) for a in arrays]


def params(name, **more):
    return pltpu.CompilerParams(vmem_limit_bytes=VMEM[name] * 1024 * 1024, **more)


def pre_call(xs, consts, batch, gathered=()):
    anywhere = pl.BlockSpec(memory_space=pl.ANY)
    count, rows = xs[0].shape[0], xs[0].shape[1]
    keys = rows * len(xs)
    shapes = [
        ((rows, ALL), BF),
        ((keys, ALL), BF),
        ((keys, ALL), BF),
        ((PAIRS, 2 * keys, rows), BF),
        ((rows, ALL), F32),
        ((rows, 128), F32),
        ((rows, D), BF),
        ((PAIRS, rows + 16, 128), F32),
        ((rows, D), BF),
    ]
    return pl.pallas_call(
        functools.partial(pre_body, len(xs)),
        grid=(count // batch,),
        in_specs=[anywhere] * len(gathered)
        + [per_row(rows, D, batch=batch)] * len(xs) + [fixed(c) for c in consts],
        out_specs=[per_row(*s, batch=batch) for s, _ in shapes] + [anywhere] * (3 * len(gathered)),
        out_shape=[
            (in_vmem if not gathered or i == 8 else pltpu.HBM)((count, *s), t)
            for i, (s, t) in enumerate(shapes)
        ]
        + [in_vmem(g.shape, g.dtype) for g in gathered] * 3,
        scratch_shapes=[pltpu.VMEM((batch, D // 128, rows + 16, 128), F32), pltpu.VMEM((24, D), F32)]
        + [pltpu.SemaphoreType.DMA((3, g.shape[0])) for g in gathered for _ in range(2)],
        compiler_params=params("pre_short", collective_id=1, has_side_effects=True)
        if gathered
        else params("pre_long"),
        cost_estimate=pl.CostEstimate(
            flops=count * rows * 6_000_000, bytes_accessed=20_000_000, transcendentals=1_000_000
        ),
        name="pre_long" if len(xs) > 1 else "pre_short",
    )(*fetched(*gathered, xs[0]), *held(*xs[1:]), *fetched(*consts))


def norm_stats(z):
    centre = z - jnp.mean(z, axis=-1, keepdims=True)
    inverse = lax.rsqrt(jnp.mean(centre * centre, axis=-1, keepdims=True) + 1e-12)
    return centre * inverse, inverse


def norm_back(upstream, normed, inverse, gain):
    scaled = upstream * gain
    plain = jnp.mean(scaled, axis=-1, keepdims=True)
    cross = jnp.mean(scaled * normed, axis=-1, keepdims=True)
    return inverse * (scaled - plain - normed * cross)


def fold8(values):
    return jnp.sum(values.reshape(values.shape[0] // 8, 8, values.shape[1]), axis=0)


def gelu_pair(v):
    cdf = 0.5 * (1.0 + lax.erf(v * ROOT_HALF))
    return v * cdf, cdf + v * jnp.exp(-0.5 * (v * v)) * DENSITY


def ffn_body(slot_rows, *refs):
    masked = slot_rows > 0
    if masked:
        live_ref, *refs = refs
    mix_ref, x_ref, cot_ref = refs[:3]
    vectors, (w_output, w_inner, w_outer) = refs[3:10], refs[10:13]
    out_ref, fig_ref, mg_ref, left, right, stat, slope, vec = refs[-8:]
    inl_ref, act_ref = right.at[:, :FF], right.at[:, FF : 2 * FF]
    step = pl.program_id(0)
    rows = x_ref.shape[1]

    @pl.when(step == 0)
    def _():
        stat[...] = jnp.zeros_like(stat)
        for i, ref in enumerate(vectors[:-1]):
            vec[2 + i : 3 + i, :] = as_row(ref)
        inner_row = as_row(vectors[-1])
        for i in range(FF // D):
            vec[8 + i : 9 + i, :] = inner_row[:, i * D : (i + 1) * D]

    x = x_ref[0]
    mixed = mix_ref[0]
    left[2 * D : 3 * D, :] = mixed.T
    left[3 * D :, :] = x.T
    first_normed, first_inverse = norm_stats(nn(mixed, w_output[...]) + vec[2:3, :] + x.astype(F32))
    first_norm = first_normed * vec[3:4, :] + vec[4:5, :]
    first_low = first_norm.astype(BF)
    left[:D, :] = first_low.T
    outer = []
    for g in range(GROUPS):
        for c in range(2):
            k = g * 2 + c
            inner = nn(first_low[:, g * ALL : (g + 1) * ALL], w_inner[g, :, c * D : (c + 1) * D])
            for r in range(0, rows, 16):
                act, slo = gelu_pair(inner[r : r + 16] + vec[8 + k : 9 + k, :])
                act_ref[r : r + 16, k * D : (k + 1) * D] = act.astype(BF)
                slope[r : r + 16, k * D : (k + 1) * D] = slo
        outer.append(nn(act_ref[:, g * 2 * D : (g + 1) * 2 * D], w_outer[g]))
    second_normed, second_inverse = norm_stats(
        jnp.concatenate(outer, axis=1) + vec[5:6, :] + first_norm
    )
    gain_second = vec[6:7, :]
    out_ref[0] = (second_normed * gain_second + vec[7:8, :]).astype(BF)
    seed = cot_ref[0].astype(F32)
    if masked:
        token = step * rows + lax.broadcasted_iota(jnp.int32, (rows, 1), 0)
        seed = jnp.where(token < live_ref[0, 0] * slot_rows, seed, 0.0)
    stat[0:8, :] += fold8(seed * second_normed)
    stat[8:16, :] += fold8(seed)
    second_grad = norm_back(seed, second_normed, second_inverse, gain_second)
    outer_low = second_grad.astype(BF)
    left[D : 2 * D, :] = outer_low.T
    stat[32:40, :] += fold8(outer_low.astype(F32))
    first_grad = []
    for g in range(GROUPS):
        for c in range(2):
            k = g * 2 + c
            back = nt(outer_low[:, g * ALL : (g + 1) * ALL], w_outer[g, c * D : (c + 1) * D, :])
            inl_ref[:, k * D : (k + 1) * D] = (back * slope[:, k * D : (k + 1) * D]).astype(BF)
        first_grad.append(nt(inl_ref[:, g * 2 * D : (g + 1) * 2 * D], w_inner[g]))
    first_grad = second_grad + jnp.concatenate(first_grad, axis=1)
    stat[16:24, :] += fold8(first_grad * first_normed)
    stat[24:32, :] += fold8(first_grad)
    first_in_grad = norm_back(first_grad, first_normed, first_inverse, vec[3:4, :])
    fig_ref[0] = first_in_grad
    attended_low = first_in_grad.astype(BF)
    right[:, 2 * FF :] = attended_low
    mg_ref[0] = nt(attended_low, w_output[...]).astype(BF)


def ffn_call(live, slot_rows, mixed, x, cotan, consts, joint, tokens):
    count, rows = x.shape[0], x.shape[1]
    total = count * rows
    masked = live is not None
    first = 0 if masked else (tokens - total) // rows
    n_in = (4 if masked else 3) + len(consts)
    out_shapes = [
        ((count, rows, D), BF, per_row(rows, D)),
        ((count, rows, D), F32, per_row(rows, D)),
        ((count, rows, D), BF, per_row(rows, D)),
        ((4 * D, tokens), BF, pl.BlockSpec((4 * D, rows), lambda i: (0, first + i))),
        ((tokens, 2 * FF + D), BF, pl.BlockSpec((rows, 2 * FF + D), lambda i: (first + i, 0))),
        ((40, D), F32, pl.BlockSpec((40, D), lambda i: (0, 0))),
    ]
    head = [live] if masked else []
    head_specs = [pl.BlockSpec(memory_space=pltpu.SMEM)] if masked else []
    return pl.pallas_call(
        functools.partial(ffn_body, slot_rows if masked else 0),
        grid=(count,),
        in_specs=head_specs
        + [per_row(rows, D)] * 3
        + [fixed(c) for c in consts]
        + [pl.BlockSpec(memory_space=pl.ANY)] * len(joint),
        out_specs=[s for _, _, s in out_shapes],
        out_shape=[
            (in_vmem if i in (1, 2) else pltpu.HBM)(s, t)
            for i, (s, t, _) in enumerate(out_shapes)
        ],
        scratch_shapes=[pltpu.VMEM((rows, FF), F32), pltpu.VMEM((16, D), F32)],
        input_output_aliases={n_in: 3, n_in + 1: 4} if masked else {},
        compiler_params=params("ffn_short" if masked else "ffn_long"),
        cost_estimate=pl.CostEstimate(
            flops=total * 12_000_000, bytes_accessed=30_000_000, transcendentals=total * FF
        ),
        name="ffn_short" if masked else "ffn_long",
    )(*head, *held(mixed), *fetched(x, cotan, *consts, *joint))


def post_body(n_x, *refs):
    is_long = n_x > 1
    x_refs = refs[:n_x]
    refs = refs[n_x:]
    (mg_ref, fig_ref, q_ref, k_ref, v_ref, p_ref, kc_ref, ker_ref, dl_ref, up_ref) = refs[:10]
    (depth_kernel, w_point, w_span, spread, perm) = refs[10:15]
    refs = refs[15:]
    if not is_long:
        (w_project, w_unfold), refs = refs[:2], refs[4:]
    (left, right, dkg), refs = refs[:3], refs[3:]
    if is_long:
        own_out, *far_outs = refs[:n_x]
        qt_out, ug_out, tg_out = refs[n_x : n_x + 3]
        xp, dgp, prp, dq_scr = refs[n_x + 3 :]
    else:
        tg_out, ru_out, dgp, prp, dq_scr = refs
    step = pl.program_id(0)
    batch, rows = x_refs[0].shape[:2]
    total_rows = batch * rows
    keys = k_ref.shape[1]
    ext = 8 if is_long else 0
    flat = lambda ref: ref[...].reshape(total_rows, ref.shape[-1])

    @pl.when(step == 0)
    def _():
        dkg[...] = jnp.zeros_like(dkg)
        dgp[...] = jnp.zeros_like(dgp)
        prp[...] = jnp.zeros_like(prp)

    if is_long:
        sides = lower, upper, odd = row_sides()
        fill_ends(xp, x_refs, sides)

        def send_rims(r, place, cols, total):
            before, after = total[:ext] * lower, total[ext + rows :] * upper
            far_outs[0][r, place : place + 8, cols] = pick(odd, before, after).astype(BF)
            far_outs[2][r, place : place + 8, cols] = pick(odd, after, before).astype(BF)


    q = flat(q_ref)
    qf = q.astype(F32)
    scaled = q * jnp.asarray(HEAD ** (-0.5), BF)
    low_half = lax.broadcasted_iota(jnp.int32, (1, 128), 1) < HEAD
    for p in range(PAIRS):
        cols = slice(p * 128, (p + 1) * 128)
        for r in range(batch):
            here = slice(r * rows, (r + 1) * rows)
            grad = mg_ref[r, :, cols]
            weight_grad = nt(head_stack(v_ref[r, :, cols], low_half), grad)
            low = []
            for half in range(2):
                part = slice(half * keys, (half + 1) * keys)
                probs = p_ref[r, p, part, :].astype(F32)
                inner = jnp.sum(probs * weight_grad[part], axis=0, keepdims=True)
                low.append((probs * (weight_grad[part] - inner)).astype(BF))
            score_low = jnp.concatenate(low, axis=0)
            value_grad = nn(p_ref[r, p], grad)
            value_grad = jnp.where(low_half, value_grad[:keys], value_grad[keys:])
            key_grad = nn(score_low, scaled[here, cols])
            key_grad = jnp.where(low_half, key_grad[:keys], key_grad[keys:])
            query_grad = tn(head_stack(k_ref[r, :, cols], low_half), score_low) * HEAD ** (-0.5)
            dq_scr[here, cols] = query_grad.T
            v_cols = slice(ALL + p * 128, ALL + (p + 1) * 128)
            if is_long:
                own_out[r, :, cols] = key_grad[:rows]
                own_out[r, :, v_cols] = value_grad[:rows]
                for i in range(1, n_x):
                    block = slice(i * rows, (i + 1) * rows)
                    far_outs[i - 1][r, :rows, cols] = key_grad[block].astype(BF)
                    far_outs[i - 1][r, :rows, v_cols] = value_grad[block].astype(BF)
            else:
                ru_out[here, 2 * ALL + p * 128 : 2 * ALL + (p + 1) * 128] = key_grad.astype(BF)
                ru_out[here, 3 * ALL + p * 128 : 3 * ALL + (p + 1) * 128] = value_grad.astype(BF)

    kernel = flat(ker_ref)
    parts = two_parts(kernel)
    kernel_grad = jnp.zeros((total_rows, 128), F32)
    span_rows = rows + 2 * ext
    for p in range(PAIRS):
        cols = slice(p * 128, (p + 1) * 128)
        table = slice(p * KERNEL * 128, (p + 1) * KERNEL * 128)
        wide = nn(parts, spread[:, table])
        all_products = []
        for r in range(batch):
            here = slice(r * rows, (r + 1) * rows)
            grad = mg_ref[r, :, ALL + p * 128 : ALL + (p + 1) * 128].astype(F32)
            products = []
            for j in range(KERNEL):
                products.append((grad * up_ref[r, p, 4 + j : 4 + j + rows, :]).astype(BF))
                prp[r, j, 16 : 16 + rows, :] = wide[here, j * 128 : (j + 1) * 128] * grad
            all_products.append(jnp.concatenate(products, axis=1))
            first = 20 - ext
            total = prp[r, 0, first : first + span_rows, :]
            for j in range(1, KERNEL):
                total += prp[r, j, first - j : first - j + span_rows, :]
            if is_long:
                ug_out[r, :, cols] = total[ext : ext + rows]
                send_rims(r, rows + 8, cols, total)
            else:
                ru_out[here, cols] = total.astype(BF)
        kernel_grad += nt(jnp.concatenate(all_products, axis=0), spread[:128, table])
    if is_long:
        zero = jnp.zeros((batch, 8, ALL), BF)
        far_outs[0][:, rows + 8 : rows + 16, ALL:] = zero
        far_outs[-1][:, rows + 8 : rows + 16, ALL:] = zero

    logit_low = (kernel * (kernel_grad - window_sum(kernel * kernel_grad))).astype(BF)
    left[D:, :] = nt(perm[...], logit_low).astype(BF)
    span_grad = nn(logit_low, tn(perm[:TAPS, :], w_span[...]).astype(BF))
    key_conv = flat(kc_ref)
    right[:, ALL:] = (key_conv * qf).astype(BF)
    left[:D, :] = flat(dl_ref).T
    point_low = (span_grad * qf).astype(BF)
    right[:, :ALL] = point_low
    query_total = (dq_scr[...] + span_grad * key_conv).astype(BF)
    depth_grad = nt(point_low, w_point[...])
    for r in range(batch):
        for c in range(D // 128):
            dgp[r, c, 16 : 16 + rows, :] = depth_grad[
                r * rows : (r + 1) * rows, c * 128 : (c + 1) * 128
            ]

    if not is_long:
        ru_out[:, ALL : 2 * ALL] = query_total
        base = nt(ru_out[:, :ALL], w_unfold[...]) + nt(ru_out[:, ALL:], w_project[...])
    else:
        qt_out[...] = query_total.reshape(batch, rows, ALL)
    for c in range(D // 128):
        cols = slice(c * 128, (c + 1) * 128)
        for r in range(batch):
            x_part = xp[r, c] if is_long else x_refs[0][r, :, cols].astype(F32)
            first = 20 - ext
            total = None
            for j in range(KERNEL):
                moved = dgp[r, c, first - j : first - j + span_rows, :]
                term = depth_kernel[j : j + 1, cols].astype(F32) * moved
                total = term if total is None else total + term
                dkg[j * 8 : (j + 1) * 8, cols] += fold8(moved * x_part)
            if is_long:
                tg_out[r, :, cols] = total[ext : ext + rows] + fig_ref[r, :, cols]
                send_rims(r, rows, cols, total)
            else:
                tg_out[r, :, cols] = total + fig_ref[r, :, cols] + base[r * rows : (r + 1) * rows, cols]


def post_call(xs, mg, fig, kept, consts, joint, tokens, batch):
    count, rows = xs[0].shape[0], xs[0].shape[1]
    keys = rows * len(xs)
    total = count * rows
    is_long = len(xs) > 1
    wide = batch * rows
    first = (tokens - total) // wide if is_long else 0
    row_args = [mg, fig, *kept]
    outs = [
        ((D + 128, tokens), BF, pl.BlockSpec((D + 128, wide), lambda i: (0, first + i))),
        ((tokens, 2 * ALL), BF, pl.BlockSpec((wide, 2 * ALL), lambda i: (first + i, 0))),
        ((KERNEL * 8, D), F32, pl.BlockSpec((KERNEL * 8, D), lambda i: (0, 0))),
    ]
    row_out = lambda r, c, t: ((count, r, c), t, per_row(r, c, batch=batch))
    scratch = []
    if is_long:
        outs.append(row_out(rows, D, F32))
        for i in range(1, len(xs)):
            outs.append(row_out(rows + 16 if i in (1, len(xs) - 1) else rows, D, BF))
        outs += [row_out(rows, ALL, BF), row_out(rows, ALL, F32), row_out(rows, D, F32)]
        scratch.append(pltpu.VMEM((batch, D // 128, rows + 16, 128), F32))
    else:
        outs += [
            row_out(rows, D, F32),
            ((tokens, 4 * ALL), BF, pl.BlockSpec((wide, 4 * ALL), lambda i: (first + i, 0))),
        ]
    scratch += [
        pltpu.VMEM((batch, D // 128, rows + 32, 128), F32),
        pltpu.VMEM((batch, KERNEL, rows + 32, 128), F32),
        pltpu.VMEM((wide, ALL), F32),
    ]
    row_args = held(*row_args) if is_long else held(mg, fig) + fetched(*row_args[2:])
    inputs = [*fetched(xs[0]), *held(*xs[1:]), *row_args, *fetched(*consts)]
    return pl.pallas_call(
        functools.partial(post_body, len(xs)),
        grid=(count // batch,),
        in_specs=[per_row(rows, D, batch=batch)] * len(xs)
        + [per_row(*a.shape[1:], batch=batch) for a in row_args]
        + [fixed(c) for c in consts]
        + [pl.BlockSpec(memory_space=pl.ANY)] * len(joint),
        out_specs=[s for _, _, s in outs],
        out_shape=[
            (in_vmem if is_long and i in (3, 7, 8, 9) else pltpu.HBM)(s, t)
            for i, (s, t, _) in enumerate(outs)
        ],
        scratch_shapes=scratch,
        input_output_aliases={len(inputs) + i: i for i in range(len(joint))},
        compiler_params=params("post_long" if is_long else "post_short"),
        cost_estimate=pl.CostEstimate(
            flops=total * 10_000_000, bytes_accessed=30_000_000, transcendentals=0
        ),
        name="post_long" if is_long else "post_short",
    )(*inputs, *fetched(*joint))


def end_body(n_x, *refs):
    own, *rest = refs[:n_x]
    qt, ug, tg, w_project, w_unfold, _, out_ref, ru_out = refs[n_x:]
    rows = own.shape[1]
    both = own[0]
    for far in rest:
        both = both + far[0, :rows, :].astype(F32)
    _, _, odd = row_sides()
    unfold = ug[0]
    after = pick(odd, rest[2][0, rows:, :], rest[0][0, rows:, :])
    before = pick(odd, rest[0][0, rows:, :], rest[2][0, rows:, :])
    middle = unfold[8 : rows - 8]
    ru_out[:, :ALL] = jnp.concatenate(
        [unfold[:8] + before[8:, :ALL], middle, unfold[rows - 8 :] + after[8:, :ALL]], axis=0
    ).astype(BF)
    ru_out[:, ALL : 2 * ALL] = qt[0]
    ru_out[:, 2 * ALL :] = both.astype(BF)
    total = nt(ru_out[:, :ALL], w_unfold[...]) + nt(ru_out[:, ALL:], w_project[...]) + tg[0]
    out_ref[0] = total
    out_ref[0, :8, :] = total[:8] + before[:8]
    out_ref[0, rows - 8 :, :] = total[rows - 8 :] + after[:8]


def end_call(own, far, qt, ug, tg, w_project, w_unfold, joint):
    count, rows = own.shape[0], own.shape[1]
    first = (joint.shape[0] - count * rows) // rows
    (own,), (qt, ug, tg) = held(own), held(qt, ug, tg)
    row_args = [own, *held(*far), qt, ug, tg]
    return pl.pallas_call(
        functools.partial(end_body, 1 + len(far)),
        grid=(count,),
        in_specs=[per_row(*a.shape[1:]) for a in row_args]
        + [fixed(w_project), fixed(w_unfold), pl.BlockSpec(memory_space=pl.ANY)],
        out_specs=[per_row(rows, D), pl.BlockSpec((rows, 4 * ALL), lambda i: (first + i, 0))],
        out_shape=[
            jax.ShapeDtypeStruct((count, rows, D), F32),
            jax.ShapeDtypeStruct(joint.shape, BF),
        ],
        input_output_aliases={len(row_args) + 2: 1},
        compiler_params=params("end"),
        cost_estimate=pl.CostEstimate(
            flops=count * rows * 2_400_000, bytes_accessed=10_000_000, transcendentals=0
        ),
        name="end_long",
    )(*row_args, *fetched(w_project, w_unfold, joint))


UNIT = 3 * ALL
CHUNK = 4 * UNIT
CHUNKS = 8
LAST = 6 * 512
PACKED = (CHUNKS - 1) * CHUNK + LAST
SPAN_ROW = (CHUNKS - 1) * CHUNK + 2 * UNIT
SMALL_ROW = SPAN_ROW + ALL
SMALL = 48
MESH = pl.DeviceIdType.MESH


CHUNK_PARTS = (
    ((0, 2048, "cyxz"), (2048, 2560, "cxyz")),
    ((4608, 2560, "cxyz"), (7168, 2048, "cyxz")),
    ((9216, 2560, "cxyz"), (11776, 2048, "cyxz")),
    ((13824, 1536, "cxyz"), (15360, 3072, "cyxz")),
    ((18432, 2048, "cyxz"), (20480, 2048, "cxyz"), (22528, 512, "czxy")),
    ((23040, 2048, "cxyz"), (25088, 1024, "czxy"), (26112, 1536, "cyxz")),
    ((27648, 1536, "cxyz"), (29184, 1024, "czyx"), (30208, 2048, "cyxz")),
    ((32256, 1024, "cyxz"), (33280, 1536, "cxyz"), (34816, 512, "cyzx")),
)
PARTS = sum(CHUNK_PARTS, ())


def rows_of(ref, start, count):
    return ref.at[pl.ds(pl.multiple_of(start, 16), count), :]


def add_rows(out, start, sources, count):
    step = next(s for s in (160, 128, 96, 80, 64, 48, 32, 16) if count % s == 0)

    def body(i, carry):
        total = None
        for ref, first in sources:
            value = rows_of(ref, first + i * step, step)[...].astype(F32)
            total = value if total is None else total + value
        rows_of(out, start + i * step, step)[...] = total.astype(BF)
        return carry

    lax.fori_loop(0, count // step, body, 0)


class Exchange:
    def __init__(self, source, res, out, got, sems):
        self.source, self.res, self.out, self.got = source, res, out, got
        self.send_sem, self.recv_sem, self.out_sem = sems
        dp, blk = lax.axis_index("dp"), lax.axis_index("blk")
        core, x, y, z = lax.rem(blk, 2), blk // 2, lax.rem(dp, 2), dp // 2
        self.index = {"c": core, "x": x, "y": y, "z": z}
        self.peers = {
            "c": [(dp, blk + 1 - 2 * core)],
            "x": [(dp, blk + 2 - 4 * x)],
            "y": [(dp + 1 - 2 * y, blk)],
            "z": [(lax.rem(z + i, 4) * 2 + y, blk) for i in (1, 2, 3)],
        }
        self.sizes, self.slots, self.places = [], [], []
        used = 0
        for _, count, order in PARTS:
            sizes, slots, places = [count], [0], []
            for axis in order:
                sizes.append(sizes[-1] // (len(self.peers[axis]) + 1))
                slots.append(slots[-1] + len(self.peers[axis]))
                places.append(used)
                used += sizes[-1] * len(self.peers[axis])
            self.sizes.append(sizes)
            self.slots.append(slots)
            self.places.append(places)

    def greet(self):
        barrier = pltpu.get_barrier_semaphore()
        for devices in self.peers.values():
            for device in devices:
                pl.semaphore_signal(barrier, inc=1, device_id=device, device_id_type=MESH)

    def await_greetings(self):
        pl.semaphore_wait(pltpu.get_barrier_semaphore(), 6)

    def sum_at(self, n, level):
        return (self.source, PARTS[n][0]) if level == 0 else (self.got, self.places[n][level - 1])

    def held(self, n, level):
        row, _, order = PARTS[n]
        for i in range(level):
            row = row + self.index[order[i]] * self.sizes[n][i + 1]
        return row

    def copies(self, n, level, back):
        axis = PARTS[n][2][level]
        size = self.sizes[n][level + 1]
        result = []
        for i, device in enumerate(self.peers[axis]):
            if back:
                source = target = rows_of(self.res, self.held(n, level + 1), size)
            else:
                ref, first = self.sum_at(n, level)
                theirs = lax.rem(self.index[axis] + i + 1, len(self.peers[axis]) + 1)
                source = rows_of(ref, first + theirs * size, size)
                target = rows_of(self.got, self.places[n][level] + i * size, size)
            slot = self.slots[n][level] + i + (6 if back else 0)
            result.append(
                pltpu.make_async_remote_copy(
                    src_ref=source,
                    dst_ref=target,
                    send_sem=self.send_sem.at[n, slot],
                    recv_sem=self.recv_sem.at[n, slot],
                    device_id=device,
                    device_id_type=MESH,
                )
            )
        return result

    def copy_out(self, n):
        row, count, _ = PARTS[n]
        return pltpu.make_async_copy(
            rows_of(self.res, row, count), rows_of(self.out, row, count), self.out_sem.at[n]
        )

    def stage(self, n, s):
        if s:
            for copy in self.copies(n, s - 1 if s <= 4 else 8 - s, s > 4):
                copy.wait_recv()
        if 1 <= s <= 4:
            level = s - 1
            axis = PARTS[n][2][level]
            size = self.sizes[n][s]
            ref, first = self.sum_at(n, level)
            terms = [(ref, first + self.index[axis] * size)]
            terms += [
                (self.got, self.places[n][level] + i * size) for i in range(len(self.peers[axis]))
            ]
            into, start = self.sum_at(n, s) if s < 4 else (self.res, self.held(n, 4))
            add_rows(into, start, terms, size)
        if s < 8:
            for copy in self.copies(n, s if s < 4 else 7 - s, s >= 4):
                copy.start()
        else:
            self.copy_out(n).start()

    def finish(self):
        for n in range(len(PARTS)):
            for level in range(4):
                for back in (False, True):
                    for copy in self.copies(n, level, back):
                        copy.wait_send()
            self.copy_out(n).wait()


def weights_body(remote, ranges, *refs):
    left, right, left_post, right_post, rows_grad, stat_a, stat_b, depth_a, depth_b, out = refs[:10]
    held_left, held_right, sums, part, load_sem = refs[10:15]
    scratch = refs[15:]
    tokens = held_left.shape[2]

    def loads(k):
        slot = k % 2
        if k < 4:
            a, a_rows, b, b_cols = left, (k * ALL, ALL), right, (k * 4 * ALL, 4 * ALL)
        elif k == 4:
            a, a_rows, b, b_cols = left, (2 * D, D), right, (2 * FF, D)
        elif k < 7:
            a, a_rows, b, b_cols = left, (3 * D + (k - 5) * ALL, ALL), rows_grad, (0, 4 * ALL)
        else:
            a, a_rows, b, b_cols = left_post, (0, D + 128), right_post, (0, D)
        copies = []
        halves = 2 if k == 0 else 1
        cols = b_cols[1] // halves
        for half in range(halves):
            for i, (to, start, size) in enumerate(ranges):
                here, there = pl.ds(to, size), pl.ds(start, size)
                if half == 0:
                    copies.append(
                        pltpu.make_async_copy(
                            a.at[pl.ds(*a_rows), there],
                            held_left.at[slot, : a_rows[1], here],
                            load_sem.at[slot, i],
                        )
                    )
                copies.append(
                    pltpu.make_async_copy(
                        b.at[there, pl.ds(b_cols[0] + half * cols, cols)],
                        held_right.at[slot, here, half * cols : (half + 1) * cols],
                        load_sem.at[slot, 2 + 2 * half + i],
                    )
                )
        return copies

    def compute(k):
        coming = loads(k)
        for copy in coming[:4]:
            copy.wait()
        if k + 1 < CHUNKS:
            for copy in loads(k + 1):
                copy.start()
        slot = k % 2
        by_left = {4: 2, 7: 1}.get(k, 4)

        def unit(j, carry):
            if by_left == 4:
                a, b = 0, j
            elif by_left == 2:
                a, b = j // 2, lax.rem(j, 2)
            else:
                a, b = j, 0
            lhs = held_left[slot, pl.ds(pl.multiple_of(a * ALL, ALL), ALL), :]
            rhs = held_right[slot, :, pl.ds(pl.multiple_of(b * ALL, ALL), ALL)]
            value = nn(lhs, rhs)
            for c in range(3):
                rows_of(part, k * CHUNK + j * UNIT + c * ALL, ALL)[...] = value[
                    :, c * 128 : (c + 1) * 128
                ].astype(BF)
            return carry

        lax.fori_loop(0, 2 if k in (0, 7) else 4, unit, 0)
        if k == 0:
            if remote:
                exchange.await_greetings()
                exchange.stage(0, 0)
            for copy in coming[4:]:
                copy.wait()
            lax.fori_loop(2, 4, unit, 0)
        ones = jnp.ones((16, tokens), BF)
        if k in (0, 1, 4, 5):
            wide = 2 if k == 4 else 4
            first = {0: 28, 1: 32, 4: 36, 5: 38}[k]
            total = nn(ones, held_right[slot, :, : wide * ALL])
            for j in range(wide):
                sums[first + j : first + j + 1, :] = total[0:1, j * ALL : (j + 1) * ALL]
        if k == 7:
            span = nn(held_left[slot, D:, :], held_right[slot, :, ALL:D])
            for c in range(3):
                part[SPAN_ROW + c * 128 : SPAN_ROW + (c + 1) * 128, :] = span[
                    :, c * 128 : (c + 1) * 128
                ].astype(BF)
            sums[42:43, :] = nn(ones, held_right[slot, :, :ALL])[0:1]
            sums[43:44, :128] = nt(ones, held_left[slot, D:, :])[0:1]
            for first, a, b in ((0, stat_a, stat_b), (10, depth_a, depth_b)):
                for i in range(a.shape[0] // 8):
                    both = jnp.sum(a[i * 8 : i * 8 + 8] + b[i * 8 : i * 8 + 8], axis=0, keepdims=True)
                    sums[first + 2 * i : first + 2 * i + 1, :] = both[:, :ALL]
                    sums[first + 2 * i + 1 : first + 2 * i + 2, :] = both[:, ALL:]
            small = sums[...].astype(BF)
            for c in range(3):
                part[SMALL_ROW + c * SMALL : SMALL_ROW + (c + 1) * SMALL, :] = small[
                    :, c * 128 : (c + 1) * 128
                ]
            part[SMALL_ROW + 3 * SMALL :, :] = jnp.zeros((PACKED - SMALL_ROW - 3 * SMALL, 128), BF)

    if remote:
        res, got, *sems = scratch
        exchange = Exchange(part, res, out, got, sems)
        exchange.greet()
    for copy in loads(0):
        copy.start()
    sums[...] = jnp.zeros_like(sums)
    if not remote:
        for k in range(CHUNKS):
            compute(k)
        pltpu.sync_copy(part, out)
        return
    for t in range(CHUNKS + 8):
        if t < CHUNKS:
            compute(t)
        for k in reversed(range(CHUNKS)):
            if 0 <= t - k <= 8:
                first = sum(len(p) for p in CHUNK_PARTS[:k])
                for n in range(first, first + len(CHUNK_PARTS[k])):
                    if (n, t) != (0, 0):
                        exchange.stage(n, t - k)
    exchange.finish()


def weights_call(remote, n_short, n_long, big, small):
    tokens = n_short + n_long
    padded = big[1].shape[0]
    n_parts = len(PARTS)
    scratch = [
        pltpu.VMEM((2, D + 128, tokens), BF),
        pltpu.VMEM((2, tokens, 4 * ALL), BF),
        pltpu.VMEM((SMALL, ALL), F32),
        pltpu.VMEM((PACKED, 128), BF),
        pltpu.SemaphoreType.DMA((2, 6)),
    ]
    if remote:
        scratch += [
            pltpu.VMEM((PACKED, 128), BF),
            pltpu.VMEM((PACKED - PACKED // 32, 128), BF),
            pltpu.SemaphoreType.DMA((n_parts, 12)),
            pltpu.SemaphoreType.DMA((n_parts, 12)),
            pltpu.SemaphoreType.DMA((n_parts,)),
        ]
    more = dict(collective_id=0, has_side_effects=True) if remote else {}
    return pl.pallas_call(
        functools.partial(weights_body, remote, ((0, 0, n_short), (n_short, padded - n_long, n_long))),
        in_specs=[pl.BlockSpec(memory_space=pl.ANY)] * len(big)
        + [pl.BlockSpec(memory_space=pltpu.VMEM)] * len(small),
        out_specs=pl.BlockSpec(memory_space=pl.ANY),
        out_shape=pltpu.VMEM((PACKED, 128), BF) if remote else jax.ShapeDtypeStruct((PACKED, 128), BF),
        scratch_shapes=scratch,
        compiler_params=params("weights", **more),
        cost_estimate=pl.CostEstimate(
            flops=2 * 31 * ALL * ALL * tokens, bytes_accessed=50_000_000, transcendentals=0
        ),
        name="weights",
    )(*fetched(*big, *small))


SMALL_OUTS = [
    ("gain_second", 0, D),
    ("shift_second", 2, D),
    ("gain_first", 4, D),
    ("shift_first", 6, D),
    ("bias_outer", 8, D),
    ("bias_inner", 28, FF),
    ("bias_output", 36, D),
    ("bias_unfold", 38, ALL),
    ("bias_query", 39, ALL),
    ("bias_value", 41, ALL),
    ("bias_point", 42, ALL),
    ("bias_span", 43, TAPS),
]


def unpack_body(block, inner, outer, output, unfold, project, point, span, depth, *small):
    step = pl.program_id(0)

    def tile(unit):
        start = unit * UNIT
        return jnp.concatenate(
            [block[start + c * ALL : start + (c + 1) * ALL, :] for c in range(3)], axis=1
        )

    @pl.when(step < 2)
    def _():
        for i in range(4):
            inner[0, :, i * ALL : (i + 1) * ALL] = tile(i).astype(F32)

    @pl.when((step >= 2) & (step < 4))
    def _():
        for i in range(4):
            outer[0, i * ALL : (i + 1) * ALL, :] = tile(i).T.astype(F32)

    @pl.when(step == 4)
    def _():
        for i in range(4):
            a, b = divmod(i, 2)
            output[a * ALL : (a + 1) * ALL, b * ALL : (b + 1) * ALL] = tile(i).astype(F32)

    @pl.when((step == 5) | (step == 6))
    def _():
        unfold[...] = tile(0).astype(F32)
        for i in range(3):
            project[:, i * ALL : (i + 1) * ALL] = tile(i + 1).astype(F32)

    @pl.when(step == 7)
    def _():
        for i in range(2):
            point[i * ALL : (i + 1) * ALL, :] = tile(i).astype(F32)
        tail = 2 * UNIT
        wide = jnp.concatenate(
            [block[tail + c * 128 : tail + (c + 1) * 128, :] for c in range(3)], axis=1
        )
        span[...] = wide[:TAPS].astype(F32)
        tail += ALL
        rows = jnp.concatenate(
            [block[tail + c * SMALL : tail + (c + 1) * SMALL, :] for c in range(3)], axis=1
        ).astype(F32)
        for j in range(KERNEL):
            for half in range(2):
                place = 10 + 2 * j + half
                depth[j : j + 1, half * ALL : (half + 1) * ALL] = rows[place : place + 1]
        for ref, (_, first, size) in zip(small, SMALL_OUTS):
            for i in range(max(1, size // ALL)):
                wide = min(size, ALL)
                ref[i * ALL : i * ALL + wide] = rows[first + i, :wide]


def unpack_call(packed):
    def at(first, count):
        return lambda s: jnp.clip(s - first, 0, count - 1)

    inner_at, outer_at, rows_at = at(0, 2), at(2, 2), at(5, 2)
    whole = lambda *shape: (shape, pl.BlockSpec(shape, lambda s: (0,) * len(shape)))
    specs = [
        ((GROUPS, ALL, 4 * ALL), pl.BlockSpec((1, ALL, 4 * ALL), lambda s: (inner_at(s), 0, 0))),
        ((GROUPS, 4 * ALL, ALL), pl.BlockSpec((1, 4 * ALL, ALL), lambda s: (outer_at(s), 0, 0))),
        whole(D, D),
        ((D, ALL), pl.BlockSpec((ALL, ALL), lambda s: (rows_at(s), 0))),
        ((D, 3 * ALL), pl.BlockSpec((ALL, 3 * ALL), lambda s: (rows_at(s), 0))),
        whole(D, ALL),
        whole(TAPS, ALL),
        whole(KERNEL, D),
    ]
    specs += [whole(size) for _, _, size in SMALL_OUTS]
    return pl.pallas_call(
        unpack_body,
        grid=(CHUNKS,),
        in_specs=[pl.BlockSpec((CHUNK, 128), lambda s: (s, 0))],
        out_specs=[b for _, b in specs],
        out_shape=[jax.ShapeDtypeStruct(s, F32) for s, _ in specs],
        compiler_params=params("unpack"),
        cost_estimate=pl.CostEstimate(flops=0, bytes_accessed=27_000_000, transcendentals=0),
        name="unpack",
    )(packed)


def shards(
    long_input,
    short_input,
    long_cotan,
    short_cotan,
    live_slots,
    w_project,
    bias_query,
    bias_value,
    depth_kernel,
    w_point,
    bias_point,
    w_span,
    bias_span,
    w_unfold,
    bias_unfold,
    w_output,
    bias_output,
    gain_first,
    shift_first,
    w_inner,
    bias_inner,
    w_outer,
    bias_outer,
    gain_second,
    shift_second,
):
    n_blk = lax.axis_size("blk")
    short_x = short_input.reshape(short_input.shape[2:])
    short_cot = short_cotan.reshape(short_cotan.shape[2:])
    perm, spread = (jnp.asarray(t) for t in tap_tables())
    span_t = w_span.T
    pre_consts = (
        bias_query, bias_value, bias_point, bias_span, bias_unfold, depth_kernel,
        w_project, w_point, span_t, w_unfold, spread, perm,
    )
    ffn_consts = (
        bias_output, gain_first, shift_first, bias_outer, gain_second, shift_second, bias_inner,
        w_output, w_inner, w_outer,
    )
    *short_kept, short_mixed, near, far, both = pre_call(
        [short_x], pre_consts, SHORT_BATCH, (long_input,)
    )
    xs = [long_input, near, far, both]
    *long_kept, long_mixed = pre_call(xs, pre_consts, long_input.shape[0])

    n_long, n_short = (a.shape[0] * a.shape[1] for a in (long_input, short_x))
    tokens = (pl.cdiv(n_short, n_long) + 1) * n_long
    as_long = lambda a: a.reshape(-1, FFN_LONG, D)
    l_out, l_fig, l_mg, *joint, l_stat = ffn_call(
        None, 0, *map(as_long, (long_mixed, long_input, long_cotan)), ffn_consts, (), tokens
    )
    l_out, l_fig, l_mg = (a.reshape(long_input.shape) for a in (l_out, l_fig, l_mg))
    s_out, s_fig, s_mg, left, right, s_stat = ffn_call(
        live_slots,
        short_x.shape[1],
        *(a.reshape(-1, FFN_ROWS, D) for a in (short_mixed, short_x, short_cot)),
        ffn_consts,
        joint,
        tokens,
    )
    s_fig, s_mg = s_fig.reshape(short_x.shape), s_mg.reshape(short_x.shape)
    post_consts = (depth_kernel, w_point, span_t, spread, perm)
    l_post = post_call(xs, l_mg, l_fig, long_kept, post_consts, (), tokens, LONG_BATCH)
    (*joint, l_dkg, own), l_rest = l_post[:4], l_post[4:]
    far, (l_qt, l_ug, l_tg) = l_rest[: n_blk - 1], l_rest[n_blk - 1 :]
    far = [
        lax.ppermute(a, "blk", [(i, i ^ k) for i in range(n_blk)])
        for k, a in enumerate(far, 1)
    ]
    left_post, right_post, s_dkg, short_grad, rows_grad = post_call(
        [short_x], s_mg, s_fig, short_kept, post_consts + (w_project, w_unfold), joint, tokens, SHORT_BATCH
    )
    long_grad, rows_grad = end_call(own, far, l_qt, l_ug, l_tg, w_project, w_unfold, rows_grad)

    remote = lax.axis_size("dp") == 8 and n_blk == 4
    packed = weights_call(
        remote, n_short, n_long, (left, right, left_post, right_post, rows_grad), (l_stat, s_stat, l_dkg, s_dkg)
    )
    if not remote:
        packed = lax.psum(packed, ("dp", "blk"))
    if remote:
        packed = pltpu.with_memory_space_constraint(packed, pltpu.VMEM)
    inner, outer, output, unfold, project, point, span, depth, *small = unpack_call(packed)
    named = {name: value for (name, _, _), value in zip(SMALL_OUTS, small)}
    return (
        l_out,
        s_out.reshape(short_input.shape),
        long_grad,
        short_grad.reshape(short_input.shape),
        project,
        named["bias_query"],
        named["bias_value"],
        depth,
        point,
        named["bias_point"],
        span.T,
        named["bias_span"],
        unfold,
        named["bias_unfold"],
        output,
        named["bias_output"],
        named["gain_first"],
        named["shift_first"],
        inner,
        named["bias_inner"],
        outer,
        named["bias_outer"],
        named["gain_second"],
        named["shift_second"],
    )


def solution(mesh):
    rows = P("dp", "blk", None)
    slots = P("dp", "blk", None, None, None)
    in_specs = (rows, slots, rows, slots, P("dp", "blk")) + (P(),) * 20
    out_specs = (rows, slots, rows, slots) + (P(),) * 20
    return jax.shard_map(shards, mesh=mesh, in_specs=in_specs, out_specs=out_specs, check_vma=False)
```

```python
import functools

import jax
import jax.numpy as jnp
import numpy as np
from jax import lax
from jax.experimental import pallas as pl
from jax.experimental.pallas import tpu as pltpu
from jax.sharding import PartitionSpec as P

D = 768
FF = 3072
HEADS = 6
HEAD = 64
KERNEL = 9
GROUPS = 2
ALL = 384
PAIRS = 3
TAPS = HEADS * KERNEL
HALF = KERNEL // 2

F32 = jnp.float32
BF = jnp.bfloat16
ROOT_HALF = 0.7071067811865476
DENSITY = 0.3989422804014327
FFN_ROWS = 256
FFN_LONG = 384
SHORT_BATCH = 2
LONG_BATCH = 1
VMEM = {
    "pre_short": 58,
    "pre_long": 36,
    "ffn_short": 42,
    "ffn_long": 46,
    "post_short": 46,
    "post_long": 34,
    "end": 34,
    "weights": 48,
    "unpack": 48,
}


def nn(a, b):
    return lax.dot_general(a, b, (((1,), (0,)), ((), ())), preferred_element_type=F32)


def nt(a, b):
    return lax.dot_general(a, b, (((1,), (1,)), ((), ())), preferred_element_type=F32)


def tn(a, b):
    return lax.dot_general(a, b, (((0,), (0,)), ((), ())), preferred_element_type=F32)


def tap_tables():
    perm = np.zeros((128, 128), np.float32)
    spread = np.zeros((256, PAIRS * KERNEL * 128), np.float32)
    for h in range(HEADS):
        for j in range(KERNEL):
            lane = j * HEADS + h
            perm[h * KERNEL + j, lane] = 1
            perm[h * KERNEL + j, TAPS + lane] = 1
            start = ((h // 2) * KERNEL + j) * 128 + (h % 2) * HEAD
            spread[lane, start : start + HEAD] = 1
            spread[128 + lane, start : start + HEAD] = 1
    return perm.astype(jnp.bfloat16), spread.astype(jnp.bfloat16)


def window(values, op):
    left = lambda v, n: pltpu.roll(v, 128 - n, 1)
    one = op(values, left(values, 6))
    two = op(one, left(one, 12))
    four = op(two, left(two, 24))
    return op(four, left(values, 48))


def window_sum(values):
    return window(values + pltpu.roll(values, TAPS, 1), jnp.add)


def head_stack(rows, low_half):
    zero = jnp.zeros_like(rows)
    return jnp.concatenate(
        [jnp.where(low_half, rows, zero), jnp.where(low_half, zero, rows)], axis=0
    )


def two_parts(values):
    high = values.astype(BF)
    rest = (values - high.astype(F32)).astype(BF)
    return jnp.concatenate([high, rest], axis=1)


def row_sides():
    place = lax.axis_index("blk")
    count = lax.axis_size("blk")
    return (place > 0).astype(F32), (place < count - 1).astype(F32), lax.rem(place, 2) == 1


def pick(odd, first, second):
    return jnp.where(odd, first.astype(F32), second.astype(F32))


def row_ends(x_refs, r, sides):
    lower, upper, odd = sides
    rows = x_refs[0].shape[1]
    before = pick(odd, x_refs[1][r, rows - 16 :, :], x_refs[3][r, rows - 16 :, :])
    after = pick(odd, x_refs[3][r, :16, :], x_refs[1][r, :16, :])
    return before * lower, after * upper


def fill_ends(xp, x_refs, sides):
    batch, rows = x_refs[0].shape[:2]
    for r in range(batch):
        if sides is not None:
            before, after = row_ends(x_refs, r, sides)
        for c in range(D // 128):
            cols = slice(c * 128, (c + 1) * 128)
            zero = jnp.zeros((8, 128), F32)
            xp[r, c, 0:8, :] = zero if sides is None else before[8:, cols]
            xp[r, c, 8 + rows : 16 + rows, :] = zero if sides is None else after[:8, cols]
            xp[r, c, 8 : 8 + rows, :] = x_refs[0][r, :, cols].astype(F32)


def as_row(ref):
    return ref[...].astype(F32).reshape(1, ref.shape[0])


class Gather:
    def __init__(self, own, outs, send_sem, recv_sem):
        self.own, self.outs, self.send_sem, self.recv_sem = own, outs, send_sem, recv_sem
        self.rows = own.shape[0]
        dp, blk = lax.axis_index("dp"), lax.axis_index("blk")
        core, x = lax.rem(blk, 2), blk // 2
        self.core_peer = (dp, blk + 1 - 2 * core)
        self.x_peer = (dp, blk + 2 - 4 * x)

    def copy(self, i, r):
        source = self.outs[1] if i == 2 else self.own
        return pltpu.make_async_remote_copy(
            src_ref=source.at[r],
            dst_ref=self.outs[i].at[r],
            send_sem=self.send_sem.at[i, r],
            recv_sem=self.recv_sem.at[i, r],
            device_id=self.x_peer if i == 1 else self.core_peer,
            device_id_type=pl.DeviceIdType.MESH,
        )

    def begin(self):
        barrier = pltpu.get_barrier_semaphore()
        for device in (self.core_peer, self.x_peer):
            pl.semaphore_signal(
                barrier, inc=1, device_id=device, device_id_type=pl.DeviceIdType.MESH
            )
        pl.semaphore_wait(barrier, 2)
        for i in (1, 0):
            for r in range(self.rows):
                self.copy(i, r).start()

    def forward(self, r):
        self.copy(1, r).wait_recv()
        self.copy(2, r).start()

    def end(self):
        for r in range(self.rows):
            for i in (0, 2):
                self.copy(i, r).wait_recv()
            for i in range(3):
                self.copy(i, r).wait_send()


def pre_body(n_x, *refs):
    gather = None
    if n_x == 1:
        own, *refs = refs
        gather = Gather(own, refs[22:25], *refs[-2:])
        refs = refs[:22] + refs[25:-2]
    x_refs, refs = refs[:n_x], refs[n_x:]
    bias_query, bias_value, bias_point, bias_span, bias_unfold, depth_kernel = refs[:6]
    w_project, w_point, w_span, w_unfold, spread, perm = refs[6:12]
    q_out, k_out, v_out, p_out, kc_out, ker_out, dl_out, up_out, mix_out = refs[12:21]
    xp, vec = refs[21:]

    @pl.when(pl.program_id(0) == 0)
    def _():
        vec[16:24, :] = jnp.zeros((8, D), F32)
        vec[0:1, :ALL] = as_row(bias_query)
        vec[0:1, ALL:] = as_row(bias_value)
        vec[1:2, :ALL] = as_row(bias_point)
        vec[1:2, ALL:] = as_row(bias_unfold)
        vec[21:22, :TAPS] = as_row(bias_span)
        vec[8:17, :] = depth_kernel[...].astype(F32)
        if gather:
            gather.begin()

    if gather:

        @pl.when(pl.program_id(0) == pl.num_programs(0) - 1)
        def _():
            for r in range(gather.rows - 1):
                gather.forward(r)

    batch, rows = x_refs[0].shape[:2]
    total_rows = batch * rows
    is_long = n_x > 1
    sides = row_sides() if is_long else None
    x = x_refs[0][...].reshape(total_rows, D)
    fill_ends(xp, x_refs, sides)
    bias_query = vec[0:1, :ALL]
    bias_value = vec[0:1, ALL:]
    by_row = lambda v: v.reshape(batch, rows, v.shape[-1])
    if is_long:
        q = (nn(x, w_project[:, :ALL]) + bias_query).astype(BF)
        for i in range(n_x):
            both = nn(x_refs[i][...].reshape(total_rows, D), w_project[:, ALL:])
            k_out[:, i * rows : (i + 1) * rows, :] = by_row(both[:, :ALL].astype(BF))
            v_out[:, i * rows : (i + 1) * rows, :] = by_row((both[:, ALL:] + bias_value).astype(BF))
    else:
        both = nn(x, w_project[...])
        q = (both[:, :ALL] + bias_query).astype(BF)
        k_out[...] = by_row(both[:, ALL : 2 * ALL].astype(BF))
        v_out[...] = by_row((both[:, 2 * ALL :] + bias_value).astype(BF))
    q_out[...] = by_row(q)

    for r in range(batch):
        for c in range(D // 128):
            cols = slice(c * 128, (c + 1) * 128)
            total = vec[8:9, cols] * xp[r, c, 4 : 4 + rows, :]
            for j in range(1, KERNEL):
                total += vec[8 + j : 9 + j, cols] * xp[r, c, 4 + j : 4 + j + rows, :]
            dl_out[r, :, cols] = total.astype(BF)
    key_conv = nn(dl_out[...].reshape(total_rows, D), w_point[...]) + vec[1:2, :ALL]
    kc_out[...] = by_row(key_conv)
    span = (key_conv * q.astype(F32)).astype(BF)
    span_weights = tn(w_span[...], perm[:TAPS, :]).astype(BF)
    span_bias = nn(vec[16:24, :128].astype(BF), perm[...])[5:6]
    logits = nn(span, span_weights) + span_bias
    lane = lax.broadcasted_iota(jnp.int32, (1, 128), 1)
    raised = jnp.where(lane < TAPS, jnp.exp(logits - window(logits, jnp.maximum)), 0.0)
    kernel = jnp.where(lane < TAPS, raised / window_sum(raised), 0.0)
    ker_out[...] = by_row(kernel)

    bias_unfold = vec[1:2, ALL:]
    unfold_rows = nn(x, w_unfold[...]) + bias_unfold
    for r in range(batch):
        if is_long:
            lower, upper, _ = sides
            ends = jnp.concatenate(row_ends(x_refs, r, sides), axis=0).astype(BF)
            unfold_ends = nn(ends, w_unfold[...]) + bias_unfold
        for c in range(PAIRS):
            cols = slice(c * 128, (c + 1) * 128)
            up_out[r, c, 8 : 8 + rows, :] = unfold_rows[r * rows : (r + 1) * rows, cols]
            if is_long:
                up_out[r, c, 0:8, :] = unfold_ends[8:16, cols] * lower
                up_out[r, c, 8 + rows : 16 + rows, :] = unfold_ends[16:24, cols] * upper
            else:
                zero = jnp.zeros((8, 128), F32)
                up_out[r, c, 0:8, :] = zero
                up_out[r, c, 8 + rows : 16 + rows, :] = zero

    if gather:

        @pl.when(pl.program_id(0) == pl.num_programs(0) - 1)
        def _():
            gather.forward(gather.rows - 1)

    low_half = lane < HEAD
    parts = two_parts(kernel)
    scaled = q * jnp.asarray(HEAD ** (-0.5), BF)
    keys = k_out.shape[1]
    for p in range(PAIRS):
        cols = slice(p * 128, (p + 1) * 128)
        wide = nn(parts, spread[:, p * KERNEL * 128 : (p + 1) * KERNEL * 128])
        for r in range(batch):
            here = slice(r * rows, (r + 1) * rows)
            total = wide[here, :128] * up_out[r, p, 4 : 4 + rows, :]
            for j in range(1, KERNEL):
                total += wide[here, j * 128 : (j + 1) * 128] * up_out[r, p, 4 + j : 4 + j + rows, :]
            mix_out[r, :, ALL + p * 128 : ALL + (p + 1) * 128] = total.astype(BF)

            scores = nt(head_stack(k_out[r, :, cols], low_half), scaled[here, cols])
            for half in range(2):
                part = scores[half * keys : (half + 1) * keys]
                top = jnp.max(part, axis=0, keepdims=True)
                grown = jnp.exp(part - top)
                share = 1.0 / jnp.sum(grown, axis=0, keepdims=True)
                p_out[r, p, half * keys : (half + 1) * keys, :] = (grown * share).astype(BF)
            context = tn(head_stack(v_out[r, :, cols], low_half), p_out[r, p])
            mix_out[r, :, cols] = context.astype(BF).T

    if gather:

        @pl.when(pl.program_id(0) == pl.num_programs(0) - 1)
        def _():
            gather.end()


def fixed(array):
    zeros = (0,) * array.ndim
    return pl.BlockSpec(array.shape, lambda *_: zeros, pipeline_mode=pl.Buffered(1))


def per_row(*shape, batch=1):
    zeros = (0,) * len(shape)
    return pl.BlockSpec((batch, *shape), lambda i: (i, *zeros))


def in_vmem(shape, dtype):
    return pltpu.VMEM(shape, dtype)


def held(*arrays):
    return [pltpu.with_memory_space_constraint(a, pltpu.VMEM) for a in arrays]


def fetched(*arrays):
    return [pltpu.with_memory_space_constraint(a, pltpu.HBM) for a in arrays]


def params(name, **more):
    return pltpu.CompilerParams(vmem_limit_bytes=VMEM[name] * 1024 * 1024, **more)


def pre_call(xs, consts, batch, gathered=()):
    anywhere = pl.BlockSpec(memory_space=pl.ANY)
    count, rows = xs[0].shape[0], xs[0].shape[1]
    keys = rows * len(xs)
    shapes = [
        ((rows, ALL), BF),
        ((keys, ALL), BF),
        ((keys, ALL), BF),
        ((PAIRS, 2 * keys, rows), BF),
        ((rows, ALL), F32),
        ((rows, 128), F32),
        ((rows, D), BF),
        ((PAIRS, rows + 16, 128), F32),
        ((rows, D), BF),
    ]
    return pl.pallas_call(
        functools.partial(pre_body, len(xs)),
        grid=(count // batch,),
        in_specs=[anywhere] * len(gathered)
        + [per_row(rows, D, batch=batch)] * len(xs) + [fixed(c) for c in consts],
        out_specs=[per_row(*s, batch=batch) for s, _ in shapes] + [anywhere] * (3 * len(gathered)),
        out_shape=[
            (in_vmem if not gathered or i == 8 else pltpu.HBM)((count, *s), t)
            for i, (s, t) in enumerate(shapes)
        ]
        + [in_vmem(g.shape, g.dtype) for g in gathered] * 3,
        scratch_shapes=[pltpu.VMEM((batch, D // 128, rows + 16, 128), F32), pltpu.VMEM((24, D), F32)]
        + [pltpu.SemaphoreType.DMA((3, g.shape[0])) for g in gathered for _ in range(2)],
        compiler_params=params("pre_short", collective_id=1, has_side_effects=True)
        if gathered
        else params("pre_long"),
        cost_estimate=pl.CostEstimate(
            flops=count * rows * 6_000_000, bytes_accessed=20_000_000, transcendentals=1_000_000
        ),
        name="pre_long" if len(xs) > 1 else "pre_short",
    )(*fetched(*gathered, xs[0]), *held(*xs[1:]), *fetched(*consts))


def norm_stats(z):
    centre = z - jnp.mean(z, axis=-1, keepdims=True)
    inverse = lax.rsqrt(jnp.mean(centre * centre, axis=-1, keepdims=True) + 1e-12)
    return centre * inverse, inverse


def norm_back(upstream, normed, inverse, gain):
    scaled = upstream * gain
    plain = jnp.mean(scaled, axis=-1, keepdims=True)
    cross = jnp.mean(scaled * normed, axis=-1, keepdims=True)
    return inverse * (scaled - plain - normed * cross)


def fold8(values):
    return jnp.sum(values.reshape(values.shape[0] // 8, 8, values.shape[1]), axis=0)


def gelu_pair(v):
    cdf = 0.5 * (1.0 + lax.erf(v * ROOT_HALF))
    return v * cdf, cdf + v * jnp.exp(-0.5 * (v * v)) * DENSITY


def ffn_body(slot_rows, *refs):
    masked = slot_rows > 0
    if masked:
        live_ref, *refs = refs
    mix_ref, x_ref, cot_ref = refs[:3]
    vectors, (w_output, w_inner, w_outer) = refs[3:10], refs[10:13]
    out_ref, fig_ref, mg_ref, left, right, stat, slope, vec = refs[-8:]
    inl_ref, act_ref = right.at[:, :FF], right.at[:, FF : 2 * FF]
    step = pl.program_id(0)
    rows = x_ref.shape[1]

    @pl.when(step == 0)
    def _():
        stat[...] = jnp.zeros_like(stat)
        for i, ref in enumerate(vectors[:-1]):
            vec[2 + i : 3 + i, :] = as_row(ref)
        inner_row = as_row(vectors[-1])
        for i in range(FF // D):
            vec[8 + i : 9 + i, :] = inner_row[:, i * D : (i + 1) * D]

    x = x_ref[0]
    mixed = mix_ref[0]
    left[2 * D : 3 * D, :] = mixed.T
    left[3 * D :, :] = x.T
    first_normed, first_inverse = norm_stats(nn(mixed, w_output[...]) + vec[2:3, :] + x.astype(F32))
    first_norm = first_normed * vec[3:4, :] + vec[4:5, :]
    first_low = first_norm.astype(BF)
    left[:D, :] = first_low.T
    outer = []
    for g in range(GROUPS):
        for c in range(2):
            k = g * 2 + c
            inner = nn(first_low[:, g * ALL : (g + 1) * ALL], w_inner[g, :, c * D : (c + 1) * D])
            for r in range(0, rows, 16):
                act, slo = gelu_pair(inner[r : r + 16] + vec[8 + k : 9 + k, :])
                act_ref[r : r + 16, k * D : (k + 1) * D] = act.astype(BF)
                slope[r : r + 16, k * D : (k + 1) * D] = slo
        outer.append(nn(act_ref[:, g * 2 * D : (g + 1) * 2 * D], w_outer[g]))
    second_normed, second_inverse = norm_stats(
        jnp.concatenate(outer, axis=1) + vec[5:6, :] + first_norm
    )
    gain_second = vec[6:7, :]
    out_ref[0] = (second_normed * gain_second + vec[7:8, :]).astype(BF)
    seed = cot_ref[0].astype(F32)
    if masked:
        token = step * rows + lax.broadcasted_iota(jnp.int32, (rows, 1), 0)
        seed = jnp.where(token < live_ref[0, 0] * slot_rows, seed, 0.0)
    stat[0:8, :] += fold8(seed * second_normed)
    stat[8:16, :] += fold8(seed)
    second_grad = norm_back(seed, second_normed, second_inverse, gain_second)
    outer_low = second_grad.astype(BF)
    left[D : 2 * D, :] = outer_low.T
    stat[32:40, :] += fold8(outer_low.astype(F32))
    first_grad = []
    for g in range(GROUPS):
        for c in range(2):
            k = g * 2 + c
            back = nt(outer_low[:, g * ALL : (g + 1) * ALL], w_outer[g, c * D : (c + 1) * D, :])
            inl_ref[:, k * D : (k + 1) * D] = (back * slope[:, k * D : (k + 1) * D]).astype(BF)
        first_grad.append(nt(inl_ref[:, g * 2 * D : (g + 1) * 2 * D], w_inner[g]))
    first_grad = second_grad + jnp.concatenate(first_grad, axis=1)
    stat[16:24, :] += fold8(first_grad * first_normed)
    stat[24:32, :] += fold8(first_grad)
    first_in_grad = norm_back(first_grad, first_normed, first_inverse, vec[3:4, :])
    fig_ref[0] = first_in_grad
    attended_low = first_in_grad.astype(BF)
    right[:, 2 * FF :] = attended_low
    mg_ref[0] = nt(attended_low, w_output[...]).astype(BF)


def ffn_call(live, slot_rows, mixed, x, cotan, consts, joint, tokens):
    count, rows = x.shape[0], x.shape[1]
    total = count * rows
    masked = live is not None
    first = 0 if masked else (tokens - total) // rows
    n_in = (4 if masked else 3) + len(consts)
    out_shapes = [
        ((count, rows, D), BF, per_row(rows, D)),
        ((count, rows, D), F32, per_row(rows, D)),
        ((count, rows, D), BF, per_row(rows, D)),
        ((4 * D, tokens), BF, pl.BlockSpec((4 * D, rows), lambda i: (0, first + i))),
        ((tokens, 2 * FF + D), BF, pl.BlockSpec((rows, 2 * FF + D), lambda i: (first + i, 0))),
        ((40, D), F32, pl.BlockSpec((40, D), lambda i: (0, 0))),
    ]
    head = [live] if masked else []
    head_specs = [pl.BlockSpec(memory_space=pltpu.SMEM)] if masked else []
    return pl.pallas_call(
        functools.partial(ffn_body, slot_rows if masked else 0),
        grid=(count,),
        in_specs=head_specs
        + [per_row(rows, D)] * 3
        + [fixed(c) for c in consts]
        + [pl.BlockSpec(memory_space=pl.ANY)] * len(joint),
        out_specs=[s for _, _, s in out_shapes],
        out_shape=[
            (in_vmem if i in (1, 2) else pltpu.HBM)(s, t)
            for i, (s, t, _) in enumerate(out_shapes)
        ],
        scratch_shapes=[pltpu.VMEM((rows, FF), F32), pltpu.VMEM((16, D), F32)],
        input_output_aliases={n_in: 3, n_in + 1: 4} if masked else {},
        compiler_params=params("ffn_short" if masked else "ffn_long"),
        cost_estimate=pl.CostEstimate(
            flops=total * 12_000_000, bytes_accessed=30_000_000, transcendentals=total * FF
        ),
        name="ffn_short" if masked else "ffn_long",
    )(*head, *held(mixed), *fetched(x, cotan, *consts, *joint))


def post_body(n_x, *refs):
    is_long = n_x > 1
    x_refs = refs[:n_x]
    refs = refs[n_x:]
    (mg_ref, fig_ref, q_ref, k_ref, v_ref, p_ref, kc_ref, ker_ref, dl_ref, up_ref) = refs[:10]
    (depth_kernel, w_point, w_span, spread, perm) = refs[10:15]
    refs = refs[15:]
    if not is_long:
        (w_project, w_unfold), refs = refs[:2], refs[4:]
    (left, right, dkg), refs = refs[:3], refs[3:]
    if is_long:
        own_out, *far_outs = refs[:n_x]
        qt_out, ug_out, tg_out = refs[n_x : n_x + 3]
        xp, dgp, prp, dq_scr = refs[n_x + 3 :]
    else:
        tg_out, ru_out, dgp, prp, dq_scr = refs
    step = pl.program_id(0)
    batch, rows = x_refs[0].shape[:2]
    total_rows = batch * rows
    keys = k_ref.shape[1]
    ext = 8 if is_long else 0
    flat = lambda ref: ref[...].reshape(total_rows, ref.shape[-1])

    @pl.when(step == 0)
    def _():
        dkg[...] = jnp.zeros_like(dkg)
        dgp[...] = jnp.zeros_like(dgp)
        prp[...] = jnp.zeros_like(prp)

    if is_long:
        sides = lower, upper, odd = row_sides()
        fill_ends(xp, x_refs, sides)

        def send_rims(r, place, cols, total):
            before, after = total[:ext] * lower, total[ext + rows :] * upper
            far_outs[0][r, place : place + 8, cols] = pick(odd, before, after).astype(BF)
            far_outs[2][r, place : place + 8, cols] = pick(odd, after, before).astype(BF)


    q = flat(q_ref)
    qf = q.astype(F32)
    scaled = q * jnp.asarray(HEAD ** (-0.5), BF)
    low_half = lax.broadcasted_iota(jnp.int32, (1, 128), 1) < HEAD
    for p in range(PAIRS):
        cols = slice(p * 128, (p + 1) * 128)
        for r in range(batch):
            here = slice(r * rows, (r + 1) * rows)
            grad = mg_ref[r, :, cols]
            weight_grad = nt(head_stack(v_ref[r, :, cols], low_half), grad)
            low = []
            for half in range(2):
                part = slice(half * keys, (half + 1) * keys)
                probs = p_ref[r, p, part, :].astype(F32)
                inner = jnp.sum(probs * weight_grad[part], axis=0, keepdims=True)
                low.append((probs * (weight_grad[part] - inner)).astype(BF))
            score_low = jnp.concatenate(low, axis=0)
            value_grad = nn(p_ref[r, p], grad)
            value_grad = jnp.where(low_half, value_grad[:keys], value_grad[keys:])
            key_grad = nn(score_low, scaled[here, cols])
            key_grad = jnp.where(low_half, key_grad[:keys], key_grad[keys:])
            query_grad = tn(head_stack(k_ref[r, :, cols], low_half), score_low) * HEAD ** (-0.5)
            dq_scr[here, cols] = query_grad.T
            v_cols = slice(ALL + p * 128, ALL + (p + 1) * 128)
            if is_long:
                own_out[r, :, cols] = key_grad[:rows]
                own_out[r, :, v_cols] = value_grad[:rows]
                for i in range(1, n_x):
                    block = slice(i * rows, (i + 1) * rows)
                    far_outs[i - 1][r, :rows, cols] = key_grad[block].astype(BF)
                    far_outs[i - 1][r, :rows, v_cols] = value_grad[block].astype(BF)
            else:
                ru_out[here, 2 * ALL + p * 128 : 2 * ALL + (p + 1) * 128] = key_grad.astype(BF)
                ru_out[here, 3 * ALL + p * 128 : 3 * ALL + (p + 1) * 128] = value_grad.astype(BF)

    kernel = flat(ker_ref)
    parts = two_parts(kernel)
    kernel_grad = jnp.zeros((total_rows, 128), F32)
    span_rows = rows + 2 * ext
    for p in range(PAIRS):
        cols = slice(p * 128, (p + 1) * 128)
        table = slice(p * KERNEL * 128, (p + 1) * KERNEL * 128)
        wide = nn(parts, spread[:, table])
        all_products = []
        for r in range(batch):
            here = slice(r * rows, (r + 1) * rows)
            grad = mg_ref[r, :, ALL + p * 128 : ALL + (p + 1) * 128].astype(F32)
            products = []
            for j in range(KERNEL):
                products.append((grad * up_ref[r, p, 4 + j : 4 + j + rows, :]).astype(BF))
                prp[r, j, 16 : 16 + rows, :] = wide[here, j * 128 : (j + 1) * 128] * grad
            all_products.append(jnp.concatenate(products, axis=1))
            first = 20 - ext
            total = prp[r, 0, first : first + span_rows, :]
            for j in range(1, KERNEL):
                total += prp[r, j, first - j : first - j + span_rows, :]
            if is_long:
                ug_out[r, :, cols] = total[ext : ext + rows]
                send_rims(r, rows + 8, cols, total)
            else:
                ru_out[here, cols] = total.astype(BF)
        kernel_grad += nt(jnp.concatenate(all_products, axis=0), spread[:128, table])
    if is_long:
        zero = jnp.zeros((batch, 8, ALL), BF)
        far_outs[0][:, rows + 8 : rows + 16, ALL:] = zero
        far_outs[-1][:, rows + 8 : rows + 16, ALL:] = zero

    logit_low = (kernel * (kernel_grad - window_sum(kernel * kernel_grad))).astype(BF)
    left[D:, :] = nt(perm[...], logit_low).astype(BF)
    span_grad = nn(logit_low, tn(perm[:TAPS, :], w_span[...]).astype(BF))
    key_conv = flat(kc_ref)
    right[:, ALL:] = (key_conv * qf).astype(BF)
    left[:D, :] = flat(dl_ref).T
    point_low = (span_grad * qf).astype(BF)
    right[:, :ALL] = point_low
    query_total = (dq_scr[...] + span_grad * key_conv).astype(BF)
    depth_grad = nt(point_low, w_point[...])
    for r in range(batch):
        for c in range(D // 128):
            dgp[r, c, 16 : 16 + rows, :] = depth_grad[
                r * rows : (r + 1) * rows, c * 128 : (c + 1) * 128
            ]

    if not is_long:
        ru_out[:, ALL : 2 * ALL] = query_total
        base = nt(ru_out[:, :ALL], w_unfold[...]) + nt(ru_out[:, ALL:], w_project[...])
    else:
        qt_out[...] = query_total.reshape(batch, rows, ALL)
    for c in range(D // 128):
        cols = slice(c * 128, (c + 1) * 128)
        for r in range(batch):
            x_part = xp[r, c] if is_long else x_refs[0][r, :, cols].astype(F32)
            first = 20 - ext
            total = None
            for j in range(KERNEL):
                moved = dgp[r, c, first - j : first - j + span_rows, :]
                term = depth_kernel[j : j + 1, cols].astype(F32) * moved
                total = term if total is None else total + term
                dkg[j * 8 : (j + 1) * 8, cols] += fold8(moved * x_part)
            if is_long:
                tg_out[r, :, cols] = total[ext : ext + rows] + fig_ref[r, :, cols]
                send_rims(r, rows, cols, total)
            else:
                tg_out[r, :, cols] = total + fig_ref[r, :, cols] + base[r * rows : (r + 1) * rows, cols]


def post_call(xs, mg, fig, kept, consts, joint, tokens, batch):
    count, rows = xs[0].shape[0], xs[0].shape[1]
    keys = rows * len(xs)
    total = count * rows
    is_long = len(xs) > 1
    wide = batch * rows
    first = (tokens - total) // wide if is_long else 0
    row_args = [mg, fig, *kept]
    outs = [
        ((D + 128, tokens), BF, pl.BlockSpec((D + 128, wide), lambda i: (0, first + i))),
        ((tokens, 2 * ALL), BF, pl.BlockSpec((wide, 2 * ALL), lambda i: (first + i, 0))),
        ((KERNEL * 8, D), F32, pl.BlockSpec((KERNEL * 8, D), lambda i: (0, 0))),
    ]
    row_out = lambda r, c, t: ((count, r, c), t, per_row(r, c, batch=batch))
    scratch = []
    if is_long:
        outs.append(row_out(rows, D, F32))
        for i in range(1, len(xs)):
            outs.append(row_out(rows + 16 if i in (1, len(xs) - 1) else rows, D, BF))
        outs += [row_out(rows, ALL, BF), row_out(rows, ALL, F32), row_out(rows, D, F32)]
        scratch.append(pltpu.VMEM((batch, D // 128, rows + 16, 128), F32))
    else:
        outs += [
            row_out(rows, D, F32),
            ((tokens, 4 * ALL), BF, pl.BlockSpec((wide, 4 * ALL), lambda i: (first + i, 0))),
        ]
    scratch += [
        pltpu.VMEM((batch, D // 128, rows + 32, 128), F32),
        pltpu.VMEM((batch, KERNEL, rows + 32, 128), F32),
        pltpu.VMEM((wide, ALL), F32),
    ]
    row_args = held(*row_args) if is_long else held(mg, fig) + fetched(*row_args[2:])
    inputs = [*fetched(xs[0]), *held(*xs[1:]), *row_args, *fetched(*consts)]
    return pl.pallas_call(
        functools.partial(post_body, len(xs)),
        grid=(count // batch,),
        in_specs=[per_row(rows, D, batch=batch)] * len(xs)
        + [per_row(*a.shape[1:], batch=batch) for a in row_args]
        + [fixed(c) for c in consts]
        + [pl.BlockSpec(memory_space=pl.ANY)] * len(joint),
        out_specs=[s for _, _, s in outs],
        out_shape=[
            (in_vmem if is_long and i in (3, 7, 8, 9) else pltpu.HBM)(s, t)
            for i, (s, t, _) in enumerate(outs)
        ],
        scratch_shapes=scratch,
        input_output_aliases={len(inputs) + i: i for i in range(len(joint))},
        compiler_params=params("post_long" if is_long else "post_short"),
        cost_estimate=pl.CostEstimate(
            flops=total * 10_000_000, bytes_accessed=30_000_000, transcendentals=0
        ),
        name="post_long" if is_long else "post_short",
    )(*inputs, *fetched(*joint))


def end_body(n_x, *refs):
    own, *rest = refs[:n_x]
    qt, ug, tg, w_project, w_unfold, _, out_ref, ru_out = refs[n_x:]
    rows = own.shape[1]
    both = own[0]
    for far in rest:
        both = both + far[0, :rows, :].astype(F32)
    _, _, odd = row_sides()
    unfold = ug[0]
    after = pick(odd, rest[2][0, rows:, :], rest[0][0, rows:, :])
    before = pick(odd, rest[0][0, rows:, :], rest[2][0, rows:, :])
    middle = unfold[8 : rows - 8]
    ru_out[:, :ALL] = jnp.concatenate(
        [unfold[:8] + before[8:, :ALL], middle, unfold[rows - 8 :] + after[8:, :ALL]], axis=0
    ).astype(BF)
    ru_out[:, ALL : 2 * ALL] = qt[0]
    ru_out[:, 2 * ALL :] = both.astype(BF)
    total = nt(ru_out[:, :ALL], w_unfold[...]) + nt(ru_out[:, ALL:], w_project[...]) + tg[0]
    out_ref[0] = total
    out_ref[0, :8, :] = total[:8] + before[:8]
    out_ref[0, rows - 8 :, :] = total[rows - 8 :] + after[:8]


def end_call(own, far, qt, ug, tg, w_project, w_unfold, joint):
    count, rows = own.shape[0], own.shape[1]
    first = (joint.shape[0] - count * rows) // rows
    (own,), (qt, ug, tg) = held(own), held(qt, ug, tg)
    row_args = [own, *held(*far), qt, ug, tg]
    return pl.pallas_call(
        functools.partial(end_body, 1 + len(far)),
        grid=(count,),
        in_specs=[per_row(*a.shape[1:]) for a in row_args]
        + [fixed(w_project), fixed(w_unfold), pl.BlockSpec(memory_space=pl.ANY)],
        out_specs=[per_row(rows, D), pl.BlockSpec((rows, 4 * ALL), lambda i: (first + i, 0))],
        out_shape=[
            jax.ShapeDtypeStruct((count, rows, D), F32),
            jax.ShapeDtypeStruct(joint.shape, BF),
        ],
        input_output_aliases={len(row_args) + 2: 1},
        compiler_params=params("end"),
        cost_estimate=pl.CostEstimate(
            flops=count * rows * 2_400_000, bytes_accessed=10_000_000, transcendentals=0
        ),
        name="end_long",
    )(*row_args, *fetched(w_project, w_unfold, joint))


UNIT = 3 * ALL
CHUNK = 4 * UNIT
CHUNKS = 8
LAST = 6 * 512
PACKED = (CHUNKS - 1) * CHUNK + LAST
SPAN_ROW = (CHUNKS - 1) * CHUNK + 2 * UNIT
SMALL_ROW = SPAN_ROW + ALL
SMALL = 48
MESH = pl.DeviceIdType.MESH


CHUNK_PARTS = (
    ((0, 2048, "cyxz"), (2048, 2560, "cxyz")),
    ((4608, 2560, "cxyz"), (7168, 2048, "cyxz")),
    ((9216, 3072, "cxyz"), (12288, 1536, "cyxz")),
    ((13824, 1536, "cyxz"), (15360, 3072, "cxyz")),
    ((18432, 2048, "cyxz"), (20480, 2560, "cxyz")),
    ((23040, 2048, "cxyz"), (25088, 2048, "cyzx"), (27136, 512, "czyx")),
    ((27648, 2560, "cxyz"), (30208, 2048, "cyzx")),
    ((32256, 1536, "cxyz"), (33792, 1024, "cyzx"), (34816, 512, "cxyz")),
)
PARTS = sum(CHUNK_PARTS, ())


def rows_of(ref, start, count):
    return ref.at[pl.ds(pl.multiple_of(start, 16), count), :]


def add_rows(out, start, sources, count):
    step = next(s for s in (160, 128, 96, 80, 64, 48, 32, 16) if count % s == 0)

    def body(i, carry):
        total = None
        for ref, first in sources:
            value = rows_of(ref, first + i * step, step)[...].astype(F32)
            total = value if total is None else total + value
        rows_of(out, start + i * step, step)[...] = total.astype(BF)
        return carry

    lax.fori_loop(0, count // step, body, 0)


class Exchange:
    def __init__(self, source, res, out, got, sems):
        self.source, self.res, self.out, self.got = source, res, out, got
        self.send_sem, self.recv_sem, self.out_sem = sems
        dp, blk = lax.axis_index("dp"), lax.axis_index("blk")
        core, x, y, z = lax.rem(blk, 2), blk // 2, lax.rem(dp, 2), dp // 2
        self.index = {"c": core, "x": x, "y": y, "z": z}
        self.peers = {
            "c": [(dp, blk + 1 - 2 * core)],
            "x": [(dp, blk + 2 - 4 * x)],
            "y": [(dp + 1 - 2 * y, blk)],
            "z": [(lax.rem(z + i, 4) * 2 + y, blk) for i in (1, 2, 3)],
        }
        self.sizes, self.slots, self.places = [], [], []
        used = 0
        for _, count, order in PARTS:
            sizes, slots, places = [count], [0], []
            for axis in order:
                sizes.append(sizes[-1] // (len(self.peers[axis]) + 1))
                slots.append(slots[-1] + len(self.peers[axis]))
                places.append(used)
                used += sizes[-1] * len(self.peers[axis])
            self.sizes.append(sizes)
            self.slots.append(slots)
            self.places.append(places)

    def greet(self):
        barrier = pltpu.get_barrier_semaphore()
        for devices in self.peers.values():
            for device in devices:
                pl.semaphore_signal(barrier, inc=1, device_id=device, device_id_type=MESH)

    def await_greetings(self):
        pl.semaphore_wait(pltpu.get_barrier_semaphore(), 6)

    def sum_at(self, n, level):
        return (self.source, PARTS[n][0]) if level == 0 else (self.got, self.places[n][level - 1])

    def held(self, n, level):
        row, _, order = PARTS[n]
        for i in range(level):
            row = row + self.index[order[i]] * self.sizes[n][i + 1]
        return row

    def copies(self, n, level, back):
        axis = PARTS[n][2][level]
        size = self.sizes[n][level + 1]
        result = []
        for i, device in enumerate(self.peers[axis]):
            if back:
                source = target = rows_of(self.res, self.held(n, level + 1), size)
            else:
                ref, first = self.sum_at(n, level)
                theirs = lax.rem(self.index[axis] + i + 1, len(self.peers[axis]) + 1)
                source = rows_of(ref, first + theirs * size, size)
                target = rows_of(self.got, self.places[n][level] + i * size, size)
            slot = self.slots[n][level] + i + (6 if back else 0)
            result.append(
                pltpu.make_async_remote_copy(
                    src_ref=source,
                    dst_ref=target,
                    send_sem=self.send_sem.at[n, slot],
                    recv_sem=self.recv_sem.at[n, slot],
                    device_id=device,
                    device_id_type=MESH,
                )
            )
        return result

    def copy_out(self, n):
        row, count, _ = PARTS[n]
        return pltpu.make_async_copy(
            rows_of(self.res, row, count), rows_of(self.out, row, count), self.out_sem.at[n]
        )

    def stage(self, n, s):
        if s:
            for copy in self.copies(n, s - 1 if s <= 4 else 8 - s, s > 4):
                copy.wait_recv()
        if 1 <= s <= 4:
            level = s - 1
            axis = PARTS[n][2][level]
            size = self.sizes[n][s]
            ref, first = self.sum_at(n, level)
            terms = [(ref, first + self.index[axis] * size)]
            terms += [
                (self.got, self.places[n][level] + i * size) for i in range(len(self.peers[axis]))
            ]
            into, start = self.sum_at(n, s) if s < 4 else (self.res, self.held(n, 4))
            add_rows(into, start, terms, size)
        if s < 8:
            for copy in self.copies(n, s if s < 4 else 7 - s, s >= 4):
                copy.start()
        else:
            self.copy_out(n).start()

    def finish(self):
        for n in range(len(PARTS)):
            for level in range(4):
                for back in (False, True):
                    for copy in self.copies(n, level, back):
                        copy.wait_send()
            self.copy_out(n).wait()


def weights_body(remote, ranges, *refs):
    left, right, left_post, right_post, rows_grad, stat_a, stat_b, depth_a, depth_b, out = refs[:10]
    held_left, held_right, sums, part, load_sem = refs[10:15]
    scratch = refs[15:]
    tokens = held_left.shape[2]

    def loads(k):
        slot = k % 2
        if k < 4:
            a, a_rows, b, b_cols = left, (k * ALL, ALL), right, (k * 4 * ALL, 4 * ALL)
        elif k == 4:
            a, a_rows, b, b_cols = left, (2 * D, D), right, (2 * FF, D)
        elif k < 7:
            a, a_rows, b, b_cols = left, (3 * D + (k - 5) * ALL, ALL), rows_grad, (0, 4 * ALL)
        else:
            a, a_rows, b, b_cols = left_post, (0, D + 128), right_post, (0, D)
        copies = []
        halves = 2 if k == 0 else 1
        cols = b_cols[1] // halves
        for half in range(halves):
            for i, (to, start, size) in enumerate(ranges):
                here, there = pl.ds(to, size), pl.ds(start, size)
                if half == 0:
                    copies.append(
                        pltpu.make_async_copy(
                            a.at[pl.ds(*a_rows), there],
                            held_left.at[slot, : a_rows[1], here],
                            load_sem.at[slot, i],
                        )
                    )
                copies.append(
                    pltpu.make_async_copy(
                        b.at[there, pl.ds(b_cols[0] + half * cols, cols)],
                        held_right.at[slot, here, half * cols : (half + 1) * cols],
                        load_sem.at[slot, 2 + 2 * half + i],
                    )
                )
        return copies

    def compute(k):
        coming = loads(k)
        for copy in coming[:4]:
            copy.wait()
        if k + 1 < CHUNKS:
            for copy in loads(k + 1):
                copy.start()
        slot = k % 2
        by_left = {4: 2, 7: 1}.get(k, 4)

        def unit(j, carry):
            if by_left == 4:
                a, b = 0, j
            elif by_left == 2:
                a, b = j // 2, lax.rem(j, 2)
            else:
                a, b = j, 0
            lhs = held_left[slot, pl.ds(pl.multiple_of(a * ALL, ALL), ALL), :]
            rhs = held_right[slot, :, pl.ds(pl.multiple_of(b * ALL, ALL), ALL)]
            value = nn(lhs, rhs)
            for c in range(3):
                rows_of(part, k * CHUNK + j * UNIT + c * ALL, ALL)[...] = value[
                    :, c * 128 : (c + 1) * 128
                ].astype(BF)
            return carry

        lax.fori_loop(0, 2 if k in (0, 7) else 4, unit, 0)
        if k == 0:
            if remote:
                exchange.await_greetings()
                exchange.stage(0, 0)
            for copy in coming[4:]:
                copy.wait()
            lax.fori_loop(2, 4, unit, 0)
        ones = jnp.ones((16, tokens), BF)
        if k in (0, 1, 4, 5):
            wide = 2 if k == 4 else 4
            first = {0: 28, 1: 32, 4: 36, 5: 38}[k]
            total = nn(ones, held_right[slot, :, : wide * ALL])
            for j in range(wide):
                sums[first + j : first + j + 1, :] = total[0:1, j * ALL : (j + 1) * ALL]
        if k == 7:
            span = nn(held_left[slot, D:, :], held_right[slot, :, ALL:D])
            for c in range(3):
                part[SPAN_ROW + c * 128 : SPAN_ROW + (c + 1) * 128, :] = span[
                    :, c * 128 : (c + 1) * 128
                ].astype(BF)
            sums[42:43, :] = nn(ones, held_right[slot, :, :ALL])[0:1]
            sums[43:44, :128] = nt(ones, held_left[slot, D:, :])[0:1]
            for first, a, b in ((0, stat_a, stat_b), (10, depth_a, depth_b)):
                for i in range(a.shape[0] // 8):
                    both = jnp.sum(a[i * 8 : i * 8 + 8] + b[i * 8 : i * 8 + 8], axis=0, keepdims=True)
                    sums[first + 2 * i : first + 2 * i + 1, :] = both[:, :ALL]
                    sums[first + 2 * i + 1 : first + 2 * i + 2, :] = both[:, ALL:]
            small = sums[...].astype(BF)
            for c in range(3):
                part[SMALL_ROW + c * SMALL : SMALL_ROW + (c + 1) * SMALL, :] = small[
                    :, c * 128 : (c + 1) * 128
                ]
            part[SMALL_ROW + 3 * SMALL :, :] = jnp.zeros((PACKED - SMALL_ROW - 3 * SMALL, 128), BF)

    if remote:
        res, got, *sems = scratch
        exchange = Exchange(part, res, out, got, sems)
        exchange.greet()
    for copy in loads(0):
        copy.start()
    sums[...] = jnp.zeros_like(sums)
    if not remote:
        for k in range(CHUNKS):
            compute(k)
        pltpu.sync_copy(part, out)
        return
    for t in range(CHUNKS + 8):
        if t < CHUNKS:
            compute(t)
        for k in reversed(range(CHUNKS)):
            if 0 <= t - k <= 8:
                first = sum(len(p) for p in CHUNK_PARTS[:k])
                for n in range(first, first + len(CHUNK_PARTS[k])):
                    if (n, t) != (0, 0):
                        exchange.stage(n, t - k)
    exchange.finish()


def weights_call(remote, n_short, n_long, big, small):
    tokens = n_short + n_long
    padded = big[1].shape[0]
    n_parts = len(PARTS)
    scratch = [
        pltpu.VMEM((2, D + 128, tokens), BF),
        pltpu.VMEM((2, tokens, 4 * ALL), BF),
        pltpu.VMEM((SMALL, ALL), F32),
        pltpu.VMEM((PACKED, 128), BF),
        pltpu.SemaphoreType.DMA((2, 6)),
    ]
    if remote:
        scratch += [
            pltpu.VMEM((PACKED, 128), BF),
            pltpu.VMEM((PACKED - PACKED // 32, 128), BF),
            pltpu.SemaphoreType.DMA((n_parts, 12)),
            pltpu.SemaphoreType.DMA((n_parts, 12)),
            pltpu.SemaphoreType.DMA((n_parts,)),
        ]
    more = dict(collective_id=0, has_side_effects=True) if remote else {}
    return pl.pallas_call(
        functools.partial(weights_body, remote, ((0, 0, n_short), (n_short, padded - n_long, n_long))),
        in_specs=[pl.BlockSpec(memory_space=pl.ANY)] * len(big)
        + [pl.BlockSpec(memory_space=pltpu.VMEM)] * len(small),
        out_specs=pl.BlockSpec(memory_space=pl.ANY),
        out_shape=pltpu.VMEM((PACKED, 128), BF) if remote else jax.ShapeDtypeStruct((PACKED, 128), BF),
        scratch_shapes=scratch,
        compiler_params=params("weights", **more),
        cost_estimate=pl.CostEstimate(
            flops=2 * 31 * ALL * ALL * tokens, bytes_accessed=50_000_000, transcendentals=0
        ),
        name="weights",
    )(*fetched(*big, *small))


SMALL_OUTS = [
    ("gain_second", 0, D),
    ("shift_second", 2, D),
    ("gain_first", 4, D),
    ("shift_first", 6, D),
    ("bias_outer", 8, D),
    ("bias_inner", 28, FF),
    ("bias_output", 36, D),
    ("bias_unfold", 38, ALL),
    ("bias_query", 39, ALL),
    ("bias_value", 41, ALL),
    ("bias_point", 42, ALL),
    ("bias_span", 43, TAPS),
]


def unpack_body(block, inner, outer, output, unfold, project, point, span, depth, *small):
    step = pl.program_id(0)

    def tile(unit):
        start = unit * UNIT
        return jnp.concatenate(
            [block[start + c * ALL : start + (c + 1) * ALL, :] for c in range(3)], axis=1
        )

    @pl.when(step < 2)
    def _():
        for i in range(4):
            inner[0, :, i * ALL : (i + 1) * ALL] = tile(i).astype(F32)

    @pl.when((step >= 2) & (step < 4))
    def _():
        for i in range(4):
            outer[0, i * ALL : (i + 1) * ALL, :] = tile(i).T.astype(F32)

    @pl.when(step == 4)
    def _():
        for i in range(4):
            a, b = divmod(i, 2)
            output[a * ALL : (a + 1) * ALL, b * ALL : (b + 1) * ALL] = tile(i).astype(F32)

    @pl.when((step == 5) | (step == 6))
    def _():
        unfold[...] = tile(0).astype(F32)
        for i in range(3):
            project[:, i * ALL : (i + 1) * ALL] = tile(i + 1).astype(F32)

    @pl.when(step == 7)
    def _():
        for i in range(2):
            point[i * ALL : (i + 1) * ALL, :] = tile(i).astype(F32)
        tail = 2 * UNIT
        wide = jnp.concatenate(
            [block[tail + c * 128 : tail + (c + 1) * 128, :] for c in range(3)], axis=1
        )
        span[...] = wide[:TAPS].astype(F32)
        tail += ALL
        rows = jnp.concatenate(
            [block[tail + c * SMALL : tail + (c + 1) * SMALL, :] for c in range(3)], axis=1
        ).astype(F32)
        for j in range(KERNEL):
            for half in range(2):
                place = 10 + 2 * j + half
                depth[j : j + 1, half * ALL : (half + 1) * ALL] = rows[place : place + 1]
        for ref, (_, first, size) in zip(small, SMALL_OUTS):
            for i in range(max(1, size // ALL)):
                wide = min(size, ALL)
                ref[i * ALL : i * ALL + wide] = rows[first + i, :wide]


def unpack_call(packed):
    def at(first, count):
        return lambda s: jnp.clip(s - first, 0, count - 1)

    inner_at, outer_at, rows_at = at(0, 2), at(2, 2), at(5, 2)
    whole = lambda *shape: (shape, pl.BlockSpec(shape, lambda s: (0,) * len(shape)))
    specs = [
        ((GROUPS, ALL, 4 * ALL), pl.BlockSpec((1, ALL, 4 * ALL), lambda s: (inner_at(s), 0, 0))),
        ((GROUPS, 4 * ALL, ALL), pl.BlockSpec((1, 4 * ALL, ALL), lambda s: (outer_at(s), 0, 0))),
        whole(D, D),
        ((D, ALL), pl.BlockSpec((ALL, ALL), lambda s: (rows_at(s), 0))),
        ((D, 3 * ALL), pl.BlockSpec((ALL, 3 * ALL), lambda s: (rows_at(s), 0))),
        whole(D, ALL),
        whole(TAPS, ALL),
        whole(KERNEL, D),
    ]
    specs += [whole(size) for _, _, size in SMALL_OUTS]
    return pl.pallas_call(
        unpack_body,
        grid=(CHUNKS,),
        in_specs=[pl.BlockSpec((CHUNK, 128), lambda s: (s, 0))],
        out_specs=[b for _, b in specs],
        out_shape=[jax.ShapeDtypeStruct(s, F32) for s, _ in specs],
        compiler_params=params("unpack"),
        cost_estimate=pl.CostEstimate(flops=0, bytes_accessed=27_000_000, transcendentals=0),
        name="unpack",
    )(packed)


def shards(
    long_input,
    short_input,
    long_cotan,
    short_cotan,
    live_slots,
    w_project,
    bias_query,
    bias_value,
    depth_kernel,
    w_point,
    bias_point,
    w_span,
    bias_span,
    w_unfold,
    bias_unfold,
    w_output,
    bias_output,
    gain_first,
    shift_first,
    w_inner,
    bias_inner,
    w_outer,
    bias_outer,
    gain_second,
    shift_second,
):
    n_blk = lax.axis_size("blk")
    short_x = short_input.reshape(short_input.shape[2:])
    short_cot = short_cotan.reshape(short_cotan.shape[2:])
    perm, spread = (jnp.asarray(t) for t in tap_tables())
    span_t = w_span.T
    pre_consts = (
        bias_query, bias_value, bias_point, bias_span, bias_unfold, depth_kernel,
        w_project, w_point, span_t, w_unfold, spread, perm,
    )
    ffn_consts = (
        bias_output, gain_first, shift_first, bias_outer, gain_second, shift_second, bias_inner,
        w_output, w_inner, w_outer,
    )
    *short_kept, short_mixed, near, far, both = pre_call(
        [short_x], pre_consts, SHORT_BATCH, (long_input,)
    )
    xs = [long_input, near, far, both]
    *long_kept, long_mixed = pre_call(xs, pre_consts, long_input.shape[0])

    n_long, n_short = (a.shape[0] * a.shape[1] for a in (long_input, short_x))
    tokens = (pl.cdiv(n_short, n_long) + 1) * n_long
    as_long = lambda a: a.reshape(-1, FFN_LONG, D)
    l_out, l_fig, l_mg, *joint, l_stat = ffn_call(
        None, 0, *map(as_long, (long_mixed, long_input, long_cotan)), ffn_consts, (), tokens
    )
    l_out, l_fig, l_mg = (a.reshape(long_input.shape) for a in (l_out, l_fig, l_mg))
    s_out, s_fig, s_mg, left, right, s_stat = ffn_call(
        live_slots,
        short_x.shape[1],
        *(a.reshape(-1, FFN_ROWS, D) for a in (short_mixed, short_x, short_cot)),
        ffn_consts,
        joint,
        tokens,
    )
    s_fig, s_mg = s_fig.reshape(short_x.shape), s_mg.reshape(short_x.shape)
    post_consts = (depth_kernel, w_point, span_t, spread, perm)
    l_post = post_call(xs, l_mg, l_fig, long_kept, post_consts, (), tokens, LONG_BATCH)
    (*joint, l_dkg, own), l_rest = l_post[:4], l_post[4:]
    far, (l_qt, l_ug, l_tg) = l_rest[: n_blk - 1], l_rest[n_blk - 1 :]
    far = [
        lax.ppermute(a, "blk", [(i, i ^ k) for i in range(n_blk)])
        for k, a in enumerate(far, 1)
    ]
    left_post, right_post, s_dkg, short_grad, rows_grad = post_call(
        [short_x], s_mg, s_fig, short_kept, post_consts + (w_project, w_unfold), joint, tokens, SHORT_BATCH
    )
    long_grad, rows_grad = end_call(own, far, l_qt, l_ug, l_tg, w_project, w_unfold, rows_grad)

    remote = lax.axis_size("dp") == 8 and n_blk == 4
    packed = weights_call(
        remote, n_short, n_long, (left, right, left_post, right_post, rows_grad), (l_stat, s_stat, l_dkg, s_dkg)
    )
    if not remote:
        packed = lax.psum(packed, ("dp", "blk"))
    if remote:
        packed = pltpu.with_memory_space_constraint(packed, pltpu.VMEM)
    inner, outer, output, unfold, project, point, span, depth, *small = unpack_call(packed)
    named = {name: value for (name, _, _), value in zip(SMALL_OUTS, small)}
    return (
        l_out,
        s_out.reshape(short_input.shape),
        long_grad,
        short_grad.reshape(short_input.shape),
        project,
        named["bias_query"],
        named["bias_value"],
        depth,
        point,
        named["bias_point"],
        span.T,
        named["bias_span"],
        unfold,
        named["bias_unfold"],
        output,
        named["bias_output"],
        named["gain_first"],
        named["shift_first"],
        inner,
        named["bias_inner"],
        outer,
        named["bias_outer"],
        named["gain_second"],
        named["shift_second"],
    )


def solution(mesh):
    rows = P("dp", "blk", None)
    slots = P("dp", "blk", None, None, None)
    in_specs = (rows, slots, rows, slots, P("dp", "blk")) + (P(),) * 20
    out_specs = (rows, slots, rows, slots) + (P(),) * 20
    return jax.shard_map(shards, mesh=mesh, in_specs=in_specs, out_specs=out_specs, check_vma=False)
```
